32 devices in a mesh: dp: 8 (over z, y), expert: 4 (over x, core).
Axes of the slice: x: 2, y: 2, z: 4, core: 2. Of those that a mesh axis runs over, the one named last changes fastest.
Arguments:
- tokens: bfloat16 [24, 1024, 384], P('expert', 'dp'), may hold values from -36 to 36
- cotangent: bfloat16 [24, 1024, 384], P('expert', 'dp'), may hold values from -6 to 6
- lengths: int32 [24], P('expert'), may hold values from 128 to 1024, as said below
- routes: int32 [8, 4, 768, 2], P('dp', 'expert'), may hold values from 0 to 7, all different within a row; in each aligned block of 768 rows (0 to 767, 768 to 1535, ..., all dimensions but the last counted through in order) at most 384 rows name the same one
- dense_weights: float32 [2363520], P(('dp', 'expert')), may hold values from -0.8164966 to 1.4
- dense_first: float32 [2363520], P(('dp', 'expert')), may hold values from -940.60406 to 940.60406
- dense_second: float32 [2363520], P(('dp', 'expert')), may hold values from 0 to 393216, as said below
- dense_average: float32 [2363520], P(('dp', 'expert')), may hold values from -0.8164966 to 1.4
- expert_weights: float32 [8, 1769472], P('expert', 'dp'), may hold values from -0.4082483 to 0.4082483
- expert_first: float32 [8, 1769472], P('expert', 'dp'), may hold values from -156.767344 to 156.767344
- expert_second: float32 [8, 1769472], P('expert', 'dp'), may hold values from 0 to 24576, as said below
- expert_average: float32 [8, 1769472], P('expert', 'dp'), may hold values from -0.4082483 to 0.4082483
Outputs:
- output: bfloat16 [24, 1024, 384], P('expert', 'dp')
- grad_tokens: float32 [24, 1024, 384], P('expert', 'dp')
- dense_grad: float32 [2363520], P(('dp', 'expert'))
- dense_first_new: float32 [2363520], P(('dp', 'expert'))
- dense_second_new: float32 [2363520], P(('dp', 'expert'))
- dense_new: float32 [2363520], P(('dp', 'expert'))
- dense_average_new: float32 [2363520], P(('dp', 'expert'))
- expert_grad: float32 [8, 1769472], P('expert', 'dp')
- expert_first_new: float32 [8, 1769472], P('expert', 'dp')
- expert_second_new: float32 [8, 1769472], P('expert', 'dp')
- expert_new: float32 [8, 1769472], P('expert', 'dp')
- expert_average_new: float32 [8, 1769472], P('expert', 'dp')
The draws below stay inside these ranges and needn't reach their ends.
Inputs may be any that keep to these rules, and one draw needn't show every extreme that they name: Series lengths run from an eighth of 1024 to 1024, the positions beyond a series' length padding; some series fills its slot. `routes`: among the positions of one device no expert is named more than 384 times. `dense_second`: positive. `expert_second`: positive.
All inputs are finite; a program needn't handle non-finite values.
Results may differ from the reference program's by a relative error of at most 0.017.
The reference program's roundings to bfloat16 on the way count: a program that leaves them out, or rounds other values in their place, can miss the bound.
Values may be sent and summed in bfloat16 or wider, within the bound.
A program may use at most 256 MiB of HBM per device.

```python
import math
import jax
import jax.numpy as jnp
import numpy as np
from jax import lax

D = 384
HEADS = 12
HEAD_DIM = 32
FF = 1536
EXPERTS = 8
TOP = 2
SEG = 128
SERIES_DEV = 6
STEP = 8
LEN = 1024
SERIES = 24
TOK_DEV = 768
TOKENS = 24576
CAP = 384
P_DENSE = 2363520
P_EXP = 1769472
N_DP = 8
N_EXPERT = 4


def draw_tokens(key, part):
    key = jax.random.fold_in(key, 3)
    key_base, key_rows, key_columns = jax.random.split(key, 3)
    full_shape = (SERIES, LEN, D)
    base = jnp.clip(jax.random.normal(key_base, full_shape, jnp.float32), -4.0, 4.0)
    row_scale = jnp.exp(jax.random.uniform(key_rows, (SERIES, LEN, 1), jnp.float32, math.log(0.3), math.log(3.0)))
    column_scale = jnp.exp(jax.random.uniform(key_columns, (1, 1, D), jnp.float32, math.log(0.3), math.log(3.0)))
    return (base * row_scale * column_scale).astype(jnp.bfloat16)


def draw_lengths(key, part):
    key = jax.random.fold_in(key, 5)
    key_level, key_extra, key_full = jax.random.split(key, 3)
    level = jax.random.randint(key_level, (SERIES,), 0, 4)
    shortest = jnp.right_shift(jnp.full((SERIES,), LEN, jnp.int32), level)
    extra = jax.random.randint(key_extra, (SERIES,), 0, 1024)
    length_drawn = jnp.minimum(shortest + shortest * extra // 1024, LEN)
    full_series = jax.random.randint(key_full, (), 0, SERIES)
    return jnp.where(jnp.arange(SERIES) == full_series, LEN, length_drawn).astype(jnp.int32)


def segment_table(entries):
    return jnp.concatenate([jnp.full((extent,), factor, jnp.float32) for extent, factor in entries])


def dense_table(factors):
    column_widths = [D, D, D, D, EXPERTS, FF, FF, FF, 1, 1, 1]
    row_factors = segment_table(list(zip(column_widths, factors)))
    return jnp.broadcast_to(row_factors[None, :], (D, row_factors.shape[0])).reshape(-1)


def dense_spread():
    root_width = D ** (-0.5)
    root_hidden = FF ** (-0.5)
    return dense_table([1.4 * root_width, 1.4 * root_width, root_width, 4.0 * root_width, 0.75 * root_width, root_width, root_width, 2.0 * root_hidden, root_width, 0.1, 0.1])


def dense_center():
    return dense_table([0.0, 0.0, 0.0, 0.0, 0.0, 0.0, 0.0, 0.0, 0.0, 1.0, 1.0])


def dense_gradient():
    tokens_root = math.sqrt(TOKENS * 0.6)
    return tokens_root * dense_table([0.5, 0.5, 1.0, 0.3, 0.2, 0.3, 0.3, 0.2, 2.0, 0.5, 0.5])


def expert_spread():
    return segment_table([(D * FF, D ** (-0.5)), (D * FF, D ** (-0.5)), (FF * D, 2.0 * FF ** (-0.5))])[None, :]


def expert_gradient():
    rows_root = math.sqrt(TOKENS * TOP / EXPERTS * 0.6)
    return rows_root * segment_table([(D * FF, 0.1), (D * FF, 0.1), (FF * D, 0.06)])[None, :]


def dense_values(key):
    noise = jnp.clip(jax.random.normal(key, (P_DENSE,), jnp.float32), -4.0, 4.0)
    return dense_center() + dense_spread() * noise


def expert_values(key):
    noise = jnp.clip(jax.random.normal(key, (EXPERTS, P_EXP), jnp.float32), -4.0, 4.0)
    return expert_spread() * noise


def draw_dense_weights(key, part):
    key = jax.random.fold_in(key, 21)
    return dense_values(key)


def draw_dense_average(key, part):
    key = jax.random.fold_in(key, 22)
    return dense_values(key)


def draw_dense_first(key, part):
    key = jax.random.fold_in(key, 23)
    return dense_gradient() * jnp.clip(jax.random.normal(key, (P_DENSE,), jnp.float32), -3.0, 3.0)


def draw_dense_second(key, part):
    key = jax.random.fold_in(key, 24)
    spread = jnp.exp(jax.random.uniform(key, (P_DENSE,), jnp.float32, 0.0, math.log(4.0)))
    return dense_gradient() * dense_gradient() * spread


def draw_expert_weights(key, part):
    key = jax.random.fold_in(key, 31)
    return expert_values(key)


def draw_expert_average(key, part):
    key = jax.random.fold_in(key, 32)
    return expert_values(key)


def draw_expert_first(key, part):
    key = jax.random.fold_in(key, 33)
    return expert_gradient() * jnp.clip(jax.random.normal(key, (EXPERTS, P_EXP), jnp.float32), -3.0, 3.0)


def draw_expert_second(key, part):
    key = jax.random.fold_in(key, 34)
    spread = jnp.exp(jax.random.uniform(key, (EXPERTS, P_EXP), jnp.float32, 0.0, math.log(4.0)))
    return expert_gradient() * expert_gradient() * spread


def level_of(own_key, shape, cuts, least, top_value):
    def one(position, parts):
        steps = jax.random.uniform(jax.random.fold_in(jax.random.fold_in(own_key, 6), position), (parts,), jnp.float32, least / len(cuts), top_value / len(cuts))
        return jnp.repeat(jnp.exp(steps), shape[position] // parts).reshape((-1,) + (1,) * (len(shape) - position - 1))

    level = one(*cuts[0])
    for cut in cuts[1:]:
        level = level * one(*cut)
    return level


def assign_block(key, own, number, rows, amount, top, limit, lean):
    ranking = jax.random.permutation(key, amount)
    crowded, usual = shares(amount, rows * top, limit, lean, True), shares(amount, rows * top, limit, lean, False)
    places = jnp.arange(amount)

    def named(sizes, turn):
        used = int((sizes > 0).sum())
        fixed = max(1, used // 4)
        shifted = fixed + (places - fixed + turn * (used - fixed)) % max(1, amount - fixed)
        return jnp.zeros((amount,), jnp.int32).at[ranking[jnp.where(places < fixed, places, shifted)]].set(jnp.asarray(sizes, jnp.int32))

    sizes = jnp.where(number % 4 == 0, named(crowded, number // 4), named(usual, number - number // 4 - 1))
    mixed = jax.random.permutation(jax.random.fold_in(own, 3), amount)
    donor, sink = mixed[0:amount // 2 * 2:2], mixed[1:amount // 2 * 2:2]
    slack = jnp.minimum(sizes[donor] - 1, limit - sizes[sink]) // 2
    slack = jnp.where((donor == ranking[0]) | (sink == ranking[0]) | (sizes[sink] == 0), 0, jnp.maximum(slack, 0))
    shifted = jax.random.randint(jax.random.fold_in(own, 4), (amount // 2,), 0, 1 << 20) % (slack + 1)
    sizes = sizes.at[donor].add(-shifted).at[sink].add(shifted)
    members = jnp.searchsorted(jnp.cumsum(sizes), jnp.arange(rows * top), side="right").astype(jnp.int32)
    listing = members.reshape(top, rows).T
    listing = listing[jax.random.permutation(jax.random.fold_in(own, 1), rows)]
    turn = jax.random.randint(jax.random.fold_in(own, 2), (rows, 1), 0, top)
    return jnp.take_along_axis(listing, (jnp.arange(top)[None, :] + turn) % top, axis=1)


def shares(count, total, bound, lean, full):
    loads = [(1 << 20) // math.isqrt(grade ** lean) + 1 for grade in range(1, count + 1)]
    largest = bound if full else min(bound, max(-(-total // count), total * loads[0] // sum(loads)))
    least = 1 if total - largest >= count - 1 else 0
    counts, surplus = [largest] + [least] * (count - 1), total - largest - least * (count - 1)
    while surplus > 0:
        movable = [i for i in range(1, count) if counts[i] < largest] or [i for i in range(1, count) if counts[i] < bound]
        mass, remaining = sum([loads[i] for i in movable]), surplus
        for i in movable:
            more = min(bound - counts[i], max(1, remaining * loads[i] // mass), surplus)
            counts[i] = counts[i] + more
            surplus = surplus - more
    return np.array(counts)


def bell_draw(key, dims, scale, reach, shards=(), kind=jnp.bfloat16):
    level = level_of(key, dims, shards, -0.22, 0.18) if shards else 1.0
    values = jax.random.normal(key, dims, jnp.float32) * scale * level
    return jnp.minimum(jnp.maximum(values, -reach), reach).astype(kind)


def setup_inputs(seed: int = 0) -> dict:
    streams_of = jax.random.split(jax.random.key(seed), 13)
    tokens = draw_tokens(jax.random.fold_in(streams_of[12], 71), 0)
    cotangent = bell_draw(streams_of[1], (SERIES, LEN, D), 1.0, 6.0, ((0, 4), (1, 8)))
    lengths = draw_lengths(jax.random.fold_in(streams_of[12], 71), 0)
    routes_keys = jax.random.split(jax.random.fold_in(streams_of[3], 1), N_DP * N_EXPERT * TOK_DEV // TOK_DEV)
    routes_turns = jax.random.permutation(jax.random.fold_in(streams_of[3], 3), N_DP * N_EXPERT * TOK_DEV // TOK_DEV)
    routes = jax.vmap(lambda own, number: assign_block(jax.random.fold_in(streams_of[3], 2), own, number, TOK_DEV, EXPERTS, TOP, CAP, 1))(routes_keys, routes_turns).reshape((N_DP, N_EXPERT, TOK_DEV, TOP))
    dense_weights = draw_dense_weights(jax.random.fold_in(streams_of[12], 71), 0)
    dense_first = draw_dense_first(jax.random.fold_in(streams_of[12], 71), 0)
    dense_second = draw_dense_second(jax.random.fold_in(streams_of[12], 71), 0)
    dense_average = draw_dense_average(jax.random.fold_in(streams_of[12], 71), 0)
    expert_weights = draw_expert_weights(jax.random.fold_in(streams_of[12], 71), 0)
    expert_first = draw_expert_first(jax.random.fold_in(streams_of[12], 71), 0)
    expert_second = draw_expert_second(jax.random.fold_in(streams_of[12], 71), 0)
    expert_average = draw_expert_average(jax.random.fold_in(streams_of[12], 71), 0)
    return {"tokens": tokens, "cotangent": cotangent, "lengths": lengths, "routes": routes, "dense_weights": dense_weights, "dense_first": dense_first, "dense_second": dense_second, "dense_average": dense_average, "expert_weights": expert_weights, "expert_first": expert_first, "expert_second": expert_second, "expert_average": expert_average}


eps_norm = 1e-06
beta_one = 0.5
beta_two = 0.5
learn_rate = 0.02
weight_decay = 0.1
eps_adam = 1e-08
average_keep = 0.9
rope_base = 10000.0
neg_fill = -1e+30
highest = lax.Precision.HIGHEST

@jax.custom_vjp
def low(v):
    return lax.optimization_barrier(v.astype(jnp.bfloat16)).astype(jnp.float32)

@jax.custom_vjp
def low_back(v):
    return v

def low_keep(v):
    return (low(v), None)

def low_pass(kept, grad):
    return (grad,)

def back_keep(v):
    return (v, None)

def back_low(kept, grad):
    return (low(grad),)
low.defvjp(low_keep, low_pass)
low_back.defvjp(back_keep, back_low)

def matmul(left, right):
    return jnp.einsum('...d,df->...f', left, right, precision=highest)

def rms_scale(values, gain):
    return values * lax.rsqrt(lax.optimization_barrier(jnp.mean(values * values, axis=-1, keepdims=True)) + eps_norm) * gain

def rotate(values, positions, direction):
    half_dim = HEAD_DIM // 2
    inverse = rope_base ** (-jnp.arange(half_dim, dtype=jnp.float32) * 2.0 / HEAD_DIM)
    angles = positions.astype(jnp.float32)[:, None] * inverse[None, :]
    cosine = jnp.cos(angles)[:, None, :]
    sine = jnp.sin(angles)[:, None, :] * direction
    first = values[..., :half_dim]
    second = values[..., half_dim:]
    return jnp.concatenate([first * cosine - second * sine, second * cosine + first * sine], axis=-1)

def dense_pieces(flat_params):
    row_width = 4 * D + EXPERTS + 3 * FF + 3
    row_table = flat_params.reshape(D, row_width)
    column_widths = [D, D, D, D, EXPERTS, FF, FF, FF, 1, 1, 1]
    pieces = []
    offset = 0
    for column_width in column_widths:
        pieces.append(row_table[:, offset:offset + column_width])
        offset = offset + column_width
    w_query, w_key, w_value, w_output, w_router, w_sgate, w_sup = pieces[:7]
    w_sdown = pieces[7].T
    return [w_query, w_key, w_value, w_output, w_router, w_sgate, w_sup, w_sdown, pieces[8][:, 0], pieces[9][:, 0], pieces[10][:, 0]]

def expert_pieces(flat_params):
    first_end = D * FF
    gate_part = flat_params[:, :first_end].reshape(-1, D, FF)
    up_part = flat_params[:, first_end:2 * first_end].reshape(-1, D, FF)
    down_part = flat_params[:, 2 * first_end:].reshape(-1, FF, D)
    return (gate_part, up_part, down_part)

def to_devices(values):
    trailing = values.shape[2:]
    grouped = values.reshape((N_EXPERT, SERIES_DEV, N_DP, SEG) + trailing)
    return jnp.moveaxis(grouped, 2, 0).reshape((N_DP * N_EXPERT, SERIES_DEV * SEG) + trailing)

def from_devices(values):
    trailing = values.shape[2:]
    grouped = values.reshape((N_DP, N_EXPERT, SERIES_DEV, SEG) + trailing)
    return jnp.moveaxis(grouped, 0, 2).reshape((N_EXPERT * SERIES_DEV, N_DP * SEG) + trailing)

def expert_ffn(items):
    expert_rows, gate_matrix, up_matrix, down_matrix = items
    gate_lin = low_back(matmul(expert_rows, gate_matrix))
    up_lin = low_back(matmul(expert_rows, up_matrix))
    hidden = low(jax.nn.silu(gate_lin) * up_lin)
    return low_back(low(matmul(hidden, down_matrix)))

def adamw_update(weights, grads, first, second, average):
    first_new = beta_one * first + (1.0 - beta_one) * grads
    second_new = beta_two * second + (1.0 - beta_two) * grads * grads
    first_hat = first_new / (1.0 - beta_one ** STEP)
    second_hat = second_new / (1.0 - beta_two ** STEP)
    weights_new = weights - learn_rate * (first_hat / (jnp.sqrt(second_hat) + eps_adam) + weight_decay * weights)
    average_new = average_keep * average + (1.0 - average_keep) * weights_new
    return (first_new, second_new, weights_new, average_new)

def reference(tokens, cotangent, lengths, routes, dense_weights, dense_first, dense_second, dense_average, expert_weights, expert_first, expert_second, expert_average):
    devices_all = N_DP * N_EXPERT
    positions = jnp.arange(LEN, dtype=jnp.int32)
    live = (positions[None, :] < lengths[:, None]).astype(jnp.float32)
    routes_flat = routes.reshape(devices_all, TOK_DEV * TOP)
    chosen = (routes_flat[..., None] == jnp.arange(EXPERTS, dtype=jnp.int32)).astype(jnp.int32)
    slot_index = lax.optimization_barrier(jnp.sum((jnp.cumsum(chosen, axis=1).astype(jnp.int32) - chosen) * chosen, axis=-1)).astype(jnp.int32)
    device_index = jnp.arange(devices_all, dtype=jnp.int32)[:, None]
    targets = (routes_flat * (devices_all * CAP) + device_index * CAP + slot_index).astype(jnp.int32).reshape(-1)
    chosen_float = chosen.reshape(devices_all, TOK_DEV, TOP, EXPERTS).astype(jnp.float32)

    def forward(residual, dense_flat, expert_flat):
        w_query, w_key, w_value, w_output, w_router, w_sgate, w_sup, w_sdown, w_svec, gain_one, gain_two = dense_pieces(dense_flat)
        e_gate, e_up, e_down = expert_pieces(expert_flat)

        def attend(items):
            series_in, series_length = items
            act_one = low(rms_scale(series_in, gain_one))
            query_lin = low_back(matmul(act_one, w_query)).reshape(LEN, HEADS, HEAD_DIM)
            key_lin = low_back(matmul(act_one, w_key)).reshape(LEN, HEADS, HEAD_DIM)
            value_low = low(low_back(matmul(act_one, w_value))).reshape(LEN, HEADS, HEAD_DIM)
            query_rot = low(rotate(query_lin, positions, 1.0))
            key_rot = low(rotate(key_lin, positions, 1.0))
            scores = low_back(jnp.einsum('qhd,khd->hqk', query_rot, key_rot, precision=highest) * HEAD_DIM ** (-0.5))
            allowed = (positions[None, :] <= positions[:, None]) & (positions[None, :] < series_length)
            attn_probs = low(jax.nn.softmax(jnp.where(allowed[None], scores, neg_fill), axis=-1))
            heads_out = jnp.einsum('hqk,khd->qhd', attn_probs, value_low, precision=highest)
            attn_low = low(low_back(heads_out.reshape(LEN, D)))
            return series_in + low_back(matmul(attn_low, w_output))
        mixed_all = lax.map(jax.checkpoint(attend), (residual, lengths))
        mixed_rows = to_devices(mixed_all)
        act_two = low(rms_scale(mixed_rows, gain_two))
        logits_low = low_back(matmul(act_two, w_router))
        router_probs = jax.nn.softmax(logits_low, axis=-1)
        route_gates = lax.optimization_barrier(jnp.sum(router_probs[:, :, None, :] * chosen_float, axis=-1))
        dispatched = jnp.repeat(act_two, TOP, axis=1).reshape(-1, D)
        buffer = jnp.zeros((EXPERTS * devices_all * CAP, D), jnp.float32).at[targets].set(dispatched)
        buffer = low_back(buffer)
        results = lax.map(jax.checkpoint(expert_ffn), (buffer.reshape(EXPERTS, devices_all * CAP, D), e_gate, e_up, e_down))
        picked = results.reshape(-1, D)[targets].reshape(devices_all, TOK_DEV, TOP, D)
        routed = lax.optimization_barrier(jnp.sum(route_gates[..., None] * picked, axis=2))
        sgate_lin = low_back(matmul(act_two, w_sgate))
        sup_lin = low_back(matmul(act_two, w_sup))
        shared_hidden = low(jax.nn.silu(sgate_lin) * sup_lin)
        shared_lin = low_back(matmul(shared_hidden, w_sdown))
        shared_gate = jax.nn.sigmoid(low_back(matmul(act_two, w_svec[:, None])))
        return from_devices(mixed_rows + routed + shared_gate * shared_lin)
    dense_low = low(dense_weights)
    expert_low = low(expert_weights)
    result, pullback = jax.vjp(forward, tokens.astype(jnp.float32), dense_low, expert_low)
    grad_tokens, dense_grad, expert_grad = pullback(cotangent.astype(jnp.float32) * live[..., None])
    dense_first_new, dense_second_new, dense_new, dense_average_new = adamw_update(dense_weights, dense_grad, dense_first, dense_second, dense_average)
    expert_first_new, expert_second_new, expert_new, expert_average_new = adamw_update(expert_weights, expert_grad, expert_first, expert_second, expert_average)
    return (result.astype(jnp.bfloat16), grad_tokens, dense_grad, dense_first_new, dense_second_new, dense_new, dense_average_new, expert_grad, expert_first_new, expert_second_new, expert_new, expert_average_new)
```

```python
import functools
import math

import jax
import jax.numpy as jnp
from jax import lax
from jax.experimental import pallas as pl
from jax.experimental.pallas import tpu as pltpu
from jax.sharding import PartitionSpec as P

D = 384
HEADS = 12
HEAD_DIM = 32
FF = 1536
EXPERTS = 8
TOP = 2
SEG = 128
SERIES_DEV = 6
STEP = 8
TOK_DEV = 768
CAP = 384
ROW_PAD = 16
MISC = 128
UNITS_ALL = SERIES_DEV * HEADS
QBLOCK = 256
MIB = 1 << 20

eps_norm = 1e-06
beta_one = 0.5
beta_two = 0.5
learn_rate = 0.02
weight_decay = 0.1
eps_adam = 1e-08
average_keep = 0.9
rope_base = 10000.0
neg_fill = -1e30

MESH = pl.DeviceIdType.MESH
F32 = jnp.float32
BF16 = jnp.bfloat16


def adamw_update(weights, grads, first, second, average):
    first_new = beta_one * first + (1.0 - beta_one) * grads
    second_new = beta_two * second + (1.0 - beta_two) * grads * grads
    first_hat = first_new / (1.0 - beta_one**STEP)
    second_hat = second_new / (1.0 - beta_two**STEP)
    weights_new = weights - learn_rate * (
        first_hat / (jnp.sqrt(second_hat) + eps_adam) + weight_decay * weights
    )
    average_new = average_keep * average + (1.0 - average_keep) * weights_new
    return (first_new, second_new, weights_new, average_new)


def dot(left, right, left_dim=1, right_dim=0):
    return lax.dot_general(
        left, right, (((left_dim,), (right_dim,)), ((), ())), preferred_element_type=F32
    )


class Grid:
    def __init__(self, ndp, nex):
        self.ndp, self.nex = ndp, nex
        self.nz = math.gcd(ndp, 4)
        self.ny = ndp // self.nz
        self.nc = math.gcd(nex, 2)
        self.nx = nex // self.nc
        self.ndev = ndp * nex
        self.units = -(-UNITS_ALL // ndp)
        spans = [
            [u // HEADS for u in range(self.units * o, min(self.units * (o + 1), UNITS_ALL))]
            for o in range(ndp)
        ]
        self.owned = [sorted(set(s)) for s in spans]
        self.slots = max(len(s) for s in self.owned)

    def first_series(self, owner):
        return (owner * self.units) // HEADS

    def holds(self, owner, slot):
        begin = owner * self.units
        end = jnp.minimum(begin + self.units, UNITS_ALL)
        return (begin // HEADS + slot) * HEADS < end


def remote(src, dst, send, recv, target):
    return pltpu.make_async_remote_copy(
        src_ref=src,
        dst_ref=dst,
        send_sem=send,
        recv_sem=recv,
        device_id=target,
        device_id_type=MESH,
    )


def greet(peers):
    barrier = pltpu.get_barrier_semaphore()
    for peer in peers:
        pl.semaphore_signal(barrier, inc=1, device_id=peer, device_id_type=MESH)
    pl.semaphore_wait(barrier, len(peers))


def any_spec():
    return pl.BlockSpec(memory_space=pl.ANY)


def far_first(n):
    return sorted(range(1, n), key=lambda d: -min(d, n - d))


def comm_params(number):
    return pltpu.CompilerParams(collective_id=number, has_side_effects=True)


def first_exchange(grid, tokens, shard, cot, ranks):
    ndp, nex, nz, ny, nx, nc = grid.ndp, grid.nex, grid.nz, grid.ny, grid.nx, grid.nc

    def kernel(tok, shd, cot_in, rank_in, tok_out, dense_out, cot_out, rank_out,
               t_send, t_recv, d_send, d_recv, e_send, e_recv, loc):
        dp, ex = lax.axis_index("dp"), lax.axis_index("expert")
        z, y = dp // ny, lax.rem(dp, ny)
        x, c = ex // nc, lax.rem(ex, nc)

        def place(zz, yy, xx, cc):
            return (zz * ny + yy, xx * nc + cc)

        def slot_of(zz, yy, xx, cc):
            return (zz * ny + yy) * nex + xx * nc + cc

        def off(value, by, n):
            return lax.rem(value + by, n)

        peers = [(off(dp, d, ndp), ex) for d in range(1, ndp)]
        peers += [(dp, off(ex, d, nex)) for d in range(1, nex)]
        greet(peers)

        local = []

        def keep(src, dst):
            copy = pltpu.make_async_copy(src, dst, loc.at[len(local)])
            copy.start()
            local.append(copy)

        sends = []

        def dense_send(src, slot, target):
            copy = remote(src, dense_out.at[slot], d_send.at[len(sends)], d_recv.at[slot], target)
            copy.start()
            sends.append(copy)

        def dense_wait(slot):
            remote(shd, dense_out.at[slot], d_send.at[0], d_recv.at[slot], (dp, ex)).wait_recv()

        own = slot_of(z, y, x, c)
        for dz in far_first(nz):
            dense_send(shd, own, place(off(z, dz, nz), y, x, c))
        for dy in range(1, ny):
            dense_send(shd, own, place(z, off(y, dy, ny), x, c))
        for dx in range(1, nx):
            dense_send(shd, own, place(z, y, off(x, dx, nx), c))
        for dc in range(1, nc):
            dense_send(shd, own, place(z, y, x, off(c, dc, nc)))

        e_sends = []
        for d in far_first(nex):
            target = (dp, off(ex, d, nex))
            for n, (src, dst) in enumerate(((cot_in, cot_out), (rank_in, rank_out))):
                copy = remote(src, dst.at[ex], e_send.at[d - 1, n], e_recv.at[d - 1, n], target)
                copy.start()
                e_sends.append(copy)

        def token_copy(d, slot, src_series, sender, target):
            return remote(
                tok.at[src_series],
                tok_out.at[slot, sender],
                t_send.at[d - 1, slot],
                t_recv.at[d - 1, slot],
                (target, ex),
            )

        for d in far_first(ndp):
            target = off(dp, d, ndp)
            for slot in range(grid.slots):

                @pl.when(grid.holds(target, slot))
                def _():
                    token_copy(d, slot, grid.first_series(target) + slot, dp, target).start()

        for slot in range(grid.slots):

            @pl.when(grid.holds(dp, slot))
            def _():
                copy = pltpu.make_async_copy(
                    tok.at[grid.first_series(dp) + slot], tok_out.at[slot, dp], loc.at[8 + slot]
                )
                copy.start()
                copy.wait()

        keep(shd, dense_out.at[own])
        keep(cot_in, cot_out.at[ex])
        keep(rank_in, rank_out.at[ex])

        zs = [0] + far_first(nz)[::-1]
        for dz in zs[1:]:
            zz = off(z, nz - dz, nz)
            slot = slot_of(zz, y, x, c)
            dense_wait(slot)
            for dy in range(1, ny):
                dense_send(dense_out.at[slot], slot, place(z, off(y, dy, ny), x, c))
            for dx in range(1, nx):
                dense_send(dense_out.at[slot], slot, place(z, y, off(x, dx, nx), c))
            for dc in range(1, nc):
                dense_send(dense_out.at[slot], slot, place(z, y, x, off(c, dc, nc)))
        for dy in range(1, ny):
            for dz in zs:
                slot = slot_of(off(z, nz - dz, nz), off(y, ny - dy, ny), x, c)
                dense_wait(slot)
                for dx in range(1, nx):
                    dense_send(dense_out.at[slot], slot, place(z, y, off(x, dx, nx), c))
                for dc in range(1, nc):
                    dense_send(dense_out.at[slot], slot, place(z, y, x, off(c, dc, nc)))
        for dx in range(1, nx):
            for dy in range(ny):
                for dz in zs:
                    slot = slot_of(
                        off(z, nz - dz, nz), off(y, ny - dy, ny), off(x, nx - dx, nx), c
                    )
                    dense_wait(slot)
                    for dc in range(1, nc):
                        dense_send(dense_out.at[slot], slot, place(z, y, x, off(c, dc, nc)))
        for dc in range(1, nc):
            for dx in range(nx):
                for dy in range(ny):
                    for dz in zs:
                        dense_wait(
                            slot_of(
                                off(z, nz - dz, nz),
                                off(y, ny - dy, ny),
                                off(x, nx - dx, nx),
                                off(c, nc - dc, nc),
                            )
                        )
        for d in range(1, ndp):
            for slot in range(grid.slots):

                @pl.when(grid.holds(dp, slot))
                def _():
                    token_copy(d, slot, 0, dp, off(dp, d, ndp)).wait_recv()

                @pl.when(grid.holds(off(dp, d, ndp), slot))
                def _():
                    token_copy(d, slot, 0, dp, off(dp, d, ndp)).wait_send()

        for copy in e_sends:
            copy.wait()
        for copy in sends:
            copy.wait_send()
        for copy in local:
            copy.wait()

    seg, width = tokens.shape[1:]
    dma = pltpu.SemaphoreType.DMA
    return pl.pallas_call(
        kernel,
        out_shape=(
            jax.ShapeDtypeStruct((grid.slots, ndp, seg, width), tokens.dtype),
            jax.ShapeDtypeStruct((grid.ndev,) + shard.shape, shard.dtype),
            jax.ShapeDtypeStruct((nex,) + cot.shape, cot.dtype),
            jax.ShapeDtypeStruct((nex,) + ranks.shape, ranks.dtype),
        ),
        in_specs=[any_spec()] * 4,
        out_specs=(any_spec(),) * 4,
        scratch_shapes=[
            dma((ndp - 1, grid.slots)),
            dma((ndp - 1, grid.slots)),
            dma((grid.ndev,)),
            dma((grid.ndev,)),
            dma((nex - 1, 2)),
            dma((nex - 1, 2)),
            dma((16,)),
        ],
        compiler_params=comm_params(0),
        name="first_exchange",
    )(tokens, shard, cot, ranks)


def heads_out(grid, values):
    ndp = grid.ndp

    def kernel(src, dst, send, recv, loc):
        dp, ex = lax.axis_index("dp"), lax.axis_index("expert")
        greet([(lax.rem(dp + d, ndp), ex) for d in range(1, ndp)])
        copies = []
        for d in far_first(ndp):
            target = lax.rem(dp + d, ndp)
            lanes = pl.ds(pl.multiple_of(target * SEG, SEG), SEG)
            copy = remote(
                src.at[:, :, lanes], dst.at[dp], send.at[d - 1], recv.at[d - 1], (target, ex)
            )
            copy.start()
            copies.append(copy)
        mine = pltpu.make_async_copy(
            src.at[:, :, pl.ds(pl.multiple_of(dp * SEG, SEG), SEG)], dst.at[dp], loc
        )
        mine.start()
        mine.wait()
        for copy in copies:
            copy.wait()

    dma = pltpu.SemaphoreType.DMA
    return pl.pallas_call(
        kernel,
        out_shape=jax.ShapeDtypeStruct((ndp,) + values.shape[:2] + (SEG,), values.dtype),
        in_specs=[any_spec()],
        out_specs=any_spec(),
        scratch_shapes=[dma((ndp - 1,)), dma((ndp - 1,)), dma],
        compiler_params=comm_params(1),
        name="heads_out",
    )(values)


def heads_in(grid, values):
    ndp = grid.ndp

    def kernel(src, dst, send, recv, loc):
        dp, ex = lax.axis_index("dp"), lax.axis_index("expert")
        greet([(lax.rem(dp + d, ndp), ex) for d in range(1, ndp)])
        lanes = pl.ds(pl.multiple_of(dp * SEG, SEG), SEG)
        copies = []
        for d in far_first(ndp):
            target = lax.rem(dp + d, ndp)
            copy = remote(
                src.at[target], dst.at[:, :, lanes], send.at[d - 1], recv.at[d - 1], (target, ex)
            )
            copy.start()
            copies.append(copy)
        mine = pltpu.make_async_copy(src.at[dp], dst.at[:, :, lanes], loc)
        mine.start()
        mine.wait()
        for copy in copies:
            copy.wait()

    dma = pltpu.SemaphoreType.DMA
    return pl.pallas_call(
        kernel,
        out_shape=jax.ShapeDtypeStruct(values.shape[1:3] + (SEG * ndp,), values.dtype),
        in_specs=[any_spec()],
        out_specs=any_spec(),
        scratch_shapes=[dma((ndp - 1,)), dma((ndp - 1,)), dma],
        compiler_params=comm_params(2),
        name="heads_in",
    )(values)


def rows_back(grid, values):
    ndp = grid.ndp

    def kernel(src, dst, send, recv, loc):
        dp, ex = lax.axis_index("dp"), lax.axis_index("expert")
        greet([(lax.rem(dp + d, ndp), ex) for d in range(1, ndp)])

        def block(d, slot):
            target = lax.rem(dp + d, ndp)
            return remote(
                src.at[slot, target],
                dst.at[dp, slot],
                send.at[d - 1, slot],
                recv.at[d - 1, slot],
                (target, ex),
            )

        for slot in range(grid.slots):

            @pl.when(grid.holds(dp, slot))
            def _():
                for d in far_first(ndp):
                    block(d, slot).start()
                mine = pltpu.make_async_copy(src.at[slot, dp], dst.at[dp, slot], loc.at[slot])
                mine.start()
                mine.wait()

        for slot in range(grid.slots):
            for d in range(1, ndp):

                @pl.when(grid.holds(lax.rem(dp + ndp - d, ndp), slot))
                def _():
                    block(d, slot).wait_recv()

            @pl.when(grid.holds(dp, slot))
            def _():
                for d in range(1, ndp):
                    block(d, slot).wait_send()

    dma = pltpu.SemaphoreType.DMA
    return pl.pallas_call(
        kernel,
        out_shape=jax.ShapeDtypeStruct((ndp, grid.slots) + values.shape[2:], values.dtype),
        in_specs=[any_spec()],
        out_specs=any_spec(),
        scratch_shapes=[
            dma((ndp - 1, grid.slots)),
            dma((ndp - 1, grid.slots)),
            dma((grid.slots,)),
        ],
        compiler_params=comm_params(3),
        name="rows_back",
    )(values)


def expert_gather(grid, rows, gates):
    nex, nx, nc = grid.nex, grid.nx, grid.nc
    parts = 3
    extent = TOK_DEV // parts

    def kernel(src, gate, dst, gate_dst, send, recv, fsend, g_send, g_recv, loc):
        dp, ex = lax.axis_index("dp"), lax.axis_index("expert")
        x, c = ex // nc, lax.rem(ex, nc)
        greet([(dp, lax.rem(ex + d, nex)) for d in range(1, nex)])
        sends = []

        def go(ref, slot, part, sem, target):
            rows_part = pl.ds(part * extent, extent)
            copy = remote(
                ref, dst.at[slot, rows_part], sem, recv.at[slot, part], (dp, target)
            )
            copy.start()
            sends.append(copy)

        def arrived(slot, part):
            rows_part = pl.ds(part * extent, extent)
            remote(
                src.at[rows_part], dst.at[slot, rows_part], send.at[0, 0], recv.at[slot, part],
                (dp, ex),
            ).wait_recv()

        gate_copies = []
        for d in range(1, nex):
            copy = remote(
                gate, gate_dst.at[ex], g_send.at[d - 1], g_recv.at[d - 1],
                (dp, lax.rem(ex + d, nex)),
            )
            copy.start()
            gate_copies.append(copy)
        for part in range(parts):
            for dx in range(1, nx):
                target = lax.rem(x + dx, nx) * nc + c
                go(src.at[pl.ds(part * extent, extent)], ex, part, send.at[dx - 1, part], target)
        for part in range(parts):
            for dc in range(1, nc):
                target = x * nc + lax.rem(c + dc, nc)
                go(
                    src.at[pl.ds(part * extent, extent)], ex, part,
                    send.at[nx - 1 + dc - 1, part], target,
                )
        own = [
            pltpu.make_async_copy(src, dst.at[ex], loc.at[0]),
            pltpu.make_async_copy(gate, gate_dst.at[ex], loc.at[1]),
        ]
        for copy in own:
            copy.start()
        for part in range(parts):
            for dx in range(1, nx):
                slot = lax.rem(x + nx - dx, nx) * nc + c
                arrived(slot, part)
                for dc in range(1, nc):
                    target = x * nc + lax.rem(c + dc, nc)
                    go(
                        dst.at[slot, pl.ds(part * extent, extent)], slot, part,
                        fsend.at[dx - 1, part], target,
                    )
        for part in range(parts):
            for dc in range(1, nc):
                for dx in range(nx):
                    arrived(lax.rem(x + nx - dx, nx) * nc + lax.rem(c + nc - dc, nc), part)
        for copy in gate_copies + own:
            copy.wait()
        for copy in sends:
            copy.wait_send()

    dma = pltpu.SemaphoreType.DMA
    return pl.pallas_call(
        kernel,
        out_shape=(
            jax.ShapeDtypeStruct((nex,) + rows.shape, rows.dtype),
            jax.ShapeDtypeStruct((nex,) + gates.shape, gates.dtype),
        ),
        in_specs=[any_spec()] * 2,
        out_specs=(any_spec(),) * 2,
        scratch_shapes=[
            dma((nx + nc, parts)),
            dma((nex, parts)),
            dma((nx, parts)),
            dma((nex - 1,)),
            dma((nex - 1,)),
            dma((2,)),
        ],
        compiler_params=comm_params(4),
        name="expert_gather",
    )(rows, gates)


def turn(values, cosine, sine):
    first, second = values[: HEAD_DIM // 2], values[HEAD_DIM // 2 :]
    return jnp.concatenate(
        [first * cosine - second * sine, second * cosine + first * sine], axis=0
    )


def allowed_mask(extent, block, length):
    keys = lax.broadcasted_iota(jnp.int32, (extent, QBLOCK), 0)
    queries = lax.broadcasted_iota(jnp.int32, (extent, QBLOCK), 1) + block * QBLOCK
    return (keys <= queries) & (keys < length)


def attend(grid, info, tok, weights, gain, cosine, sine):
    units, length = grid.units, tok.shape[1]
    blocks = length // QBLOCK

    def kernel(info_ref, tok_ref, w_ref, gain_ref, cos_ref, sin_ref,
               out_ref, act_ref, q_ref, k_ref, v_ref, lse_ref):
        i = pl.program_id(0)
        fresh = (i == 0) | (info_ref[0, i] != info_ref[0, jnp.maximum(i - 1, 0)])

        @pl.when(fresh)
        def _():
            residual = tok_ref[0].astype(F32)
            scale = lax.rsqrt(jnp.mean(residual * residual, axis=-1, keepdims=True) + eps_norm)
            act_ref[0] = (residual * scale * gain_ref[...]).astype(BF16)

        cos, sin = cos_ref[...], sin_ref[...]
        qkv = dot(w_ref[:, 0].reshape(3 * HEAD_DIM, D), act_ref[0], 1, 1)
        query = turn(qkv[:HEAD_DIM], cos, sin).astype(BF16)
        key_wide = turn(qkv[HEAD_DIM : 2 * HEAD_DIM], cos, sin)
        key = key_wide.astype(BF16)
        value = qkv[2 * HEAD_DIM :].astype(BF16)
        key_rows = key_wide.T.astype(BF16)
        q_ref[0], k_ref[0], v_ref[0] = query, key, value
        live = info_ref[2, i]
        for block in range(blocks):
            extent = QBLOCK * (block + 1)
            lanes = slice(QBLOCK * block, extent)
            scores = dot(key_rows[:extent], query[:, lanes]) * HEAD_DIM ** (-0.5)
            scores = jnp.where(allowed_mask(extent, block, live), scores, neg_fill)
            top = jnp.max(scores, axis=0, keepdims=True)
            probs = jnp.exp(scores - top)
            total = jnp.sum(probs, axis=0, keepdims=True)
            result = dot(value[:, :extent], probs.astype(BF16))
            out_ref[0, :, lanes] = (result * (1.0 / total)).astype(BF16)
            lse_ref[0, :, lanes] = top + jnp.log(total)

    def unit(i, info_ref):
        return (i, 0, 0)

    feature = jax.ShapeDtypeStruct((units, HEAD_DIM, length), BF16)
    flops = units * length * length * HEAD_DIM * 2 * 8
    return pl.pallas_call(
        kernel,
        out_shape=(
            feature,
            jax.ShapeDtypeStruct((grid.slots, length, D), BF16),
            feature,
            feature,
            feature,
            jax.ShapeDtypeStruct((units, 1, length), F32),
        ),
        grid_spec=pltpu.PrefetchScalarGridSpec(
            num_scalar_prefetch=1,
            grid=(units,),
            in_specs=[
                pl.BlockSpec((1, length, D), lambda i, n: (n[0, i], 0, 0)),
                pl.BlockSpec((3, 1, HEAD_DIM, D), lambda i, n: (0, n[1, i], 0, 0)),
                pl.BlockSpec((1, D), lambda i, n: (0, 0)),
                pl.BlockSpec((HEAD_DIM // 2, length), lambda i, n: (0, 0)),
                pl.BlockSpec((HEAD_DIM // 2, length), lambda i, n: (0, 0)),
            ],
            out_specs=(
                pl.BlockSpec((1, HEAD_DIM, length), unit),
                pl.BlockSpec((1, length, D), lambda i, n: (n[0, i], 0, 0)),
                pl.BlockSpec((1, HEAD_DIM, length), unit),
                pl.BlockSpec((1, HEAD_DIM, length), unit),
                pl.BlockSpec((1, HEAD_DIM, length), unit),
                pl.BlockSpec((1, 1, length), unit),
            ),
        ),
        compiler_params=pltpu.CompilerParams(vmem_limit_bytes=40 * MIB),
        cost_estimate=pl.CostEstimate(
            flops=flops, bytes_accessed=8 * MIB, transcendentals=units * length * length
        ),
        name="attend",
    )(info, tok, weights, gain, cosine, sine)


def attend_back(grid, info, act, weights, query, key, value, lse, grad_heads, cosine, sine):
    units, length = grid.units, act.shape[1]
    blocks = length // QBLOCK
    scale = HEAD_DIM ** (-0.5)

    def kernel(info_ref, act_ref, w_ref, q_ref, k_ref, v_ref, lse_ref, do_ref, cos_ref, sin_ref,
               back_ref, grad_ref, acc, dq, dk, dv):
        i = pl.program_id(0)
        live_unit = info_ref[3, i] == 1

        @pl.when((i == 0) | (info_ref[0, i] != info_ref[0, jnp.maximum(i - 1, 0)]))
        def _():
            acc[...] = jnp.zeros_like(acc)

        @pl.when(jnp.logical_not(live_unit))
        def _():
            grad_ref[...] = jnp.zeros_like(grad_ref)

        @pl.when(live_unit)
        def _():
            live = info_ref[2, i]
            query, key, value, grad = q_ref[0], k_ref[0], v_ref[0], do_ref[0]
            key_rows = key.astype(F32).T.astype(BF16)
            value_rows = value.astype(F32).T.astype(BF16)
            dk[...] = jnp.zeros_like(dk)
            dv[...] = jnp.zeros_like(dv)
            for block in range(blocks):
                extent = QBLOCK * (block + 1)
                lanes = slice(QBLOCK * block, extent)
                scores = dot(key_rows[:extent], query[:, lanes]) * scale
                scores = jnp.where(allowed_mask(extent, block, live), scores, neg_fill)
                probs = jnp.exp(scores - lse_ref[0, :, lanes])
                grad_probs = dot(value_rows[:extent], grad[:, lanes])
                delta = jnp.sum(probs * grad_probs, axis=0, keepdims=True)
                grad_scores = (probs * (grad_probs - delta)).astype(BF16)
                probs_low = probs.astype(BF16)
                dq[:, lanes] = dot(key[:, :extent], grad_scores)
                dk[:, :extent] += dot(query[:, lanes], grad_scores, 1, 1)
                dv[:, :extent] += dot(grad[:, lanes], probs_low, 1, 1)
            cos, sin = cos_ref[...], -sin_ref[...]
            stacked = jnp.concatenate(
                [
                    turn(dq[...] * scale, cos, sin),
                    turn(dk[...] * scale, cos, sin),
                    dv[...],
                ],
                axis=0,
            ).astype(BF16)
            w_rows = w_ref[:, 0].reshape(3 * HEAD_DIM, D)
            grad_ref[:, 0] = dot(stacked, act_ref[0]).reshape(3, HEAD_DIM, D)
            acc[...] += dot(stacked, w_rows, 0, 0)
            back_ref[0] = acc[...].astype(BF16)

    def unit(i, n):
        return (jnp.minimum(i, units - 1), 0, 0)

    feature = pl.BlockSpec((1, HEAD_DIM, length), unit)
    table = pl.BlockSpec((HEAD_DIM // 2, length), lambda i, n: (0, 0))
    return pl.pallas_call(
        kernel,
        out_shape=(
            jax.ShapeDtypeStruct((grid.slots, length, D), BF16),
            jax.ShapeDtypeStruct((3, HEADS, HEAD_DIM, D), F32),
        ),
        grid_spec=pltpu.PrefetchScalarGridSpec(
            num_scalar_prefetch=1,
            grid=(HEADS,),
            in_specs=[
                pl.BlockSpec((1, length, D), lambda i, n: (n[0, i], 0, 0)),
                pl.BlockSpec((3, 1, HEAD_DIM, D), lambda i, n: (0, n[1, i], 0, 0)),
                feature,
                feature,
                feature,
                pl.BlockSpec((1, 1, length), unit),
                feature,
                table,
                table,
            ],
            out_specs=(
                pl.BlockSpec((1, length, D), lambda i, n: (n[0, i], 0, 0)),
                pl.BlockSpec((3, 1, HEAD_DIM, D), lambda i, n: (0, n[1, i], 0, 0)),
            ),
            scratch_shapes=[
                pltpu.VMEM((length, D), F32),
                pltpu.VMEM((HEAD_DIM, length), F32),
                pltpu.VMEM((HEAD_DIM, length), F32),
                pltpu.VMEM((HEAD_DIM, length), F32),
            ],
        ),
        compiler_params=pltpu.CompilerParams(vmem_limit_bytes=40 * MIB),
        cost_estimate=pl.CostEstimate(
            flops=units * length * length * HEAD_DIM * 2 * 20,
            bytes_accessed=12 * MIB,
            transcendentals=units * length * length,
        ),
        name="attend_back",
    )(info, act, weights, query, key, value, lse, grad_heads, cosine, sine)


def experts_step(weights, act_all, cot_all, rank_row, rank_col, gates):
    sources, rows = act_all.shape[:2]
    local = weights.shape[0]
    parts = FF // D

    def kernel(w_ref, act_ref, cot_ref, rrow_ref, rcol_ref, gate_ref,
               routed_ref, gin_ref, ggate_ref, x_ref, dg_ref, du_ref, hid_ref, dy_ref):
        act, cot = act_ref[0], cot_ref[0]
        slot_down = lax.broadcasted_iota(jnp.int32, (CAP, rows), 0)
        slot_across = lax.broadcasted_iota(jnp.int32, (rows, CAP), 1)
        routed = jnp.zeros((rows, D), F32)
        grad_in = jnp.zeros((rows, D), F32)
        for e in range(local):
            pick = slot_down == rrow_ref[0, e : e + 1, :]
            pick_low = pick.astype(F32).astype(BF16)
            spread = (slot_across == rcol_ref[0, :, e : e + 1]).astype(F32).astype(BF16)
            taken = dot(pick_low, act).astype(BF16)
            grad_rows = dot(pick_low, cot)
            gate = jnp.sum(jnp.where(pick, gate_ref[0, e : e + 1, :], 0.0), axis=1, keepdims=True)
            grad_result = (gate * grad_rows).astype(BF16)
            x_ref[e, 0] = taken
            dy_ref[e, 0] = grad_result
            result = jnp.zeros((CAP, D), F32)
            grad_taken = jnp.zeros((CAP, D), F32)
            for part in range(parts):
                lanes = slice(part * D, (part + 1) * D)
                w_gate = w_ref[e, 0:D, lanes]
                w_up = w_ref[e, D : 2 * D, lanes]
                w_down = w_ref[e, 2 * D : 3 * D, lanes]
                gate_lin = dot(taken, w_gate)
                up_lin = dot(taken, w_up)
                sig = jax.nn.sigmoid(gate_lin)
                silu = gate_lin * sig
                hidden = (silu * up_lin).astype(BF16)
                result += dot(hidden, w_down)
                grad_hidden = dot(grad_result, w_down, 1, 1)
                slope = sig * (1.0 + gate_lin * (1.0 - sig))
                grad_gate = (grad_hidden * up_lin * slope).astype(BF16)
                grad_up = (grad_hidden * silu).astype(BF16)
                hid_ref[e, 0, :, lanes] = hidden
                dg_ref[e, 0, :, lanes] = grad_gate
                du_ref[e, 0, :, lanes] = grad_up
                grad_taken += dot(grad_gate, w_gate, 1, 1) + dot(grad_up, w_up, 1, 1)
            result = result.astype(BF16).astype(F32)
            grad_gate_slot = jnp.sum(grad_rows * result, axis=1, keepdims=True)
            ggate_ref[0, e : e + 1, :] = jnp.sum(
                jnp.where(pick, grad_gate_slot, 0.0), axis=0, keepdims=True
            )
            routed += dot(spread, (gate * result).astype(BF16))
            grad_in += dot(spread, grad_taken.astype(BF16))
        routed_ref[0] = routed.astype(BF16)
        gin_ref[0] = grad_in.astype(BF16)

    def per_source(*tail):
        return pl.BlockSpec((1,) + tail, lambda s: (s,) + (0,) * len(tail))

    def kept(width):
        return pl.BlockSpec((local, 1, CAP, width), lambda s: (0, s, 0, 0))

    def kept_shape(width):
        return jax.ShapeDtypeStruct((local, sources, CAP, width), BF16)

    return pl.pallas_call(
        kernel,
        grid=(sources,),
        out_shape=(
            jax.ShapeDtypeStruct((sources, rows, D), BF16),
            jax.ShapeDtypeStruct((sources, rows, D), BF16),
            jax.ShapeDtypeStruct((sources, local, rows), F32),
            kept_shape(D),
            kept_shape(FF),
            kept_shape(FF),
            kept_shape(FF),
            kept_shape(D),
        ),
        in_specs=[
            pl.BlockSpec(weights.shape, lambda s: (0, 0, 0), pipeline_mode=pl.Buffered(1)),
            per_source(rows, D),
            per_source(rows, D),
            per_source(local, rows),
            per_source(rows, local),
            per_source(local, rows),
        ],
        out_specs=(
            per_source(rows, D),
            per_source(rows, D),
            per_source(local, rows),
            kept(D),
            kept(FF),
            kept(FF),
            kept(FF),
            kept(D),
        ),
        compiler_params=pltpu.CompilerParams(vmem_limit_bytes=56 * MIB),
        cost_estimate=pl.CostEstimate(
            flops=sources * local * CAP * D * FF * 2 * 8,
            bytes_accessed=50 * MIB,
            transcendentals=sources * local * CAP * FF,
        ),
        name="experts_step",
    )(weights, act_all, cot_all, rank_row, rank_col, gates)


def local(
    tokens,
    cotangent,
    lengths,
    routes,
    dense_weights,
    dense_first,
    dense_second,
    dense_average,
    expert_weights,
    expert_first,
    expert_second,
    expert_average,
):
    ndp, nex = lax.axis_size("dp"), lax.axis_size("expert")
    dp, ex = lax.axis_index("dp"), lax.axis_index("expert")
    grid = Grid(ndp, nex)
    local_experts = EXPERTS // nex
    length = SEG * ndp
    rows_dev = D // grid.ndev
    shard_rows = 3 * D // ndp

    spot = jnp.arange(FF, dtype=jnp.int32)
    order = (FF // D) * (spot % D) + spot // D
    mix = (spot[:, None] == order[None, :]).astype(BF16)
    shard_row = dp * shard_rows + jnp.arange(shard_rows, dtype=jnp.int32)
    is_down = (shard_row >= 2 * D)[None, :, None]
    expert_low = expert_weights.astype(BF16).reshape(local_experts, shard_rows, FF)
    mixed_low = jnp.einsum(
        "erf,fg->erg", expert_low, mix, preferred_element_type=F32
    ).astype(BF16)
    expert_send = jnp.where(is_down, expert_low, mixed_low)
    expert_all = lax.all_gather(expert_send, "dp", axis=0, tiled=False)
    expert_all = expert_all.transpose(1, 0, 2, 3).reshape(local_experts, 3 * D, FF)

    table = dense_weights.astype(BF16).reshape(rows_dev, -1)
    after = 4 * D + EXPERTS
    shard = jnp.concatenate(
        [
            table[:, : 4 * D],
            table[:, after : after + 3 * FF],
            table[:, 4 * D : after],
            table[:, after + 3 * FF :],
            jnp.zeros((rows_dev, MISC - EXPERTS - 3), BF16),
        ],
        axis=1,
    )
    shard = jnp.pad(shard, ((0, ROW_PAD - rows_dev), (0, 0)))

    names = jnp.arange(EXPERTS, dtype=jnp.int32)
    routes_rows = routes.reshape(TOK_DEV, TOP)
    member = (routes_rows[:, :, None] == names[None, None, :]).any(axis=1)
    before = jnp.arange(TOK_DEV)
    earlier = (before[None, :] < before[:, None]).astype(BF16)
    count = jnp.dot(earlier, member.astype(BF16), preferred_element_type=F32)
    ranks = jnp.where(member, count.astype(jnp.int32), -1).T

    local_pos = dp * SEG + jnp.arange(SEG, dtype=jnp.int32)
    live = (local_pos[None, :] < lengths[:, None]).astype(F32)
    grad_out_low = (cotangent.astype(F32) * live[..., None]).astype(BF16).reshape(TOK_DEV, D)

    tok_all, dense_all, cot_all, rank_all = first_exchange(
        grid, tokens, shard, grad_out_low, ranks
    )

    dense_all = dense_all.reshape(grid.ndev * ROW_PAD, -1)
    row = jnp.arange(D, dtype=jnp.int32)
    row_from = (row // rows_dev) * ROW_PAD + row % rows_dev
    unpad = (row_from[:, None] == jnp.arange(grid.ndev * ROW_PAD)[None, :]).astype(BF16)
    qkv_rows = dot(dense_all[:, : 3 * D], unpad, 0, 1).astype(BF16)
    qkv_rows = qkv_rows.reshape(3, HEADS, HEAD_DIM, D)
    rest = dot(unpad, dense_all[:, 3 * D :]).astype(BF16)
    w_output = rest[:, :D]
    w_sgate = rest[:, D : D + FF]
    w_sup = rest[:, D + FF : D + 2 * FF]
    w_sdown = rest[:, D + 2 * FF : D + 3 * FF]
    w_misc = rest[:, D + 3 * FF :]
    gain_first = w_misc[:, EXPERTS + 1].astype(F32)
    gain_second = w_misc[:, EXPERTS + 2].astype(F32)

    unit = dp * grid.units + jnp.arange(HEADS, dtype=jnp.int32)
    working = (jnp.arange(HEADS) < grid.units) & (unit < UNITS_ALL)
    last = jnp.minimum(dp * grid.units + grid.units, UNITS_ALL) - 1
    series = jnp.clip(jnp.minimum(unit, last) // HEADS, 0, SERIES_DEV - 1)
    slot = jnp.clip(series - grid.first_series(dp), 0, grid.slots - 1)
    info = jnp.stack(
        [slot, unit % HEADS, lengths[series], working.astype(jnp.int32)]
    ).astype(jnp.int32)
    half = HEAD_DIM // 2
    inverse = rope_base ** (-jnp.arange(half, dtype=F32) * 2.0 / HEAD_DIM)
    angles = inverse[:, None] * jnp.arange(length, dtype=jnp.int32).astype(F32)[None, :]
    cosine, sine = jnp.cos(angles), jnp.sin(angles)
    heads, act_one, query, key, value, lse = attend(
        grid,
        info,
        tok_all.reshape(grid.slots, length, D),
        qkv_rows,
        gain_first[None, :],
        cosine,
        sine,
    )
    heads_here = heads_out(grid, heads).reshape(-1, HEAD_DIM, SEG)[:UNITS_ALL]
    attn_low = heads_here.reshape(SERIES_DEV, D, SEG).transpose(0, 2, 1).reshape(TOK_DEV, D)

    residual = tokens.astype(F32).reshape(TOK_DEV, D)
    mixed_rows = residual + dot(attn_low, w_output)
    scale_two = lax.rsqrt(jnp.mean(mixed_rows * mixed_rows, axis=-1, keepdims=True) + eps_norm)
    normed_two = mixed_rows * scale_two
    act_two = (normed_two * gain_second).astype(BF16)
    misc = dot(act_two, w_misc)
    router_probs = jax.nn.softmax(misc[:, :EXPERTS], axis=-1)
    shared_gate = jax.nn.sigmoid(misc[:, EXPERTS : EXPERTS + 1])

    act_all, gates_all = expert_gather(grid, act_two, router_probs.T)
    rank_row = lax.dynamic_slice_in_dim(rank_all, ex * local_experts, local_experts, 1)
    gate_row = lax.dynamic_slice_in_dim(gates_all, ex * local_experts, local_experts, 1)
    routed_parts, gin_parts, ggate, taken, grad_gate_lin, grad_up_lin, hidden, grad_result = (
        experts_step(
            expert_all, act_all, cot_all, rank_row, rank_row.transpose(0, 2, 1), gate_row
        )
    )
    gin_back = lax.all_to_all(gin_parts, "expert", split_axis=0, concat_axis=0, tiled=True)
    ggate_back = lax.all_to_all(ggate, "expert", split_axis=0, concat_axis=0, tiled=True)
    routed_back = lax.all_to_all(routed_parts, "expert", split_axis=0, concat_axis=0, tiled=True)

    def by_expert(rows):
        return rows.reshape(local_experts, nex * CAP, -1)

    taken, grad_gate_lin, grad_up_lin, hidden, grad_result = (
        by_expert(v) for v in (taken, grad_gate_lin, grad_up_lin, hidden, grad_result)
    )
    grad_e_gate = jnp.einsum("erd,erf->edf", taken, grad_gate_lin, preferred_element_type=F32)
    grad_e_up = jnp.einsum("erd,erf->edf", taken, grad_up_lin, preferred_element_type=F32)
    grad_e_down = [
        jnp.einsum(
            "erh,erd->ehd", hidden[..., at : at + D], grad_result, preferred_element_type=F32
        )
        for at in range(0, FF, D)
    ]
    expert_terms = jnp.concatenate(
        [
            grad_e_gate.astype(BF16),
            grad_e_up.astype(BF16),
            jnp.concatenate(grad_e_down, axis=2).astype(BF16),
        ],
        axis=1,
    )
    expert_terms = expert_terms.reshape(local_experts, ndp, shard_rows, FF).transpose(1, 0, 2, 3)
    expert_sum = lax.psum_scatter(expert_terms, "dp", scatter_dimension=0, tiled=False)
    unmixed = jnp.einsum("erg,fg->erf", expert_sum, mix, preferred_element_type=F32)
    expert_grad = jnp.where(is_down, expert_sum.astype(F32), unmixed)
    expert_grad = expert_grad.reshape(expert_weights.shape)

    sgate_lin = dot(act_two, w_sgate)
    sup_lin = dot(act_two, w_sup)
    sgate_sigmoid = jax.nn.sigmoid(sgate_lin)
    sgate_silu = sgate_lin * sgate_sigmoid
    shared_hidden = (sgate_silu * sup_lin).astype(BF16)
    shared_lin = dot(shared_hidden, w_sdown, 1, 1)
    grad_out = grad_out_low.astype(F32)
    grad_shared_lin = (grad_out * shared_gate).astype(BF16)
    grad_svec_logit = (
        shared_gate * (1.0 - shared_gate) * jnp.sum(grad_out * shared_lin, axis=-1, keepdims=True)
    ).astype(BF16)
    grad_shared_hidden = dot(grad_shared_lin, w_sdown)
    grad_sgate_lin = (
        grad_shared_hidden * sup_lin * sgate_sigmoid * (1.0 + sgate_lin * (1.0 - sgate_sigmoid))
    ).astype(BF16)
    grad_sup_lin = (grad_shared_hidden * sgate_silu).astype(BF16)

    routed = jnp.sum(routed_back.astype(F32), axis=0)
    output = (mixed_rows + routed + shared_gate * shared_lin).astype(BF16)
    grad_router_probs = ggate_back.reshape(EXPERTS, TOK_DEV).T
    grad_logits = (
        router_probs
        * (grad_router_probs - jnp.sum(router_probs * grad_router_probs, axis=-1, keepdims=True))
    ).astype(BF16)
    grad_misc = jnp.concatenate(
        [grad_logits, grad_svec_logit, jnp.zeros((TOK_DEV, MISC - EXPERTS - 1), BF16)], axis=1
    )
    grad_act_two = (
        jnp.sum(gin_back.astype(F32), axis=0)
        + dot(grad_sgate_lin, w_sgate, 1, 1)
        + dot(grad_sup_lin, w_sup, 1, 1)
        + dot(grad_misc, w_misc, 1, 1)
    )
    grad_gain_two = jnp.sum(grad_act_two * normed_two, axis=0)
    weighted_two = grad_act_two * gain_second
    grad_mixed = grad_out + scale_two * (
        weighted_two - normed_two * jnp.mean(weighted_two * normed_two, axis=-1, keepdims=True)
    )
    grad_attn_low = grad_mixed.astype(BF16)
    grad_heads = dot(grad_attn_low, w_output, 1, 1).astype(BF16)
    grad_heads = grad_heads.reshape(SERIES_DEV, SEG, D).transpose(0, 2, 1)
    grad_heads = grad_heads.reshape(UNITS_ALL, HEAD_DIM, SEG)
    grad_heads = jnp.pad(grad_heads, ((0, grid.units * ndp - UNITS_ALL), (0, 0), (0, 0)))
    grad_heads = heads_in(grid, grad_heads.reshape(ndp, grid.units, HEAD_DIM, SEG))

    back, qkv_grads = attend_back(
        grid, info, act_one, qkv_rows, query, key, value, lse, grad_heads, cosine, sine
    )
    back = rows_back(grid, back.reshape(grid.slots, ndp, SEG, D))
    grad_act_one = jnp.stack(
        [
            sum(
                back[owner, owned.index(s)].astype(F32)
                for owner, owned in enumerate(grid.owned)
                if s in owned
            )
            for s in range(SERIES_DEV)
        ]
    ).reshape(TOK_DEV, D)
    scale_one = lax.rsqrt(jnp.mean(residual * residual, axis=-1, keepdims=True) + eps_norm)
    normed_one = residual * scale_one
    grad_gain_one = jnp.sum(grad_act_one * normed_one, axis=0)
    weighted_one = grad_act_one * gain_first
    grad_tokens = grad_mixed + scale_one * (
        weighted_one - normed_one * jnp.mean(weighted_one * normed_one, axis=-1, keepdims=True)
    )

    row_dev = row // rows_dev
    row_to = ((row_dev % nex) * ndp + row_dev // nex) * ROW_PAD + row % rows_dev
    group = (jnp.arange(grid.ndev * ROW_PAD)[:, None] == row_to[None, :]).astype(BF16)

    def scatter_rows(padded):
        width = padded.shape[1]
        first = lax.all_to_all(
            padded.reshape(nex, ndp * ROW_PAD, width), "expert", split_axis=0, concat_axis=0,
            tiled=True,
        )
        first = jnp.sum(first.astype(F32), axis=0).astype(BF16)
        second = lax.all_to_all(
            first.reshape(ndp, ROW_PAD, width), "dp", split_axis=0, concat_axis=0, tiled=True
        )
        return jnp.sum(second.astype(F32), axis=0)[:rows_dev]

    def weight_grad(left, right):
        return dot(left, right, 0, 0).astype(BF16)

    g_misc = dot(act_two, grad_misc, 0, 0).astype(BF16)
    g_misc = jnp.where(
        jnp.arange(MISC)[None, :] == EXPERTS + 2, grad_gain_two[:, None].astype(BF16), g_misc
    )
    early = jnp.concatenate(
        [
            weight_grad(attn_low, grad_attn_low),
            weight_grad(act_two, grad_sgate_lin),
            weight_grad(act_two, grad_sup_lin),
            weight_grad(grad_shared_lin, shared_hidden),
            g_misc,
        ],
        axis=1,
    )
    early = scatter_rows(dot(group, early).astype(BF16))
    late = jnp.concatenate(
        [
            dot(group, qkv_grads.reshape(3 * D, D).astype(BF16), 1, 1).astype(BF16),
            dot(group, jnp.broadcast_to(grad_gain_one[:, None], (D, MISC)).astype(BF16)).astype(
                BF16
            ),
        ],
        axis=1,
    )
    late = scatter_rows(late)
    misc_at = D + 3 * FF
    dense_grad = jnp.concatenate(
        [
            late[:, : 3 * D],
            early[:, :D],
            early[:, misc_at : misc_at + EXPERTS],
            early[:, D:misc_at],
            early[:, misc_at + EXPERTS : misc_at + EXPERTS + 1],
            late[:, 3 * D : 3 * D + 1],
            early[:, misc_at + EXPERTS + 2 : misc_at + EXPERTS + 3],
        ],
        axis=1,
    ).reshape(-1)

    dense_first_new, dense_second_new, dense_new, dense_average_new = adamw_update(
        dense_weights, dense_grad, dense_first, dense_second, dense_average
    )
    expert_first_new, expert_second_new, expert_new, expert_average_new = adamw_update(
        expert_weights, expert_grad, expert_first, expert_second, expert_average
    )
    return (
        output.reshape(tokens.shape),
        grad_tokens.reshape(tokens.shape),
        dense_grad,
        dense_first_new,
        dense_second_new,
        dense_new,
        dense_average_new,
        expert_grad,
        expert_first_new,
        expert_second_new,
        expert_new,
        expert_average_new,
    )


def solution(mesh):
    rows = P("expert", "dp", None)
    dense = P(("dp", "expert"))
    experts = P("expert", "dp")
    return jax.shard_map(
        local,
        mesh=mesh,
        in_specs=(
            (rows, rows, P("expert"), P("dp", "expert", None, None)) + (dense,) * 4 + (experts,) * 4
        ),
        out_specs=(rows, rows) + (dense,) * 5 + (experts,) * 5,
        check_vma=False,
    )
```

```python
import functools
import math

import jax
import jax.numpy as jnp
from jax import lax
from jax.experimental import pallas as pl
from jax.experimental.pallas import tpu as pltpu
from jax.sharding import PartitionSpec as P

D = 384
HEADS = 12
HEAD_DIM = 32
FF = 1536
EXPERTS = 8
TOP = 2
SEG = 128
SERIES_DEV = 6
STEP = 8
TOK_DEV = 768
CAP = 384
ROW_PAD = 16
MISC = 128
UNITS_ALL = SERIES_DEV * HEADS
QBLOCK = 256
MIB = 1 << 20

eps_norm = 1e-06
beta_one = 0.5
beta_two = 0.5
learn_rate = 0.02
weight_decay = 0.1
eps_adam = 1e-08
average_keep = 0.9
rope_base = 10000.0
neg_fill = -1e30

MESH = pl.DeviceIdType.MESH
F32 = jnp.float32
BF16 = jnp.bfloat16


def adamw_update(weights, grads, first, second, average):
    first_new = beta_one * first + (1.0 - beta_one) * grads
    second_new = beta_two * second + (1.0 - beta_two) * grads * grads
    first_hat = first_new / (1.0 - beta_one**STEP)
    second_hat = second_new / (1.0 - beta_two**STEP)
    weights_new = weights - learn_rate * (
        first_hat / (jnp.sqrt(second_hat) + eps_adam) + weight_decay * weights
    )
    average_new = average_keep * average + (1.0 - average_keep) * weights_new
    return (first_new, second_new, weights_new, average_new)


def dot(left, right, left_dim=1, right_dim=0):
    return lax.dot_general(
        left, right, (((left_dim,), (right_dim,)), ((), ())), preferred_element_type=F32
    )


class Grid:
    def __init__(self, ndp, nex):
        self.ndp, self.nex = ndp, nex
        self.nz = math.gcd(ndp, 4)
        self.ny = ndp // self.nz
        self.nc = math.gcd(nex, 2)
        self.nx = nex // self.nc
        self.ndev = ndp * nex
        self.units = -(-UNITS_ALL // ndp)
        spans = [
            [u // HEADS for u in range(self.units * o, min(self.units * (o + 1), UNITS_ALL))]
            for o in range(ndp)
        ]
        self.owned = [sorted(set(s)) for s in spans]
        self.slots = max(len(s) for s in self.owned)

    def first_series(self, owner):
        return (owner * self.units) // HEADS

    def holds(self, owner, slot):
        begin = owner * self.units
        end = jnp.minimum(begin + self.units, UNITS_ALL)
        return (begin // HEADS + slot) * HEADS < end


def remote(src, dst, send, recv, target):
    return pltpu.make_async_remote_copy(
        src_ref=src,
        dst_ref=dst,
        send_sem=send,
        recv_sem=recv,
        device_id=target,
        device_id_type=MESH,
    )


def greet(peers):
    barrier = pltpu.get_barrier_semaphore()
    for peer in peers:
        pl.semaphore_signal(barrier, inc=1, device_id=peer, device_id_type=MESH)
    pl.semaphore_wait(barrier, len(peers))


def any_spec():
    return pl.BlockSpec(memory_space=pl.ANY)


def far_first(n):
    return sorted(range(1, n), key=lambda d: -min(d, n - d))


def comm_params(number):
    return pltpu.CompilerParams(collective_id=number, has_side_effects=True)


def first_exchange(grid, tokens, shard, cot, ranks):
    ndp, nex, nz, ny, nx, nc = grid.ndp, grid.nex, grid.nz, grid.ny, grid.nx, grid.nc

    def kernel(tok, shd, cot_in, rank_in, tok_out, dense_out, cot_out, rank_out,
               t_send, t_recv, d_send, d_recv, e_send, e_recv, loc):
        dp, ex = lax.axis_index("dp"), lax.axis_index("expert")
        z, y = dp // ny, lax.rem(dp, ny)
        x, c = ex // nc, lax.rem(ex, nc)

        def place(zz, yy, xx, cc):
            return (zz * ny + yy, xx * nc + cc)

        def slot_of(zz, yy, xx, cc):
            return (zz * ny + yy) * nex + xx * nc + cc

        def off(value, by, n):
            return lax.rem(value + by, n)

        peers = [(off(dp, d, ndp), ex) for d in range(1, ndp)]
        peers += [(dp, off(ex, d, nex)) for d in range(1, nex)]
        greet(peers)

        local = []

        def keep(src, dst):
            copy = pltpu.make_async_copy(src, dst, loc.at[len(local)])
            copy.start()
            local.append(copy)

        sends = []

        def dense_send(src, slot, target):
            copy = remote(src, dense_out.at[slot], d_send.at[len(sends)], d_recv.at[slot], target)
            copy.start()
            sends.append(copy)

        def dense_wait(slot):
            remote(shd, dense_out.at[slot], d_send.at[0], d_recv.at[slot], (dp, ex)).wait_recv()

        own = slot_of(z, y, x, c)
        for dz in far_first(nz):
            dense_send(shd, own, place(off(z, dz, nz), y, x, c))
        for dy in range(1, ny):
            dense_send(shd, own, place(z, off(y, dy, ny), x, c))
        for dx in range(1, nx):
            dense_send(shd, own, place(z, y, off(x, dx, nx), c))
        for dc in range(1, nc):
            dense_send(shd, own, place(z, y, x, off(c, dc, nc)))

        e_sends = []
        for d in far_first(nex):
            target = (dp, off(ex, d, nex))
            for n, (src, dst) in enumerate(((cot_in, cot_out), (rank_in, rank_out))):
                copy = remote(src, dst.at[ex], e_send.at[d - 1, n], e_recv.at[d - 1, n], target)
                copy.start()
                e_sends.append(copy)

        def token_copy(d, slot, src_series, sender, target):
            return remote(
                tok.at[src_series],
                tok_out.at[slot, sender],
                t_send.at[d - 1, slot],
                t_recv.at[d - 1, slot],
                (target, ex),
            )

        for d in far_first(ndp):
            target = off(dp, d, ndp)
            for slot in range(grid.slots):

                @pl.when(grid.holds(target, slot))
                def _():
                    token_copy(d, slot, grid.first_series(target) + slot, dp, target).start()

        for slot in range(grid.slots):

            @pl.when(grid.holds(dp, slot))
            def _():
                copy = pltpu.make_async_copy(
                    tok.at[grid.first_series(dp) + slot], tok_out.at[slot, dp], loc.at[8 + slot]
                )
                copy.start()
                copy.wait()

        keep(shd, dense_out.at[own])
        keep(cot_in, cot_out.at[ex])
        keep(rank_in, rank_out.at[ex])

        zs = [0] + far_first(nz)[::-1]
        for dz in zs[1:]:
            zz = off(z, nz - dz, nz)
            slot = slot_of(zz, y, x, c)
            dense_wait(slot)
            for dy in range(1, ny):
                dense_send(dense_out.at[slot], slot, place(z, off(y, dy, ny), x, c))
            for dx in range(1, nx):
                dense_send(dense_out.at[slot], slot, place(z, y, off(x, dx, nx), c))
            for dc in range(1, nc):
                dense_send(dense_out.at[slot], slot, place(z, y, x, off(c, dc, nc)))
        for dy in range(1, ny):
            for dz in zs:
                slot = slot_of(off(z, nz - dz, nz), off(y, ny - dy, ny), x, c)
                dense_wait(slot)
                for dx in range(1, nx):
                    dense_send(dense_out.at[slot], slot, place(z, y, off(x, dx, nx), c))
                for dc in range(1, nc):
                    dense_send(dense_out.at[slot], slot, place(z, y, x, off(c, dc, nc)))
        for dx in range(1, nx):
            for dy in range(ny):
                for dz in zs:
                    slot = slot_of(
                        off(z, nz - dz, nz), off(y, ny - dy, ny), off(x, nx - dx, nx), c
                    )
                    dense_wait(slot)
                    for dc in range(1, nc):
                        dense_send(dense_out.at[slot], slot, place(z, y, x, off(c, dc, nc)))
        for dc in range(1, nc):
            for dx in range(nx):
                for dy in range(ny):
                    for dz in zs:
                        dense_wait(
                            slot_of(
                                off(z, nz - dz, nz),
                                off(y, ny - dy, ny),
                                off(x, nx - dx, nx),
                                off(c, nc - dc, nc),
                            )
                        )
        for d in range(1, ndp):
            for slot in range(grid.slots):

                @pl.when(grid.holds(dp, slot))
                def _():
                    token_copy(d, slot, 0, dp, off(dp, d, ndp)).wait_recv()

                @pl.when(grid.holds(off(dp, d, ndp), slot))
                def _():
                    token_copy(d, slot, 0, dp, off(dp, d, ndp)).wait_send()

        for copy in e_sends:
            copy.wait()
        for copy in sends:
            copy.wait_send()
        for copy in local:
            copy.wait()

    seg, width = tokens.shape[1:]
    dma = pltpu.SemaphoreType.DMA
    return pl.pallas_call(
        kernel,
        out_shape=(
            jax.ShapeDtypeStruct((grid.slots, ndp, seg, width), tokens.dtype),
            jax.ShapeDtypeStruct((grid.ndev,) + shard.shape, shard.dtype),
            jax.ShapeDtypeStruct((nex,) + cot.shape, cot.dtype),
            jax.ShapeDtypeStruct((nex,) + ranks.shape, ranks.dtype),
        ),
        in_specs=[any_spec()] * 4,
        out_specs=(any_spec(),) * 4,
        scratch_shapes=[
            dma((ndp - 1, grid.slots)),
            dma((ndp - 1, grid.slots)),
            dma((grid.ndev,)),
            dma((grid.ndev,)),
            dma((nex - 1, 2)),
            dma((nex - 1, 2)),
            dma((16,)),
        ],
        compiler_params=comm_params(0),
        name="first_exchange",
    )(tokens, shard, cot, ranks)


def heads_out(grid, values):
    ndp = grid.ndp

    def kernel(src, dst, send, recv, loc):
        dp, ex = lax.axis_index("dp"), lax.axis_index("expert")
        greet([(lax.rem(dp + d, ndp), ex) for d in range(1, ndp)])
        copies = []
        for d in far_first(ndp):
            target = lax.rem(dp + d, ndp)
            lanes = pl.ds(pl.multiple_of(target * SEG, SEG), SEG)
            copy = remote(
                src.at[:, :, lanes], dst.at[dp], send.at[d - 1], recv.at[d - 1], (target, ex)
            )
            copy.start()
            copies.append(copy)
        mine = pltpu.make_async_copy(
            src.at[:, :, pl.ds(pl.multiple_of(dp * SEG, SEG), SEG)], dst.at[dp], loc
        )
        mine.start()
        mine.wait()
        for copy in copies:
            copy.wait()

    dma = pltpu.SemaphoreType.DMA
    return pl.pallas_call(
        kernel,
        out_shape=jax.ShapeDtypeStruct((ndp,) + values.shape[:2] + (SEG,), values.dtype),
        in_specs=[any_spec()],
        out_specs=any_spec(),
        scratch_shapes=[dma((ndp - 1,)), dma((ndp - 1,)), dma],
        compiler_params=comm_params(1),
        name="heads_out",
    )(values)


def heads_in(grid, values, act, shared, attn, grads, hidden):
    ndp = grid.ndp
    grad_attn, grad_sgate, grad_sup, grad_misc = grads
    tile = FF // 3

    def kernel(src, act_ref, shared_ref, attn_ref, ga_ref, gs_ref, gu_ref, gm_ref, hid_ref,
               dst, out_ref, send, recv, loc):
        dp, ex = lax.axis_index("dp"), lax.axis_index("expert")
        greet([(lax.rem(dp + d, ndp), ex) for d in range(1, ndp)])
        lanes = pl.ds(pl.multiple_of(dp * SEG, SEG), SEG)
        copies = []
        for d in far_first(ndp):
            target = lax.rem(dp + d, ndp)
            copy = remote(
                src.at[target], dst.at[:, :, lanes], send.at[d - 1], recv.at[d - 1], (target, ex)
            )
            copy.start()
            copies.append(copy)
        mine = pltpu.make_async_copy(src.at[dp], dst.at[:, :, lanes], loc)
        mine.start()
        out_ref[:, :D] = dot(attn_ref[...], ga_ref[...]).astype(BF16)
        out_ref[:, D + 3 * FF :] = dot(act_ref[...], gm_ref[...]).astype(BF16)

        def column(step, carry):
            at = pl.multiple_of(step * tile, tile)
            for n, (left, right) in enumerate(
                ((act_ref, gs_ref), (act_ref, gu_ref), (shared_ref, hid_ref))
            ):
                part = dot(left[...], right[:, pl.ds(at, tile)]).astype(BF16)
                out_ref[:, pl.ds(pl.multiple_of(D + n * FF + at, MISC), tile)] = part
            return carry

        lax.fori_loop(0, FF // tile, column, 0)
        mine.wait()
        for copy in copies:
            copy.wait()

    dma = pltpu.SemaphoreType.DMA
    vmem = pl.BlockSpec(memory_space=pltpu.VMEM)
    return pl.pallas_call(
        kernel,
        out_shape=(
            jax.ShapeDtypeStruct(values.shape[1:3] + (SEG * ndp,), values.dtype),
            jax.ShapeDtypeStruct((D, D + 3 * FF + MISC), BF16),
        ),
        in_specs=[any_spec()] + [vmem] * 8,
        out_specs=(any_spec(), vmem),
        scratch_shapes=[dma((ndp - 1,)), dma((ndp - 1,)), dma],
        compiler_params=pltpu.CompilerParams(
            collective_id=2, has_side_effects=True, vmem_limit_bytes=40 * MIB
        ),
        name="heads_in",
    )(values, act, shared, attn, grad_attn, grad_sgate, grad_sup, grad_misc, hidden)


class RowScatter:
    def __init__(self, grid, width):
        self.grid, self.width = grid, width
        self.rows = D // grid.nex
        self.rows_dev = D // grid.ndev

    def scratch(self):
        g, w = self.grid, self.width
        dma = pltpu.SemaphoreType.DMA
        return [
            pltpu.VMEM((g.nx, self.rows, w), BF16),
            pltpu.VMEM((g.nx, self.rows, w), BF16),
            pltpu.VMEM((g.nx, self.rows, w), BF16),
            pltpu.VMEM((g.ndp * ROW_PAD, w), BF16),
            pltpu.VMEM((g.ndp, ROW_PAD, w), BF16),
            dma((2, 2)),
            dma((g.nx, 2)),
            dma((g.ndp, 2)),
        ]

    def bind(self, source, refs):
        self.source = source
        (self.got_core, self.by_x, self.got_x, self.spread, self.got_dp,
         self.sem_core, self.sem_x, self.sem_dp) = refs
        g = self.grid
        self.dp, self.ex = lax.axis_index("dp"), lax.axis_index("expert")
        self.x, self.c = self.ex // g.nc, lax.rem(self.ex, g.nc)

    def core_copy(self):
        other = 1 - self.c
        return remote(
            self.source.at[:, other], self.got_core, self.sem_core.at[0, 0],
            self.sem_core.at[0, 1], (self.dp, self.x * 2 + other),
        )

    def x_copy(self, d):
        target = lax.rem(self.x + d, self.grid.nx)
        return remote(
            self.by_x.at[target], self.got_x.at[d], self.sem_x.at[d, 0], self.sem_x.at[d, 1],
            (self.dp, target * self.grid.nc + self.c),
        )

    def dp_copy(self, d):
        target = lax.rem(self.dp + d, self.grid.ndp)
        rows = pl.ds(pl.multiple_of(target * ROW_PAD, ROW_PAD), ROW_PAD)
        return remote(
            self.spread.at[rows], self.got_dp.at[d], self.sem_dp.at[d, 0], self.sem_dp.at[d, 1],
            (target, self.ex),
        )

    def start(self):
        self.core_copy().start()

    def along_x(self):
        g = self.grid
        self.core_copy().wait()
        for n in range(g.nx):
            mine = self.source[n, pl.ds(self.c, 1)][0]
            self.by_x[n] = (mine.astype(F32) + self.got_core[n].astype(F32)).astype(BF16)
        for d in range(1, g.nx):
            self.x_copy(d).start()

    def along_dp(self):
        g = self.grid
        for d in range(1, g.nx):
            self.x_copy(d).wait()
        total = self.by_x[pl.ds(self.x, 1)][0].astype(F32)
        for d in range(1, g.nx):
            total += self.got_x[d].astype(F32)
        to = lax.broadcasted_iota(jnp.int32, (g.ndp * ROW_PAD, self.rows), 0)
        of = lax.broadcasted_iota(jnp.int32, (g.ndp * ROW_PAD, self.rows), 1)
        place = (of // self.rows_dev) * ROW_PAD + lax.rem(of, self.rows_dev)
        move = (to == place).astype(F32).astype(BF16)
        self.spread[...] = dot(move, total.astype(BF16)).astype(BF16)
        for d in far_first(g.ndp):
            self.dp_copy(d).start()

    def finish(self, out):
        g = self.grid
        rows = pl.ds(pl.multiple_of(self.dp * ROW_PAD, ROW_PAD), ROW_PAD)
        total = self.spread[rows].astype(F32)
        for d in range(1, g.ndp):
            self.dp_copy(d).wait()
            total += self.got_dp[d].astype(F32)
        out[...] = total


def expert_gather(grid, rows, gates):
    nex, nx, nc = grid.nex, grid.nx, grid.nc
    parts = 3
    extent = TOK_DEV // parts

    def kernel(src, gate, dst, gate_dst, send, recv, fsend, g_send, g_recv, loc):
        dp, ex = lax.axis_index("dp"), lax.axis_index("expert")
        x, c = ex // nc, lax.rem(ex, nc)
        greet([(dp, lax.rem(ex + d, nex)) for d in range(1, nex)])
        sends = []

        def go(ref, slot, part, sem, target):
            rows_part = pl.ds(part * extent, extent)
            copy = remote(
                ref, dst.at[slot, rows_part], sem, recv.at[slot, part], (dp, target)
            )
            copy.start()
            sends.append(copy)

        def arrived(slot, part):
            rows_part = pl.ds(part * extent, extent)
            remote(
                src.at[rows_part], dst.at[slot, rows_part], send.at[0, 0], recv.at[slot, part],
                (dp, ex),
            ).wait_recv()

        gate_copies = []
        for d in range(1, nex):
            copy = remote(
                gate, gate_dst.at[ex], g_send.at[d - 1], g_recv.at[d - 1],
                (dp, lax.rem(ex + d, nex)),
            )
            copy.start()
            gate_copies.append(copy)
        for part in range(parts):
            for dx in range(1, nx):
                target = lax.rem(x + dx, nx) * nc + c
                go(src.at[pl.ds(part * extent, extent)], ex, part, send.at[dx - 1, part], target)
        for part in range(parts):
            for dc in range(1, nc):
                target = x * nc + lax.rem(c + dc, nc)
                go(
                    src.at[pl.ds(part * extent, extent)], ex, part,
                    send.at[nx - 1 + dc - 1, part], target,
                )
        own = [
            pltpu.make_async_copy(src, dst.at[ex], loc.at[0]),
            pltpu.make_async_copy(gate, gate_dst.at[ex], loc.at[1]),
        ]
        for copy in own:
            copy.start()
        for part in range(parts):
            for dx in range(1, nx):
                slot = lax.rem(x + nx - dx, nx) * nc + c
                arrived(slot, part)
                for dc in range(1, nc):
                    target = x * nc + lax.rem(c + dc, nc)
                    go(
                        dst.at[slot, pl.ds(part * extent, extent)], slot, part,
                        fsend.at[dx - 1, part], target,
                    )
        for part in range(parts):
            for dc in range(1, nc):
                for dx in range(nx):
                    arrived(lax.rem(x + nx - dx, nx) * nc + lax.rem(c + nc - dc, nc), part)
        for copy in gate_copies + own:
            copy.wait()
        for copy in sends:
            copy.wait_send()

    dma = pltpu.SemaphoreType.DMA
    return pl.pallas_call(
        kernel,
        out_shape=(
            jax.ShapeDtypeStruct((nex,) + rows.shape, rows.dtype),
            jax.ShapeDtypeStruct((nex,) + gates.shape, gates.dtype),
        ),
        in_specs=[any_spec()] * 2,
        out_specs=(any_spec(),) * 2,
        scratch_shapes=[
            dma((nx + nc, parts)),
            dma((nex, parts)),
            dma((nx, parts)),
            dma((nex - 1,)),
            dma((nex - 1,)),
            dma((2,)),
        ],
        compiler_params=comm_params(4),
        name="expert_gather",
    )(rows, gates)


def turn(values, cosine, sine):
    first, second = values[: HEAD_DIM // 2], values[HEAD_DIM // 2 :]
    return jnp.concatenate(
        [first * cosine - second * sine, second * cosine + first * sine], axis=0
    )


def allowed_mask(extent, block, length):
    keys = lax.broadcasted_iota(jnp.int32, (extent, QBLOCK), 0)
    queries = lax.broadcasted_iota(jnp.int32, (extent, QBLOCK), 1) + block * QBLOCK
    return (keys <= queries) & (keys < length)


def attend(grid, info, tok, weights, gain, cosine, sine):
    units, length = grid.units, tok.shape[1]
    blocks = length // QBLOCK

    def kernel(info_ref, tok_ref, w_ref, gain_ref, cos_ref, sin_ref,
               out_ref, act_ref, q_ref, k_ref, v_ref, lse_ref):
        i = pl.program_id(0)
        fresh = (i == 0) | (info_ref[0, i] != info_ref[0, jnp.maximum(i - 1, 0)])

        @pl.when(fresh)
        def _():
            residual = tok_ref[0].astype(F32)
            scale = lax.rsqrt(jnp.mean(residual * residual, axis=-1, keepdims=True) + eps_norm)
            act_ref[0] = (residual * scale * gain_ref[...]).astype(BF16)

        cos, sin = cos_ref[...], sin_ref[...]
        qkv = dot(w_ref[:, 0].reshape(3 * HEAD_DIM, D), act_ref[0], 1, 1)
        query = turn(qkv[:HEAD_DIM], cos, sin).astype(BF16)
        key_wide = turn(qkv[HEAD_DIM : 2 * HEAD_DIM], cos, sin)
        key = key_wide.astype(BF16)
        value = qkv[2 * HEAD_DIM :].astype(BF16)
        key_rows = key_wide.T.astype(BF16)
        q_ref[0], k_ref[0], v_ref[0] = query, key, value
        live = info_ref[2, i]
        for block in range(blocks):
            extent = QBLOCK * (block + 1)
            lanes = slice(QBLOCK * block, extent)
            scores = dot(key_rows[:extent], query[:, lanes]) * HEAD_DIM ** (-0.5)
            scores = jnp.where(allowed_mask(extent, block, live), scores, neg_fill)
            top = jnp.max(scores, axis=0, keepdims=True)
            probs = jnp.exp(scores - top)
            total = jnp.sum(probs, axis=0, keepdims=True)
            result = dot(value[:, :extent], probs.astype(BF16))
            out_ref[0, :, lanes] = (result * (1.0 / total)).astype(BF16)
            lse_ref[0, :, lanes] = top + jnp.log(total)

    def unit(i, info_ref):
        return (i, 0, 0)

    feature = jax.ShapeDtypeStruct((units, HEAD_DIM, length), BF16)
    flops = units * length * length * HEAD_DIM * 2 * 8
    return pl.pallas_call(
        kernel,
        out_shape=(
            feature,
            jax.ShapeDtypeStruct((grid.slots, length, D), BF16),
            feature,
            feature,
            feature,
            jax.ShapeDtypeStruct((units, 1, length), F32),
        ),
        grid_spec=pltpu.PrefetchScalarGridSpec(
            num_scalar_prefetch=1,
            grid=(units,),
            in_specs=[
                pl.BlockSpec((1, length, D), lambda i, n: (n[0, i], 0, 0)),
                pl.BlockSpec((3, 1, HEAD_DIM, D), lambda i, n: (0, n[1, i], 0, 0)),
                pl.BlockSpec((1, D), lambda i, n: (0, 0)),
                pl.BlockSpec((HEAD_DIM // 2, length), lambda i, n: (0, 0)),
                pl.BlockSpec((HEAD_DIM // 2, length), lambda i, n: (0, 0)),
            ],
            out_specs=(
                pl.BlockSpec((1, HEAD_DIM, length), unit),
                pl.BlockSpec((1, length, D), lambda i, n: (n[0, i], 0, 0)),
                pl.BlockSpec((1, HEAD_DIM, length), unit),
                pl.BlockSpec((1, HEAD_DIM, length), unit),
                pl.BlockSpec((1, HEAD_DIM, length), unit),
                pl.BlockSpec((1, 1, length), unit),
            ),
        ),
        compiler_params=pltpu.CompilerParams(vmem_limit_bytes=40 * MIB),
        cost_estimate=pl.CostEstimate(
            flops=flops, bytes_accessed=8 * MIB, transcendentals=units * length * length
        ),
        name="attend",
    )(info, tok, weights, gain, cosine, sine)


def attend_back(grid, lives, tok, act, weights, query, key, value, lse, grad_heads, cosine, sine,
                group, early):
    units, length, ndp, nex = grid.units, act.shape[1], grid.ndp, grid.nex
    blocks = length // QBLOCK
    scale = HEAD_DIM ** (-0.5)
    early_width, late_width = early.shape[1], 3 * D + MISC
    early_sum, late_sum = RowScatter(grid, early_width), RowScatter(grid, late_width)
    early = early.reshape(grid.nx, grid.nc, early_sum.rows, early_width)
    n_early = len(early_sum.scratch())
    steps = [min(n, units - 1) for n in (2, 5)]

    def kernel(*refs):
        (live_ref, tok_ref, act_ref, w_ref, q_ref, k_ref, v_ref, lse_ref, do_ref, cos_ref, sin_ref,
         group_ref, early_ref, rows_out, early_out, late_out,
         acc, back, dq, dk, dv, grads, gain, late_ref, b_send, b_recv, b_loc) = refs[:27]
        early_sum.bind(early_ref, refs[27 : 27 + n_early])
        late_sum.bind(late_ref, refs[27 + n_early :])
        i = pl.program_id(0)
        dp, ex = lax.axis_index("dp"), lax.axis_index("expert")
        unit = dp * units + i
        working = unit < UNITS_ALL
        series, head = unit // HEADS, lax.rem(unit, HEADS)
        slot = jnp.minimum(series - grid.first_series(dp), grid.slots - 1)

        def back_copy(d, which):
            target = lax.rem(dp + d, ndp)
            return remote(
                back.at[which, pl.ds(pl.multiple_of(target * SEG, SEG), SEG)],
                rows_out.at[dp, which],
                b_send.at[d - 1, which],
                b_recv.at[d - 1, which],
                (target, ex),
            )

        def back_local(which):
            return pltpu.make_async_copy(
                back.at[which, pl.ds(pl.multiple_of(dp * SEG, SEG), SEG)],
                rows_out.at[dp, which],
                b_loc.at[which],
            )

        @pl.when(i == 0)
        def _():
            greet(
                [(lax.rem(dp + d, ndp), ex) for d in range(1, ndp)]
                + [(dp, lax.rem(ex + d, nex)) for d in range(1, nex)]
            )
            early_sum.start()
            grads[...] = jnp.zeros_like(grads)
            gain[...] = jnp.zeros_like(gain)

        @pl.when((i == 0) | (head == 0))
        def _():
            acc[...] = jnp.zeros_like(acc)

        @pl.when(working)
        def _():
            live = live_ref[i]
            query, key, value, grad = q_ref[i], k_ref[i], v_ref[i], do_ref[i]
            key_rows = key.astype(F32).T.astype(BF16)
            value_rows = value.astype(F32).T.astype(BF16)
            dk[...] = jnp.zeros_like(dk)
            dv[...] = jnp.zeros_like(dv)
            for block in range(blocks):
                extent = QBLOCK * (block + 1)
                lanes = slice(QBLOCK * block, extent)
                scores = dot(key_rows[:extent], query[:, lanes]) * scale
                scores = jnp.where(allowed_mask(extent, block, live), scores, neg_fill)
                probs = jnp.exp(scores - lse_ref[i, :, lanes])
                grad_probs = dot(value_rows[:extent], grad[:, lanes])
                delta = jnp.sum(probs * grad_probs, axis=0, keepdims=True)
                grad_scores = (probs * (grad_probs - delta)).astype(BF16)
                probs_low = probs.astype(BF16)
                dq[:, lanes] = dot(key[:, :extent], grad_scores)
                dk[:, :extent] += dot(query[:, lanes], grad_scores, 1, 1)
                dv[:, :extent] += dot(grad[:, lanes], probs_low, 1, 1)
            cos, sin = cos_ref[...], -sin_ref[...]
            stacked = jnp.concatenate(
                [
                    turn(dq[...] * scale, cos, sin),
                    turn(dk[...] * scale, cos, sin),
                    dv[...],
                ],
                axis=0,
            ).astype(BF16)
            weight_grads = dot(stacked, act_ref[slot]).astype(BF16)
            w_rows = []
            for n in range(3):
                at = pl.multiple_of(n * D + head * HEAD_DIM, HEAD_DIM)
                part = slice(n * HEAD_DIM, (n + 1) * HEAD_DIM)
                grads[pl.ds(at, HEAD_DIM)] = weight_grads[part]
                w_rows.append(w_ref[pl.ds(at, HEAD_DIM)])
            acc[...] += dot(stacked, jnp.concatenate(w_rows, axis=0), 0, 0)

        @pl.when(working & ((head == HEADS - 1) | (i == units - 1)))
        def _():
            share = acc[...]
            residual = tok_ref[slot].astype(F32)
            normed = residual * lax.rsqrt(
                jnp.mean(residual * residual, axis=-1, keepdims=True) + eps_norm
            )
            gain[...] += jnp.sum(share * normed, axis=0, keepdims=True)
            back[slot] = share.astype(BF16)
            for d in far_first(ndp):
                back_copy(d, slot).start()
            back_local(slot).start()

        @pl.when(i == steps[0])
        def _():
            early_sum.along_x()

        @pl.when(i == steps[1])
        def _():
            early_sum.along_dp()

        @pl.when(i == units - 1)
        def _():
            grads[3 * D :] = jnp.broadcast_to(gain[...], (ROW_PAD, D)).astype(BF16)
            late = dot(group_ref[...], grads[...], 1, 1).astype(BF16)
            late = late.reshape(late_ref.shape[:3] + (late.shape[1],))
            late_ref[:, :, :, : late.shape[3]] = late
            late_ref[:, :, :, late.shape[3] :] = jnp.zeros(
                late_ref.shape[:3] + (late_width - late.shape[3],), BF16
            )
            late_sum.start()
            early_sum.finish(early_out)
            late_sum.along_x()
            late_sum.along_dp()
            for which in range(grid.slots):
                for d in range(1, ndp):

                    @pl.when(grid.holds(lax.rem(dp + ndp - d, ndp), which))
                    def _():
                        back_copy(d, which).wait_recv()

                @pl.when(grid.holds(dp, which))
                def _():
                    for d in range(1, ndp):
                        back_copy(d, which).wait_send()
                    back_local(which).wait()

            late_sum.finish(late_out)

    def whole(array):
        return pl.BlockSpec(
            array.shape, lambda i: (0,) * array.ndim, pipeline_mode=pl.Buffered(1)
        )

    def whole_out(shape):
        return pl.BlockSpec(shape, lambda i: (0,) * len(shape))

    dma = pltpu.SemaphoreType.DMA
    inputs = (tok, act, weights, query, key, value, lse, grad_heads, cosine, sine, group, early)
    return pl.pallas_call(
        kernel,
        grid=(units,),
        out_shape=(
            jax.ShapeDtypeStruct((ndp, grid.slots, SEG, D), BF16),
            jax.ShapeDtypeStruct((ROW_PAD, early_width), F32),
            jax.ShapeDtypeStruct((ROW_PAD, late_width), F32),
        ),
        in_specs=[pl.BlockSpec(memory_space=pltpu.SMEM)] + [whole(v) for v in inputs],
        out_specs=(
            any_spec(),
            whole_out((ROW_PAD, early_width)),
            whole_out((ROW_PAD, late_width)),
        ),
        scratch_shapes=[
            pltpu.VMEM((length, D), F32),
            pltpu.VMEM((grid.slots, length, D), BF16),
            pltpu.VMEM((HEAD_DIM, length), F32),
            pltpu.VMEM((HEAD_DIM, length), F32),
            pltpu.VMEM((HEAD_DIM, length), F32),
            pltpu.VMEM((3 * D + ROW_PAD, D), BF16),
            pltpu.VMEM((1, D), F32),
            pltpu.VMEM((grid.nx, grid.nc, late_sum.rows, late_width), BF16),
            dma((ndp - 1, grid.slots)),
            dma((ndp - 1, grid.slots)),
            dma((grid.slots,)),
        ]
        + early_sum.scratch()
        + late_sum.scratch(),
        compiler_params=pltpu.CompilerParams(
            collective_id=3, has_side_effects=True, vmem_limit_bytes=56 * MIB
        ),
        cost_estimate=pl.CostEstimate(
            flops=units * length * length * HEAD_DIM * 2 * 20,
            bytes_accessed=12 * MIB,
            transcendentals=units * length * length,
        ),
        name="attend_back",
    )(lives, *inputs)


def experts_step(weights, act_all, cot_all, rank_row, rank_col, gates):
    sources, rows = act_all.shape[:2]
    local = weights.shape[0]
    parts = FF // D

    def kernel(w_ref, act_ref, cot_ref, rrow_ref, rcol_ref, gate_ref,
               routed_ref, gin_ref, ggate_ref, x_ref, dg_ref, du_ref, hid_ref, dy_ref):
        act, cot = act_ref[0], cot_ref[0]
        slot_down = lax.broadcasted_iota(jnp.int32, (CAP, rows), 0)
        slot_across = lax.broadcasted_iota(jnp.int32, (rows, CAP), 1)
        routed = jnp.zeros((rows, D), F32)
        grad_in = jnp.zeros((rows, D), F32)
        for e in range(local):
            pick = slot_down == rrow_ref[0, e : e + 1, :]
            pick_low = pick.astype(F32).astype(BF16)
            spread = (slot_across == rcol_ref[0, :, e : e + 1]).astype(F32).astype(BF16)
            taken = dot(pick_low, act).astype(BF16)
            grad_rows = dot(pick_low, cot)
            gate = jnp.sum(jnp.where(pick, gate_ref[0, e : e + 1, :], 0.0), axis=1, keepdims=True)
            grad_result = (gate * grad_rows).astype(BF16)
            x_ref[e, 0] = taken
            dy_ref[e, 0] = grad_result
            result = jnp.zeros((CAP, D), F32)
            grad_taken = jnp.zeros((CAP, D), F32)
            for part in range(parts):
                lanes = slice(part * D, (part + 1) * D)
                w_gate = w_ref[e, 0:D, lanes]
                w_up = w_ref[e, D : 2 * D, lanes]
                w_down = w_ref[e, 2 * D : 3 * D, lanes]
                gate_lin = dot(taken, w_gate)
                up_lin = dot(taken, w_up)
                sig = jax.nn.sigmoid(gate_lin)
                silu = gate_lin * sig
                hidden = (silu * up_lin).astype(BF16)
                result += dot(hidden, w_down)
                grad_hidden = dot(grad_result, w_down, 1, 1)
                slope = sig * (1.0 + gate_lin * (1.0 - sig))
                grad_gate = (grad_hidden * up_lin * slope).astype(BF16)
                grad_up = (grad_hidden * silu).astype(BF16)
                hid_ref[e, 0, :, lanes] = hidden
                dg_ref[e, 0, :, lanes] = grad_gate
                du_ref[e, 0, :, lanes] = grad_up
                grad_taken += dot(grad_gate, w_gate, 1, 1) + dot(grad_up, w_up, 1, 1)
            result = result.astype(BF16).astype(F32)
            grad_gate_slot = jnp.sum(grad_rows * result, axis=1, keepdims=True)
            ggate_ref[0, e : e + 1, :] = jnp.sum(
                jnp.where(pick, grad_gate_slot, 0.0), axis=0, keepdims=True
            )
            routed += dot(spread, (gate * result).astype(BF16))
            grad_in += dot(spread, grad_taken.astype(BF16))
        routed_ref[0] = routed.astype(BF16)
        gin_ref[0] = grad_in.astype(BF16)

    def per_source(*tail):
        return pl.BlockSpec((1,) + tail, lambda s: (s,) + (0,) * len(tail))

    def kept(width):
        return pl.BlockSpec((local, 1, CAP, width), lambda s: (0, s, 0, 0))

    def kept_shape(width):
        return jax.ShapeDtypeStruct((local, sources, CAP, width), BF16)

    return pl.pallas_call(
        kernel,
        grid=(sources,),
        out_shape=(
            jax.ShapeDtypeStruct((sources, rows, D), BF16),
            jax.ShapeDtypeStruct((sources, rows, D), BF16),
            jax.ShapeDtypeStruct((sources, local, rows), F32),
            kept_shape(D),
            kept_shape(FF),
            kept_shape(FF),
            kept_shape(FF),
            kept_shape(D),
        ),
        in_specs=[
            pl.BlockSpec(weights.shape, lambda s: (0, 0, 0), pipeline_mode=pl.Buffered(1)),
            per_source(rows, D),
            per_source(rows, D),
            per_source(local, rows),
            per_source(rows, local),
            per_source(local, rows),
        ],
        out_specs=(
            per_source(rows, D),
            per_source(rows, D),
            per_source(local, rows),
            kept(D),
            kept(FF),
            kept(FF),
            kept(FF),
            kept(D),
        ),
        compiler_params=pltpu.CompilerParams(vmem_limit_bytes=56 * MIB),
        cost_estimate=pl.CostEstimate(
            flops=sources * local * CAP * D * FF * 2 * 8,
            bytes_accessed=50 * MIB,
            transcendentals=sources * local * CAP * FF,
        ),
        name="experts_step",
    )(weights, act_all, cot_all, rank_row, rank_col, gates)


def local(
    tokens,
    cotangent,
    lengths,
    routes,
    dense_weights,
    dense_first,
    dense_second,
    dense_average,
    expert_weights,
    expert_first,
    expert_second,
    expert_average,
):
    ndp, nex = lax.axis_size("dp"), lax.axis_size("expert")
    dp, ex = lax.axis_index("dp"), lax.axis_index("expert")
    grid = Grid(ndp, nex)
    local_experts = EXPERTS // nex
    length = SEG * ndp
    rows_dev = D // grid.ndev
    shard_rows = 3 * D // ndp

    spot = jnp.arange(FF, dtype=jnp.int32)
    order = (FF // D) * (spot % D) + spot // D
    mix = (spot[:, None] == order[None, :]).astype(BF16)
    shard_row = dp * shard_rows + jnp.arange(shard_rows, dtype=jnp.int32)
    is_down = (shard_row >= 2 * D)[None, :, None]
    expert_low = expert_weights.astype(BF16).reshape(local_experts, shard_rows, FF)
    mixed_low = jnp.einsum(
        "erf,fg->erg", expert_low, mix, preferred_element_type=F32
    ).astype(BF16)
    expert_send = jnp.where(is_down, expert_low, mixed_low)
    expert_all = lax.all_gather(expert_send, "dp", axis=0, tiled=False)
    expert_all = expert_all.transpose(1, 0, 2, 3).reshape(local_experts, 3 * D, FF)

    table = dense_weights.astype(BF16).reshape(rows_dev, -1)
    after = 4 * D + EXPERTS
    shard = jnp.concatenate(
        [
            table[:, : 4 * D],
            table[:, after : after + 3 * FF],
            table[:, 4 * D : after],
            table[:, after + 3 * FF :],
            jnp.zeros((rows_dev, MISC - EXPERTS - 3), BF16),
        ],
        axis=1,
    )
    shard = jnp.pad(shard, ((0, ROW_PAD - rows_dev), (0, 0)))

    names = jnp.arange(EXPERTS, dtype=jnp.int32)
    routes_rows = routes.reshape(TOK_DEV, TOP)
    member = (routes_rows[:, :, None] == names[None, None, :]).any(axis=1)
    before = jnp.arange(TOK_DEV)
    earlier = (before[None, :] < before[:, None]).astype(BF16)
    count = jnp.dot(earlier, member.astype(BF16), preferred_element_type=F32)
    ranks = jnp.where(member, count.astype(jnp.int32), -1).T

    local_pos = dp * SEG + jnp.arange(SEG, dtype=jnp.int32)
    live = (local_pos[None, :] < lengths[:, None]).astype(F32)
    grad_out_low = (cotangent.astype(F32) * live[..., None]).astype(BF16).reshape(TOK_DEV, D)

    tok_all, dense_all, cot_all, rank_all = first_exchange(
        grid, tokens, shard, grad_out_low, ranks
    )

    tok_all = tok_all.reshape(grid.slots, length, D)

    dense_all = dense_all.reshape(grid.ndev * ROW_PAD, -1)
    row = jnp.arange(D, dtype=jnp.int32)
    row_from = (row // rows_dev) * ROW_PAD + row % rows_dev
    unpad = (row_from[:, None] == jnp.arange(grid.ndev * ROW_PAD)[None, :]).astype(BF16)
    qkv_rows = dot(dense_all[:, : 3 * D], unpad, 0, 1).astype(BF16)
    qkv_rows = qkv_rows.reshape(3, HEADS, HEAD_DIM, D)
    rest = dot(unpad, dense_all[:, 3 * D :]).astype(BF16)
    w_output = rest[:, :D]
    w_sgate = rest[:, D : D + FF]
    w_sup = rest[:, D + FF : D + 2 * FF]
    w_sdown = rest[:, D + 2 * FF : D + 3 * FF]
    w_misc = rest[:, D + 3 * FF :]
    gain_first = w_misc[:, EXPERTS + 1].astype(F32)
    gain_second = w_misc[:, EXPERTS + 2].astype(F32)

    unit = dp * grid.units + jnp.arange(HEADS, dtype=jnp.int32)
    working = (jnp.arange(HEADS) < grid.units) & (unit < UNITS_ALL)
    last = jnp.minimum(dp * grid.units + grid.units, UNITS_ALL) - 1
    series = jnp.clip(jnp.minimum(unit, last) // HEADS, 0, SERIES_DEV - 1)
    slot = jnp.clip(series - grid.first_series(dp), 0, grid.slots - 1)
    info = jnp.stack(
        [slot, unit % HEADS, lengths[series], working.astype(jnp.int32)]
    ).astype(jnp.int32)
    half = HEAD_DIM // 2
    inverse = rope_base ** (-jnp.arange(half, dtype=F32) * 2.0 / HEAD_DIM)
    angles = inverse[:, None] * jnp.arange(length, dtype=jnp.int32).astype(F32)[None, :]
    cosine, sine = jnp.cos(angles), jnp.sin(angles)
    heads, act_one, query, key, value, lse = attend(
        grid,
        info,
        tok_all,
        qkv_rows,
        gain_first[None, :],
        cosine,
        sine,
    )
    heads_here = heads_out(grid, heads).reshape(-1, HEAD_DIM, SEG)[:UNITS_ALL]
    attn_low = heads_here.reshape(SERIES_DEV, D, SEG).transpose(0, 2, 1).reshape(TOK_DEV, D)

    residual = tokens.astype(F32).reshape(TOK_DEV, D)
    mixed_rows = residual + dot(attn_low, w_output)
    scale_two = lax.rsqrt(jnp.mean(mixed_rows * mixed_rows, axis=-1, keepdims=True) + eps_norm)
    normed_two = mixed_rows * scale_two
    act_two = (normed_two * gain_second).astype(BF16)
    misc = dot(act_two, w_misc)
    router_probs = jax.nn.softmax(misc[:, :EXPERTS], axis=-1)
    shared_gate = jax.nn.sigmoid(misc[:, EXPERTS : EXPERTS + 1])

    act_all, gates_all = expert_gather(grid, act_two, router_probs.T)
    rank_row = lax.dynamic_slice_in_dim(rank_all, ex * local_experts, local_experts, 1)
    gate_row = lax.dynamic_slice_in_dim(gates_all, ex * local_experts, local_experts, 1)
    routed_parts, gin_parts, ggate, taken, grad_gate_lin, grad_up_lin, hidden, grad_result = (
        experts_step(
            expert_all, act_all, cot_all, rank_row, rank_row.transpose(0, 2, 1), gate_row
        )
    )
    gin_back = lax.all_to_all(gin_parts, "expert", split_axis=0, concat_axis=0, tiled=True)
    ggate_back = lax.all_to_all(ggate, "expert", split_axis=0, concat_axis=0, tiled=True)
    routed_back = lax.all_to_all(routed_parts, "expert", split_axis=0, concat_axis=0, tiled=True)

    def by_expert(rows):
        return rows.reshape(local_experts, nex * CAP, -1)

    taken, grad_gate_lin, grad_up_lin, hidden, grad_result = (
        by_expert(v) for v in (taken, grad_gate_lin, grad_up_lin, hidden, grad_result)
    )
    grad_e_gate = jnp.einsum("erd,erf->edf", taken, grad_gate_lin, preferred_element_type=F32)
    grad_e_up = jnp.einsum("erd,erf->edf", taken, grad_up_lin, preferred_element_type=F32)
    grad_e_down = [
        jnp.einsum(
            "erh,erd->ehd", hidden[..., at : at + D], grad_result, preferred_element_type=F32
        )
        for at in range(0, FF, D)
    ]
    expert_terms = jnp.concatenate(
        [
            grad_e_gate.astype(BF16),
            grad_e_up.astype(BF16),
            jnp.concatenate(grad_e_down, axis=2).astype(BF16),
        ],
        axis=1,
    )
    expert_terms = expert_terms.reshape(local_experts, ndp, shard_rows, FF).transpose(1, 0, 2, 3)
    expert_sum = lax.psum_scatter(expert_terms, "dp", scatter_dimension=0, tiled=False)
    unmixed = jnp.einsum("erg,fg->erf", expert_sum, mix, preferred_element_type=F32)
    expert_grad = jnp.where(is_down, expert_sum.astype(F32), unmixed)
    expert_grad = expert_grad.reshape(expert_weights.shape)

    sgate_lin = dot(act_two, w_sgate)
    sup_lin = dot(act_two, w_sup)
    sgate_sigmoid = jax.nn.sigmoid(sgate_lin)
    sgate_silu = sgate_lin * sgate_sigmoid
    shared_hidden = (sgate_silu * sup_lin).astype(BF16)
    shared_lin = dot(shared_hidden, w_sdown, 1, 1)
    grad_out = grad_out_low.astype(F32)
    grad_shared_lin = (grad_out * shared_gate).astype(BF16)
    grad_svec_logit = (
        shared_gate * (1.0 - shared_gate) * jnp.sum(grad_out * shared_lin, axis=-1, keepdims=True)
    ).astype(BF16)
    grad_shared_hidden = dot(grad_shared_lin, w_sdown)
    grad_sgate_lin = (
        grad_shared_hidden * sup_lin * sgate_sigmoid * (1.0 + sgate_lin * (1.0 - sgate_sigmoid))
    ).astype(BF16)
    grad_sup_lin = (grad_shared_hidden * sgate_silu).astype(BF16)

    routed = jnp.sum(routed_back.astype(F32), axis=0)
    output = (mixed_rows + routed + shared_gate * shared_lin).astype(BF16)
    grad_router_probs = ggate_back.reshape(EXPERTS, TOK_DEV).T
    grad_logits = (
        router_probs
        * (grad_router_probs - jnp.sum(router_probs * grad_router_probs, axis=-1, keepdims=True))
    ).astype(BF16)
    grad_misc = jnp.concatenate(
        [grad_logits, grad_svec_logit, jnp.zeros((TOK_DEV, MISC - EXPERTS - 1), BF16)], axis=1
    )
    grad_act_two = (
        jnp.sum(gin_back.astype(F32), axis=0)
        + dot(grad_sgate_lin, w_sgate, 1, 1)
        + dot(grad_sup_lin, w_sup, 1, 1)
        + dot(grad_misc, w_misc, 1, 1)
    )
    grad_gain_two = jnp.sum(grad_act_two * normed_two, axis=0)
    weighted_two = grad_act_two * gain_second
    grad_mixed = grad_out + scale_two * (
        weighted_two - normed_two * jnp.mean(weighted_two * normed_two, axis=-1, keepdims=True)
    )
    grad_attn_low = grad_mixed.astype(BF16)
    grad_heads = dot(grad_attn_low, w_output, 1, 1).astype(BF16)
    grad_heads = grad_heads.reshape(SERIES_DEV, SEG, D).transpose(0, 2, 1)
    grad_heads = grad_heads.reshape(UNITS_ALL, HEAD_DIM, SEG)
    grad_heads = jnp.pad(grad_heads, ((0, grid.units * ndp - UNITS_ALL), (0, 0), (0, 0)))
    row_dev = row // rows_dev
    row_to = ((row_dev % nex) * ndp + row_dev // nex) * rows_dev + row % rows_dev
    group = (row[:, None] == row_to[None, :]).astype(BF16)
    attn_grouped = jnp.einsum(
        "gf,sfp->gsp", group, heads_here.reshape(SERIES_DEV, D, SEG), preferred_element_type=F32
    )
    grad_heads, early = heads_in(
        grid,
        grad_heads.reshape(ndp, grid.units, HEAD_DIM, SEG),
        dot(group, act_two, 1, 1).astype(BF16),
        dot(group, grad_shared_lin, 1, 1).astype(BF16),
        attn_grouped.astype(BF16).reshape(D, TOK_DEV),
        (grad_attn_low, grad_sgate_lin, grad_sup_lin, grad_misc),
        shared_hidden,
    )
    gain_two_grouped = dot(group, grad_gain_two.astype(BF16)[:, None]).astype(BF16)
    early = early.at[:, D + 3 * FF + EXPERTS + 2].set(gain_two_grouped[:, 0])

    back, early, late = attend_back(
        grid, info[2], tok_all, act_one, qkv_rows.reshape(3 * D, D), query, key, value, lse,
        grad_heads, cosine, sine, group, early,
    )
    grad_act_one = jnp.stack(
        [
            sum(
                back[owner, owned.index(s)].astype(F32)
                for owner, owned in enumerate(grid.owned)
                if s in owned
            )
            for s in range(SERIES_DEV)
        ]
    ).reshape(TOK_DEV, D)
    scale_one = lax.rsqrt(jnp.mean(residual * residual, axis=-1, keepdims=True) + eps_norm)
    normed_one = residual * scale_one
    weighted_one = grad_act_one * gain_first
    grad_tokens = grad_mixed + scale_one * (
        weighted_one - normed_one * jnp.mean(weighted_one * normed_one, axis=-1, keepdims=True)
    )

    early, late = early[:rows_dev], late[:rows_dev]
    misc_at = D + 3 * FF
    dense_grad = jnp.concatenate(
        [
            late[:, : 3 * D],
            early[:, :D],
            early[:, misc_at : misc_at + EXPERTS],
            early[:, D:misc_at],
            early[:, misc_at + EXPERTS : misc_at + EXPERTS + 1],
            late[:, 3 * D : 3 * D + 1],
            early[:, misc_at + EXPERTS + 2 : misc_at + EXPERTS + 3],
        ],
        axis=1,
    ).reshape(-1)

    dense_first_new, dense_second_new, dense_new, dense_average_new = adamw_update(
        dense_weights, dense_grad, dense_first, dense_second, dense_average
    )
    expert_first_new, expert_second_new, expert_new, expert_average_new = adamw_update(
        expert_weights, expert_grad, expert_first, expert_second, expert_average
    )
    return (
        output.reshape(tokens.shape),
        grad_tokens.reshape(tokens.shape),
        dense_grad,
        dense_first_new,
        dense_second_new,
        dense_new,
        dense_average_new,
        expert_grad,
        expert_first_new,
        expert_second_new,
        expert_new,
        expert_average_new,
    )


def solution(mesh):
    rows = P("expert", "dp", None)
    dense = P(("dp", "expert"))
    experts = P("expert", "dp")
    return jax.shard_map(
        local,
        mesh=mesh,
        in_specs=(
            (rows, rows, P("expert"), P("dp", "expert", None, None)) + (dense,) * 4 + (experts,) * 4
        ),
        out_specs=(rows, rows) + (dense,) * 5 + (experts,) * 5,
        check_vma=False,
    )
```

```python
import functools
import math

import jax
import jax.numpy as jnp
from jax import lax
from jax.experimental import pallas as pl
from jax.experimental.pallas import tpu as pltpu
from jax.sharding import PartitionSpec as P

D = 384
HEADS = 12
HEAD_DIM = 32
FF = 1536
EXPERTS = 8
TOP = 2
SEG = 128
SERIES_DEV = 6
STEP = 8
TOK_DEV = 768
CAP = 384
ROW_PAD = 16
MISC = 128
UNITS_ALL = SERIES_DEV * HEADS
QBLOCK = 256
MIB = 1 << 20

eps_norm = 1e-06
beta_one = 0.5
beta_two = 0.5
learn_rate = 0.02
weight_decay = 0.1
eps_adam = 1e-08
average_keep = 0.9
rope_base = 10000.0
neg_fill = -1e30

MESH = pl.DeviceIdType.MESH
F32 = jnp.float32
BF16 = jnp.bfloat16


def adamw_update(weights, grads, first, second, average):
    first_new = beta_one * first + (1.0 - beta_one) * grads
    second_new = beta_two * second + (1.0 - beta_two) * grads * grads
    first_hat = first_new / (1.0 - beta_one**STEP)
    second_hat = second_new / (1.0 - beta_two**STEP)
    weights_new = weights - learn_rate * (
        first_hat / (jnp.sqrt(second_hat) + eps_adam) + weight_decay * weights
    )
    average_new = average_keep * average + (1.0 - average_keep) * weights_new
    return (first_new, second_new, weights_new, average_new)


def dot(left, right, left_dim=1, right_dim=0):
    return lax.dot_general(
        left, right, (((left_dim,), (right_dim,)), ((), ())), preferred_element_type=F32
    )


class Grid:
    def __init__(self, ndp, nex):
        self.ndp, self.nex = ndp, nex
        self.nz = math.gcd(ndp, 4)
        self.ny = ndp // self.nz
        self.nc = math.gcd(nex, 2)
        self.nx = nex // self.nc
        self.ndev = ndp * nex
        self.units = -(-UNITS_ALL // ndp)
        spans = [
            [u // HEADS for u in range(self.units * o, min(self.units * (o + 1), UNITS_ALL))]
            for o in range(ndp)
        ]
        self.owned = [sorted(set(s)) for s in spans]
        self.slots = max(len(s) for s in self.owned)

    def first_series(self, owner):
        return (owner * self.units) // HEADS

    def holds(self, owner, slot):
        begin = owner * self.units
        end = jnp.minimum(begin + self.units, UNITS_ALL)
        return (begin // HEADS + slot) * HEADS < end


def remote(src, dst, send, recv, target):
    return pltpu.make_async_remote_copy(
        src_ref=src,
        dst_ref=dst,
        send_sem=send,
        recv_sem=recv,
        device_id=target,
        device_id_type=MESH,
    )


def greet(peers):
    barrier = pltpu.get_barrier_semaphore()
    for peer in peers:
        pl.semaphore_signal(barrier, inc=1, device_id=peer, device_id_type=MESH)
    pl.semaphore_wait(barrier, len(peers))


def any_spec():
    return pl.BlockSpec(memory_space=pl.ANY)


def far_first(n):
    return sorted(range(1, n), key=lambda d: -min(d, n - d))


def comm_params(number):
    return pltpu.CompilerParams(collective_id=number, has_side_effects=True)


class DenseGather:
    def __init__(self, grid):
        self.grid = grid

    def scratch(self):
        dma = pltpu.SemaphoreType.DMA
        return [dma((self.grid.ndev,)), dma((self.grid.ndev,)), dma]

    def bind(self, shard, out, refs):
        g = self.grid
        self.shard, self.out = shard, out
        self.send, self.recv, self.loc = refs
        dp, ex = lax.axis_index("dp"), lax.axis_index("expert")
        self.z, self.y = dp // g.ny, lax.rem(dp, g.ny)
        self.x, self.c = ex // g.nc, lax.rem(ex, g.nc)
        self.zs = [0] + far_first(g.nz)[::-1]
        self.count = 0
        self.ends = []

    def place(self, dz, dy, dx, dc):
        g = self.grid
        return (
            lax.rem(self.z + dz, g.nz) * g.ny + lax.rem(self.y + dy, g.ny),
            lax.rem(self.x + dx, g.nx) * g.nc + lax.rem(self.c + dc, g.nc),
        )

    def slot(self, dz, dy, dx, dc):
        g = self.grid
        dp, ex = self.place(g.nz - dz, g.ny - dy, g.nx - dx, g.nc - dc)
        return dp * g.nex + ex

    def copy(self, ref, slot, number, target):
        return remote(ref, self.out.at[slot], self.send.at[number], self.recv.at[slot], target)

    def go(self, slot, target):
        ref = self.out.at[slot]
        if self.count < self.own_sends():
            ref = self.shard
        self.copy(ref, slot, self.count, target).start()
        self.count += 1

    def own_sends(self):
        g = self.grid
        return g.nz + g.ny + g.nx + g.nc - 4

    def wait(self, slot):
        self.copy(self.shard, slot, 0, self.place(0, 0, 0, 0)).wait_recv()

    def onward(self, slot, axes):
        g = self.grid
        if "y" in axes:
            for dy in range(1, g.ny):
                self.go(slot, self.place(0, dy, 0, 0))
        if "x" in axes:
            for dx in range(1, g.nx):
                self.go(slot, self.place(0, 0, dx, 0))
        for dc in range(1, g.nc):
            self.go(slot, self.place(0, 0, 0, dc))

    def own(self):
        return pltpu.make_async_copy(self.shard, self.out.at[self.slot(0, 0, 0, 0)], self.loc)

    def start(self):
        own = self.slot(0, 0, 0, 0)
        for dz in far_first(self.grid.nz):
            self.go(own, self.place(dz, 0, 0, 0))
        self.onward(own, "yx")
        self.own().start()

    def pass_z(self):
        for dz in self.zs[1:]:
            slot = self.slot(dz, 0, 0, 0)
            self.wait(slot)
            self.onward(slot, "yx")

    def pass_y(self):
        for dy in range(1, self.grid.ny):
            for dz in self.zs:
                slot = self.slot(dz, dy, 0, 0)
                self.wait(slot)
                self.onward(slot, "x")

    def pass_x(self):
        g = self.grid
        for dx in range(1, g.nx):
            for dy in range(g.ny):
                for dz in self.zs:
                    slot = self.slot(dz, dy, dx, 0)
                    self.wait(slot)
                    self.onward(slot, "")

    def finish(self):
        g = self.grid
        for dc in range(1, g.nc):
            for dx in range(g.nx):
                for dy in range(g.ny):
                    for dz in self.zs:
                        self.wait(self.slot(dz, dy, dx, dc))
        for number in range(g.ndev - 1):
            self.copy(self.shard, 0, number, self.place(0, 0, 0, 0)).wait_send()
        self.own().wait()


class RowGather:
    parts = 3

    def __init__(self, grid):
        self.grid = grid

    def scratch(self):
        g, n = self.grid, self.parts
        dma = pltpu.SemaphoreType.DMA
        return [dma((g.nx + g.nc, n)), dma((g.nex, n)), dma((g.nx, n)), dma]

    def bind(self, src, dst, refs):
        g = self.grid
        self.src, self.dst = src, dst
        self.send, self.recv, self.fsend, self.loc = refs
        self.dp, self.ex = lax.axis_index("dp"), lax.axis_index("expert")
        self.x, self.c = self.ex // g.nc, lax.rem(self.ex, g.nc)
        self.sends = []

    def rows(self, part):
        extent = TOK_DEV // self.parts
        return pl.ds(part * extent, extent)

    def slot_at(self, owner, target):
        return lax.rem(owner - target - 1 + 2 * self.grid.nex, self.grid.nex)

    def go(self, ref, owner, part, sem, target):
        slot = self.slot_at(owner, target)
        copy = remote(
            ref, self.dst.at[slot, self.rows(part)], sem, self.recv.at[slot, part],
            (self.dp, target),
        )
        copy.start()
        self.sends.append(copy)

    def arrived(self, owner, part):
        slot = self.slot_at(owner, self.ex)
        remote(
            self.src.at[self.rows(part)], self.dst.at[slot, self.rows(part)], self.send.at[0, 0],
            self.recv.at[slot, part], (self.dp, self.ex),
        ).wait_recv()

    def beside(self, dc):
        g = self.grid
        return self.x * g.nc + lax.rem(self.c + dc, g.nc)

    def start(self):
        g = self.grid
        for part in range(self.parts):
            for dx in range(1, g.nx):
                target = lax.rem(self.x + dx, g.nx) * g.nc + self.c
                ref = self.src.at[self.rows(part)]
                self.go(ref, self.ex, part, self.send.at[dx - 1, part], target)
        for part in range(self.parts):
            for dc in range(1, g.nc):
                ref = self.src.at[self.rows(part)]
                self.go(ref, self.ex, part, self.send.at[g.nx + dc - 2, part], self.beside(dc))
        self.own = pltpu.make_async_copy(self.src, self.dst.at[g.nex - 1], self.loc)
        self.own.start()

    def pass_on(self, part):
        g = self.grid
        for dx in range(1, g.nx):
            owner = lax.rem(self.x + g.nx - dx, g.nx) * g.nc + self.c
            self.arrived(owner, part)
            for dc in range(1, g.nc):
                ref = self.dst.at[self.slot_at(owner, self.ex), self.rows(part)]
                self.go(ref, owner, part, self.fsend.at[dx - 1, part], self.beside(dc))

    def finish(self):
        g = self.grid
        for part in range(self.parts):
            for dc in range(1, g.nc):
                for dx in range(g.nx):
                    owner = lax.rem(self.x + g.nx - dx, g.nx) * g.nc
                    self.arrived(owner + lax.rem(self.c + g.nc - dc, g.nc), part)
        for copy in self.sends:
            copy.wait_send()
        self.own.wait()


def first_exchange(grid, tokens, shard, cot, ranks):
    ndp, nex = grid.ndp, grid.nex

    def kernel(tok, shd, cot_in, rank_in, tok_out, dense_out, cot_out, rank_out,
               t_send, t_recv, e_send, e_recv, loc, *more_refs):
        dp, ex = lax.axis_index("dp"), lax.axis_index("expert")

        def off(value, by, n):
            return lax.rem(value + by, n)

        peers = [(off(dp, d, ndp), ex) for d in range(1, ndp)]
        peers += [(dp, off(ex, d, nex)) for d in range(1, nex)]
        greet(peers)
        dense = DenseGather(grid)
        dense.bind(shd, dense_out, more_refs[4:])
        dense.start()

        def token_copy(d, slot, src_series, sender, target):
            return remote(
                tok.at[src_series],
                tok_out.at[slot, sender],
                t_send.at[d - 1, slot],
                t_recv.at[d - 1, slot],
                (target, ex),
            )

        for d in far_first(ndp):
            target = off(dp, d, ndp)
            for slot in range(grid.slots):

                @pl.when(grid.holds(target, slot))
                def _():
                    token_copy(d, slot, grid.first_series(target) + slot, dp, target).start()

        rows = RowGather(grid)
        rows.bind(cot_in, cot_out, more_refs[:4])
        rows.start()
        e_sends = []
        for d in range(1, nex):
            target = off(ex, d, nex)
            copy = remote(
                rank_in.at[target], rank_out.at[nex - 1 - d], e_send.at[d - 1], e_recv.at[d - 1],
                (dp, target),
            )
            copy.start()
            e_sends.append(copy)
        copy = pltpu.make_async_copy(rank_in.at[ex], rank_out.at[nex - 1], loc.at[0])
        copy.start()
        e_sends.append(copy)

        for slot in range(grid.slots):

            @pl.when(grid.holds(dp, slot))
            def _():
                copy = pltpu.make_async_copy(
                    tok.at[grid.first_series(dp) + slot], tok_out.at[slot, dp], loc.at[1 + slot]
                )
                copy.start()
                copy.wait()

        dense.pass_z()
        rows.pass_on(0)
        dense.pass_y()
        for part in range(1, rows.parts):
            rows.pass_on(part)
        dense.pass_x()
        dense.finish()
        rows.finish()
        for d in range(1, ndp):
            for slot in range(grid.slots):

                @pl.when(grid.holds(dp, slot))
                def _():
                    token_copy(d, slot, 0, dp, off(dp, d, ndp)).wait_recv()

                @pl.when(grid.holds(off(dp, d, ndp), slot))
                def _():
                    token_copy(d, slot, 0, dp, off(dp, d, ndp)).wait_send()

        for copy in e_sends:
            copy.wait()

    seg, width = tokens.shape[1:]
    dma = pltpu.SemaphoreType.DMA
    return pl.pallas_call(
        kernel,
        out_shape=(
            jax.ShapeDtypeStruct((grid.slots, ndp, seg, width), tokens.dtype),
            jax.ShapeDtypeStruct((grid.ndev,) + shard.shape, shard.dtype),
            jax.ShapeDtypeStruct((nex,) + cot.shape, cot.dtype),
            jax.ShapeDtypeStruct(ranks.shape, ranks.dtype),
        ),
        in_specs=[any_spec()] * 4,
        out_specs=(any_spec(),) * 4,
        scratch_shapes=[
            dma((ndp - 1, grid.slots)),
            dma((ndp - 1, grid.slots)),
            dma((nex - 1,)),
            dma((nex - 1,)),
            dma((1 + grid.slots,)),
        ]
        + RowGather(grid).scratch()
        + DenseGather(grid).scratch(),
        compiler_params=comm_params(0),
        name="first_exchange",
    )(tokens, shard, cot, ranks)


def heads_in(grid, values, act, attn, grad_attn, grad_misc):
    ndp = grid.ndp

    def kernel(src, act_ref, attn_ref, ga_ref, gm_ref, dst, out_ref, send, recv, loc):
        dp, ex = lax.axis_index("dp"), lax.axis_index("expert")
        greet([(lax.rem(dp + d, ndp), ex) for d in range(1, ndp)])
        lanes = pl.ds(pl.multiple_of(dp * SEG, SEG), SEG)
        copies = []
        for d in far_first(ndp):
            target = lax.rem(dp + d, ndp)
            copy = remote(
                src.at[target], dst.at[:, :, lanes], send.at[d - 1], recv.at[d - 1], (target, ex)
            )
            copy.start()
            copies.append(copy)
        mine = pltpu.make_async_copy(src.at[dp], dst.at[:, :, lanes], loc)
        mine.start()
        out_ref[:, :D] = dot(attn_ref[...], ga_ref[...]).astype(BF16)
        out_ref[:, D:] = dot(act_ref[...], gm_ref[...]).astype(BF16)
        mine.wait()
        for copy in copies:
            copy.wait()

    dma = pltpu.SemaphoreType.DMA
    vmem = pl.BlockSpec(memory_space=pltpu.VMEM)
    return pl.pallas_call(
        kernel,
        out_shape=(
            jax.ShapeDtypeStruct(values.shape[1:3] + (SEG * ndp,), values.dtype),
            jax.ShapeDtypeStruct((D, D + MISC), BF16),
        ),
        in_specs=[any_spec()] + [vmem] * 4,
        out_specs=(any_spec(), vmem),
        scratch_shapes=[dma((ndp - 1,)), dma((ndp - 1,)), dma],
        compiler_params=pltpu.CompilerParams(
            collective_id=2, has_side_effects=True, vmem_limit_bytes=40 * MIB
        ),
        name="heads_in",
    )(values, act, attn, grad_attn, grad_misc)


class RowScatter:
    def __init__(self, grid, width):
        self.grid, self.width = grid, width
        self.rows = D // grid.nex
        self.rows_dev = D // grid.ndev

    def scratch_x(self):
        g = self.grid
        dma = pltpu.SemaphoreType.DMA
        blocks = pltpu.VMEM((g.nx, self.rows, self.width), BF16)
        return [blocks, blocks, blocks, dma((2, 2)), dma((g.nx, 2))]

    def scratch_dp(self):
        g = self.grid
        return [
            pltpu.VMEM((g.ndp, ROW_PAD, self.width), BF16),
            pltpu.SemaphoreType.DMA((g.ndp, 2)),
        ]

    def spread_shape(self):
        return (self.grid.ndp * ROW_PAD, self.width)

    def bind(self, spread):
        g = self.grid
        self.spread = spread
        self.dp, self.ex = lax.axis_index("dp"), lax.axis_index("expert")
        self.x, self.c = self.ex // g.nc, lax.rem(self.ex, g.nc)

    def bind_x(self, source, refs):
        self.source = source
        self.got_core, self.by_x, self.got_x, self.sem_core, self.sem_x = refs

    def bind_dp(self, refs):
        self.got_dp, self.sem_dp = refs

    def core_copy(self):
        other = 1 - self.c
        return remote(
            self.source.at[:, other], self.got_core, self.sem_core.at[0, 0],
            self.sem_core.at[0, 1], (self.dp, self.x * 2 + other),
        )

    def x_copy(self, d):
        target = lax.rem(self.x + d, self.grid.nx)
        return remote(
            self.by_x.at[target], self.got_x.at[d], self.sem_x.at[d, 0], self.sem_x.at[d, 1],
            (self.dp, target * self.grid.nc + self.c),
        )

    def dp_copy(self, d):
        target = lax.rem(self.dp + d, self.grid.ndp)
        rows = pl.ds(pl.multiple_of(target * ROW_PAD, ROW_PAD), ROW_PAD)
        return remote(
            self.spread.at[rows], self.got_dp.at[d], self.sem_dp.at[d, 0], self.sem_dp.at[d, 1],
            (target, self.ex),
        )

    def start(self):
        self.core_copy().start()

    def along_x(self):
        g = self.grid
        self.core_copy().wait()
        for n in range(g.nx):
            mine = self.source[n, pl.ds(self.c, 1)][0]
            self.by_x[n] = (mine.astype(F32) + self.got_core[n].astype(F32)).astype(BF16)
        for d in range(1, g.nx):
            self.x_copy(d).start()

    def after_x(self):
        g = self.grid
        for d in range(1, g.nx):
            self.x_copy(d).wait()
        total = self.by_x[pl.ds(self.x, 1)][0].astype(F32)
        for d in range(1, g.nx):
            total += self.got_x[d].astype(F32)
        to = lax.broadcasted_iota(jnp.int32, (g.ndp * ROW_PAD, self.rows), 0)
        of = lax.broadcasted_iota(jnp.int32, (g.ndp * ROW_PAD, self.rows), 1)
        place = (of // self.rows_dev) * ROW_PAD + lax.rem(of, self.rows_dev)
        move = (to == place).astype(F32).astype(BF16)
        self.spread[...] = dot(move, total.astype(BF16)).astype(BF16)

    def along_dp(self):
        for d in far_first(self.grid.ndp):
            self.dp_copy(d).start()

    def finish(self, out):
        g = self.grid
        rows = pl.ds(pl.multiple_of(self.dp * ROW_PAD, ROW_PAD), ROW_PAD)
        total = self.spread[rows].astype(F32)
        for d in range(1, g.ndp):
            self.dp_copy(d).wait()
            total += self.got_dp[d].astype(F32)
        out[...] = total


class ShardScatter:
    def __init__(self, grid, rows, width):
        self.grid, self.rows, self.width = grid, rows, width

    def scratch(self):
        g = self.grid
        block = (self.rows, self.width)
        dma = pltpu.SemaphoreType.DMA
        return [
            pltpu.VMEM((g.nz,) + block, BF16),
            pltpu.VMEM((max(g.ny - 1, 1), g.nz) + block, BF16),
            pltpu.VMEM((max(g.nz - 1, 1),) + block, BF16),
            dma((g.ny, g.nz, 2)),
            dma((g.nz, 2)),
            dma((g.nz,)),
        ]

    def bind(self, source, refs):
        self.source = source
        self.mine, self.got_y, self.got_z, self.sem_y, self.sem_z, self.loc = refs
        g = self.grid
        self.dp, self.ex = lax.axis_index("dp"), lax.axis_index("expert")
        self.z, self.y = self.dp // g.ny, lax.rem(self.dp, g.ny)
        self.order = far_first(g.nz) + [0]

    def place(self, dz, dy):
        g = self.grid
        return lax.rem(self.z + dz, g.nz) * g.ny + lax.rem(self.y + dy, g.ny)

    def y_copy(self, dy, dz):
        return remote(
            self.source.at[self.place(dz, dy)], self.got_y.at[dy - 1, dz],
            self.sem_y.at[dy, dz, 0], self.sem_y.at[dy, dz, 1], (self.place(0, dy), self.ex),
        )

    def z_copy(self, dz):
        return remote(
            self.mine.at[dz], self.got_z.at[dz - 1], self.sem_z.at[dz, 0], self.sem_z.at[dz, 1],
            (self.place(dz, 0), self.ex),
        )

    def own(self, dz):
        return pltpu.make_async_copy(
            self.source.at[self.place(dz, 0)], self.mine.at[dz], self.loc.at[dz]
        )

    def start(self):
        for dz in self.order:
            for dy in range(1, self.grid.ny):
                self.y_copy(dy, dz).start()
            self.own(dz).start()

    def along_z(self, which):
        g = self.grid
        for dz in which:
            self.own(dz).wait()
            for dy in range(1, g.ny):
                self.y_copy(dy, dz).wait()
            if g.ny > 1:
                total = self.mine[dz].astype(F32)
                for dy in range(1, g.ny):
                    total += self.got_y[dy - 1, dz].astype(F32)
                self.mine[dz] = total.astype(BF16)
            if dz:
                self.z_copy(dz).start()

    def finish(self, out):
        total = self.mine[0].astype(F32)
        for dz in range(1, self.grid.nz):
            self.z_copy(dz).wait()
            total += self.got_z[dz - 1].astype(F32)
        out[...] = total.astype(BF16)


def gather_shared(grid, rows, gates, shared_gate, grad_out, weights, group):
    nex = grid.nex

    def kernel(src, gate, sg_ref, go_ref, w_ref, group_ref,
               dst, gate_dst, lin_ref, gact_ref, early_ref, g_send, g_recv, loc, *row_refs):
        dp, ex = lax.axis_index("dp"), lax.axis_index("expert")
        greet([(dp, lax.rem(ex + d, nex)) for d in range(1, nex)])
        gather = RowGather(grid)
        gather.bind(src, dst, row_refs)
        gather.start()
        gate_copies = []
        for d in range(1, nex):
            target = lax.rem(ex + d, nex)
            copy = remote(
                gate.at[target], gate_dst.at[nex - 1 - d], g_send.at[d - 1], g_recv.at[d - 1],
                (dp, target),
            )
            copy.start()
            gate_copies.append(copy)
        copy = pltpu.make_async_copy(gate.at[ex], gate_dst.at[nex - 1], loc)
        copy.start()
        gate_copies.append(copy)

        act = src[...]
        grad_lin = (go_ref[...].astype(F32) * sg_ref[...]).astype(BF16)
        act_across = dot(group_ref[...], act, 1, 1).astype(BF16)
        grad_across = dot(group_ref[...], grad_lin, 1, 1).astype(BF16)
        wide = 2 * D
        for n in range(FF // wide):
            gate_w, up_w, down_w = (
                w_ref[:, m * FF + n * wide : m * FF + (n + 1) * wide] for m in range(3)
            )
            gate_lin, up_lin = dot(act, gate_w), dot(act, up_w)
            sig = 0.5 * jnp.tanh(0.5 * gate_lin) + 0.5
            silu = gate_lin * sig
            hidden = (silu * up_lin).astype(BF16)
            grad_hidden = dot(grad_lin, down_w)
            grad_gate = (grad_hidden * up_lin * (sig + silu * (1.0 - sig))).astype(BF16)
            grad_up = (grad_hidden * silu).astype(BF16)
            lin = dot(hidden, down_w, 1, 1)
            gact = dot(grad_gate, gate_w, 1, 1) + dot(grad_up, up_w, 1, 1)
            if n:
                lin_ref[...] += lin
                gact_ref[...] += gact
            else:
                lin_ref[...] = lin
                gact_ref[...] = gact
            if n == 0:
                gather.pass_on(0)
            for m, (left, right) in enumerate(
                ((act_across, grad_gate), (act_across, grad_up), (grad_across, hidden))
            ):
                lanes = slice(m * FF + n * wide, m * FF + (n + 1) * wide)
                early_ref[:, lanes] = dot(left, right).astype(BF16)
            if n == 0:
                gather.pass_on(1)
        for part in range(2, gather.parts):
            gather.pass_on(part)
        gather.finish()
        for copy in gate_copies:
            copy.wait()

    dma = pltpu.SemaphoreType.DMA
    vmem = pl.BlockSpec(memory_space=pltpu.VMEM)
    return pl.pallas_call(
        kernel,
        out_shape=(
            jax.ShapeDtypeStruct((nex,) + rows.shape, rows.dtype),
            jax.ShapeDtypeStruct(gates.shape, gates.dtype),
            jax.ShapeDtypeStruct((TOK_DEV, D), F32),
            jax.ShapeDtypeStruct((TOK_DEV, D), F32),
            jax.ShapeDtypeStruct((D, 3 * FF), BF16),
        ),
        in_specs=[vmem] * 6,
        out_specs=(any_spec(), any_spec(), vmem, vmem, vmem),
        scratch_shapes=[dma((nex - 1,)), dma((nex - 1,)), dma] + RowGather(grid).scratch(),
        compiler_params=pltpu.CompilerParams(
            collective_id=4, has_side_effects=True, vmem_limit_bytes=40 * MIB
        ),
        name="gather_shared",
    )(rows, gates, shared_gate, grad_out, weights, group)


def turn(values, cosine, sine):
    first, second = values[: HEAD_DIM // 2], values[HEAD_DIM // 2 :]
    return jnp.concatenate(
        [first * cosine - second * sine, second * cosine + first * sine], axis=0
    )


def allowed_mask(extent, block, length):
    keys = lax.broadcasted_iota(jnp.int32, (extent, QBLOCK), 0)
    queries = lax.broadcasted_iota(jnp.int32, (extent, QBLOCK), 1) + block * QBLOCK
    return (keys <= queries) & (keys < length)


def attend(grid, lives, tok, weights, gain, cosine, sine, shard):
    units, length, ndp, nex = grid.units, tok.shape[1], grid.ndp, grid.nex
    blocks = length // QBLOCK
    chunk = 1
    ends = sorted(set(range(chunk - 1, units, chunk)) | {units - 1})

    def kernel(live_ref, tok_ref, w_ref, gain_ref, cos_ref, sin_ref, shard_ref,
               heads_ref, dense_ref, act_ref, q_ref, k_ref, v_ref, lse_ref,
               buf, h_send, h_recv, h_loc, *dense_refs):
        i = pl.program_id(0)
        dp, ex = lax.axis_index("dp"), lax.axis_index("expert")
        unit = jnp.minimum(dp * units + i, UNITS_ALL - 1)
        head = lax.rem(unit, HEADS)
        slot = jnp.minimum(unit // HEADS - grid.first_series(dp), grid.slots - 1)
        slot = jnp.maximum(slot, 0)
        dense = DenseGather(grid)
        dense.bind(shard_ref, dense_ref, dense_refs)

        def heads_copy(d, n):
            begin = ends[n - 1] + 1 if n else 0
            count = ends[n] + 1 - begin
            target = lax.rem(dp + d, ndp)
            lanes = pl.ds(pl.multiple_of(target * SEG, SEG), SEG)
            return remote(
                buf.at[pl.ds(begin, count), :, lanes],
                heads_ref.at[dp, pl.ds(begin, count)],
                h_send.at[d - 1, n],
                h_recv.at[d - 1, n],
                (target, ex),
            )

        @pl.when(i == 0)
        def _():
            greet(
                [(lax.rem(dp + d, ndp), ex) for d in range(1, ndp)]
                + [(dp, lax.rem(ex + d, nex)) for d in range(1, nex)]
            )
            dense.start()

        @pl.when((i == 0) | (head == 0))
        def _():
            residual = tok_ref[slot].astype(F32)
            scale = lax.rsqrt(jnp.mean(residual * residual, axis=-1, keepdims=True) + eps_norm)
            act_ref[slot] = (residual * scale * gain_ref[...]).astype(BF16)

        cos, sin = cos_ref[...], sin_ref[...]
        w_rows = [
            w_ref[pl.ds(pl.multiple_of(n * D + head * HEAD_DIM, HEAD_DIM), HEAD_DIM)]
            for n in range(3)
        ]
        qkv = dot(jnp.concatenate(w_rows, axis=0), act_ref[slot], 1, 1)
        query = turn(qkv[:HEAD_DIM], cos, sin).astype(BF16)
        key_wide = turn(qkv[HEAD_DIM : 2 * HEAD_DIM], cos, sin)
        value = qkv[2 * HEAD_DIM :].astype(BF16)
        key_rows = key_wide.T.astype(BF16)
        q_ref[0], k_ref[0], v_ref[0] = query, key_wide.astype(BF16), value
        live = live_ref[i]
        for block in range(blocks):
            extent = QBLOCK * (block + 1)
            lanes = slice(QBLOCK * block, extent)
            scores = dot(key_rows[:extent], query[:, lanes]) * HEAD_DIM ** (-0.5)
            scores = jnp.where(allowed_mask(extent, block, live), scores, neg_fill)
            top = jnp.max(scores, axis=0, keepdims=True)
            probs = jnp.exp(scores - top)
            total = jnp.sum(probs, axis=0, keepdims=True)
            result = dot(value[:, :extent], probs.astype(BF16))
            buf[i, :, lanes] = (result * (1.0 / total)).astype(BF16)
            lse_ref[0, :, lanes] = top + jnp.log(total)

        for n, end in enumerate(ends):

            @pl.when(i == end)
            def _():
                for d in far_first(ndp):
                    heads_copy(d, n).start()

        pl.when(i == min(3, units - 1))(dense.pass_z)
        pl.when(i == min(5, units - 1))(dense.pass_y)

        @pl.when(i == units - 1)
        def _():
            mine = pltpu.make_async_copy(
                buf.at[:, :, pl.ds(pl.multiple_of(dp * SEG, SEG), SEG)], heads_ref.at[dp], h_loc
            )
            mine.start()
            dense.pass_x()
            dense.finish()
            for n in range(len(ends)):
                for d in range(1, ndp):
                    heads_copy(d, n).wait()
            mine.wait()

    def whole(array):
        return pl.BlockSpec(
            array.shape, lambda i: (0,) * array.ndim, pipeline_mode=pl.Buffered(1)
        )

    def per_unit(*tail):
        return pl.BlockSpec((1,) + tail, lambda i: (i, 0, 0))

    feature = jax.ShapeDtypeStruct((units, HEAD_DIM, length), BF16)
    inputs = (tok, weights, gain, cosine, sine)
    dma = pltpu.SemaphoreType.DMA
    return pl.pallas_call(
        kernel,
        grid=(units,),
        out_shape=(
            jax.ShapeDtypeStruct((ndp, units, HEAD_DIM, SEG), BF16),
            jax.ShapeDtypeStruct((grid.ndev,) + shard.shape, BF16),
            jax.ShapeDtypeStruct((grid.slots, length, D), BF16),
            feature,
            feature,
            feature,
            jax.ShapeDtypeStruct((units, 1, length), F32),
        ),
        in_specs=[pl.BlockSpec(memory_space=pltpu.SMEM)]
        + [whole(v) for v in inputs]
        + [any_spec()],
        out_specs=(
            any_spec(),
            any_spec(),
            pl.BlockSpec((grid.slots, length, D), lambda i: (0, 0, 0)),
            per_unit(HEAD_DIM, length),
            per_unit(HEAD_DIM, length),
            per_unit(HEAD_DIM, length),
            per_unit(1, length),
        ),
        scratch_shapes=[
            pltpu.VMEM((units, HEAD_DIM, length), BF16),
            dma((ndp - 1, len(ends))),
            dma((ndp - 1, len(ends))),
            dma,
        ]
        + DenseGather(grid).scratch(),
        compiler_params=pltpu.CompilerParams(
            collective_id=1, has_side_effects=True, vmem_limit_bytes=40 * MIB
        ),
        cost_estimate=pl.CostEstimate(
            flops=units * length * length * HEAD_DIM * 2 * 8,
            bytes_accessed=8 * MIB,
            transcendentals=units * length * length,
        ),
        name="attend",
    )(lives, *inputs, shard)


def attend_back(grid, lives, tok, act, weights, query, key, value, lse, grad_heads, cosine, sine,
                group, early, routed):
    units, length, ndp, nex = grid.units, act.shape[1], grid.ndp, grid.nex
    blocks = length // QBLOCK
    scale = HEAD_DIM ** (-0.5)
    early_width, late_width = early.shape[1], 3 * D + MISC
    early_sum, late_sum = RowScatter(grid, early_width), RowScatter(grid, late_width)
    early = early.reshape(grid.nx, grid.nc, early_sum.rows, early_width)
    steps = [min(n, units - 1) for n in (0, 3)]

    def kernel(*refs):
        (live_ref, tok_ref, act_ref, w_ref, q_ref, k_ref, v_ref, lse_ref, do_ref, cos_ref, sin_ref,
         group_ref, early_ref, routed_ref, rows_out, early_out, late_out, routed_out,
         acc, back, dq, dk, dv, grads, gain, late_ref, b_send, b_recv, b_loc,
         early_spread, late_spread, r_send, r_recv) = refs[:33]
        at = 33
        for work, source, spread in (
            (early_sum, early_ref, early_spread),
            (late_sum, late_ref, late_spread),
        ):
            work.bind(spread)
            work.bind_x(source, refs[at : at + 5])
            work.bind_dp(refs[at + 5 : at + 7])
            at += 7

        def routed_copy(step):
            return remote(
                routed_ref.at[step], routed_out.at[step], r_send.at[step], r_recv.at[step],
                (dp, lax.rem(ex + 1 + step, nex)),
            )

        i = pl.program_id(0)
        dp, ex = lax.axis_index("dp"), lax.axis_index("expert")
        unit = dp * units + i
        working = unit < UNITS_ALL
        series, head = unit // HEADS, lax.rem(unit, HEADS)
        slot = jnp.minimum(series - grid.first_series(dp), grid.slots - 1)

        def back_copy(d, which):
            target = lax.rem(dp + d, ndp)
            return remote(
                back.at[which, pl.ds(pl.multiple_of(target * SEG, SEG), SEG)],
                rows_out.at[dp, which],
                b_send.at[d - 1, which],
                b_recv.at[d - 1, which],
                (target, ex),
            )

        def back_local(which):
            return pltpu.make_async_copy(
                back.at[which, pl.ds(pl.multiple_of(dp * SEG, SEG), SEG)],
                rows_out.at[dp, which],
                b_loc.at[which],
            )

        @pl.when(i == 0)
        def _():
            greet(
                [(lax.rem(dp + d, ndp), ex) for d in range(1, ndp)]
                + [(dp, lax.rem(ex + d, nex)) for d in range(1, nex)]
            )
            early_sum.start()
            grads[...] = jnp.zeros_like(grads)
            gain[...] = jnp.zeros_like(gain)

        @pl.when((i == 0) | (head == 0))
        def _():
            acc[...] = jnp.zeros_like(acc)

        @pl.when(working)
        def _():
            live = live_ref[i]
            query, key, value, grad = q_ref[i], k_ref[i], v_ref[i], do_ref[i]
            key_rows = key.astype(F32).T.astype(BF16)
            value_rows = value.astype(F32).T.astype(BF16)
            dk[...] = jnp.zeros_like(dk)
            dv[...] = jnp.zeros_like(dv)
            for block in range(blocks):
                extent = QBLOCK * (block + 1)
                lanes = slice(QBLOCK * block, extent)
                scores = dot(key_rows[:extent], query[:, lanes]) * scale
                scores = jnp.where(allowed_mask(extent, block, live), scores, neg_fill)
                probs = jnp.exp(scores - lse_ref[i, :, lanes])
                grad_probs = dot(value_rows[:extent], grad[:, lanes])
                delta = jnp.sum(probs * grad_probs, axis=0, keepdims=True)
                grad_scores = (probs * (grad_probs - delta)).astype(BF16)
                probs_low = probs.astype(BF16)
                dq[:, lanes] = dot(key[:, :extent], grad_scores)
                dk[:, :extent] += dot(query[:, lanes], grad_scores, 1, 1)
                dv[:, :extent] += dot(grad[:, lanes], probs_low, 1, 1)
            cos, sin = cos_ref[...], -sin_ref[...]
            stacked = jnp.concatenate(
                [
                    turn(dq[...] * scale, cos, sin),
                    turn(dk[...] * scale, cos, sin),
                    dv[...],
                ],
                axis=0,
            ).astype(BF16)
            weight_grads = dot(stacked, act_ref[slot]).astype(BF16)
            w_rows = []
            for n in range(3):
                at = pl.multiple_of(n * D + head * HEAD_DIM, HEAD_DIM)
                part = slice(n * HEAD_DIM, (n + 1) * HEAD_DIM)
                grads[pl.ds(at, HEAD_DIM)] = weight_grads[part]
                w_rows.append(w_ref[pl.ds(at, HEAD_DIM)])
            acc[...] += dot(stacked, jnp.concatenate(w_rows, axis=0), 0, 0)

        @pl.when(working & ((head == HEADS - 1) | (i == units - 1)))
        def _():
            share = acc[...]
            residual = tok_ref[slot].astype(F32)
            normed = residual * lax.rsqrt(
                jnp.mean(residual * residual, axis=-1, keepdims=True) + eps_norm
            )
            gain[...] += jnp.sum(share * normed, axis=0, keepdims=True)
            back[slot] = share.astype(BF16)
            for d in far_first(ndp):
                back_copy(d, slot).start()
            back_local(slot).start()

        @pl.when(i == steps[0])
        def _():
            early_sum.along_x()
            for step in range(nex - 1):
                routed_copy(step).start()

        @pl.when(i == steps[1])
        def _():
            early_sum.after_x()
            early_sum.along_dp()

        @pl.when(i == units - 1)
        def _():
            grads[3 * D :] = jnp.broadcast_to(gain[...], (ROW_PAD, D)).astype(BF16)
            late = dot(group_ref[...], grads[...], 1, 1).astype(BF16)
            late = late.reshape(late_ref.shape[:3] + (late.shape[1],))
            late_ref[:, :, :, : late.shape[3]] = late
            late_ref[:, :, :, late.shape[3] :] = jnp.zeros(
                late_ref.shape[:3] + (late_width - late.shape[3],), BF16
            )
            late_sum.start()
            early_sum.finish(early_out)
            late_sum.along_x()
            late_sum.after_x()
            late_sum.along_dp()
            for which in range(grid.slots):
                for d in range(1, ndp):

                    @pl.when(grid.holds(lax.rem(dp + ndp - d, ndp), which))
                    def _():
                        back_copy(d, which).wait_recv()

                @pl.when(grid.holds(dp, which))
                def _():
                    for d in range(1, ndp):
                        back_copy(d, which).wait_send()
                    back_local(which).wait()

            late_sum.finish(late_out)
            for step in range(nex - 1):
                routed_copy(step).wait()

    def whole(array):
        return pl.BlockSpec(
            array.shape, lambda i: (0,) * array.ndim, pipeline_mode=pl.Buffered(1)
        )

    def whole_out(shape):
        return pl.BlockSpec(shape, lambda i: (0,) * len(shape))

    dma = pltpu.SemaphoreType.DMA
    inputs = (tok, act, weights, query, key, value, lse, grad_heads, cosine, sine, group, early)
    return pl.pallas_call(
        kernel,
        grid=(units,),
        out_shape=(
            jax.ShapeDtypeStruct((ndp, grid.slots, SEG, D), BF16),
            jax.ShapeDtypeStruct((ROW_PAD, early_width), F32),
            jax.ShapeDtypeStruct((ROW_PAD, late_width), F32),
            jax.ShapeDtypeStruct((nex - 1,) + routed.shape[1:], BF16),
        ),
        in_specs=[pl.BlockSpec(memory_space=pltpu.SMEM)] + [whole(v) for v in inputs] + [any_spec()],
        out_specs=(
            any_spec(),
            whole_out((ROW_PAD, early_width)),
            whole_out((ROW_PAD, late_width)),
            any_spec(),
        ),
        scratch_shapes=[
            pltpu.VMEM((length, D), F32),
            pltpu.VMEM((grid.slots, length, D), BF16),
            pltpu.VMEM((HEAD_DIM, length), F32),
            pltpu.VMEM((HEAD_DIM, length), F32),
            pltpu.VMEM((HEAD_DIM, length), F32),
            pltpu.VMEM((3 * D + ROW_PAD, D), BF16),
            pltpu.VMEM((1, D), F32),
            pltpu.VMEM((grid.nx, grid.nc, late_sum.rows, late_width), BF16),
            dma((ndp - 1, grid.slots)),
            dma((ndp - 1, grid.slots)),
            dma((grid.slots,)),
            pltpu.VMEM(early_sum.spread_shape(), BF16),
            pltpu.VMEM(late_sum.spread_shape(), BF16),
            dma((nex - 1,)),
            dma((nex - 1,)),
        ]
        + early_sum.scratch_x()
        + early_sum.scratch_dp()
        + late_sum.scratch_x()
        + late_sum.scratch_dp(),
        compiler_params=pltpu.CompilerParams(
            collective_id=3, has_side_effects=True, vmem_limit_bytes=56 * MIB
        ),
        cost_estimate=pl.CostEstimate(
            flops=units * length * length * HEAD_DIM * 2 * 20,
            bytes_accessed=12 * MIB,
            transcendentals=units * length * length,
        ),
        name="attend_back",
    )(lives, *inputs, routed)


def experts_step(grid, number, weights, act_all, cot_all, ranks, gates, before, early, done=None):
    nex, nc, ndp = grid.nex, grid.nc, grid.ndp
    rows = act_all.shape[1]
    local = EXPERTS // nex
    parts, wide = FF // D, 2 * D
    first, last = number == 0, number == local - 1
    batch = math.gcd(nex, 4)
    flushes = nex // batch
    scatter = RowScatter(grid, 3 * FF) if first or last else None
    talks = first or last
    settle = None if done is None else ShardScatter(grid, *done.shape[1:])
    if first:
        early = early.reshape(grid.nx, nc, scatter.rows, 3 * FF)

    def kernel(*refs):
        refs = list(refs)

        def take(count):
            taken = refs[:count]
            del refs[:count]
            return taken

        w_ref, act_ref, cot_ref, rank_ref, gate_ref = take(5)
        prev = take(3) if before is not None else None
        early_ref = take(1)[0] if talks else None
        done_ref = take(1)[0] if settle is not None else None
        if last:
            gin_out, ggate_out = take(2)
            routed_ref, grad_ref = take(2)
        else:
            gin_ref, ggate_ref = take(2)
            routed_ref, grad_ref = take(2)
        early_out = take(1)[0] if talks else None
        done_out = take(1)[0] if settle is not None else None
        xt_ref, dyt_ref, dg_ref, du_ref, hid_ref, down_ref = take(6)
        acc_ref = take(1)[0] if flushes > 1 else None
        if last:
            gin_buf, ggate_buf, send, recv, loc = take(5)
        if first:
            scatter.bind_x(early_ref, take(len(scatter.scratch_x())))
        if last:
            scatter.bind_dp(take(len(scatter.scratch_dp())))
        if talks:
            spread_ref = early_out if not last else take(1)[0] if first else early_ref
            scatter.bind(spread_ref)
        if settle is not None:
            settle.bind(done_ref, take(len(settle.scratch())))
        s = pl.program_id(0)
        dp, ex = lax.axis_index("dp"), lax.axis_index("expert")

        def copies(step):
            target = lax.rem(ex + 1 + step, nex)
            pairs = (
                (gin_buf.at[step], gin_out.at[step]),
                (ggate_buf.at[step], ggate_out.at[ex]),
            )
            return [
                remote(src, dst, send.at[step, n], recv.at[step, n], (dp, target))
                for n, (src, dst) in enumerate(pairs)
            ]

        if talks:

            @pl.when(s == 0)
            def _():
                peers = [(dp, lax.rem(ex + d, nex)) for d in range(1, nex)]
                if last:
                    peers += [(lax.rem(dp + d, ndp), ex) for d in range(1, ndp)]
                greet(peers)
                if settle is not None:
                    settle.start()
                if first:
                    scatter.start()
                else:
                    scatter.along_dp()

        @pl.when(s == 0)
        def _():
            for part in range(parts):
                lanes = slice(part * D, (part + 1) * D)
                down_ref[lanes] = w_ref[2 * D : 3 * D, lanes]

        rank = rank_ref[0, number : number + 1, :]
        rank_column = jnp.broadcast_to(rank, (8, rows)).T[:, :1]
        slot_down = lax.broadcasted_iota(jnp.int32, (CAP, rows), 0).astype(F32)
        slot_across = lax.broadcasted_iota(jnp.int32, (rows, CAP), 1).astype(F32)
        pick = slot_down == rank
        pick_low = pick.astype(F32).astype(BF16)
        spread = (slot_across == rank_column).astype(F32).astype(BF16)
        picked = dot(pick_low, jnp.concatenate([act_ref[0], cot_ref[0]], axis=1))
        taken_wide, grad_rows = picked[:, :D], picked[:, D:]
        taken = taken_wide.astype(BF16)
        gate_row = gate_ref[0, number : number + 1, :]
        gate = jnp.sum(jnp.where(pick, gate_row, 0.0), axis=1, keepdims=True)
        grad_wide = gate * grad_rows
        grad_result = grad_wide.astype(BF16)
        block = pl.ds(pl.multiple_of(lax.rem(s, batch) * CAP, CAP), CAP)
        xt_ref[:, block] = taken_wide.T.astype(BF16)
        dyt_ref[:, block] = grad_wide.T.astype(BF16)
        result = jnp.zeros((CAP, D), F32)
        grad_taken = jnp.zeros((CAP, D), F32)
        for part in range(0, FF, wide):
            lanes = slice(part, part + wide)
            w_gate = w_ref[0:D, lanes]
            w_up = w_ref[D : 2 * D, lanes]
            w_down = down_ref[lanes]
            gate_lin = dot(taken, w_gate)
            up_lin = dot(taken, w_up)
            sig = 0.5 * jnp.tanh(0.5 * gate_lin) + 0.5
            silu = gate_lin * sig
            hidden = (silu * up_lin).astype(BF16)
            result += dot(hidden, w_down)
            grad_hidden = dot(grad_result, w_down, 1, 1)
            grad_gate = (grad_hidden * up_lin * (sig + silu * (1.0 - sig))).astype(BF16)
            grad_up = (grad_hidden * silu).astype(BF16)
            hid_ref[block, lanes] = hidden
            dg_ref[block, lanes] = grad_gate
            du_ref[block, lanes] = grad_up
            grad_taken += dot(grad_gate, w_gate, 1, 1) + dot(grad_up, w_up, 1, 1)
        result = result.astype(BF16).astype(F32)
        grad_gate_slot = jnp.sum(grad_rows * result, axis=1, keepdims=True)
        grad_gate_row = jnp.sum(jnp.where(pick, grad_gate_slot, 0.0), axis=0, keepdims=True)
        both = jnp.concatenate([gate * result, grad_taken], axis=1).astype(BF16)
        both = dot(spread, both)
        routed, grad_in = both[:, :D], both[:, D:]
        if prev is not None:
            grad_in += prev[0][0]
            routed += prev[2][0]
        if last:
            routed_ref[0] = routed.astype(BF16)
            gin_buf[s] = grad_in.astype(BF16)
            if prev is not None:
                ggate_buf[s, 0:number] = prev[1][0]
            ggate_buf[s, number : number + 1] = grad_gate_row

            @pl.when(s < nex - 1)
            def _():
                for copy in copies(s):
                    copy.start()
        else:
            routed_ref[0] = routed
            gin_ref[0] = grad_in
            if prev is not None:
                ggate_ref[0, 0:number] = prev[1][0]
            ggate_ref[0, number : number + 1] = grad_gate_row

        if first:

            @pl.when(s == 0)
            def _():
                scatter.along_x()

            @pl.when(s == min(2, nex - 1))
            def _():
                scatter.after_x()
                if last:
                    scatter.along_dp()

        if settle is not None:
            for n, which in enumerate(settle.order):

                @pl.when(s == min(n, nex - 2))
                def _():
                    settle.along_z([which])

        own = []
        if last:
            own = [
                pltpu.make_async_copy(src, dst, loc.at[n])
                for n, (src, dst) in enumerate(
                    (
                        (gin_buf.at[nex - 1], gin_out.at[nex - 1]),
                        (ggate_buf.at[nex - 1], ggate_out.at[ex]),
                    )
                )
            ]

        @pl.when(s == nex - 1)
        def _():
            for copy in own:
                copy.start()

        def weight_grads(flush):
            def put(at, lanes, value):
                if flush:
                    value += acc_ref[at : at + D, lanes]
                if flush < flushes - 1:
                    acc_ref[at : at + D, lanes] = value
                else:
                    grad_ref[at : at + D, lanes] = value.astype(BF16)

            def columns(part, carry):
                begin = pl.multiple_of(part * wide, wide)
                lanes = pl.ds(begin, wide)
                put(0, lanes, dot(xt_ref[...], dg_ref[:, lanes]))
                put(D, lanes, dot(xt_ref[...], du_ref[:, lanes]))
                down = dot(dyt_ref[...], hid_ref[:, lanes])
                for n in range(0, wide, D):
                    put(2 * D, pl.ds(begin + n, D), down[:, n : n + D].T)
                return carry

            lax.fori_loop(0, FF // wide, columns, 0)

        for flush in range(flushes):
            pl.when(s == (flush + 1) * batch - 1)(functools.partial(weight_grads, flush))

        @pl.when(s == nex - 1)
        def _():
            if settle is not None:
                settle.finish(done_out)
            if last:
                scatter.finish(early_out)
                for step in range(nex - 1):
                    for copy in copies(step):
                        copy.wait()
                for copy in own:
                    copy.wait()

    def per_source(*tail):
        return pl.BlockSpec((1,) + tail, lambda s: (s,) + (0,) * len(tail))

    def whole(shape):
        return pl.BlockSpec(shape, lambda s: (0,) * len(shape), pipeline_mode=pl.Buffered(1))

    def whole_out(shape):
        return pl.BlockSpec(shape, lambda s: (0,) * len(shape))

    inputs = [weights, act_all, cot_all, ranks, gates]
    in_specs = [
        whole(weights.shape),
        per_source(rows, D),
        per_source(rows, D),
        per_source(local, rows),
        per_source(local, rows),
    ]
    if before is not None:
        inputs += list(before)
        in_specs += [per_source(rows, D), per_source(number, rows), per_source(rows, D)]
    if talks:
        inputs.append(early)
        in_specs.append(whole(early.shape))
    if settle is not None:
        inputs.append(done)
        in_specs.append(any_spec())
    dma = pltpu.SemaphoreType.DMA
    kind = BF16 if last else F32
    out_shape = [
        jax.ShapeDtypeStruct((nex, rows, D), kind),
        jax.ShapeDtypeStruct((nex, number + 1, rows), F32),
        jax.ShapeDtypeStruct((nex, rows, D), kind),
        jax.ShapeDtypeStruct(weights.shape, BF16),
    ]
    if last:
        out_specs = [any_spec()] * 2
    else:
        out_specs = [per_source(rows, D), per_source(number + 1, rows)]
    out_specs += [per_source(rows, D), whole_out(weights.shape)]
    if talks:
        shape = (ROW_PAD, 3 * FF) if last else scatter.spread_shape()
        out_shape.append(jax.ShapeDtypeStruct(shape, F32 if last else BF16))
        out_specs.append(whole_out(shape))
    if settle is not None:
        out_shape.append(jax.ShapeDtypeStruct(done.shape[1:], BF16))
        out_specs.append(whole_out(done.shape[1:]))
    scratch = [
        pltpu.VMEM((D, batch * CAP), BF16),
        pltpu.VMEM((D, batch * CAP), BF16),
        pltpu.VMEM((batch * CAP, FF), BF16),
        pltpu.VMEM((batch * CAP, FF), BF16),
        pltpu.VMEM((batch * CAP, FF), BF16),
        pltpu.VMEM((FF, D), BF16),
    ]
    if flushes > 1:
        scratch.append(pltpu.VMEM(weights.shape, F32))
    if last:
        scratch += [
            pltpu.VMEM((nex, rows, D), BF16),
            pltpu.VMEM((nex, local, rows), F32),
            dma((nex - 1, 2)),
            dma((nex - 1, 2)),
            dma((2,)),
        ]
    if first:
        scratch += scatter.scratch_x()
    if last:
        scratch += scatter.scratch_dp()
    if first and last:
        scratch.append(pltpu.VMEM(scatter.spread_shape(), BF16))
    if settle is not None:
        scratch += settle.scratch()
    return pl.pallas_call(
        kernel,
        grid=(nex,),
        out_shape=tuple(out_shape),
        in_specs=in_specs,
        out_specs=tuple(out_specs),
        scratch_shapes=scratch,
        compiler_params=pltpu.CompilerParams(
            vmem_limit_bytes=60 * MIB,
            collective_id=5 + number if talks else None,
            has_side_effects=talks,
        ),
        cost_estimate=pl.CostEstimate(
            flops=nex * CAP * D * FF * 2 * 11,
            bytes_accessed=25 * MIB,
            transcendentals=nex * CAP * FF,
        ),
        name="experts_step",
    )(*inputs)


def local(
    tokens,
    cotangent,
    lengths,
    routes,
    dense_weights,
    dense_first,
    dense_second,
    dense_average,
    expert_weights,
    expert_first,
    expert_second,
    expert_average,
):
    ndp, nex = lax.axis_size("dp"), lax.axis_size("expert")
    dp, ex = lax.axis_index("dp"), lax.axis_index("expert")
    grid = Grid(ndp, nex)
    local_experts = EXPERTS // nex
    length = SEG * ndp
    rows_dev = D // grid.ndev
    shard_rows = 3 * D // ndp

    spot = jnp.arange(FF, dtype=jnp.int32)
    order = (FF // D) * (spot % D) + spot // D
    mix = (spot[:, None] == order[None, :]).astype(BF16)
    shard_row = dp * shard_rows + jnp.arange(shard_rows, dtype=jnp.int32)
    is_down = (shard_row >= 2 * D)[None, :, None]
    expert_low = expert_weights.astype(BF16).reshape(local_experts, shard_rows, FF)
    mixed_low = jnp.einsum(
        "erf,fg->erg", expert_low, mix, preferred_element_type=F32
    ).astype(BF16)
    expert_send = jnp.where(is_down, expert_low, mixed_low)
    table = dense_weights.astype(BF16).reshape(rows_dev, -1)
    after = 4 * D + EXPERTS

    def padded(*columns):
        return jnp.pad(jnp.concatenate(columns, axis=1), ((0, ROW_PAD - rows_dev), (0, 0)))

    shard_first = padded(
        table[:, : 3 * D],
        table[:, 4 * D : after],
        table[:, after + 3 * FF :],
        jnp.zeros((rows_dev, MISC - EXPERTS - 3), BF16),
        table[:, 3 * D : 4 * D],
    )
    shard_rest = padded(table[:, after : after + 3 * FF])

    names = jnp.arange(EXPERTS, dtype=jnp.int32)
    routes_rows = routes.reshape(TOK_DEV, TOP)
    member = (routes_rows[:, :, None] == names[None, None, :]).any(axis=1)
    before = jnp.arange(TOK_DEV)
    earlier = (before[None, :] < before[:, None]).astype(BF16)
    count = jnp.dot(earlier, member.astype(BF16), preferred_element_type=F32)
    ranks = jnp.where(member, count, -1.0).T.reshape(nex, local_experts, TOK_DEV)

    local_pos = dp * SEG + jnp.arange(SEG, dtype=jnp.int32)
    live = (local_pos[None, :] < lengths[:, None]).astype(F32)
    grad_out_low = (cotangent.astype(F32) * live[..., None]).astype(BF16).reshape(TOK_DEV, D)

    tok_all, dense_all, cot_all, rank_all = first_exchange(
        grid, tokens, shard_first, grad_out_low, ranks
    )
    tok_all, expert_send = lax.optimization_barrier((tok_all, expert_send))
    expert_all = [
        lax.all_gather(expert_send[e], "dp", axis=0, tiled=True) for e in range(local_experts)
    ]
    tok_all = tok_all.reshape(grid.slots, length, D)

    dense_all = dense_all.reshape(grid.ndev * ROW_PAD, -1)
    row = jnp.arange(D, dtype=jnp.int32)
    row_from = (row // rows_dev) * ROW_PAD + row % rows_dev
    unpad = (row_from[:, None] == jnp.arange(grid.ndev * ROW_PAD)[None, :]).astype(BF16)
    qkv_rows = dot(dense_all[:, : 3 * D], unpad, 0, 1).astype(BF16)
    w_misc = dot(unpad, dense_all[:, 3 * D :]).astype(BF16)
    w_misc, w_output = w_misc[:, :MISC], w_misc[:, MISC:]
    gain_first = w_misc[:, EXPERTS + 1].astype(F32)
    gain_second = w_misc[:, EXPERTS + 2].astype(F32)

    unit = jnp.minimum(dp * grid.units + jnp.arange(grid.units, dtype=jnp.int32), UNITS_ALL - 1)
    lives = lengths[unit // HEADS]
    half = HEAD_DIM // 2
    inverse = rope_base ** (-jnp.arange(half, dtype=F32) * 2.0 / HEAD_DIM)
    angles = inverse[:, None] * jnp.arange(length, dtype=jnp.int32).astype(F32)[None, :]
    cosine, sine = jnp.cos(angles), jnp.sin(angles)
    heads_here, rest, act_one, query, key, value, lse = attend(
        grid, lives, tok_all, qkv_rows, gain_first[None, :], cosine, sine, shard_rest
    )
    w_shared = dot(unpad, rest.reshape(grid.ndev * ROW_PAD, -1)).astype(BF16)
    heads_here = heads_here.reshape(-1, HEAD_DIM, SEG)[:UNITS_ALL]
    attn_low = heads_here.reshape(SERIES_DEV, D, SEG).transpose(0, 2, 1).reshape(TOK_DEV, D)

    residual = tokens.astype(F32).reshape(TOK_DEV, D)
    mixed_rows = residual + dot(attn_low, w_output)
    scale_two = lax.rsqrt(jnp.mean(mixed_rows * mixed_rows, axis=-1, keepdims=True) + eps_norm)
    normed_two = mixed_rows * scale_two
    act_two = (normed_two * gain_second).astype(BF16)
    misc = dot(act_two, w_misc)
    router_probs = jax.nn.softmax(misc[:, :EXPERTS], axis=-1)
    shared_gate = jax.nn.sigmoid(misc[:, EXPERTS : EXPERTS + 1])

    row_dev = row // rows_dev
    row_to = ((row_dev % nex) * ndp + row_dev // nex) * rows_dev + row % rows_dev
    group = (row[:, None] == row_to[None, :]).astype(BF16)
    act_all, gates_all, shared_lin, grad_act_shared, early = gather_shared(
        grid,
        act_two,
        router_probs.T.reshape(nex, local_experts, TOK_DEV),
        shared_gate,
        grad_out_low,
        w_shared,
        group,
    )
    before, terms, expert_sums = None, None, []
    for e in range(local_experts):
        results = experts_step(
            grid, e, expert_all[e], act_all, cot_all, rank_all, gates_all, before, early, terms
        )
        before, terms, early = results[:3], results[3], results[4]
        expert_sums += results[5:]
        if e + 1 < local_experts:
            terms = terms.reshape(ndp, shard_rows, FF)
    expert_sums.append(lax.psum_scatter(terms, "dp", scatter_dimension=0, tiled=True))
    gin_back, ggate_back, routed_parts = before

    grad_out = grad_out_low.astype(F32)
    grad_svec_logit = (
        shared_gate * (1.0 - shared_gate) * jnp.sum(grad_out * shared_lin, axis=-1, keepdims=True)
    ).astype(BF16)
    grad_router_probs = ggate_back.reshape(EXPERTS, TOK_DEV).T
    grad_logits = (
        router_probs
        * (grad_router_probs - jnp.sum(router_probs * grad_router_probs, axis=-1, keepdims=True))
    ).astype(BF16)
    grad_misc = jnp.concatenate(
        [grad_logits, grad_svec_logit, jnp.zeros((TOK_DEV, MISC - EXPERTS - 1), BF16)], axis=1
    )
    grad_act_two = (
        jnp.sum(gin_back.astype(F32), axis=0)
        + grad_act_shared
        + dot(grad_misc, w_misc, 1, 1)
    )
    grad_gain_two = jnp.sum(grad_act_two * normed_two, axis=0)
    weighted_two = grad_act_two * gain_second
    grad_mixed = grad_out + scale_two * (
        weighted_two - normed_two * jnp.mean(weighted_two * normed_two, axis=-1, keepdims=True)
    )
    grad_attn_low = grad_mixed.astype(BF16)
    grad_heads = dot(grad_attn_low, w_output, 1, 1).astype(BF16)
    grad_heads = grad_heads.reshape(SERIES_DEV, SEG, D).transpose(0, 2, 1)
    grad_heads = grad_heads.reshape(UNITS_ALL, HEAD_DIM, SEG)
    grad_heads = jnp.pad(grad_heads, ((0, grid.units * ndp - UNITS_ALL), (0, 0), (0, 0)))
    attn_grouped = jnp.einsum(
        "gf,sfp->gsp", group, heads_here.reshape(SERIES_DEV, D, SEG), preferred_element_type=F32
    )
    grad_heads, middle = heads_in(
        grid,
        grad_heads.reshape(ndp, grid.units, HEAD_DIM, SEG),
        dot(group, act_two, 1, 1).astype(BF16),
        attn_grouped.astype(BF16).reshape(D, TOK_DEV),
        grad_attn_low,
        grad_misc,
    )
    gain_two_grouped = dot(group, grad_gain_two.astype(BF16)[:, None]).astype(BF16)
    middle = middle.at[:, D + EXPERTS + 2].set(gain_two_grouped[:, 0])

    back, middle, late, routed_back = attend_back(
        grid, lives, tok_all, act_one, qkv_rows, query, key, value, lse,
        grad_heads, cosine, sine, group, middle, routed_parts,
    )
    routed = jnp.sum(routed_back.astype(F32), axis=0) + routed_parts[nex - 1].astype(F32)
    output = (mixed_rows + routed + shared_gate * shared_lin).astype(BF16)
    grad_act_one = jnp.stack(
        [
            sum(
                back[owner, owned.index(s)].astype(F32)
                for owner, owned in enumerate(grid.owned)
                if s in owned
            )
            for s in range(SERIES_DEV)
        ]
    ).reshape(TOK_DEV, D)
    scale_one = lax.rsqrt(jnp.mean(residual * residual, axis=-1, keepdims=True) + eps_norm)
    normed_one = residual * scale_one
    weighted_one = grad_act_one * gain_first
    grad_tokens = grad_mixed + scale_one * (
        weighted_one - normed_one * jnp.mean(weighted_one * normed_one, axis=-1, keepdims=True)
    )

    early, middle, late = early[:rows_dev], middle[:rows_dev], late[:rows_dev]
    dense_grad = jnp.concatenate(
        [
            late[:, : 3 * D],
            middle[:, : D + EXPERTS],
            early,
            middle[:, D + EXPERTS : D + EXPERTS + 1],
            late[:, 3 * D : 3 * D + 1],
            middle[:, D + EXPERTS + 2 : D + EXPERTS + 3],
        ],
        axis=1,
    ).reshape(-1)

    expert_sums = jnp.stack(expert_sums)
    unmixed = jnp.einsum("erg,fg->erf", expert_sums, mix, preferred_element_type=F32)
    expert_grad = jnp.where(is_down, expert_sums.astype(F32), unmixed)
    expert_grad = expert_grad.reshape(expert_weights.shape)

    dense_first_new, dense_second_new, dense_new, dense_average_new = adamw_update(
        dense_weights, dense_grad, dense_first, dense_second, dense_average
    )
    expert_first_new, expert_second_new, expert_new, expert_average_new = adamw_update(
        expert_weights, expert_grad, expert_first, expert_second, expert_average
    )
    return (
        output.reshape(tokens.shape),
        grad_tokens.reshape(tokens.shape),
        dense_grad,
        dense_first_new,
        dense_second_new,
        dense_new,
        dense_average_new,
        expert_grad,
        expert_first_new,
        expert_second_new,
        expert_new,
        expert_average_new,
    )


def solution(mesh):
    rows = P("expert", "dp", None)
    dense = P(("dp", "expert"))
    experts = P("expert", "dp")
    return jax.shard_map(
        local,
        mesh=mesh,
        in_specs=(
            (rows, rows, P("expert"), P("dp", "expert", None, None)) + (dense,) * 4 + (experts,) * 4
        ),
        out_specs=(rows, rows) + (dense,) * 5 + (experts,) * 5,
        check_vma=False,
    )
```

```python
import functools
import math

import jax
import jax.numpy as jnp
from jax import lax
from jax.experimental import pallas as pl
from jax.experimental.pallas import tpu as pltpu
from jax.sharding import PartitionSpec as P

D = 384
HEADS = 12
HEAD_DIM = 32
FF = 1536
EXPERTS = 8
TOP = 2
SEG = 128
SERIES_DEV = 6
STEP = 8
TOK_DEV = 768
CAP = 384
ROW_PAD = 16
MISC = 128
UNITS_ALL = SERIES_DEV * HEADS
QBLOCK = 256
MIB = 1 << 20

eps_norm = 1e-06
beta_one = 0.5
beta_two = 0.5
learn_rate = 0.02
weight_decay = 0.1
eps_adam = 1e-08
average_keep = 0.9
rope_base = 10000.0
neg_fill = -1e30

MESH = pl.DeviceIdType.MESH
F32 = jnp.float32
BF16 = jnp.bfloat16


def adamw_update(weights, grads, first, second, average):
    first_new = beta_one * first + (1.0 - beta_one) * grads
    second_new = beta_two * second + (1.0 - beta_two) * grads * grads
    first_hat = first_new / (1.0 - beta_one**STEP)
    second_hat = second_new / (1.0 - beta_two**STEP)
    weights_new = weights - learn_rate * (
        first_hat / (jnp.sqrt(second_hat) + eps_adam) + weight_decay * weights
    )
    average_new = average_keep * average + (1.0 - average_keep) * weights_new
    return (first_new, second_new, weights_new, average_new)


def dot(left, right, left_dim=1, right_dim=0):
    return lax.dot_general(
        left, right, (((left_dim,), (right_dim,)), ((), ())), preferred_element_type=F32
    )


class Grid:
    def __init__(self, ndp, nex):
        self.ndp, self.nex = ndp, nex
        self.nz = math.gcd(ndp, 4)
        self.ny = ndp // self.nz
        self.nc = math.gcd(nex, 2)
        self.nx = nex // self.nc
        self.ndev = ndp * nex
        self.units = -(-UNITS_ALL // ndp)
        spans = [
            [u // HEADS for u in range(self.units * o, min(self.units * (o + 1), UNITS_ALL))]
            for o in range(ndp)
        ]
        self.owned = [sorted(set(s)) for s in spans]
        self.slots = max(len(s) for s in self.owned)

    def first_series(self, owner):
        return (owner * self.units) // HEADS

    def holds(self, owner, slot):
        begin = owner * self.units
        end = jnp.minimum(begin + self.units, UNITS_ALL)
        return (begin // HEADS + slot) * HEADS < end


def remote(src, dst, send, recv, target):
    return pltpu.make_async_remote_copy(
        src_ref=src,
        dst_ref=dst,
        send_sem=send,
        recv_sem=recv,
        device_id=target,
        device_id_type=MESH,
    )


def greet(peers):
    barrier = pltpu.get_barrier_semaphore()
    for peer in peers:
        pl.semaphore_signal(barrier, inc=1, device_id=peer, device_id_type=MESH)
    pl.semaphore_wait(barrier, len(peers))


def any_spec():
    return pl.BlockSpec(memory_space=pl.ANY)


def far_first(n):
    return sorted(range(1, n), key=lambda d: -min(d, n - d))


def comm_params(number):
    return pltpu.CompilerParams(collective_id=number, has_side_effects=True)


def unpad_matrix(grid):
    shape = (D, grid.ndev * ROW_PAD)
    rows_dev = D // grid.ndev
    row = lax.broadcasted_iota(jnp.int32, shape, 0)
    at = (row // rows_dev) * ROW_PAD + lax.rem(row, rows_dev)
    return (lax.broadcasted_iota(jnp.int32, shape, 1) == at).astype(F32).astype(BF16)


def group_matrix(grid):
    rows_dev = D // grid.ndev
    row = lax.broadcasted_iota(jnp.int32, (D, D), 1)
    owner = row // rows_dev
    at = (lax.rem(owner, grid.nex) * grid.ndp + owner // grid.nex) * rows_dev
    at = at + lax.rem(row, rows_dev)
    return (lax.broadcasted_iota(jnp.int32, (D, D), 0) == at).astype(F32).astype(BF16)


class DenseGather:
    def __init__(self, grid):
        self.grid = grid

    def scratch(self):
        dma = pltpu.SemaphoreType.DMA
        return [dma((self.grid.ndev,)), dma((self.grid.ndev,)), dma]

    def bind(self, shard, out, refs):
        g = self.grid
        self.shard, self.out = shard, out
        self.send, self.recv, self.loc = refs
        dp, ex = lax.axis_index("dp"), lax.axis_index("expert")
        self.z, self.y = dp // g.ny, lax.rem(dp, g.ny)
        self.x, self.c = ex // g.nc, lax.rem(ex, g.nc)
        self.zs = [0] + far_first(g.nz)[::-1]
        self.count = 0
        self.ends = []

    def place(self, dz, dy, dx, dc):
        g = self.grid
        return (
            lax.rem(self.z + dz, g.nz) * g.ny + lax.rem(self.y + dy, g.ny),
            lax.rem(self.x + dx, g.nx) * g.nc + lax.rem(self.c + dc, g.nc),
        )

    def slot(self, dz, dy, dx, dc):
        g = self.grid
        dp, ex = self.place(g.nz - dz, g.ny - dy, g.nx - dx, g.nc - dc)
        return dp * g.nex + ex

    def copy(self, ref, slot, number, target):
        return remote(ref, self.out.at[slot], self.send.at[number], self.recv.at[slot], target)

    def go(self, slot, target):
        ref = self.out.at[slot]
        if self.count < self.own_sends():
            ref = self.shard
        self.copy(ref, slot, self.count, target).start()
        self.count += 1

    def own_sends(self):
        g = self.grid
        return g.nz + g.ny + g.nx + g.nc - 4

    def wait(self, slot):
        self.copy(self.shard, slot, 0, self.place(0, 0, 0, 0)).wait_recv()

    def onward(self, slot, axes):
        g = self.grid
        if "y" in axes:
            for dy in range(1, g.ny):
                self.go(slot, self.place(0, dy, 0, 0))
        if "x" in axes:
            for dx in range(1, g.nx):
                self.go(slot, self.place(0, 0, dx, 0))
        for dc in range(1, g.nc):
            self.go(slot, self.place(0, 0, 0, dc))

    def own(self):
        return pltpu.make_async_copy(self.shard, self.out.at[self.slot(0, 0, 0, 0)], self.loc)

    def start(self):
        own = self.slot(0, 0, 0, 0)
        for dz in far_first(self.grid.nz):
            self.go(own, self.place(dz, 0, 0, 0))
        self.onward(own, "yx")
        self.own().start()

    def pass_z(self):
        for dz in self.zs[1:]:
            slot = self.slot(dz, 0, 0, 0)
            self.wait(slot)
            self.onward(slot, "yx")

    def pass_y(self):
        for dy in range(1, self.grid.ny):
            for dz in self.zs:
                slot = self.slot(dz, dy, 0, 0)
                self.wait(slot)
                self.onward(slot, "x")

    def pass_x(self):
        g = self.grid
        for dx in range(1, g.nx):
            for dy in range(g.ny):
                for dz in self.zs:
                    slot = self.slot(dz, dy, dx, 0)
                    self.wait(slot)
                    self.onward(slot, "")

    def finish(self):
        g = self.grid
        for dc in range(1, g.nc):
            for dx in range(g.nx):
                for dy in range(g.ny):
                    for dz in self.zs:
                        self.wait(self.slot(dz, dy, dx, dc))
        for number in range(g.ndev - 1):
            self.copy(self.shard, 0, number, self.place(0, 0, 0, 0)).wait_send()
        self.own().wait()


class RowGather:
    parts = 3

    def __init__(self, grid):
        self.grid = grid

    def scratch(self):
        g, n = self.grid, self.parts
        dma = pltpu.SemaphoreType.DMA
        return [dma((g.nx + g.nc, n)), dma((g.nex, n)), dma((g.nx, n)), dma]

    def bind(self, src, dst, refs):
        g = self.grid
        self.src, self.dst = src, dst
        self.send, self.recv, self.fsend, self.loc = refs
        self.dp, self.ex = lax.axis_index("dp"), lax.axis_index("expert")
        self.x, self.c = self.ex // g.nc, lax.rem(self.ex, g.nc)
        self.sends = []

    def rows(self, part):
        extent = TOK_DEV // self.parts
        return pl.ds(part * extent, extent)

    def slot_at(self, owner, target):
        return lax.rem(owner - target - 1 + 2 * self.grid.nex, self.grid.nex)

    def go(self, ref, owner, part, sem, target):
        slot = self.slot_at(owner, target)
        copy = remote(
            ref, self.dst.at[slot, self.rows(part)], sem, self.recv.at[slot, part],
            (self.dp, target),
        )
        copy.start()
        self.sends.append(copy)

    def arrived(self, owner, part):
        slot = self.slot_at(owner, self.ex)
        remote(
            self.src.at[self.rows(part)], self.dst.at[slot, self.rows(part)], self.send.at[0, 0],
            self.recv.at[slot, part], (self.dp, self.ex),
        ).wait_recv()

    def beside(self, dc):
        g = self.grid
        return self.x * g.nc + lax.rem(self.c + dc, g.nc)

    def start(self):
        g = self.grid
        for part in range(self.parts):
            for dx in range(1, g.nx):
                target = lax.rem(self.x + dx, g.nx) * g.nc + self.c
                ref = self.src.at[self.rows(part)]
                self.go(ref, self.ex, part, self.send.at[dx - 1, part], target)
        for part in range(self.parts):
            for dc in range(1, g.nc):
                ref = self.src.at[self.rows(part)]
                self.go(ref, self.ex, part, self.send.at[g.nx + dc - 2, part], self.beside(dc))
        self.own = pltpu.make_async_copy(self.src, self.dst.at[g.nex - 1], self.loc)
        self.own.start()

    def pass_on(self, part):
        g = self.grid
        for dx in range(1, g.nx):
            owner = lax.rem(self.x + g.nx - dx, g.nx) * g.nc + self.c
            self.arrived(owner, part)
            for dc in range(1, g.nc):
                ref = self.dst.at[self.slot_at(owner, self.ex), self.rows(part)]
                self.go(ref, owner, part, self.fsend.at[dx - 1, part], self.beside(dc))

    def finish(self):
        g = self.grid
        for part in range(self.parts):
            for dc in range(1, g.nc):
                for dx in range(g.nx):
                    owner = lax.rem(self.x + g.nx - dx, g.nx) * g.nc
                    self.arrived(owner + lax.rem(self.c + g.nc - dc, g.nc), part)
        for copy in self.sends:
            copy.wait_send()
        self.own.wait()


def first_exchange(grid, tokens, shard, cot, ranks):
    ndp, nex = grid.ndp, grid.nex

    def kernel(tok, shd, cot_in, rank_in, tok_out, dense_out, cot_out, rank_out,
               t_send, t_recv, e_send, e_recv, loc, *more_refs):
        dp, ex = lax.axis_index("dp"), lax.axis_index("expert")

        def off(value, by, n):
            return lax.rem(value + by, n)

        peers = [(off(dp, d, ndp), ex) for d in range(1, ndp)]
        peers += [(dp, off(ex, d, nex)) for d in range(1, nex)]
        greet(peers)
        dense = DenseGather(grid)
        dense.bind(shd, dense_out, more_refs[4:])
        dense.start()

        def token_copy(d, slot, src_series, sender, target):
            return remote(
                tok.at[src_series],
                tok_out.at[slot, sender],
                t_send.at[d - 1, slot],
                t_recv.at[d - 1, slot],
                (target, ex),
            )

        for d in far_first(ndp):
            target = off(dp, d, ndp)
            for slot in range(grid.slots):

                @pl.when(grid.holds(target, slot))
                def _():
                    token_copy(d, slot, grid.first_series(target) + slot, dp, target).start()

        rows = RowGather(grid)
        rows.bind(cot_in, cot_out, more_refs[:4])
        rows.start()
        e_sends = []
        for d in range(1, nex):
            target = off(ex, d, nex)
            copy = remote(
                rank_in.at[target], rank_out.at[nex - 1 - d], e_send.at[d - 1], e_recv.at[d - 1],
                (dp, target),
            )
            copy.start()
            e_sends.append(copy)
        copy = pltpu.make_async_copy(rank_in.at[ex], rank_out.at[nex - 1], loc.at[0])
        copy.start()
        e_sends.append(copy)

        for slot in range(grid.slots):

            @pl.when(grid.holds(dp, slot))
            def _():
                copy = pltpu.make_async_copy(
                    tok.at[grid.first_series(dp) + slot], tok_out.at[slot, dp], loc.at[1 + slot]
                )
                copy.start()
                copy.wait()

        dense.pass_z()
        rows.pass_on(0)
        dense.pass_y()
        for part in range(1, rows.parts):
            rows.pass_on(part)
        dense.pass_x()
        dense.finish()
        rows.finish()
        for d in range(1, ndp):
            for slot in range(grid.slots):

                @pl.when(grid.holds(dp, slot))
                def _():
                    token_copy(d, slot, 0, dp, off(dp, d, ndp)).wait_recv()

                @pl.when(grid.holds(off(dp, d, ndp), slot))
                def _():
                    token_copy(d, slot, 0, dp, off(dp, d, ndp)).wait_send()

        for copy in e_sends:
            copy.wait()

    seg, width = tokens.shape[1:]
    dma = pltpu.SemaphoreType.DMA
    return pl.pallas_call(
        kernel,
        out_shape=(
            jax.ShapeDtypeStruct((grid.slots, ndp, seg, width), tokens.dtype),
            jax.ShapeDtypeStruct((grid.ndev,) + shard.shape, shard.dtype),
            jax.ShapeDtypeStruct((nex,) + cot.shape, cot.dtype),
            jax.ShapeDtypeStruct(ranks.shape, ranks.dtype),
        ),
        in_specs=[any_spec()] * 4,
        out_specs=(any_spec(),) * 4,
        scratch_shapes=[
            dma((ndp - 1, grid.slots)),
            dma((ndp - 1, grid.slots)),
            dma((nex - 1,)),
            dma((nex - 1,)),
            dma((1 + grid.slots,)),
        ]
        + RowGather(grid).scratch()
        + DenseGather(grid).scratch(),
        compiler_params=comm_params(0),
        name="first_exchange",
    )(tokens, shard, cot, ranks)


class RowScatter:
    def __init__(self, grid, width):
        self.grid, self.width = grid, width
        self.rows = D // grid.nex
        self.rows_dev = D // grid.ndev

    def scratch_x(self):
        g = self.grid
        dma = pltpu.SemaphoreType.DMA
        blocks = pltpu.VMEM((g.nx, self.rows, self.width), BF16)
        return [blocks, blocks, blocks, dma((2, 2)), dma((g.nx, 2))]

    def scratch_dp(self):
        g = self.grid
        return [
            pltpu.VMEM((g.ndp, ROW_PAD, self.width), BF16),
            pltpu.SemaphoreType.DMA((g.ndp, 2)),
        ]

    def spread_shape(self):
        return (self.grid.ndp * ROW_PAD, self.width)

    def bind(self, spread):
        g = self.grid
        self.spread = spread
        self.dp, self.ex = lax.axis_index("dp"), lax.axis_index("expert")
        self.x, self.c = self.ex // g.nc, lax.rem(self.ex, g.nc)

    def bind_x(self, source, refs):
        self.source = source
        self.got_core, self.by_x, self.got_x, self.sem_core, self.sem_x = refs

    def bind_dp(self, refs):
        self.got_dp, self.sem_dp = refs

    def core_copy(self):
        other = 1 - self.c
        return remote(
            self.source.at[:, other], self.got_core, self.sem_core.at[0, 0],
            self.sem_core.at[0, 1], (self.dp, self.x * 2 + other),
        )

    def x_copy(self, d):
        target = lax.rem(self.x + d, self.grid.nx)
        return remote(
            self.by_x.at[target], self.got_x.at[d], self.sem_x.at[d, 0], self.sem_x.at[d, 1],
            (self.dp, target * self.grid.nc + self.c),
        )

    def dp_copy(self, d):
        target = lax.rem(self.dp + d, self.grid.ndp)
        rows = pl.ds(pl.multiple_of(target * ROW_PAD, ROW_PAD), ROW_PAD)
        return remote(
            self.spread.at[rows], self.got_dp.at[d], self.sem_dp.at[d, 0], self.sem_dp.at[d, 1],
            (target, self.ex),
        )

    def start(self):
        self.core_copy().start()

    def along_x(self):
        g = self.grid
        self.core_copy().wait()
        for n in range(g.nx):
            mine = self.source[n, pl.ds(self.c, 1)][0]
            self.by_x[n] = (mine.astype(F32) + self.got_core[n].astype(F32)).astype(BF16)
        for d in range(1, g.nx):
            self.x_copy(d).start()

    def after_x(self):
        g = self.grid
        for d in range(1, g.nx):
            self.x_copy(d).wait()
        total = self.by_x[pl.ds(self.x, 1)][0].astype(F32)
        for d in range(1, g.nx):
            total += self.got_x[d].astype(F32)
        to = lax.broadcasted_iota(jnp.int32, (g.ndp * ROW_PAD, self.rows), 0)
        of = lax.broadcasted_iota(jnp.int32, (g.ndp * ROW_PAD, self.rows), 1)
        place = (of // self.rows_dev) * ROW_PAD + lax.rem(of, self.rows_dev)
        move = (to == place).astype(F32).astype(BF16)
        self.spread[...] = dot(move, total.astype(BF16)).astype(BF16)

    def along_dp(self):
        for d in far_first(self.grid.ndp):
            self.dp_copy(d).start()

    def finish(self, out):
        g = self.grid
        rows = pl.ds(pl.multiple_of(self.dp * ROW_PAD, ROW_PAD), ROW_PAD)
        total = self.spread[rows].astype(F32)
        for d in range(1, g.ndp):
            self.dp_copy(d).wait()
            total += self.got_dp[d].astype(F32)
        out[...] = total


class ShardScatter:
    def __init__(self, grid, rows, width):
        self.grid, self.rows, self.width = grid, rows, width

    def scratch_y(self):
        g = self.grid
        block = (self.rows, self.width)
        dma = pltpu.SemaphoreType.DMA
        return [
            pltpu.VMEM((g.nz,) + block, BF16),
            pltpu.VMEM((max(g.ny - 1, 1), g.nz) + block, BF16),
            dma((g.ny, g.nz, 2)),
            dma((g.nz,)),
        ]

    def scratch_z(self):
        g = self.grid
        block = (self.rows, self.width)
        dma = pltpu.SemaphoreType.DMA
        return [pltpu.VMEM(block, BF16), pltpu.VMEM((g.nz,) + block, BF16), dma((g.nz, 2)), dma]

    def bind(self, source):
        self.source = source
        g = self.grid
        self.dp, self.ex = lax.axis_index("dp"), lax.axis_index("expert")
        self.z, self.y = self.dp // g.ny, lax.rem(self.dp, g.ny)
        self.order = far_first(g.nz) + [0]

    def bind_y(self, out, refs):
        self.out = out
        self.mine, self.got_y, self.sem_y, self.loc = refs

    def bind_z(self, refs):
        self.own, self.got_z, self.sem_z, self.loc = refs

    def place(self, dz, dy):
        g = self.grid
        return lax.rem(self.z + dz, g.nz) * g.ny + lax.rem(self.y + dy, g.ny)

    def y_copy(self, dy, dz):
        return remote(
            self.source.at[self.place(dz, dy)], self.got_y.at[dy - 1, dz],
            self.sem_y.at[dy, dz, 0], self.sem_y.at[dy, dz, 1], (self.place(0, dy), self.ex),
        )

    def load(self, dz):
        return pltpu.make_async_copy(
            self.source.at[self.place(dz, 0)], self.mine.at[dz], self.loc.at[dz]
        )

    def store(self, dz):
        return pltpu.make_async_copy(self.mine.at[dz], self.out.at[dz], self.loc.at[dz])

    def start_y(self):
        for dz in self.order:
            for dy in range(1, self.grid.ny):
                self.y_copy(dy, dz).start()
            self.load(dz).start()

    def finish_y(self):
        g = self.grid
        for dz in self.order:
            self.load(dz).wait()
            for dy in range(1, g.ny):
                self.y_copy(dy, dz).wait()
            if g.ny > 1:
                total = self.mine[dz].astype(F32)
                for dy in range(1, g.ny):
                    total += self.got_y[dy - 1, dz].astype(F32)
                self.mine[dz] = total.astype(BF16)
            self.store(dz).start()
        for dz in self.order:
            self.store(dz).wait()

    def z_copy(self, dz):
        return remote(
            self.source.at[dz], self.got_z.at[dz], self.sem_z.at[dz, 0], self.sem_z.at[dz, 1],
            (self.place(dz, 0), self.ex),
        )

    def own_copy(self):
        return pltpu.make_async_copy(self.source.at[0], self.own, self.loc)

    def start_z(self):
        for dz in far_first(self.grid.nz):
            self.z_copy(dz).start()
        self.own_copy().start()

    def finish_z(self, out):
        self.own_copy().wait()
        total = self.own[...].astype(F32)
        for dz in range(1, self.grid.nz):
            self.z_copy(dz).wait()
            total += self.got_z[dz].astype(F32)
        out[...] = total.astype(BF16)


def route_rows(grid, heads, tokens, table, grad_out, weights):
    nex = grid.nex
    local = EXPERTS // nex
    count = len(OUTS_ROUTE)

    def kernel(heads_ref, tok_ref, table_ref, go_ref, w_ref, dst, gate_dst, *refs):
        outs, bufs = refs[:count], refs[count : 2 * count]
        mixed_buf, probs_buf, lin_ref, gact_ref, early_ref, across_ref, small_ref, gain_ref = bufs
        act_buf, gate_buf, g_send, g_recv, loc, out_sem = refs[2 * count : 2 * count + 6]
        row_refs = refs[2 * count + 6 :]
        dp, ex = lax.axis_index("dp"), lax.axis_index("expert")
        greet([(dp, lax.rem(ex + d, nex)) for d in range(1, nex)])

        def keep(n):
            return pltpu.make_async_copy(bufs[n], outs[n], out_sem.at[n])

        unpad, group = unpad_matrix(grid), group_matrix(grid)
        small_ref[...] = dot(unpad, table_ref[:, 3 * D :]).astype(BF16)
        gain_ref[...] = dot(table_ref[:, 3 * D : 3 * D + MISC], unpad, 0, 1)[
            EXPERTS : EXPERTS + 8
        ]
        for s in range(SERIES_DEV):
            attn = heads_ref[s * HEADS : (s + 1) * HEADS].reshape(D, SEG)
            rows = slice(s * SEG, (s + 1) * SEG)
            mixed_buf[rows] = tok_ref[s].astype(F32) + dot(attn, small_ref[:, MISC:], 0, 0)
        mixed = mixed_buf[...]
        scale = lax.rsqrt(jnp.mean(mixed * mixed, axis=-1, keepdims=True) + eps_norm)
        act = (mixed * scale * gain_ref[2:3]).astype(BF16)
        act_buf[...] = act
        gather = RowGather(grid)
        gather.bind(act_buf, dst, row_refs)
        gather.start()
        misc = dot(act, small_ref[:, :MISC])
        lane = lax.broadcasted_iota(jnp.int32, misc.shape, 1)
        logits = jnp.where(lane < EXPERTS, misc, neg_fill)
        powers = jnp.exp(logits - jnp.max(logits, axis=1, keepdims=True))
        probs = powers / jnp.sum(powers, axis=1, keepdims=True)
        shared_gate = 0.5 * jnp.tanh(0.5 * misc[:, EXPERTS : EXPERTS + 1]) + 0.5
        probs_buf[...] = jnp.where(lane == EXPERTS, shared_gate, probs)
        flipped = probs.T
        for n in range(nex):
            gate_buf[n] = flipped[n * local : (n + 1) * local]
        gate_copies = []
        for d in range(1, nex):
            target = lax.rem(ex + d, nex)
            copy = remote(
                gate_buf.at[target], gate_dst.at[nex - 1 - d], g_send.at[d - 1], g_recv.at[d - 1],
                (dp, target),
            )
            copy.start()
            gate_copies.append(copy)
        copy = pltpu.make_async_copy(gate_buf.at[ex], gate_dst.at[nex - 1], loc)
        copy.start()
        gate_copies.append(copy)
        for n in (0, 1, 6, 7):
            keep(n).start()

        grad_lin = (go_ref[...].astype(F32) * shared_gate).astype(BF16)
        across_ref[...] = dot(group, act, 1, 1).astype(BF16)
        keep(5).start()
        grad_across = dot(group, grad_lin, 1, 1).astype(BF16)
        wide = 2 * D
        for n in range(FF // wide):
            gate_w, up_w, down_w = (
                dot(unpad, w_ref[:, m * FF + n * wide : m * FF + (n + 1) * wide]).astype(BF16)
                for m in range(3)
            )
            gate_lin, up_lin = dot(act, gate_w), dot(act, up_w)
            sig = 0.5 * jnp.tanh(0.5 * gate_lin) + 0.5
            silu = gate_lin * sig
            hidden = (silu * up_lin).astype(BF16)
            grad_hidden = dot(grad_lin, down_w)
            grad_gate = (grad_hidden * up_lin * (sig + silu * (1.0 - sig))).astype(BF16)
            grad_up = (grad_hidden * silu).astype(BF16)
            lin = dot(hidden, down_w, 1, 1)
            gact = dot(grad_gate, gate_w, 1, 1) + dot(grad_up, up_w, 1, 1)
            if n:
                lin_ref[...] += lin
                gact_ref[...] += gact
            else:
                lin_ref[...] = lin
                gact_ref[...] = gact
            if n == 0:
                gather.pass_on(0)
            else:
                keep(2).start()
                keep(3).start()
            for m, (left, right) in enumerate(
                ((across_ref[...], grad_gate), (across_ref[...], grad_up), (grad_across, hidden))
            ):
                lanes = slice(m * FF + n * wide, m * FF + (n + 1) * wide)
                early_ref[:, lanes] = dot(left, right).astype(BF16)
            if n == 0:
                gather.pass_on(1)
        keep(4).start()
        for part in range(2, gather.parts):
            gather.pass_on(part)
        gather.finish()
        for copy in gate_copies:
            copy.wait()
        for n in range(count):
            keep(n).wait()

    dma = pltpu.SemaphoreType.DMA
    vmem = pl.BlockSpec(memory_space=pltpu.VMEM)
    hbm = pl.BlockSpec(memory_space=pltpu.HBM)
    inputs = (heads, tokens, table, grad_out, weights)
    return pl.pallas_call(
        kernel,
        out_shape=(
            jax.ShapeDtypeStruct((nex, TOK_DEV, D), BF16),
            jax.ShapeDtypeStruct((nex, local, TOK_DEV), F32),
        )
        + tuple(jax.ShapeDtypeStruct(shape, kind) for shape, kind in OUTS_ROUTE),
        in_specs=[vmem] * len(inputs),
        out_specs=(hbm,) * (2 + count),
        scratch_shapes=[pltpu.VMEM(shape, kind) for shape, kind in OUTS_ROUTE]
        + [
            pltpu.VMEM((TOK_DEV, D), BF16),
            pltpu.VMEM((nex, local, TOK_DEV), F32),
            dma((nex - 1,)),
            dma((nex - 1,)),
            dma,
            dma((count,)),
        ]
        + RowGather(grid).scratch(),
        compiler_params=pltpu.CompilerParams(
            collective_id=4, has_side_effects=True, vmem_limit_bytes=60 * MIB
        ),
        name="route_rows",
    )(*inputs)


OUTS_ROUTE = (
    ((TOK_DEV, D), F32),
    ((TOK_DEV, MISC), F32),
    ((TOK_DEV, D), F32),
    ((TOK_DEV, D), F32),
    ((D, 3 * FF), BF16),
    ((D, TOK_DEV), BF16),
    ((D, MISC + D), BF16),
    ((8, D), F32),
)


def turn(values, cosine, sine):
    first, second = values[: HEAD_DIM // 2], values[HEAD_DIM // 2 :]
    return jnp.concatenate(
        [first * cosine - second * sine, second * cosine + first * sine], axis=0
    )


def allowed_mask(extent, block, length):
    keys = lax.broadcasted_iota(jnp.int32, (extent, QBLOCK), 0)
    queries = lax.broadcasted_iota(jnp.int32, (extent, QBLOCK), 1) + block * QBLOCK
    return (keys <= queries) & (keys < length)


def attend(grid, lengths, tok, table, cosine, sine, shard):
    units, length, ndp, nex = grid.units, tok.shape[1], grid.ndp, grid.nex
    blocks = length // QBLOCK
    chunk = 1
    ends = sorted(set(range(chunk - 1, units, chunk)) | {units - 1})

    def kernel(len_ref, tok_ref, table_ref, cos_ref, sin_ref, shard_ref,
               heads_ref, dense_ref, act_out, q_out, k_out, v_out, lse_out, w_out,
               act_ref, q_ref, k_ref, v_ref, lse_ref, w_ref, k_sem,
               buf, h_send, h_recv, h_loc, *dense_refs):
        i = pl.program_id(0)
        dp, ex = lax.axis_index("dp"), lax.axis_index("expert")
        unit = jnp.minimum(dp * units + i, UNITS_ALL - 1)
        head = lax.rem(unit, HEADS)
        slot = jnp.minimum(unit // HEADS - grid.first_series(dp), grid.slots - 1)
        slot = jnp.maximum(slot, 0)
        dense = DenseGather(grid)
        dense.bind(shard_ref, dense_ref, dense_refs)

        def keep():
            pairs = (
                (act_ref, act_out), (q_ref, q_out), (k_ref, k_out), (v_ref, v_out),
                (lse_ref, lse_out), (w_ref, w_out),
            )
            return [
                pltpu.make_async_copy(src, dst, k_sem.at[n]) for n, (src, dst) in enumerate(pairs)
            ]

        def heads_copy(d, n):
            begin = ends[n - 1] + 1 if n else 0
            count = ends[n] + 1 - begin
            target = lax.rem(dp + d, ndp)
            lanes = pl.ds(pl.multiple_of(target * SEG, SEG), SEG)
            return remote(
                buf.at[pl.ds(begin, count), :, lanes],
                heads_ref.at[dp, pl.ds(begin, count)],
                h_send.at[d - 1, n],
                h_recv.at[d - 1, n],
                (target, ex),
            )

        @pl.when(i == 0)
        def _():
            greet(
                [(lax.rem(dp + d, ndp), ex) for d in range(1, ndp)]
                + [(dp, lax.rem(ex + d, nex)) for d in range(1, nex)]
            )
            dense.start()
            w_ref[...] = dot(table_ref[:, : 3 * D + MISC], unpad_matrix(grid), 0, 1).astype(BF16)

        @pl.when((i == 0) | (head == 0))
        def _():
            residual = tok_ref[slot].astype(F32)
            scale = lax.rsqrt(jnp.mean(residual * residual, axis=-1, keepdims=True) + eps_norm)
            gain = w_ref[3 * D : 3 * D + ROW_PAD].astype(F32)[EXPERTS + 1 : EXPERTS + 2]
            act_ref[slot] = (residual * scale * gain).astype(BF16)

        cos, sin = cos_ref[...], sin_ref[...]
        w_rows = [
            w_ref[pl.ds(pl.multiple_of(n * D + head * HEAD_DIM, HEAD_DIM), HEAD_DIM)]
            for n in range(3)
        ]
        qkv = dot(jnp.concatenate(w_rows, axis=0), act_ref[slot], 1, 1)
        query = turn(qkv[:HEAD_DIM], cos, sin).astype(BF16)
        key_wide = turn(qkv[HEAD_DIM : 2 * HEAD_DIM], cos, sin)
        value = qkv[2 * HEAD_DIM :].astype(BF16)
        key_rows = key_wide.T.astype(BF16)
        q_ref[i], k_ref[i], v_ref[i] = query, key_wide.astype(BF16), value
        live = len_ref[unit // HEADS]
        for block in range(blocks):
            extent = QBLOCK * (block + 1)
            lanes = slice(QBLOCK * block, extent)
            scores = dot(key_rows[:extent], query[:, lanes]) * HEAD_DIM ** (-0.5)
            scores = jnp.where(allowed_mask(extent, block, live), scores, neg_fill)
            top = jnp.max(scores, axis=0, keepdims=True)
            probs = jnp.exp(scores - top)
            total = jnp.sum(probs, axis=0, keepdims=True)
            result = dot(value[:, :extent], probs.astype(BF16))
            buf[i, :, lanes] = (result * (1.0 / total)).astype(BF16)
            lse_ref[i, :, lanes] = top + jnp.log(total)

        for n, end in enumerate(ends):

            @pl.when(i == end)
            def _():
                for d in far_first(ndp):
                    heads_copy(d, n).start()

        pl.when(i == min(3, units - 1))(dense.pass_z)
        pl.when(i == min(5, units - 1))(dense.pass_y)

        @pl.when(i == units - 1)
        def _():
            mine = pltpu.make_async_copy(
                buf.at[:, :, pl.ds(pl.multiple_of(dp * SEG, SEG), SEG)], heads_ref.at[dp], h_loc
            )
            mine.start()
            for copy in keep():
                copy.start()
            dense.pass_x()
            dense.finish()
            for n in range(len(ends)):
                for d in range(1, ndp):
                    heads_copy(d, n).wait()
            mine.wait()
            for copy in keep():
                copy.wait()

    def whole(array):
        return pl.BlockSpec(
            array.shape, lambda i: (0,) * array.ndim, pipeline_mode=pl.Buffered(1)
        )

    feature = jax.ShapeDtypeStruct((units, HEAD_DIM, length), BF16)
    inputs = (tok, table, cosine, sine)
    dma = pltpu.SemaphoreType.DMA
    return pl.pallas_call(
        kernel,
        grid=(units,),
        out_shape=(
            jax.ShapeDtypeStruct((ndp, units, HEAD_DIM, SEG), BF16),
            jax.ShapeDtypeStruct((grid.ndev,) + shard.shape, BF16),
            jax.ShapeDtypeStruct((grid.slots, length, D), BF16),
            feature,
            feature,
            feature,
            jax.ShapeDtypeStruct((units, 1, length), F32),
            jax.ShapeDtypeStruct((3 * D + MISC, D), BF16),
        ),
        in_specs=[pl.BlockSpec(memory_space=pltpu.SMEM)]
        + [whole(v) for v in inputs]
        + [any_spec()],
        out_specs=(
            any_spec(),
            any_spec(),
        )
        + (pl.BlockSpec(memory_space=pltpu.HBM),) * 6,
        scratch_shapes=[
            pltpu.VMEM((grid.slots, length, D), BF16),
            pltpu.VMEM(feature.shape, BF16),
            pltpu.VMEM(feature.shape, BF16),
            pltpu.VMEM(feature.shape, BF16),
            pltpu.VMEM((units, 1, length), F32),
            pltpu.VMEM((3 * D + MISC, D), BF16),
            dma((6,)),
            pltpu.VMEM((units, HEAD_DIM, length), BF16),
            dma((ndp - 1, len(ends))),
            dma((ndp - 1, len(ends))),
            dma,
        ]
        + DenseGather(grid).scratch(),
        compiler_params=pltpu.CompilerParams(
            collective_id=1, has_side_effects=True, vmem_limit_bytes=60 * MIB
        ),
        cost_estimate=pl.CostEstimate(
            flops=units * length * length * HEAD_DIM * 2 * 8,
            bytes_accessed=8 * MIB,
            transcendentals=units * length * length,
        ),
        name="attend",
    )(lengths, *inputs, shard)


def attend_back(grid, lengths, tok, act, weights, query, key, value, lse, grad_heads, cosine, sine,
                early, routed, partial, tokens, mixed, grad_mixed, probs, lin, gains, shared):
    units, length, ndp, nex = grid.units, act.shape[1], grid.ndp, grid.nex
    blocks = length // QBLOCK
    scale = HEAD_DIM ** (-0.5)
    early_width, late_width = early.shape[1], 3 * D + MISC
    early_sum, late_sum = RowScatter(grid, early_width), RowScatter(grid, late_width)
    early = early.reshape(grid.nx, grid.nc, early_sum.rows, early_width)
    steps = [min(n, units - 1) for n in (0, 3)]
    settle = ShardScatter(grid, *partial.shape[1:])

    def kernel(*refs):
        (len_ref, tok_ref, act_ref, w_ref, q_ref, k_ref, v_ref, lse_ref, do_ref, cos_ref, sin_ref,
         early_ref, tokens_ref, mixed_ref, grad_mixed_ref, probs_ref, lin_ref, gains_ref, shared_ref,
         routed_ref, partial_ref,
         output_ref, grad_tokens_ref, table_ref, settle_out,
         rows_out, early_out, late_out, routed_out,
         acc, back, dq, dk, dv, grads, gain, late_ref, b_send, b_recv, b_loc,
         early_spread, late_spread, r_send, r_recv) = refs[:44]
        at = 44
        for work, source, spread in (
            (early_sum, early_ref, early_spread),
            (late_sum, late_ref, late_spread),
        ):
            work.bind(spread)
            work.bind_x(source, refs[at : at + 5])
            work.bind_dp(refs[at + 5 : at + 7])
            at += 7
        settle.bind(partial_ref)
        settle.bind_z(refs[at:])

        def routed_copy(step):
            return remote(
                routed_ref.at[step], routed_out.at[step], r_send.at[step], r_recv.at[step],
                (dp, lax.rem(ex + 1 + step, nex)),
            )

        i = pl.program_id(0)
        dp, ex = lax.axis_index("dp"), lax.axis_index("expert")
        unit = dp * units + i
        working = unit < UNITS_ALL
        series, head = unit // HEADS, lax.rem(unit, HEADS)
        slot = jnp.minimum(series - grid.first_series(dp), grid.slots - 1)

        def back_copy(d, which):
            target = lax.rem(dp + d, ndp)
            return remote(
                back.at[which, pl.ds(pl.multiple_of(target * SEG, SEG), SEG)],
                rows_out.at[dp, which],
                b_send.at[d - 1, which],
                b_recv.at[d - 1, which],
                (target, ex),
            )

        def back_local(which):
            return pltpu.make_async_copy(
                back.at[which, pl.ds(pl.multiple_of(dp * SEG, SEG), SEG)],
                rows_out.at[dp, which],
                b_loc.at[which],
            )

        @pl.when(i == 0)
        def _():
            greet(
                [(lax.rem(dp + d, ndp), ex) for d in range(1, ndp)]
                + [(dp, lax.rem(ex + d, nex)) for d in range(1, nex)]
            )
            settle.start_z()
            early_sum.start()
            grads[...] = jnp.zeros_like(grads)
            gain[...] = jnp.zeros_like(gain)

        @pl.when((i == 0) | (head == 0))
        def _():
            acc[...] = jnp.zeros_like(acc)

        @pl.when(working)
        def _():
            live = len_ref[series]
            query, key, value, grad = q_ref[i], k_ref[i], v_ref[i], do_ref[i]
            key_rows = key.astype(F32).T.astype(BF16)
            value_rows = value.astype(F32).T.astype(BF16)
            dk[...] = jnp.zeros_like(dk)
            dv[...] = jnp.zeros_like(dv)
            for block in range(blocks):
                extent = QBLOCK * (block + 1)
                lanes = slice(QBLOCK * block, extent)
                scores = dot(key_rows[:extent], query[:, lanes]) * scale
                scores = jnp.where(allowed_mask(extent, block, live), scores, neg_fill)
                probs = jnp.exp(scores - lse_ref[i, :, lanes])
                grad_probs = dot(value_rows[:extent], grad[:, lanes])
                delta = jnp.sum(probs * grad_probs, axis=0, keepdims=True)
                grad_scores = (probs * (grad_probs - delta)).astype(BF16)
                probs_low = probs.astype(BF16)
                dq[:, lanes] = dot(key[:, :extent], grad_scores)
                dk[:, :extent] += dot(query[:, lanes], grad_scores, 1, 1)
                dv[:, :extent] += dot(grad[:, lanes], probs_low, 1, 1)
            cos, sin = cos_ref[...], -sin_ref[...]
            stacked = jnp.concatenate(
                [
                    turn(dq[...] * scale, cos, sin),
                    turn(dk[...] * scale, cos, sin),
                    dv[...],
                ],
                axis=0,
            ).astype(BF16)
            weight_grads = dot(stacked, act_ref[slot]).astype(BF16)
            w_rows = []
            for n in range(3):
                at = pl.multiple_of(n * D + head * HEAD_DIM, HEAD_DIM)
                part = slice(n * HEAD_DIM, (n + 1) * HEAD_DIM)
                grads[pl.ds(at, HEAD_DIM)] = weight_grads[part]
                w_rows.append(w_ref[pl.ds(at, HEAD_DIM)])
            acc[...] += dot(stacked, jnp.concatenate(w_rows, axis=0), 0, 0)

        @pl.when(working & ((head == HEADS - 1) | (i == units - 1)))
        def _():
            share = acc[...]
            residual = tok_ref[slot].astype(F32)
            normed = residual * lax.rsqrt(
                jnp.mean(residual * residual, axis=-1, keepdims=True) + eps_norm
            )
            gain[...] += jnp.sum(share * normed, axis=0, keepdims=True)
            back[slot] = share.astype(BF16)
            for d in far_first(ndp):
                back_copy(d, slot).start()
            back_local(slot).start()

        @pl.when(i == steps[0])
        def _():
            early_sum.along_x()
            for step in range(nex - 1):
                routed_copy(step).start()

        @pl.when(i == steps[1])
        def _():
            early_sum.after_x()
            early_sum.along_dp()

        @pl.when(i == units - 1)
        def _():
            grads[3 * D :] = jnp.broadcast_to(gain[...], (ROW_PAD, D)).astype(BF16)
            late = dot(group_matrix(grid), grads[...], 1, 1).astype(BF16)
            late = late.reshape(late_ref.shape[:3] + (late.shape[1],))
            late_ref[:, :, :, : late.shape[3]] = late
            late_ref[:, :, :, late.shape[3] :] = jnp.zeros(
                late_ref.shape[:3] + (late_width - late.shape[3],), BF16
            )
            late_sum.start()
            early_sum.finish(early_out)
            late_sum.along_x()
            for step in range(nex - 1):
                routed_copy(step).wait()
            total = routed_ref[nex - 1].astype(F32)
            for step in range(nex - 1):
                total += routed_out[step].astype(F32)
            shared_gate = probs_ref[:, EXPERTS : EXPERTS + 1]
            output_ref[...] = (mixed_ref[...] + total + shared_gate * lin_ref[...]).astype(BF16)
            late_sum.after_x()
            late_sum.along_dp()
            for which in range(grid.slots):
                for d in range(1, ndp):

                    @pl.when(grid.holds(lax.rem(dp + ndp - d, ndp), which))
                    def _():
                        back_copy(d, which).wait_recv()

                @pl.when(grid.holds(dp, which))
                def _():
                    for d in range(1, ndp):
                        back_copy(d, which).wait_send()
                    back_local(which).wait()

            for n in range(SERIES_DEV):
                rows = slice(n * SEG, (n + 1) * SEG)
                grad_act = sum(
                    rows_out[owner, owned.index(n)].astype(F32)
                    for owner, owned in enumerate(grid.owned)
                    if n in owned
                )
                residual = tokens_ref[n].astype(F32)
                scale_one = lax.rsqrt(
                    jnp.mean(residual * residual, axis=-1, keepdims=True) + eps_norm
                )
                normed = residual * scale_one
                weighted = grad_act * gains_ref[1:2]
                inner = jnp.mean(weighted * normed, axis=-1, keepdims=True)
                grad_tokens_ref[rows] = grad_mixed_ref[rows] + scale_one * (
                    weighted - normed * inner
                )
            late_sum.finish(late_out)
            late, mid = late_out[...], early_out[...]
            misc = mid[:, D:]
            lane = lax.broadcasted_iota(jnp.int32, misc.shape, 1)
            wide = jnp.concatenate([shared_ref[...], jnp.zeros_like(misc)], axis=1)
            wide = pltpu.roll(wide, EXPERTS, 1)
            table_ref[:, : 3 * D] = late[:, : 3 * D]
            table_ref[:, 3 * D : 4 * D] = mid[:, :D]
            table_ref[:, 4 * D : 4 * D + MISC] = wide[:, :MISC] + jnp.where(
                lane < EXPERTS, misc, 0.0
            )
            table_ref[:, 4 * D + MISC : 4 * D + 3 * FF] = wide[:, MISC : 3 * FF]
            ends = jnp.where(lane == EXPERTS + 1, late[:, 3 * D :], misc)
            ends = jnp.where((lane >= EXPERTS) & (lane < EXPERTS + 3), ends, 0.0)
            table_ref[:, 4 * D + 3 * FF :] = wide[:, 3 * FF :] + ends
            settle.finish_z(settle_out)

    def whole(array):
        return pl.BlockSpec(
            array.shape, lambda i: (0,) * array.ndim, pipeline_mode=pl.Buffered(1)
        )

    def whole_out(shape):
        return pl.BlockSpec(shape, lambda i: (0,) * len(shape))

    dma = pltpu.SemaphoreType.DMA
    inputs = (tok, act, weights, query, key, value, lse, grad_heads, cosine, sine, early, tokens, mixed,
              grad_mixed, probs, lin, gains, shared, routed)
    table_shape = (ROW_PAD, 4 * D + 3 * FF + MISC)
    return pl.pallas_call(
        kernel,
        grid=(units,),
        out_shape=(
            jax.ShapeDtypeStruct((TOK_DEV, D), BF16),
            jax.ShapeDtypeStruct((TOK_DEV, D), F32),
            jax.ShapeDtypeStruct(table_shape, F32),
            jax.ShapeDtypeStruct(partial.shape[1:], BF16),
        ),
        in_specs=[pl.BlockSpec(memory_space=pltpu.SMEM)]
        + [whole(v) for v in inputs]
        + [any_spec()],
        out_specs=(
            whole_out((TOK_DEV, D)),
            whole_out((TOK_DEV, D)),
            whole_out(table_shape),
            whole_out(partial.shape[1:]),
        ),
        scratch_shapes=[
            pltpu.VMEM((ndp, grid.slots, SEG, D), BF16),
            pltpu.VMEM((ROW_PAD, early_width), F32),
            pltpu.VMEM((ROW_PAD, late_width), F32),
            pltpu.VMEM((nex - 1,) + routed.shape[1:], BF16),
            pltpu.VMEM((length, D), F32),
            pltpu.VMEM((grid.slots, length, D), BF16),
            pltpu.VMEM((HEAD_DIM, length), F32),
            pltpu.VMEM((HEAD_DIM, length), F32),
            pltpu.VMEM((HEAD_DIM, length), F32),
            pltpu.VMEM((3 * D + ROW_PAD, D), BF16),
            pltpu.VMEM((1, D), F32),
            pltpu.VMEM((grid.nx, grid.nc, late_sum.rows, late_width), BF16),
            dma((ndp - 1, grid.slots)),
            dma((ndp - 1, grid.slots)),
            dma((grid.slots,)),
            pltpu.VMEM(early_sum.spread_shape(), BF16),
            pltpu.VMEM(late_sum.spread_shape(), BF16),
            dma((nex - 1,)),
            dma((nex - 1,)),
        ]
        + early_sum.scratch_x()
        + early_sum.scratch_dp()
        + late_sum.scratch_x()
        + late_sum.scratch_dp()
        + settle.scratch_z(),
        compiler_params=pltpu.CompilerParams(
            collective_id=3, has_side_effects=True, vmem_limit_bytes=60 * MIB
        ),
        cost_estimate=pl.CostEstimate(
            flops=units * length * length * HEAD_DIM * 2 * 20,
            bytes_accessed=12 * MIB,
            transcendentals=units * length * length,
        ),
        name="attend_back",
    )(lengths, *inputs, partial)


def experts_step(grid, number, weights, act_all, cot_all, ranks, gates, before, early, done=None):
    nex, nc, ndp = grid.nex, grid.nc, grid.ndp
    rows = act_all.shape[1]
    local = EXPERTS // nex
    parts, wide = FF // D, 2 * D
    first, last = number == 0, number == local - 1
    batch = math.gcd(nex, 4)
    flushes = nex // batch
    scatter = RowScatter(grid, 3 * FF) if first or last else None
    talks = first or last
    settle = None if done is None else ShardScatter(grid, *done.shape[1:])
    if first:
        early = early.reshape(grid.nx, nc, scatter.rows, 3 * FF)

    def kernel(*refs):
        refs = list(refs)

        def take(count):
            taken = refs[:count]
            del refs[:count]
            return taken

        w_ref, act_ref, cot_ref, rank_ref, gate_ref = take(5)
        prev = take(3) if before is not None else None
        early_ref = take(1)[0] if talks else None
        done_ref = take(1)[0] if settle is not None else None
        if last:
            gin_out, ggate_out = take(2)
            routed_ref, grad_ref = take(2)
        else:
            gin_ref, ggate_ref = take(2)
            routed_ref, grad_ref = take(2)
        early_out = take(1)[0] if talks else None
        done_out = take(1)[0] if settle is not None else None
        xt_ref, dyt_ref, dg_ref, du_ref, hid_ref, down_ref = take(6)
        acc_ref = take(1)[0] if flushes > 1 else None
        if last:
            gin_buf, ggate_buf, send, recv, loc = take(5)
        if first:
            scatter.bind_x(early_ref, take(len(scatter.scratch_x())))
        if last:
            scatter.bind_dp(take(len(scatter.scratch_dp())))
        if talks:
            spread_ref = early_out if not last else take(1)[0] if first else early_ref
            scatter.bind(spread_ref)
        if settle is not None:
            settle.bind(done_ref)
            settle.bind_y(done_out, take(len(settle.scratch_y())))
        s = pl.program_id(0)
        dp, ex = lax.axis_index("dp"), lax.axis_index("expert")

        def copies(step):
            target = lax.rem(ex + 1 + step, nex)
            pairs = (
                (gin_buf.at[step], gin_out.at[step]),
                (ggate_buf.at[step], ggate_out.at[ex]),
            )
            return [
                remote(src, dst, send.at[step, n], recv.at[step, n], (dp, target))
                for n, (src, dst) in enumerate(pairs)
            ]

        if talks:

            @pl.when(s == 0)
            def _():
                peers = [(dp, lax.rem(ex + d, nex)) for d in range(1, nex)]
                if last:
                    peers += [(lax.rem(dp + d, ndp), ex) for d in range(1, ndp)]
                greet(peers)
                if settle is not None:
                    settle.start_y()
                if first:
                    scatter.start()
                else:
                    scatter.along_dp()

        @pl.when(s == 0)
        def _():
            for part in range(parts):
                lanes = slice(part * D, (part + 1) * D)
                down_ref[lanes] = w_ref[2 * D : 3 * D, lanes]

        rank = rank_ref[0, number : number + 1, :]
        rank_column = jnp.broadcast_to(rank, (8, rows)).T[:, :1]
        slot_down = lax.broadcasted_iota(jnp.int32, (CAP, rows), 0).astype(F32)
        slot_across = lax.broadcasted_iota(jnp.int32, (rows, CAP), 1).astype(F32)
        pick = slot_down == rank
        pick_low = pick.astype(F32).astype(BF16)
        spread = (slot_across == rank_column).astype(F32).astype(BF16)
        picked = dot(pick_low, jnp.concatenate([act_ref[0], cot_ref[0]], axis=1))
        taken_wide, grad_rows = picked[:, :D], picked[:, D:]
        taken = taken_wide.astype(BF16)
        gate_row = gate_ref[0, number : number + 1, :]
        gate = jnp.sum(jnp.where(pick, gate_row, 0.0), axis=1, keepdims=True)
        grad_wide = gate * grad_rows
        grad_result = grad_wide.astype(BF16)
        block = pl.ds(pl.multiple_of(lax.rem(s, batch) * CAP, CAP), CAP)
        xt_ref[:, block] = taken_wide.T.astype(BF16)
        dyt_ref[:, block] = grad_wide.T.astype(BF16)
        result = jnp.zeros((CAP, D), F32)
        grad_taken = jnp.zeros((CAP, D), F32)
        for part in range(0, FF, wide):
            lanes = slice(part, part + wide)
            w_gate = w_ref[0:D, lanes]
            w_up = w_ref[D : 2 * D, lanes]
            w_down = down_ref[lanes]
            gate_lin = dot(taken, w_gate)
            up_lin = dot(taken, w_up)
            sig = 0.5 * jnp.tanh(0.5 * gate_lin) + 0.5
            silu = gate_lin * sig
            hidden = (silu * up_lin).astype(BF16)
            result += dot(hidden, w_down)
            grad_hidden = dot(grad_result, w_down, 1, 1)
            grad_gate = (grad_hidden * up_lin * (sig + silu * (1.0 - sig))).astype(BF16)
            grad_up = (grad_hidden * silu).astype(BF16)
            hid_ref[block, lanes] = hidden
            dg_ref[block, lanes] = grad_gate
            du_ref[block, lanes] = grad_up
            grad_taken += dot(grad_gate, w_gate, 1, 1) + dot(grad_up, w_up, 1, 1)
        result = result.astype(BF16).astype(F32)
        grad_gate_slot = jnp.sum(grad_rows * result, axis=1, keepdims=True)
        grad_gate_row = jnp.sum(jnp.where(pick, grad_gate_slot, 0.0), axis=0, keepdims=True)
        both = jnp.concatenate([gate * result, grad_taken], axis=1).astype(BF16)
        both = dot(spread, both)
        routed, grad_in = both[:, :D], both[:, D:]
        if prev is not None:
            grad_in += prev[0][0]
            routed += prev[2][0]
        if last:
            routed_ref[0] = routed.astype(BF16)
            gin_buf[s] = grad_in.astype(BF16)
            if prev is not None:
                ggate_buf[s, 0:number] = prev[1][0]
            ggate_buf[s, number : number + 1] = grad_gate_row

            @pl.when(s < nex - 1)
            def _():
                for copy in copies(s):
                    copy.start()
        else:
            routed_ref[0] = routed
            gin_ref[0] = grad_in
            if prev is not None:
                ggate_ref[0, 0:number] = prev[1][0]
            ggate_ref[0, number : number + 1] = grad_gate_row

        if first:

            @pl.when(s == 0)
            def _():
                scatter.along_x()

            @pl.when(s == min(2, nex - 1))
            def _():
                scatter.after_x()
                if last:
                    scatter.along_dp()

        own = []
        if last:
            own = [
                pltpu.make_async_copy(src, dst, loc.at[n])
                for n, (src, dst) in enumerate(
                    (
                        (gin_buf.at[nex - 1], gin_out.at[nex - 1]),
                        (ggate_buf.at[nex - 1], ggate_out.at[ex]),
                    )
                )
            ]

        @pl.when(s == nex - 1)
        def _():
            for copy in own:
                copy.start()

        def weight_grads(flush):
            def put(at, lanes, value):
                if flush:
                    value += acc_ref[at : at + D, lanes]
                if flush < flushes - 1:
                    acc_ref[at : at + D, lanes] = value
                else:
                    grad_ref[at : at + D, lanes] = value.astype(BF16)

            def columns(part, carry):
                begin = pl.multiple_of(part * wide, wide)
                lanes = pl.ds(begin, wide)
                put(0, lanes, dot(xt_ref[...], dg_ref[:, lanes]))
                put(D, lanes, dot(xt_ref[...], du_ref[:, lanes]))
                down = dot(dyt_ref[...], hid_ref[:, lanes])
                for n in range(0, wide, D):
                    put(2 * D, pl.ds(begin + n, D), down[:, n : n + D].T)
                return carry

            lax.fori_loop(0, FF // wide, columns, 0)

        for flush in range(flushes):
            pl.when(s == (flush + 1) * batch - 1)(functools.partial(weight_grads, flush))

        @pl.when(s == nex - 1)
        def _():
            if settle is not None:
                settle.finish_y()
            if last:
                scatter.finish(early_out)
                for step in range(nex - 1):
                    for copy in copies(step):
                        copy.wait()
                for copy in own:
                    copy.wait()

    def per_source(*tail):
        return pl.BlockSpec((1,) + tail, lambda s: (s,) + (0,) * len(tail))

    def whole(shape):
        return pl.BlockSpec(shape, lambda s: (0,) * len(shape), pipeline_mode=pl.Buffered(1))

    def whole_out(shape):
        return pl.BlockSpec(shape, lambda s: (0,) * len(shape))

    inputs = [weights, act_all, cot_all, ranks, gates]
    in_specs = [
        whole(weights.shape),
        per_source(rows, D),
        per_source(rows, D),
        per_source(local, rows),
        per_source(local, rows),
    ]
    if before is not None:
        inputs += list(before)
        in_specs += [per_source(rows, D), per_source(number, rows), per_source(rows, D)]
    if talks:
        inputs.append(early)
        in_specs.append(whole(early.shape))
    if settle is not None:
        inputs.append(done)
        in_specs.append(any_spec())
    dma = pltpu.SemaphoreType.DMA
    kind = BF16 if last else F32
    out_shape = [
        jax.ShapeDtypeStruct((nex, rows, D), kind),
        jax.ShapeDtypeStruct((nex, number + 1, rows), F32),
        jax.ShapeDtypeStruct((nex, rows, D), kind),
        jax.ShapeDtypeStruct(weights.shape, BF16),
    ]
    if last:
        out_specs = [any_spec()] * 2
    else:
        out_specs = [per_source(rows, D), per_source(number + 1, rows)]
    out_specs += [per_source(rows, D), whole_out(weights.shape)]
    if talks:
        shape = (ROW_PAD, 3 * FF) if last else scatter.spread_shape()
        out_shape.append(jax.ShapeDtypeStruct(shape, F32 if last else BF16))
        out_specs.append(whole_out(shape))
    if settle is not None:
        out_shape.append(jax.ShapeDtypeStruct((grid.nz,) + done.shape[1:], BF16))
        out_specs.append(any_spec())
    scratch = [
        pltpu.VMEM((D, batch * CAP), BF16),
        pltpu.VMEM((D, batch * CAP), BF16),
        pltpu.VMEM((batch * CAP, FF), BF16),
        pltpu.VMEM((batch * CAP, FF), BF16),
        pltpu.VMEM((batch * CAP, FF), BF16),
        pltpu.VMEM((FF, D), BF16),
    ]
    if flushes > 1:
        scratch.append(pltpu.VMEM(weights.shape, F32))
    if last:
        scratch += [
            pltpu.VMEM((nex, rows, D), BF16),
            pltpu.VMEM((nex, local, rows), F32),
            dma((nex - 1, 2)),
            dma((nex - 1, 2)),
            dma((2,)),
        ]
    if first:
        scratch += scatter.scratch_x()
    if last:
        scratch += scatter.scratch_dp()
    if first and last:
        scratch.append(pltpu.VMEM(scatter.spread_shape(), BF16))
    if settle is not None:
        scratch += settle.scratch_y()
    return pl.pallas_call(
        kernel,
        grid=(nex,),
        out_shape=tuple(out_shape),
        in_specs=in_specs,
        out_specs=tuple(out_specs),
        scratch_shapes=scratch,
        compiler_params=pltpu.CompilerParams(
            vmem_limit_bytes=60 * MIB,
            collective_id=5 + number if talks else None,
            has_side_effects=talks,
        ),
        cost_estimate=pl.CostEstimate(
            flops=nex * CAP * D * FF * 2 * 11,
            bytes_accessed=25 * MIB,
            transcendentals=nex * CAP * FF,
        ),
        name="experts_step",
    )(*inputs)


def middle_step(grid, gin, ggate, mixed, probs, lin, gact, act_across, heads, grad_out, small, gain, terms,
                partial):
    ndp, nex, units = grid.ndp, grid.nex, grid.units
    local = EXPERTS // nex
    settle = ShardScatter(grid, *terms.shape[1:])
    settle_before = None if partial is None else ShardScatter(grid, *partial.shape[1:])

    def kernel(gin_ref, ggate_ref, mixed_ref, probs_ref, lin_ref, gact_ref, across_ref, heads_ref,
               go_ref, small_ref, gain_ref, terms_ref, *refs):
        refs = list(refs)
        partial_ref = refs.pop(0) if settle_before is not None else None
        dst, grad_mixed_ref, middle_ref, settle_out = refs[:4]
        del refs[:4]
        before_out = refs.pop(0) if settle_before is not None else None
        flipped, buf, send, recv, loc = refs[:5]
        settle_refs, before_refs = refs[5:9], refs[9:]
        dp, ex = lax.axis_index("dp"), lax.axis_index("expert")
        greet([(lax.rem(dp + d, ndp), ex) for d in range(1, ndp)])
        settle.bind(terms_ref)
        settle.bind_y(settle_out, settle_refs)
        settle.start_y()
        if settle_before is not None:
            settle_before.bind(partial_ref)
            settle_before.bind_z(before_refs)
            settle_before.start_z()

        grad_out = go_ref[...].astype(F32)
        probs = probs_ref[...]
        shared_gate = probs[:, EXPERTS : EXPERTS + 1]
        flipped[...] = jnp.zeros_like(flipped)
        for n in range(nex):
            flipped[n * local : (n + 1) * local] = ggate_ref[n]
        grad_probs = flipped[...].T
        lane = lax.broadcasted_iota(jnp.int32, probs.shape, 1)
        inner = jnp.sum(
            jnp.where(lane < EXPERTS, probs * grad_probs, 0.0), axis=1, keepdims=True
        )
        svec = shared_gate * (1.0 - shared_gate)
        svec = svec * jnp.sum(grad_out * lin_ref[...], axis=1, keepdims=True)
        grad_misc = jnp.where(
            lane < EXPERTS,
            probs * (grad_probs - inner),
            jnp.where(lane == EXPERTS, svec, 0.0),
        ).astype(BF16)
        grad_act = gact_ref[...] + dot(grad_misc, small_ref[:, :MISC], 1, 1)
        for n in range(nex):
            grad_act += gin_ref[n].astype(F32)
        mixed = mixed_ref[...]
        scale = lax.rsqrt(jnp.mean(mixed * mixed, axis=-1, keepdims=True) + eps_norm)
        normed = mixed * scale
        gain_grad = jnp.sum(grad_act * normed, axis=0, keepdims=True)
        weighted = grad_act * gain_ref[2:3]
        grad_mixed = grad_out + scale * (
            weighted - normed * jnp.mean(weighted * normed, axis=-1, keepdims=True)
        )
        grad_mixed_ref[...] = grad_mixed
        grad_low = grad_mixed.astype(BF16)
        for s in range(SERIES_DEV):
            rows = slice(s * SEG, (s + 1) * SEG)
            grad = dot(small_ref[:, MISC:], grad_low[rows], 1, 1).astype(BF16)
            buf[s * HEADS : (s + 1) * HEADS] = grad.reshape(HEADS, HEAD_DIM, SEG)
        if units * ndp > UNITS_ALL:
            buf[UNITS_ALL:] = jnp.zeros((units * ndp - UNITS_ALL, HEAD_DIM, SEG), BF16)
        lanes = pl.ds(pl.multiple_of(dp * SEG, SEG), SEG)
        copies = []
        for d in far_first(ndp):
            target = lax.rem(dp + d, ndp)
            copy = remote(
                buf.at[pl.ds(target * units, units)], dst.at[:, :, lanes],
                send.at[d - 1], recv.at[d - 1], (target, ex),
            )
            copy.start()
            copies.append(copy)
        copy = pltpu.make_async_copy(
            buf.at[pl.ds(dp * units, units)], dst.at[:, :, lanes], loc
        )
        copy.start()
        copies.append(copy)
        group = group_matrix(grid)
        total = jnp.zeros((D, D), F32)
        for s in range(SERIES_DEV):
            attn = heads_ref[s * HEADS : (s + 1) * HEADS].reshape(D, SEG)
            attn = dot(group, attn).astype(BF16)
            total += dot(attn, grad_low[s * SEG : (s + 1) * SEG])
        middle_ref[:, :D] = total.astype(BF16)
        gain_rows = jnp.broadcast_to(gain_grad, (MISC, D)).astype(BF16)
        gain_column = dot(group, gain_rows, 1, 1)
        misc_grad = dot(across_ref[...], grad_misc)
        lane = lax.broadcasted_iota(jnp.int32, misc_grad.shape, 1)
        misc_grad = jnp.where(lane == EXPERTS + 2, gain_column, misc_grad)
        middle_ref[:, D:] = misc_grad.astype(BF16)
        settle.finish_y()
        for copy in copies:
            copy.wait()
        if settle_before is not None:
            settle_before.finish_z(before_out)

    dma = pltpu.SemaphoreType.DMA
    vmem = pl.BlockSpec(memory_space=pltpu.VMEM)
    hbm = pl.BlockSpec(memory_space=pltpu.HBM)
    inputs = [gin, ggate, mixed, probs, lin, gact, act_across, heads, grad_out, small, gain]
    in_specs = [vmem] * len(inputs) + [any_spec()]
    out_shape = [
        jax.ShapeDtypeStruct((units, HEAD_DIM, SEG * ndp), BF16),
        jax.ShapeDtypeStruct((TOK_DEV, D), F32),
        jax.ShapeDtypeStruct((D, D + MISC), BF16),
        jax.ShapeDtypeStruct((grid.nz,) + terms.shape[1:], BF16),
    ]
    out_specs = [any_spec(), vmem, vmem, hbm]
    scratch = [
        pltpu.VMEM((MISC, TOK_DEV), F32),
        pltpu.VMEM((units * ndp, HEAD_DIM, SEG), BF16),
        dma((ndp - 1,)),
        dma((ndp - 1,)),
        dma,
    ] + settle.scratch_y()
    inputs.append(terms)
    if settle_before is not None:
        inputs.append(partial)
        in_specs.append(any_spec())
        out_shape.append(jax.ShapeDtypeStruct(partial.shape[1:], BF16))
        out_specs.append(vmem)
        scratch += settle_before.scratch_z()
    return pl.pallas_call(
        kernel,
        out_shape=tuple(out_shape),
        in_specs=in_specs,
        out_specs=tuple(out_specs),
        scratch_shapes=scratch,
        compiler_params=pltpu.CompilerParams(
            collective_id=2, has_side_effects=True, vmem_limit_bytes=60 * MIB
        ),
        name="middle_step",
    )(*inputs)


def local(
    tokens,
    cotangent,
    lengths,
    routes,
    dense_weights,
    dense_first,
    dense_second,
    dense_average,
    expert_weights,
    expert_first,
    expert_second,
    expert_average,
):
    ndp, nex = lax.axis_size("dp"), lax.axis_size("expert")
    dp, ex = lax.axis_index("dp"), lax.axis_index("expert")
    grid = Grid(ndp, nex)
    local_experts = EXPERTS // nex
    length = SEG * ndp
    rows_dev = D // grid.ndev
    shard_rows = 3 * D // ndp

    spot = jnp.arange(FF, dtype=jnp.int32)
    order = (FF // D) * (spot % D) + spot // D
    mix = (spot[:, None] == order[None, :]).astype(BF16)
    shard_row = dp * shard_rows + jnp.arange(shard_rows, dtype=jnp.int32)
    is_down = (shard_row >= 2 * D)[None, :, None]
    expert_low = expert_weights.astype(BF16).reshape(local_experts, shard_rows, FF)
    mixed_low = jnp.einsum(
        "erf,fg->erg", expert_low, mix, preferred_element_type=F32
    ).astype(BF16)
    expert_send = jnp.where(is_down, expert_low, mixed_low)
    table = dense_weights.astype(BF16).reshape(rows_dev, -1)
    after = 4 * D + EXPERTS

    def padded(*columns):
        return jnp.pad(jnp.concatenate(columns, axis=1), ((0, ROW_PAD - rows_dev), (0, 0)))

    shard_first = padded(
        table[:, : 3 * D],
        table[:, 4 * D : after],
        table[:, after + 3 * FF :],
        jnp.zeros((rows_dev, MISC - EXPERTS - 3), BF16),
        table[:, 3 * D : 4 * D],
    )
    shard_rest = padded(table[:, after : after + 3 * FF])

    names = jnp.arange(EXPERTS, dtype=jnp.int32)
    routes_rows = routes.reshape(TOK_DEV, TOP)
    member = (routes_rows[:, :, None] == names[None, None, :]).any(axis=1)
    before = jnp.arange(TOK_DEV)
    earlier = (before[None, :] < before[:, None]).astype(BF16)
    count = jnp.dot(earlier, member.astype(BF16), preferred_element_type=F32)
    ranks = jnp.where(member, count, -1.0).T.reshape(nex, local_experts, TOK_DEV)

    local_pos = dp * SEG + jnp.arange(SEG, dtype=jnp.int32)
    live = (local_pos[None, :] < lengths[:, None]).astype(F32)
    grad_out_low = (cotangent.astype(F32) * live[..., None]).astype(BF16).reshape(TOK_DEV, D)

    tok_all, dense_all, cot_all, rank_all = first_exchange(
        grid, tokens, shard_first, grad_out_low, ranks
    )
    expert_all = [
        lax.all_gather(expert_send[e], "dp", axis=0, tiled=True) for e in range(local_experts)
    ]
    tok_all = tok_all.reshape(grid.slots, length, D)

    dense_all = dense_all.reshape(grid.ndev * ROW_PAD, -1)

    half = HEAD_DIM // 2
    inverse = rope_base ** (-jnp.arange(half, dtype=F32) * 2.0 / HEAD_DIM)
    angles = inverse[:, None] * jnp.arange(length, dtype=jnp.int32).astype(F32)[None, :]
    cosine, sine = jnp.cos(angles), jnp.sin(angles)
    heads_here, rest, act_one, query, key, value, lse, qkv_rows = attend(
        grid, lengths, tok_all, dense_all, cosine, sine, shard_rest
    )
    heads_here = heads_here.reshape(-1, HEAD_DIM, SEG)[:UNITS_ALL]

    (act_all, gates_all, mixed_rows, probs, shared_lin, grad_act_shared, early, act_across, small,
     gains) = route_rows(
        grid, heads_here, tokens, dense_all, grad_out_low, rest.reshape(grid.ndev * ROW_PAD, -1)
    )
    before, terms, partial = None, None, None
    for e in range(local_experts):
        results = experts_step(
            grid, e, expert_all[e], act_all, cot_all, rank_all, gates_all, before, early, terms
        )
        before, early = results[:3], results[4]
        terms = results[3].reshape(ndp, shard_rows, FF)
        partial = results[5] if e else None
    gin_back, ggate_back, routed_parts = before

    grad_heads, grad_mixed, middle, partial, *expert_sums = middle_step(
        grid, gin_back, ggate_back, mixed_rows, probs, shared_lin, grad_act_shared, act_across,
        heads_here, grad_out_low, small, gains, terms, partial,
    )

    output, grad_tokens, dense_table, last_sum = attend_back(
        grid, lengths, tok_all, act_one, qkv_rows, query, key, value, lse, grad_heads, cosine, sine,
        middle, routed_parts, partial, tokens, mixed_rows, grad_mixed, probs, shared_lin, gains, early,
    )
    dense_grad = dense_table[:rows_dev, : dense_weights.shape[0] // rows_dev].reshape(-1)
    expert_sums.append(last_sum)
    expert_sums = jnp.stack(expert_sums)
    unmixed = jnp.einsum("erg,fg->erf", expert_sums, mix, preferred_element_type=F32)
    expert_grad = jnp.where(is_down, expert_sums.astype(F32), unmixed)
    expert_grad = expert_grad.reshape(expert_weights.shape)

    dense_first_new, dense_second_new, dense_new, dense_average_new = adamw_update(
        dense_weights, dense_grad, dense_first, dense_second, dense_average
    )
    expert_first_new, expert_second_new, expert_new, expert_average_new = adamw_update(
        expert_weights, expert_grad, expert_first, expert_second, expert_average
    )
    return (
        output.reshape(tokens.shape),
        grad_tokens.reshape(tokens.shape),
        dense_grad,
        dense_first_new,
        dense_second_new,
        dense_new,
        dense_average_new,
        expert_grad,
        expert_first_new,
        expert_second_new,
        expert_new,
        expert_average_new,
    )


def solution(mesh):
    rows = P("expert", "dp", None)
    dense = P(("dp", "expert"))
    experts = P("expert", "dp")
    return jax.shard_map(
        local,
        mesh=mesh,
        in_specs=(
            (rows, rows, P("expert"), P("dp", "expert", None, None)) + (dense,) * 4 + (experts,) * 4
        ),
        out_specs=(rows, rows) + (dense,) * 5 + (experts,) * 5,
        check_vma=False,
    )
```

```python
import functools
import math

import jax
import jax.numpy as jnp
from jax import lax
from jax.experimental import pallas as pl
from jax.experimental.pallas import tpu as pltpu
from jax.sharding import PartitionSpec as P

D = 384
HEADS = 12
HEAD_DIM = 32
FF = 1536
EXPERTS = 8
TOP = 2
SEG = 128
SERIES_DEV = 6
STEP = 8
TOK_DEV = 768
CAP = 384
ROW_PAD = 16
MISC = 128
UNITS_ALL = SERIES_DEV * HEADS
QBLOCK = 256
MIB = 1 << 20

eps_norm = 1e-06
beta_one = 0.5
beta_two = 0.5
learn_rate = 0.02
weight_decay = 0.1
eps_adam = 1e-08
average_keep = 0.9
rope_base = 10000.0
neg_fill = -1e30

MESH = pl.DeviceIdType.MESH
F32 = jnp.float32
BF16 = jnp.bfloat16


def adamw_update(weights, grads, first, second, average):
    first_new = beta_one * first + (1.0 - beta_one) * grads
    second_new = beta_two * second + (1.0 - beta_two) * grads * grads
    first_hat = first_new / (1.0 - beta_one**STEP)
    second_hat = second_new / (1.0 - beta_two**STEP)
    weights_new = weights - learn_rate * (
        first_hat / (jnp.sqrt(second_hat) + eps_adam) + weight_decay * weights
    )
    average_new = average_keep * average + (1.0 - average_keep) * weights_new
    return (first_new, second_new, weights_new, average_new)


def dot(left, right, left_dim=1, right_dim=0):
    return lax.dot_general(
        left, right, (((left_dim,), (right_dim,)), ((), ())), preferred_element_type=F32
    )


class Grid:
    def __init__(self, ndp, nex):
        self.ndp, self.nex = ndp, nex
        self.nz = math.gcd(ndp, 4)
        self.ny = ndp // self.nz
        self.nc = math.gcd(nex, 2)
        self.nx = nex // self.nc
        self.ndev = ndp * nex
        self.units = -(-UNITS_ALL // ndp)
        spans = [
            [u // HEADS for u in range(self.units * o, min(self.units * (o + 1), UNITS_ALL))]
            for o in range(ndp)
        ]
        self.owned = [sorted(set(s)) for s in spans]
        self.slots = max(len(s) for s in self.owned)

    def first_series(self, owner):
        return (owner * self.units) // HEADS

    def holds(self, owner, slot):
        begin = owner * self.units
        end = jnp.minimum(begin + self.units, UNITS_ALL)
        return (begin // HEADS + slot) * HEADS < end


def remote(src, dst, send, recv, target):
    return pltpu.make_async_remote_copy(
        src_ref=src,
        dst_ref=dst,
        send_sem=send,
        recv_sem=recv,
        device_id=target,
        device_id_type=MESH,
    )


def greet(peers):
    barrier = pltpu.get_barrier_semaphore()
    for peer in peers:
        pl.semaphore_signal(barrier, inc=1, device_id=peer, device_id_type=MESH)
    pl.semaphore_wait(barrier, len(peers))


def any_spec():
    return pl.BlockSpec(memory_space=pl.ANY)


def far_first(n):
    return sorted(range(1, n), key=lambda d: -min(d, n - d))


def comm_params(number):
    return pltpu.CompilerParams(collective_id=number, has_side_effects=True)


def unpad_matrix(grid):
    shape = (D, grid.ndev * ROW_PAD)
    rows_dev = D // grid.ndev
    row = lax.broadcasted_iota(jnp.int32, shape, 0)
    at = (row // rows_dev) * ROW_PAD + lax.rem(row, rows_dev)
    return (lax.broadcasted_iota(jnp.int32, shape, 1) == at).astype(F32).astype(BF16)


def group_matrix(grid):
    rows_dev = D // grid.ndev
    row = lax.broadcasted_iota(jnp.int32, (D, D), 1)
    owner = row // rows_dev
    at = (lax.rem(owner, grid.nex) * grid.ndp + owner // grid.nex) * rows_dev
    at = at + lax.rem(row, rows_dev)
    return (lax.broadcasted_iota(jnp.int32, (D, D), 0) == at).astype(F32).astype(BF16)


class DenseGather:
    def __init__(self, grid):
        self.grid = grid

    def scratch(self):
        dma = pltpu.SemaphoreType.DMA
        return [dma((self.grid.ndev,)), dma((self.grid.ndev,)), dma]

    def bind(self, shard, out, refs):
        g = self.grid
        self.shard, self.out = shard, out
        self.send, self.recv, self.loc = refs
        dp, ex = lax.axis_index("dp"), lax.axis_index("expert")
        self.z, self.y = dp // g.ny, lax.rem(dp, g.ny)
        self.x, self.c = ex // g.nc, lax.rem(ex, g.nc)
        self.zs = [0] + far_first(g.nz)[::-1]
        self.count = 0
        self.ends = []

    def place(self, dz, dy, dx, dc):
        g = self.grid
        return (
            lax.rem(self.z + dz, g.nz) * g.ny + lax.rem(self.y + dy, g.ny),
            lax.rem(self.x + dx, g.nx) * g.nc + lax.rem(self.c + dc, g.nc),
        )

    def slot(self, dz, dy, dx, dc):
        g = self.grid
        dp, ex = self.place(g.nz - dz, g.ny - dy, g.nx - dx, g.nc - dc)
        return dp * g.nex + ex

    def copy(self, ref, slot, number, target):
        return remote(ref, self.out.at[slot], self.send.at[number], self.recv.at[slot], target)

    def go(self, slot, target):
        ref = self.out.at[slot]
        if self.count < self.own_sends():
            ref = self.shard
        self.copy(ref, slot, self.count, target).start()
        self.count += 1

    def own_sends(self):
        g = self.grid
        return g.nz + g.ny + g.nx + g.nc - 4

    def wait(self, slot):
        self.copy(self.shard, slot, 0, self.place(0, 0, 0, 0)).wait_recv()

    def onward(self, slot, axes):
        g = self.grid
        if "y" in axes:
            for dy in range(1, g.ny):
                self.go(slot, self.place(0, dy, 0, 0))
        if "x" in axes:
            for dx in range(1, g.nx):
                self.go(slot, self.place(0, 0, dx, 0))
        for dc in range(1, g.nc):
            self.go(slot, self.place(0, 0, 0, dc))

    def own(self):
        return pltpu.make_async_copy(self.shard, self.out.at[self.slot(0, 0, 0, 0)], self.loc)

    def start(self):
        own = self.slot(0, 0, 0, 0)
        for dz in far_first(self.grid.nz):
            self.go(own, self.place(dz, 0, 0, 0))
        self.onward(own, "yx")
        self.own().start()

    def pass_z(self):
        for dz in self.zs[1:]:
            slot = self.slot(dz, 0, 0, 0)
            self.wait(slot)
            self.onward(slot, "yx")

    def pass_y(self):
        for dy in range(1, self.grid.ny):
            for dz in self.zs:
                slot = self.slot(dz, dy, 0, 0)
                self.wait(slot)
                self.onward(slot, "x")

    def pass_x(self):
        g = self.grid
        for dx in range(1, g.nx):
            for dy in range(g.ny):
                for dz in self.zs:
                    slot = self.slot(dz, dy, dx, 0)
                    self.wait(slot)
                    self.onward(slot, "")

    def finish(self):
        g = self.grid
        for dc in range(1, g.nc):
            for dx in range(g.nx):
                for dy in range(g.ny):
                    for dz in self.zs:
                        self.wait(self.slot(dz, dy, dx, dc))
        for number in range(g.ndev - 1):
            self.copy(self.shard, 0, number, self.place(0, 0, 0, 0)).wait_send()
        self.own().wait()


class RowGather:
    parts = 3

    def __init__(self, grid):
        self.grid = grid

    def scratch(self):
        g, n = self.grid, self.parts
        dma = pltpu.SemaphoreType.DMA
        return [dma((g.nx + g.nc, n)), dma((g.nex, n)), dma((g.nx, n)), dma]

    def bind(self, src, dst, refs):
        g = self.grid
        self.src, self.dst = src, dst
        self.send, self.recv, self.fsend, self.loc = refs
        self.dp, self.ex = lax.axis_index("dp"), lax.axis_index("expert")
        self.x, self.c = self.ex // g.nc, lax.rem(self.ex, g.nc)
        self.sends = []

    def rows(self, part):
        extent = TOK_DEV // self.parts
        return pl.ds(part * extent, extent)

    def slot_at(self, owner, target):
        return lax.rem(owner - target - 1 + 2 * self.grid.nex, self.grid.nex)

    def go(self, ref, owner, part, sem, target):
        slot = self.slot_at(owner, target)
        copy = remote(
            ref, self.dst.at[slot, self.rows(part)], sem, self.recv.at[slot, part],
            (self.dp, target),
        )
        copy.start()
        self.sends.append(copy)

    def arrived(self, owner, part):
        slot = self.slot_at(owner, self.ex)
        remote(
            self.src.at[self.rows(part)], self.dst.at[slot, self.rows(part)], self.send.at[0, 0],
            self.recv.at[slot, part], (self.dp, self.ex),
        ).wait_recv()

    def beside(self, dc):
        g = self.grid
        return self.x * g.nc + lax.rem(self.c + dc, g.nc)

    def start(self):
        g = self.grid
        for part in range(self.parts):
            for dx in range(1, g.nx):
                target = lax.rem(self.x + dx, g.nx) * g.nc + self.c
                ref = self.src.at[self.rows(part)]
                self.go(ref, self.ex, part, self.send.at[dx - 1, part], target)
        for part in range(self.parts):
            for dc in range(1, g.nc):
                ref = self.src.at[self.rows(part)]
                self.go(ref, self.ex, part, self.send.at[g.nx + dc - 2, part], self.beside(dc))
        self.own = pltpu.make_async_copy(self.src, self.dst.at[g.nex - 1], self.loc)
        self.own.start()

    def pass_on(self, part):
        g = self.grid
        for dx in range(1, g.nx):
            owner = lax.rem(self.x + g.nx - dx, g.nx) * g.nc + self.c
            self.arrived(owner, part)
            for dc in range(1, g.nc):
                ref = self.dst.at[self.slot_at(owner, self.ex), self.rows(part)]
                self.go(ref, owner, part, self.fsend.at[dx - 1, part], self.beside(dc))

    def finish(self):
        g = self.grid
        for part in range(self.parts):
            for dc in range(1, g.nc):
                for dx in range(g.nx):
                    owner = lax.rem(self.x + g.nx - dx, g.nx) * g.nc
                    self.arrived(owner + lax.rem(self.c + g.nc - dc, g.nc), part)
        for copy in self.sends:
            copy.wait_send()
        self.own.wait()


def first_exchange(grid, tokens, shard, cot, ranks):
    ndp, nex = grid.ndp, grid.nex

    def kernel(tok, shd, cot_in, rank_in, tok_out, dense_out, cot_out, rank_out,
               t_send, t_recv, e_send, e_recv, loc, *more_refs):
        dp, ex = lax.axis_index("dp"), lax.axis_index("expert")

        def off(value, by, n):
            return lax.rem(value + by, n)

        peers = [(off(dp, d, ndp), ex) for d in range(1, ndp)]
        peers += [(dp, off(ex, d, nex)) for d in range(1, nex)]
        greet(peers)
        dense = DenseGather(grid)
        dense.bind(shd, dense_out, more_refs[4:])
        dense.start()

        def token_copy(d, slot, src_series, sender, target):
            return remote(
                tok.at[src_series],
                tok_out.at[slot, sender],
                t_send.at[d - 1, slot],
                t_recv.at[d - 1, slot],
                (target, ex),
            )

        for d in far_first(ndp):
            target = off(dp, d, ndp)
            for slot in range(grid.slots):

                @pl.when(grid.holds(target, slot))
                def _():
                    token_copy(d, slot, grid.first_series(target) + slot, dp, target).start()

        rows = RowGather(grid)
        rows.bind(cot_in, cot_out, more_refs[:4])
        rows.start()
        e_sends = []
        for d in range(1, nex):
            target = off(ex, d, nex)
            copy = remote(
                rank_in.at[target], rank_out.at[nex - 1 - d], e_send.at[d - 1], e_recv.at[d - 1],
                (dp, target),
            )
            copy.start()
            e_sends.append(copy)
        copy = pltpu.make_async_copy(rank_in.at[ex], rank_out.at[nex - 1], loc.at[0])
        copy.start()
        e_sends.append(copy)

        for slot in range(grid.slots):

            @pl.when(grid.holds(dp, slot))
            def _():
                copy = pltpu.make_async_copy(
                    tok.at[grid.first_series(dp) + slot], tok_out.at[slot, dp], loc.at[1 + slot]
                )
                copy.start()
                copy.wait()

        dense.pass_z()
        rows.pass_on(0)
        dense.pass_y()
        for part in range(1, rows.parts):
            rows.pass_on(part)
        dense.pass_x()
        dense.finish()
        rows.finish()
        for d in range(1, ndp):
            for slot in range(grid.slots):

                @pl.when(grid.holds(dp, slot))
                def _():
                    token_copy(d, slot, 0, dp, off(dp, d, ndp)).wait_recv()

                @pl.when(grid.holds(off(dp, d, ndp), slot))
                def _():
                    token_copy(d, slot, 0, dp, off(dp, d, ndp)).wait_send()

        for copy in e_sends:
            copy.wait()

    seg, width = tokens.shape[1:]
    dma = pltpu.SemaphoreType.DMA
    return pl.pallas_call(
        kernel,
        out_shape=(
            jax.ShapeDtypeStruct((grid.slots, ndp, seg, width), tokens.dtype),
            jax.ShapeDtypeStruct((grid.ndev,) + shard.shape, shard.dtype),
            jax.ShapeDtypeStruct((nex,) + cot.shape, cot.dtype),
            jax.ShapeDtypeStruct(ranks.shape, ranks.dtype),
        ),
        in_specs=[any_spec()] * 4,
        out_specs=(any_spec(),) * 4,
        scratch_shapes=[
            dma((ndp - 1, grid.slots)),
            dma((ndp - 1, grid.slots)),
            dma((nex - 1,)),
            dma((nex - 1,)),
            dma((1 + grid.slots,)),
        ]
        + RowGather(grid).scratch()
        + DenseGather(grid).scratch(),
        compiler_params=comm_params(0),
        name="first_exchange",
    )(tokens, shard, cot, ranks)


class RowScatter:
    def __init__(self, grid, width):
        self.grid, self.width = grid, width
        self.rows = D // grid.nex
        self.rows_dev = D // grid.ndev

    def scratch_x(self):
        g = self.grid
        dma = pltpu.SemaphoreType.DMA
        blocks = pltpu.VMEM((g.nx, self.rows, self.width), BF16)
        return [blocks, blocks, blocks, dma((2, 2)), dma((g.nx, 2))]

    def scratch_dp(self):
        g = self.grid
        return [
            pltpu.VMEM((g.ndp, ROW_PAD, self.width), BF16),
            pltpu.SemaphoreType.DMA((g.ndp, 2)),
        ]

    def spread_shape(self):
        return (self.grid.ndp * ROW_PAD, self.width)

    def bind(self, spread):
        g = self.grid
        self.spread = spread
        self.dp, self.ex = lax.axis_index("dp"), lax.axis_index("expert")
        self.x, self.c = self.ex // g.nc, lax.rem(self.ex, g.nc)

    def bind_x(self, source, refs):
        self.source = source
        self.got_core, self.by_x, self.got_x, self.sem_core, self.sem_x = refs

    def bind_dp(self, refs):
        self.got_dp, self.sem_dp = refs

    def core_copy(self):
        other = 1 - self.c
        return remote(
            self.source.at[:, other], self.got_core, self.sem_core.at[0, 0],
            self.sem_core.at[0, 1], (self.dp, self.x * 2 + other),
        )

    def x_copy(self, d):
        target = lax.rem(self.x + d, self.grid.nx)
        return remote(
            self.by_x.at[target], self.got_x.at[d], self.sem_x.at[d, 0], self.sem_x.at[d, 1],
            (self.dp, target * self.grid.nc + self.c),
        )

    def dp_copy(self, d):
        target = lax.rem(self.dp + d, self.grid.ndp)
        rows = pl.ds(pl.multiple_of(target * ROW_PAD, ROW_PAD), ROW_PAD)
        return remote(
            self.spread.at[rows], self.got_dp.at[d], self.sem_dp.at[d, 0], self.sem_dp.at[d, 1],
            (target, self.ex),
        )

    def start(self):
        self.core_copy().start()

    def along_x(self):
        g = self.grid
        self.core_copy().wait()
        for n in range(g.nx):
            mine = self.source[n, pl.ds(self.c, 1)][0]
            self.by_x[n] = (mine.astype(F32) + self.got_core[n].astype(F32)).astype(BF16)
        for d in range(1, g.nx):
            self.x_copy(d).start()

    def after_x(self):
        g = self.grid
        for d in range(1, g.nx):
            self.x_copy(d).wait()
        total = self.by_x[pl.ds(self.x, 1)][0].astype(F32)
        for d in range(1, g.nx):
            total += self.got_x[d].astype(F32)
        to = lax.broadcasted_iota(jnp.int32, (g.ndp * ROW_PAD, self.rows), 0)
        of = lax.broadcasted_iota(jnp.int32, (g.ndp * ROW_PAD, self.rows), 1)
        place = (of // self.rows_dev) * ROW_PAD + lax.rem(of, self.rows_dev)
        move = (to == place).astype(F32).astype(BF16)
        self.spread[...] = dot(move, total.astype(BF16)).astype(BF16)

    def along_dp(self):
        for d in far_first(self.grid.ndp):
            self.dp_copy(d).start()

    def finish(self, out):
        g = self.grid
        rows = pl.ds(pl.multiple_of(self.dp * ROW_PAD, ROW_PAD), ROW_PAD)
        total = self.spread[rows].astype(F32)
        for d in range(1, g.ndp):
            self.dp_copy(d).wait()
            total += self.got_dp[d].astype(F32)
        out[...] = total


class ShardScatter:
    def __init__(self, grid, rows, width):
        self.grid, self.rows, self.width = grid, rows, width

    def scratch_y(self):
        g = self.grid
        block = (self.rows, self.width)
        dma = pltpu.SemaphoreType.DMA
        return [
            pltpu.VMEM((g.nz,) + block, BF16),
            pltpu.VMEM((max(g.ny - 1, 1), g.nz) + block, BF16),
            dma((g.ny, g.nz, 2)),
            dma((g.nz,)),
        ]

    def scratch_z(self):
        g = self.grid
        dma = pltpu.SemaphoreType.DMA
        return [pltpu.VMEM((g.nz, self.rows, self.width), BF16), dma((g.nz, 2))]

    def scratch_own(self):
        return [pltpu.VMEM((self.rows, self.width), BF16), pltpu.SemaphoreType.DMA]

    def where(self):
        g = self.grid
        self.dp, self.ex = lax.axis_index("dp"), lax.axis_index("expert")
        self.z, self.y = self.dp // g.ny, lax.rem(self.dp, g.ny)
        self.order = far_first(g.nz) + [0]

    def bind_y(self, source, refs):
        self.where()
        self.source = source
        self.mine, self.got_y, self.sem_y, self.loc = refs
        self.sums = self.mine

    def bind_z(self, refs):
        self.got_z, self.sem_z = refs

    def bind_own(self, sums, refs):
        self.where()
        self.sums = sums
        self.own, self.own_sem = refs

    def place(self, dz, dy):
        g = self.grid
        return lax.rem(self.z + dz, g.nz) * g.ny + lax.rem(self.y + dy, g.ny)

    def block(self, number):
        if len(self.source.shape) == 3:
            return self.source.at[number]
        return self.source.at[pl.ds(pl.multiple_of(number * self.rows, ROW_PAD), self.rows)]

    def y_copy(self, dy, dz):
        return remote(
            self.block(self.place(dz, dy)), self.got_y.at[dy - 1, dz],
            self.sem_y.at[dy, dz, 0], self.sem_y.at[dy, dz, 1], (self.place(0, dy), self.ex),
        )

    def load(self, dz):
        return pltpu.make_async_copy(
            self.block(self.place(dz, 0)), self.mine.at[dz], self.loc.at[dz]
        )

    def start_y(self):
        for dz in self.order:
            for dy in range(1, self.grid.ny):
                self.y_copy(dy, dz).start()
            self.load(dz).start()

    def sum_y(self, then=None):
        g = self.grid
        for dz in self.order:
            self.load(dz).wait()
            for dy in range(1, g.ny):
                self.y_copy(dy, dz).wait()
            if g.ny > 1:
                total = self.mine[dz].astype(F32)
                for dy in range(1, g.ny):
                    total += self.got_y[dy - 1, dz].astype(F32)
                self.mine[dz] = total.astype(BF16)
            if then is not None:
                then(dz)

    def store_y(self, out):
        def store(dz):
            return pltpu.make_async_copy(self.mine.at[dz], out.at[dz], self.loc.at[dz])

        self.sum_y(lambda dz: store(dz).start())
        for dz in self.order:
            store(dz).wait()

    def z_copy(self, dz):
        return remote(
            self.sums.at[dz], self.got_z.at[dz], self.sem_z.at[dz, 0], self.sem_z.at[dz, 1],
            (self.place(dz, 0), self.ex),
        )

    def own_copy(self):
        return pltpu.make_async_copy(self.sums.at[0], self.own, self.own_sem)

    def start_z(self):
        for dz in far_first(self.grid.nz):
            self.z_copy(dz).start()
        if self.sums is not getattr(self, "mine", None):
            self.own_copy().start()

    def finish_z(self, out):
        if self.sums is getattr(self, "mine", None):
            total = self.mine[0].astype(F32)
        else:
            self.own_copy().wait()
            total = self.own[...].astype(F32)
        for dz in range(1, self.grid.nz):
            self.z_copy(dz).wait()
            total += self.got_z[dz].astype(F32)
        out[...] = total.astype(out.dtype)


def route_rows(grid, heads, tokens, table, grad_out, weights):
    nex = grid.nex
    local = EXPERTS // nex
    count = len(OUTS_ROUTE)

    def kernel(heads_ref, tok_ref, table_ref, go_ref, w_ref, dst, gate_dst, *refs):
        outs, bufs = refs[:count], refs[count : 2 * count]
        mixed_buf, probs_buf, lin_ref, gact_ref, early_ref, across_ref, small_ref, gain_ref = bufs
        act_buf, gate_buf, g_send, g_recv, loc, out_sem = refs[2 * count : 2 * count + 6]
        row_refs = refs[2 * count + 6 :]
        dp, ex = lax.axis_index("dp"), lax.axis_index("expert")
        greet([(dp, lax.rem(ex + d, nex)) for d in range(1, nex)])

        def keep(n):
            return pltpu.make_async_copy(bufs[n], outs[n], out_sem.at[n])

        unpad, group = unpad_matrix(grid), group_matrix(grid)
        small_ref[...] = dot(unpad, table_ref[:, 3 * D :]).astype(BF16)
        gain_ref[...] = dot(table_ref[:, 3 * D : 3 * D + MISC], unpad, 0, 1)[
            EXPERTS : EXPERTS + 8
        ]
        for s in range(SERIES_DEV):
            attn = heads_ref[s * HEADS : (s + 1) * HEADS].reshape(D, SEG)
            rows = slice(s * SEG, (s + 1) * SEG)
            mixed_buf[rows] = tok_ref[s].astype(F32) + dot(attn, small_ref[:, MISC:], 0, 0)
        mixed = mixed_buf[...]
        scale = lax.rsqrt(jnp.mean(mixed * mixed, axis=-1, keepdims=True) + eps_norm)
        act = (mixed * scale * gain_ref[2:3]).astype(BF16)
        act_buf[...] = act
        gather = RowGather(grid)
        gather.bind(act_buf, dst, row_refs)
        gather.start()
        misc = dot(act, small_ref[:, :MISC])
        lane = lax.broadcasted_iota(jnp.int32, misc.shape, 1)
        logits = jnp.where(lane < EXPERTS, misc, neg_fill)
        powers = jnp.exp(logits - jnp.max(logits, axis=1, keepdims=True))
        probs = powers / jnp.sum(powers, axis=1, keepdims=True)
        shared_gate = 0.5 * jnp.tanh(0.5 * misc[:, EXPERTS : EXPERTS + 1]) + 0.5
        probs_buf[...] = jnp.where(lane == EXPERTS, shared_gate, probs)
        flipped = probs.T
        for n in range(nex):
            gate_buf[n] = flipped[n * local : (n + 1) * local]
        gate_copies = []
        for d in range(1, nex):
            target = lax.rem(ex + d, nex)
            copy = remote(
                gate_buf.at[target], gate_dst.at[nex - 1 - d], g_send.at[d - 1], g_recv.at[d - 1],
                (dp, target),
            )
            copy.start()
            gate_copies.append(copy)
        copy = pltpu.make_async_copy(gate_buf.at[ex], gate_dst.at[nex - 1], loc)
        copy.start()
        gate_copies.append(copy)
        for n in (0, 1, 6, 7):
            keep(n).start()

        grad_lin = (go_ref[...].astype(F32) * shared_gate).astype(BF16)
        across_ref[...] = dot(group, act, 1, 1).astype(BF16)
        keep(5).start()
        grad_across = dot(group, grad_lin, 1, 1).astype(BF16)
        wide = 2 * D
        for n in range(FF // wide):
            gate_w, up_w, down_w = (
                dot(unpad, w_ref[:, m * FF + n * wide : m * FF + (n + 1) * wide]).astype(BF16)
                for m in range(3)
            )
            gate_lin, up_lin = dot(act, gate_w), dot(act, up_w)
            sig = 0.5 * jnp.tanh(0.5 * gate_lin) + 0.5
            silu = gate_lin * sig
            hidden = (silu * up_lin).astype(BF16)
            grad_hidden = dot(grad_lin, down_w)
            grad_gate = (grad_hidden * up_lin * (sig + silu * (1.0 - sig))).astype(BF16)
            grad_up = (grad_hidden * silu).astype(BF16)
            lin = dot(hidden, down_w, 1, 1)
            gact = dot(grad_gate, gate_w, 1, 1) + dot(grad_up, up_w, 1, 1)
            if n:
                lin_ref[...] += lin
                gact_ref[...] += gact
            else:
                lin_ref[...] = lin
                gact_ref[...] = gact
            if n == 0:
                gather.pass_on(0)
            else:
                keep(2).start()
                keep(3).start()
            for m, (left, right) in enumerate(
                ((across_ref[...], grad_gate), (across_ref[...], grad_up), (grad_across, hidden))
            ):
                lanes = slice(m * FF + n * wide, m * FF + (n + 1) * wide)
                early_ref[:, lanes] = dot(left, right).astype(BF16)
            if n == 0:
                gather.pass_on(1)
        keep(4).start()
        for part in range(2, gather.parts):
            gather.pass_on(part)
        gather.finish()
        for copy in gate_copies:
            copy.wait()
        for n in range(count):
            keep(n).wait()

    dma = pltpu.SemaphoreType.DMA
    vmem = pl.BlockSpec(memory_space=pltpu.VMEM)
    hbm = pl.BlockSpec(memory_space=pltpu.HBM)
    inputs = (heads, tokens, table, grad_out, weights)
    return pl.pallas_call(
        kernel,
        out_shape=(
            jax.ShapeDtypeStruct((nex, TOK_DEV, D), BF16),
            jax.ShapeDtypeStruct((nex, local, TOK_DEV), F32),
        )
        + tuple(jax.ShapeDtypeStruct(shape, kind) for shape, kind in OUTS_ROUTE),
        in_specs=[vmem] * len(inputs),
        out_specs=(hbm,) * (2 + count),
        scratch_shapes=[pltpu.VMEM(shape, kind) for shape, kind in OUTS_ROUTE]
        + [
            pltpu.VMEM((TOK_DEV, D), BF16),
            pltpu.VMEM((nex, local, TOK_DEV), F32),
            dma((nex - 1,)),
            dma((nex - 1,)),
            dma,
            dma((count,)),
        ]
        + RowGather(grid).scratch(),
        compiler_params=pltpu.CompilerParams(
            collective_id=4, has_side_effects=True, vmem_limit_bytes=60 * MIB
        ),
        name="route_rows",
    )(*inputs)


OUTS_ROUTE = (
    ((TOK_DEV, D), F32),
    ((TOK_DEV, MISC), F32),
    ((TOK_DEV, D), F32),
    ((TOK_DEV, D), F32),
    ((D, 3 * FF), BF16),
    ((D, TOK_DEV), BF16),
    ((D, MISC + D), BF16),
    ((8, D), F32),
)


def turn(values, cosine, sine):
    first, second = values[: HEAD_DIM // 2], values[HEAD_DIM // 2 :]
    return jnp.concatenate(
        [first * cosine - second * sine, second * cosine + first * sine], axis=0
    )


def allowed_mask(extent, block, length):
    keys = lax.broadcasted_iota(jnp.int32, (extent, QBLOCK), 0)
    queries = lax.broadcasted_iota(jnp.int32, (extent, QBLOCK), 1) + block * QBLOCK
    return (keys <= queries) & (keys < length)


def attend(grid, lengths, tok, table, cosine, sine, shard):
    units, length, ndp, nex = grid.units, tok.shape[1], grid.ndp, grid.nex
    blocks = length // QBLOCK
    chunk = 1
    ends = sorted(set(range(chunk - 1, units, chunk)) | {units - 1})

    def kernel(len_ref, tok_ref, table_ref, cos_ref, sin_ref, shard_ref,
               heads_ref, dense_ref, act_out, q_out, k_out, v_out, lse_out, w_out,
               act_ref, q_ref, k_ref, v_ref, lse_ref, w_ref, k_sem,
               buf, h_send, h_recv, h_loc, *dense_refs):
        i = pl.program_id(0)
        dp, ex = lax.axis_index("dp"), lax.axis_index("expert")
        unit = jnp.minimum(dp * units + i, UNITS_ALL - 1)
        head = lax.rem(unit, HEADS)
        slot = jnp.minimum(unit // HEADS - grid.first_series(dp), grid.slots - 1)
        slot = jnp.maximum(slot, 0)
        dense = DenseGather(grid)
        dense.bind(shard_ref, dense_ref, dense_refs)

        def keep():
            pairs = (
                (act_ref, act_out), (q_ref, q_out), (k_ref, k_out), (v_ref, v_out),
                (lse_ref, lse_out), (w_ref, w_out),
            )
            return [
                pltpu.make_async_copy(src, dst, k_sem.at[n]) for n, (src, dst) in enumerate(pairs)
            ]

        def heads_copy(d, n):
            begin = ends[n - 1] + 1 if n else 0
            count = ends[n] + 1 - begin
            target = lax.rem(dp + d, ndp)
            lanes = pl.ds(pl.multiple_of(target * SEG, SEG), SEG)
            return remote(
                buf.at[pl.ds(begin, count), :, lanes],
                heads_ref.at[dp, pl.ds(begin, count)],
                h_send.at[d - 1, n],
                h_recv.at[d - 1, n],
                (target, ex),
            )

        @pl.when(i == 0)
        def _():
            greet(
                [(lax.rem(dp + d, ndp), ex) for d in range(1, ndp)]
                + [(dp, lax.rem(ex + d, nex)) for d in range(1, nex)]
            )
            dense.start()
            w_ref[...] = dot(table_ref[:, : 3 * D + MISC], unpad_matrix(grid), 0, 1).astype(BF16)

        @pl.when((i == 0) | (head == 0))
        def _():
            residual = tok_ref[slot].astype(F32)
            scale = lax.rsqrt(jnp.mean(residual * residual, axis=-1, keepdims=True) + eps_norm)
            gain = w_ref[3 * D : 3 * D + ROW_PAD].astype(F32)[EXPERTS + 1 : EXPERTS + 2]
            act_ref[slot] = (residual * scale * gain).astype(BF16)

        cos, sin = cos_ref[...], sin_ref[...]
        w_rows = [
            w_ref[pl.ds(pl.multiple_of(n * D + head * HEAD_DIM, HEAD_DIM), HEAD_DIM)]
            for n in range(3)
        ]
        qkv = dot(jnp.concatenate(w_rows, axis=0), act_ref[slot], 1, 1)
        query = turn(qkv[:HEAD_DIM], cos, sin).astype(BF16)
        key_wide = turn(qkv[HEAD_DIM : 2 * HEAD_DIM], cos, sin)
        value = qkv[2 * HEAD_DIM :].astype(BF16)
        key_rows = key_wide.T.astype(BF16)
        q_ref[i], k_ref[i], v_ref[i] = query, key_wide.astype(BF16), value
        live = len_ref[unit // HEADS]
        for block in range(blocks):
            extent = QBLOCK * (block + 1)
            lanes = slice(QBLOCK * block, extent)
            scores = dot(key_rows[:extent], query[:, lanes]) * HEAD_DIM ** (-0.5)
            scores = jnp.where(allowed_mask(extent, block, live), scores, neg_fill)
            top = jnp.max(scores, axis=0, keepdims=True)
            probs = jnp.exp(scores - top)
            total = jnp.sum(probs, axis=0, keepdims=True)
            result = dot(value[:, :extent], probs.astype(BF16))
            buf[i, :, lanes] = (result * (1.0 / total)).astype(BF16)
            lse_ref[i, :, lanes] = top + jnp.log(total)

        for n, end in enumerate(ends):

            @pl.when(i == end)
            def _():
                for d in far_first(ndp):
                    heads_copy(d, n).start()

        pl.when(i == min(3, units - 1))(dense.pass_z)
        pl.when(i == min(5, units - 1))(dense.pass_y)

        @pl.when(i == units - 1)
        def _():
            mine = pltpu.make_async_copy(
                buf.at[:, :, pl.ds(pl.multiple_of(dp * SEG, SEG), SEG)], heads_ref.at[dp], h_loc
            )
            mine.start()
            for copy in keep():
                copy.start()
            dense.pass_x()
            dense.finish()
            for n in range(len(ends)):
                for d in range(1, ndp):
                    heads_copy(d, n).wait()
            mine.wait()
            for copy in keep():
                copy.wait()

    def whole(array):
        return pl.BlockSpec(
            array.shape, lambda i: (0,) * array.ndim, pipeline_mode=pl.Buffered(1)
        )

    feature = jax.ShapeDtypeStruct((units, HEAD_DIM, length), BF16)
    inputs = (tok, table, cosine, sine)
    dma = pltpu.SemaphoreType.DMA
    return pl.pallas_call(
        kernel,
        grid=(units,),
        out_shape=(
            jax.ShapeDtypeStruct((ndp, units, HEAD_DIM, SEG), BF16),
            jax.ShapeDtypeStruct((grid.ndev,) + shard.shape, BF16),
            jax.ShapeDtypeStruct((grid.slots, length, D), BF16),
            feature,
            feature,
            feature,
            jax.ShapeDtypeStruct((units, 1, length), F32),
            jax.ShapeDtypeStruct((3 * D + MISC, D), BF16),
        ),
        in_specs=[pl.BlockSpec(memory_space=pltpu.SMEM)]
        + [whole(v) for v in inputs]
        + [any_spec()],
        out_specs=(
            any_spec(),
            any_spec(),
        )
        + (pl.BlockSpec(memory_space=pltpu.HBM),) * 6,
        scratch_shapes=[
            pltpu.VMEM((grid.slots, length, D), BF16),
            pltpu.VMEM(feature.shape, BF16),
            pltpu.VMEM(feature.shape, BF16),
            pltpu.VMEM(feature.shape, BF16),
            pltpu.VMEM((units, 1, length), F32),
            pltpu.VMEM((3 * D + MISC, D), BF16),
            dma((6,)),
            pltpu.VMEM((units, HEAD_DIM, length), BF16),
            dma((ndp - 1, len(ends))),
            dma((ndp - 1, len(ends))),
            dma,
        ]
        + DenseGather(grid).scratch(),
        compiler_params=pltpu.CompilerParams(
            collective_id=1, has_side_effects=True, vmem_limit_bytes=60 * MIB
        ),
        cost_estimate=pl.CostEstimate(
            flops=units * length * length * HEAD_DIM * 2 * 8,
            bytes_accessed=8 * MIB,
            transcendentals=units * length * length,
        ),
        name="attend",
    )(lengths, *inputs, shard)


def attend_back(grid, lengths, tok, act, weights, query, key, value, lse, grad_heads, cosine, sine,
                early, routed, zs, tokens, mixed, grad_mixed, probs, lin, gains, shared):
    units, length, ndp, nex = grid.units, act.shape[1], grid.ndp, grid.nex
    blocks = length // QBLOCK
    scale = HEAD_DIM ** (-0.5)
    early_width, late_width = early.shape[1], 3 * D + MISC
    early_sum, late_sum = RowScatter(grid, early_width), RowScatter(grid, late_width)
    early = early.reshape(grid.nx, grid.nc, early_sum.rows, early_width)
    steps = [min(n, units - 1) for n in (0, 3)]
    works_z = [ShardScatter(grid, *v.shape[1:]) for v in zs]
    many = len(zs)

    def kernel(*refs):
        refs = list(refs)
        z_refs, z_outs = refs[20 : 20 + many], refs[23 + many : 23 + 2 * many]
        del refs[23 + many : 23 + 2 * many], refs[20 : 20 + many]
        (len_ref, tok_ref, act_ref, w_ref, q_ref, k_ref, v_ref, lse_ref, do_ref, cos_ref, sin_ref,
         early_ref, tokens_ref, mixed_ref, grad_mixed_ref, probs_ref, lin_ref, gains_ref, shared_ref,
         routed_ref,
         output_ref, grad_tokens_ref, table_ref,
         rows_out, early_out, late_out, routed_out,
         acc, back, dq, dk, dv, grads, gain, late_ref, b_send, b_recv, b_loc,
         early_spread, late_spread, r_send, r_recv) = refs[:42]
        at = 42
        for work, source, spread in (
            (early_sum, early_ref, early_spread),
            (late_sum, late_ref, late_spread),
        ):
            work.bind(spread)
            work.bind_x(source, refs[at : at + 5])
            work.bind_dp(refs[at + 5 : at + 7])
            at += 7
        for work, ref in zip(works_z, z_refs):
            work.bind_own(ref, refs[at : at + 2])
            work.bind_z(refs[at + 2 : at + 4])
            at += 4

        def routed_copy(step):
            return remote(
                routed_ref.at[step], routed_out.at[step], r_send.at[step], r_recv.at[step],
                (dp, lax.rem(ex + 1 + step, nex)),
            )

        i = pl.program_id(0)
        dp, ex = lax.axis_index("dp"), lax.axis_index("expert")
        unit = dp * units + i
        working = unit < UNITS_ALL
        series, head = unit // HEADS, lax.rem(unit, HEADS)
        slot = jnp.minimum(series - grid.first_series(dp), grid.slots - 1)

        def back_copy(d, which):
            target = lax.rem(dp + d, ndp)
            return remote(
                back.at[which, pl.ds(pl.multiple_of(target * SEG, SEG), SEG)],
                rows_out.at[dp, which],
                b_send.at[d - 1, which],
                b_recv.at[d - 1, which],
                (target, ex),
            )

        def back_local(which):
            return pltpu.make_async_copy(
                back.at[which, pl.ds(pl.multiple_of(dp * SEG, SEG), SEG)],
                rows_out.at[dp, which],
                b_loc.at[which],
            )

        @pl.when(i == 0)
        def _():
            greet(
                [(lax.rem(dp + d, ndp), ex) for d in range(1, ndp)]
                + [(dp, lax.rem(ex + d, nex)) for d in range(1, nex)]
            )
            for work in works_z:
                work.start_z()
            early_sum.start()
            grads[...] = jnp.zeros_like(grads)
            gain[...] = jnp.zeros_like(gain)

        @pl.when((i == 0) | (head == 0))
        def _():
            acc[...] = jnp.zeros_like(acc)

        @pl.when(working)
        def _():
            live = len_ref[series]
            query, key, value, grad = q_ref[i], k_ref[i], v_ref[i], do_ref[i]
            key_rows = key.astype(F32).T.astype(BF16)
            value_rows = value.astype(F32).T.astype(BF16)
            dk[...] = jnp.zeros_like(dk)
            dv[...] = jnp.zeros_like(dv)
            for block in range(blocks):
                extent = QBLOCK * (block + 1)
                lanes = slice(QBLOCK * block, extent)
                scores = dot(key_rows[:extent], query[:, lanes]) * scale
                scores = jnp.where(allowed_mask(extent, block, live), scores, neg_fill)
                probs = jnp.exp(scores - lse_ref[i, :, lanes])
                grad_probs = dot(value_rows[:extent], grad[:, lanes])
                delta = jnp.sum(probs * grad_probs, axis=0, keepdims=True)
                grad_scores = (probs * (grad_probs - delta)).astype(BF16)
                probs_low = probs.astype(BF16)
                dq[:, lanes] = dot(key[:, :extent], grad_scores)
                dk[:, :extent] += dot(query[:, lanes], grad_scores, 1, 1)
                dv[:, :extent] += dot(grad[:, lanes], probs_low, 1, 1)
            cos, sin = cos_ref[...], -sin_ref[...]
            stacked = jnp.concatenate(
                [
                    turn(dq[...] * scale, cos, sin),
                    turn(dk[...] * scale, cos, sin),
                    dv[...],
                ],
                axis=0,
            ).astype(BF16)
            weight_grads = dot(stacked, act_ref[slot]).astype(BF16)
            w_rows = []
            for n in range(3):
                at = pl.multiple_of(n * D + head * HEAD_DIM, HEAD_DIM)
                part = slice(n * HEAD_DIM, (n + 1) * HEAD_DIM)
                grads[pl.ds(at, HEAD_DIM)] = weight_grads[part]
                w_rows.append(w_ref[pl.ds(at, HEAD_DIM)])
            acc[...] += dot(stacked, jnp.concatenate(w_rows, axis=0), 0, 0)

        @pl.when(working & ((head == HEADS - 1) | (i == units - 1)))
        def _():
            share = acc[...]
            residual = tok_ref[slot].astype(F32)
            normed = residual * lax.rsqrt(
                jnp.mean(residual * residual, axis=-1, keepdims=True) + eps_norm
            )
            gain[...] += jnp.sum(share * normed, axis=0, keepdims=True)
            back[slot] = share.astype(BF16)
            for d in far_first(ndp):
                back_copy(d, slot).start()
            back_local(slot).start()

        @pl.when(i == steps[0])
        def _():
            early_sum.along_x()
            for step in range(nex - 1):
                routed_copy(step).start()

        @pl.when(i == steps[1])
        def _():
            early_sum.after_x()
            early_sum.along_dp()

        @pl.when(i == units - 1)
        def _():
            grads[3 * D :] = jnp.broadcast_to(gain[...], (ROW_PAD, D)).astype(BF16)
            late = dot(group_matrix(grid), grads[...], 1, 1).astype(BF16)
            late = late.reshape(late_ref.shape[:3] + (late.shape[1],))
            late_ref[:, :, :, : late.shape[3]] = late
            late_ref[:, :, :, late.shape[3] :] = jnp.zeros(
                late_ref.shape[:3] + (late_width - late.shape[3],), BF16
            )
            late_sum.start()
            early_sum.finish(early_out)
            late_sum.along_x()
            for step in range(nex - 1):
                routed_copy(step).wait()
            total = routed_ref[nex - 1].astype(F32)
            for step in range(nex - 1):
                total += routed_out[step].astype(F32)
            shared_gate = probs_ref[:, EXPERTS : EXPERTS + 1]
            output_ref[...] = (mixed_ref[...] + total + shared_gate * lin_ref[...]).astype(BF16)
            late_sum.after_x()
            late_sum.along_dp()
            for which in range(grid.slots):
                for d in range(1, ndp):

                    @pl.when(grid.holds(lax.rem(dp + ndp - d, ndp), which))
                    def _():
                        back_copy(d, which).wait_recv()

                @pl.when(grid.holds(dp, which))
                def _():
                    for d in range(1, ndp):
                        back_copy(d, which).wait_send()
                    back_local(which).wait()

            for n in range(SERIES_DEV):
                rows = slice(n * SEG, (n + 1) * SEG)
                grad_act = sum(
                    rows_out[owner, owned.index(n)].astype(F32)
                    for owner, owned in enumerate(grid.owned)
                    if n in owned
                )
                residual = tokens_ref[n].astype(F32)
                scale_one = lax.rsqrt(
                    jnp.mean(residual * residual, axis=-1, keepdims=True) + eps_norm
                )
                normed = residual * scale_one
                weighted = grad_act * gains_ref[1:2]
                inner = jnp.mean(weighted * normed, axis=-1, keepdims=True)
                grad_tokens_ref[rows] = grad_mixed_ref[rows] + scale_one * (
                    weighted - normed * inner
                )
            late_sum.finish(late_out)
            late, mid = late_out[...], early_out[...]
            misc = mid[:, D:]
            lane = lax.broadcasted_iota(jnp.int32, misc.shape, 1)
            wide = jnp.concatenate([shared_ref[...], jnp.zeros_like(misc)], axis=1)
            wide = pltpu.roll(wide, EXPERTS, 1)
            table_ref[:, : 3 * D] = late[:, : 3 * D]
            table_ref[:, 3 * D : 4 * D] = mid[:, :D]
            table_ref[:, 4 * D : 4 * D + MISC] = wide[:, :MISC] + jnp.where(
                lane < EXPERTS, misc, 0.0
            )
            table_ref[:, 4 * D + MISC : 4 * D + 3 * FF] = wide[:, MISC : 3 * FF]
            ends = jnp.where(lane == EXPERTS + 1, late[:, 3 * D :], misc)
            ends = jnp.where((lane >= EXPERTS) & (lane < EXPERTS + 3), ends, 0.0)
            table_ref[:, 4 * D + 3 * FF :] = wide[:, 3 * FF :] + ends
            for work, out in zip(works_z, z_outs):
                work.finish_z(out)

    def whole(array):
        return pl.BlockSpec(
            array.shape, lambda i: (0,) * array.ndim, pipeline_mode=pl.Buffered(1)
        )

    def whole_out(shape):
        return pl.BlockSpec(shape, lambda i: (0,) * len(shape))

    dma = pltpu.SemaphoreType.DMA
    inputs = (tok, act, weights, query, key, value, lse, grad_heads, cosine, sine, early, tokens, mixed,
              grad_mixed, probs, lin, gains, shared, routed)
    table_shape = (ROW_PAD, 4 * D + 3 * FF + MISC)
    return pl.pallas_call(
        kernel,
        grid=(units,),
        out_shape=(
            jax.ShapeDtypeStruct((TOK_DEV, D), BF16),
            jax.ShapeDtypeStruct((TOK_DEV, D), F32),
            jax.ShapeDtypeStruct(table_shape, F32),
        )
        + tuple(jax.ShapeDtypeStruct((work.rows, work.width), BF16) for work in works_z),
        in_specs=[pl.BlockSpec(memory_space=pltpu.SMEM)]
        + [whole(v) for v in inputs]
        + [any_spec()] * many,
        out_specs=(
            whole_out((TOK_DEV, D)),
            whole_out((TOK_DEV, D)),
            whole_out(table_shape),
        )
        + tuple(whole_out((work.rows, work.width)) for work in works_z),
        scratch_shapes=[
            pltpu.VMEM((ndp, grid.slots, SEG, D), BF16),
            pltpu.VMEM((ROW_PAD, early_width), F32),
            pltpu.VMEM((ROW_PAD, late_width), F32),
            pltpu.VMEM((nex - 1,) + routed.shape[1:], BF16),
            pltpu.VMEM((length, D), F32),
            pltpu.VMEM((grid.slots, length, D), BF16),
            pltpu.VMEM((HEAD_DIM, length), F32),
            pltpu.VMEM((HEAD_DIM, length), F32),
            pltpu.VMEM((HEAD_DIM, length), F32),
            pltpu.VMEM((3 * D + ROW_PAD, D), BF16),
            pltpu.VMEM((1, D), F32),
            pltpu.VMEM((grid.nx, grid.nc, late_sum.rows, late_width), BF16),
            dma((ndp - 1, grid.slots)),
            dma((ndp - 1, grid.slots)),
            dma((grid.slots,)),
            pltpu.VMEM(early_sum.spread_shape(), BF16),
            pltpu.VMEM(late_sum.spread_shape(), BF16),
            dma((nex - 1,)),
            dma((nex - 1,)),
        ]
        + early_sum.scratch_x()
        + early_sum.scratch_dp()
        + late_sum.scratch_x()
        + late_sum.scratch_dp()
        + sum((work.scratch_own() + work.scratch_z() for work in works_z), []),
        compiler_params=pltpu.CompilerParams(
            collective_id=3, has_side_effects=True, vmem_limit_bytes=60 * MIB
        ),
        cost_estimate=pl.CostEstimate(
            flops=units * length * length * HEAD_DIM * 2 * 20,
            bytes_accessed=12 * MIB,
            transcendentals=units * length * length,
        ),
        name="attend_back",
    )(lengths, *inputs, *zs)


def experts_step(grid, number, weights, act_all, cot_all, ranks, gates, before, early, ys, zs):
    nex, nc, ndp = grid.nex, grid.nc, grid.ndp
    rows = act_all.shape[1]
    local = EXPERTS // nex
    parts, wide = FF // D, FF // 2
    first, last = number == 0, number == local - 1
    batch = math.gcd(nex, 4)
    flushes = nex // batch
    steps = 2 * nex
    shard_rows = 3 * D // ndp
    inline = shard_rows % ROW_PAD == 0
    scatter = RowScatter(grid, 3 * FF) if first or last else None
    early_work = ShardScatter(grid, ROW_PAD, 3 * FF) if last else None
    works_y = [ShardScatter(grid, *v.shape[1:]) for v in ys]
    works_z = [ShardScatter(grid, *v.shape[1:]) for v in zs]
    work_own = ShardScatter(grid, shard_rows, wide) if inline else None
    if first:
        early = early.reshape(grid.nx, nc, scatter.rows, 3 * FF)

    def kernel(*refs):
        refs = list(refs)

        def take(count):
            taken = refs[:count]
            del refs[:count]
            return taken

        w_ref, act_ref, cot_ref, rank_ref, gate_ref = take(5)
        prev = take(3) if before is not None else None
        early_ref = take(1)[0] if scatter is not None else None
        y_refs, z_refs = take(len(ys)), take(len(zs))
        gin_ref, ggate_ref, routed_ref = take(3)
        early_out = take(1)[0] if scatter is not None else None
        own_outs = take(2)
        sum_outs = take(len(ys) + len(zs))
        xt_ref, dyt_ref, dg_ref, du_ref, hid_ref, down_ref = take(6)
        taken_ref, rows_ref, result_ref, back_ref, grad_ref, own_sem = take(6)
        acc_ref = take(1)[0] if flushes > 1 else None
        if last:
            gin_buf, ggate_buf, send, recv, loc = take(5)
        if first:
            scatter.bind_x(early_ref, take(len(scatter.scratch_x())))
        if scatter is not None:
            spread_ref = early_out if not last else take(1)[0] if first else early_ref
            scatter.bind(spread_ref)
        if last:
            early_work.bind_y(spread_ref, take(4))
            early_work.bind_z(take(2))
        for work, ref in zip(works_y, y_refs):
            work.bind_y(ref, take(4))
            work.bind_z(take(2))
        for work, ref in zip(works_z, z_refs):
            work.bind_own(ref, take(2))
            work.bind_z(take(2))
        if inline:
            work_own.bind_y(grad_ref.at[0], take(4))
        t = pl.program_id(0)
        half, part = lax.rem(t // batch, 2), lax.rem(t, batch)
        s = (t // (2 * batch)) * batch + part
        dp, ex = lax.axis_index("dp"), lax.axis_index("expert")

        def copies(step):
            target = lax.rem(ex + 1 + step, nex)
            pairs = (
                (gin_buf.at[step], gin_ref.at[step]),
                (ggate_buf.at[step], ggate_ref.at[ex]),
            )
            return [
                remote(src, dst, send.at[step, n], recv.at[step, n], (dp, target))
                for n, (src, dst) in enumerate(pairs)
            ]

        @pl.when(t == 0)
        def _():
            greet(
                [(dp, lax.rem(ex + d, nex)) for d in range(1, nex)]
                + [(lax.rem(dp + d, ndp), ex) for d in range(1, ndp)]
            )
            for work in works_y:
                work.start_y()
            for work in works_z:
                work.start_z()
            if first:
                scatter.start()
            elif last:
                early_work.start_y()
            for n in range(parts):
                lanes = slice(n * D, (n + 1) * D)
                down_ref[lanes] = w_ref[2 * D : 3 * D, lanes]

        rank = rank_ref[0, number : number + 1, :]
        slot_down = lax.broadcasted_iota(jnp.int32, (CAP, rows), 0).astype(F32)
        pick = slot_down == rank
        gate_row = gate_ref[0, number : number + 1, :]
        gate = jnp.sum(jnp.where(pick, gate_row, 0.0), axis=1, keepdims=True)
        block = pl.ds(pl.multiple_of(part * CAP, CAP), CAP)

        @pl.when(half == 0)
        def _():
            pick_low = pick.astype(F32).astype(BF16)
            picked = dot(pick_low, jnp.concatenate([act_ref[0], cot_ref[0]], axis=1))
            taken_ref[part] = picked[:, :D].astype(BF16)
            rows_ref[part] = picked[:, D:].astype(BF16)
            xt_ref[:, block] = picked[:, :D].T.astype(BF16)
            dyt_ref[:, block] = (gate * picked[:, D:]).T.astype(BF16)

        taken, grad_rows = taken_ref[part], rows_ref[part].astype(F32)
        grad_result = (gate * grad_rows).astype(BF16)
        lanes = pl.ds(pl.multiple_of(half * wide, wide), wide)
        w_gate, w_up, w_down = w_ref[0:D, lanes], w_ref[D : 2 * D, lanes], down_ref[lanes]
        gate_lin = dot(taken, w_gate)
        up_lin = dot(taken, w_up)
        sig = 0.5 * jnp.tanh(0.5 * gate_lin) + 0.5
        silu = gate_lin * sig
        hidden = (silu * up_lin).astype(BF16)
        result = dot(hidden, w_down)
        grad_hidden = dot(grad_result, w_down, 1, 1)
        grad_gate = (grad_hidden * up_lin * (sig + silu * (1.0 - sig))).astype(BF16)
        grad_up = (grad_hidden * silu).astype(BF16)
        hid_ref[block], dg_ref[block], du_ref[block] = hidden, grad_gate, grad_up
        grad_taken = dot(grad_gate, w_gate, 1, 1) + dot(grad_up, w_up, 1, 1)

        @pl.when(half == 0)
        def _():
            result_ref[part], back_ref[part] = result, grad_taken

        @pl.when(half == 1)
        def _():
            out = (result_ref[part] + result).astype(BF16).astype(F32)
            grad_gate_slot = jnp.sum(grad_rows * out, axis=1, keepdims=True)
            grad_gate_row = jnp.sum(jnp.where(pick, grad_gate_slot, 0.0), axis=0, keepdims=True)
            rank_column = jnp.broadcast_to(rank, (8, rows)).T[:, :1]
            slot_across = lax.broadcasted_iota(jnp.int32, (rows, CAP), 1).astype(F32)
            spread = (slot_across == rank_column).astype(F32).astype(BF16)
            both = jnp.concatenate([gate * out, back_ref[part] + grad_taken], axis=1)
            both = dot(spread, both.astype(BF16))
            routed, grad_in = both[:, :D], both[:, D:]
            if prev is not None:
                grad_in += prev[0][0]
                routed += prev[2][0]
            if last:
                routed_ref[0] = routed.astype(BF16)
                gin_buf[s] = grad_in.astype(BF16)
                if prev is not None:
                    ggate_buf[s, 0:number] = prev[1][0]
                ggate_buf[s, number : number + 1] = grad_gate_row
            else:
                routed_ref[0] = routed
                gin_ref[0] = grad_in
                if prev is not None:
                    ggate_ref[0, 0:number] = prev[1][0]
                ggate_ref[0, number : number + 1] = grad_gate_row

        if last:

            @pl.when((half == 1) & (s < nex - 1))
            def _():
                for copy in copies(s):
                    copy.start()

        if first:

            @pl.when(t == 0)
            def _():
                scatter.along_x()

            @pl.when(t == nex)
            def _():
                scatter.after_x()
                if last:
                    early_work.start_y()

        if last:

            @pl.when(t == (steps - 1 if first else nex + 1))
            def _():
                early_work.sum_y()
                early_work.start_z()

        @pl.when(t == nex)
        def _():
            for work in works_y:
                work.sum_y()
                work.start_z()

        def weight_grads(flush, which):
            def put(at, lanes, value):
                if flush:
                    value += acc_ref[which, at : at + D, lanes]
                if flush < flushes - 1:
                    acc_ref[which, at : at + D, lanes] = value
                else:
                    grad_ref[which, at : at + D, lanes] = value.astype(BF16)

            every = slice(0, wide)
            put(0, every, dot(xt_ref[...], dg_ref[...]))
            put(D, every, dot(xt_ref[...], du_ref[...]))
            down = dot(dyt_ref[...], hid_ref[...])
            for n in range(0, wide, D):
                put(2 * D, slice(n, n + D), down[:, n : n + D].T)

        def keep(which):
            return pltpu.make_async_copy(grad_ref.at[which], own_outs[which], own_sem.at[which])

        for flush in range(flushes):
            for which in range(2):
                end = (2 * flush + which + 1) * batch - 1
                pl.when(t == end)(functools.partial(weight_grads, flush, which))

        @pl.when(t == steps - batch - 1)
        def _():
            if inline:
                work_own.start_y()
            else:
                keep(0).start()

        @pl.when(t == steps - 1)
        def _():
            keep(1).start()
            own = []
            if last:
                own = [
                    pltpu.make_async_copy(src, dst, loc.at[n])
                    for n, (src, dst) in enumerate(
                        (
                            (gin_buf.at[nex - 1], gin_ref.at[nex - 1]),
                            (ggate_buf.at[nex - 1], ggate_ref.at[ex]),
                        )
                    )
                ]
                for copy in own:
                    copy.start()
            if inline:
                work_own.store_y(own_outs[0])
            else:
                keep(0).wait()
            for work, out in zip(works_y + works_z, sum_outs):
                work.finish_z(out)
            if last:
                early_work.finish_z(early_out)
                for step in range(nex - 1):
                    for copy in copies(step):
                        copy.wait()
                for copy in own:
                    copy.wait()
            keep(1).wait()

    def source(t):
        return (t // (2 * batch)) * batch + t % batch

    def early_source(t):
        half = (t // batch) % 2
        return (t // (2 * batch)) * batch + (1 - half) * (t % batch) + half * (batch - 1)

    def late_source(t):
        return (t // (2 * batch)) * batch + ((t // batch) % 2) * (t % batch)

    def per_source(which, *tail):
        return pl.BlockSpec((1,) + tail, lambda t: (which(t),) + (0,) * len(tail))

    def whole(shape):
        return pl.BlockSpec(shape, lambda t: (0,) * len(shape), pipeline_mode=pl.Buffered(1))

    def whole_out(shape):
        return pl.BlockSpec(shape, lambda t: (0,) * len(shape))

    dma = pltpu.SemaphoreType.DMA
    kind = BF16 if last else F32
    inputs = [weights, act_all, cot_all, ranks, gates]
    in_specs = [
        whole(weights.shape),
        per_source(early_source, rows, D),
        per_source(early_source, rows, D),
        per_source(source, local, rows),
        per_source(source, local, rows),
    ]
    out_shape = [
        jax.ShapeDtypeStruct((nex, rows, D), kind),
        jax.ShapeDtypeStruct((nex, number + 1, rows), F32),
        jax.ShapeDtypeStruct((nex, rows, D), kind),
    ]
    out_specs = [
        any_spec() if last else per_source(late_source, rows, D),
        any_spec() if last else per_source(late_source, number + 1, rows),
        per_source(late_source, rows, D),
    ]
    scratch = [
        pltpu.VMEM((D, batch * CAP), BF16),
        pltpu.VMEM((D, batch * CAP), BF16),
        pltpu.VMEM((batch * CAP, wide), BF16),
        pltpu.VMEM((batch * CAP, wide), BF16),
        pltpu.VMEM((batch * CAP, wide), BF16),
        pltpu.VMEM((FF, D), BF16),
        pltpu.VMEM((batch, CAP, D), BF16),
        pltpu.VMEM((batch, CAP, D), BF16),
        pltpu.VMEM((batch, CAP, D), F32),
        pltpu.VMEM((batch, CAP, D), F32),
        pltpu.VMEM((2, 3 * D, wide), BF16),
        dma((2,)),
    ]
    if before is not None:
        inputs += list(before)
        in_specs += [
            per_source(late_source, rows, D),
            per_source(late_source, number, rows),
            per_source(late_source, rows, D),
        ]
    if scatter is not None:
        inputs.append(early)
        in_specs.append(whole(early.shape))
        shape = (ROW_PAD, 3 * FF) if last else scatter.spread_shape()
        out_shape.append(jax.ShapeDtypeStruct(shape, F32 if last else BF16))
        out_specs.append(whole_out(shape))
    inputs += list(ys) + list(zs)
    in_specs += [any_spec()] * (len(ys) + len(zs))
    own_shape = (grid.nz, shard_rows, wide) if inline else (3 * D, wide)
    for shape in (own_shape, (3 * D, wide)):
        out_shape.append(jax.ShapeDtypeStruct(shape, BF16))
        out_specs.append(any_spec())
    for work in works_y + works_z:
        out_shape.append(jax.ShapeDtypeStruct((work.rows, work.width), BF16))
        out_specs.append(whole_out((work.rows, work.width)))
    if flushes > 1:
        scratch.append(pltpu.VMEM((2, 3 * D, wide), F32))
    if last:
        scratch += [
            pltpu.VMEM((nex, rows, D), BF16),
            pltpu.VMEM((nex, local, rows), F32),
            dma((nex - 1, 2)),
            dma((nex - 1, 2)),
            dma((2,)),
        ]
    if first:
        scratch += scatter.scratch_x()
    if first and last:
        scratch.append(pltpu.VMEM(scatter.spread_shape(), BF16))
    if last:
        scratch += early_work.scratch_y() + early_work.scratch_z()
    for work in works_y:
        scratch += work.scratch_y() + work.scratch_z()
    for work in works_z:
        scratch += work.scratch_own() + work.scratch_z()
    if inline:
        scratch += work_own.scratch_y()
    results = pl.pallas_call(
        kernel,
        grid=(steps,),
        out_shape=tuple(out_shape),
        in_specs=in_specs,
        out_specs=tuple(out_specs),
        scratch_shapes=scratch,
        compiler_params=pltpu.CompilerParams(
            vmem_limit_bytes=62 * MIB, collective_id=5 + number, has_side_effects=True
        ),
        cost_estimate=pl.CostEstimate(
            flops=nex * CAP * D * FF * 2 * 11,
            bytes_accessed=25 * MIB,
            transcendentals=nex * CAP * FF,
        ),
        name="experts_step",
    )(*inputs)
    results = list(results)
    sums = results[:3]
    del results[:3]
    if scatter is not None:
        early = results.pop(0)
    return sums, early, results[:2], results[2:]


def middle_step(grid, gin, ggate, mixed, probs, lin, gact, act_across, heads, grad_out, small, gain, ys,
                zs):
    ndp, nex, units = grid.ndp, grid.nex, grid.units
    local = EXPERTS // nex
    works_y = [ShardScatter(grid, *v.shape[1:]) for v in ys]
    works_z = [ShardScatter(grid, *v.shape[1:]) for v in zs]

    def kernel(gin_ref, ggate_ref, mixed_ref, probs_ref, lin_ref, gact_ref, across_ref, heads_ref,
               go_ref, small_ref, gain_ref, *refs):
        refs = list(refs)

        def take(count):
            taken = refs[:count]
            del refs[:count]
            return taken

        y_refs, z_refs = take(len(ys)), take(len(zs))
        dst, grad_mixed_ref, middle_ref = take(3)
        y_outs, z_outs = take(len(ys)), take(len(zs))
        flipped, buf, send, recv, loc = take(5)
        for work, ref in zip(works_y, y_refs):
            work.bind_y(ref, take(4))
        for work, ref in zip(works_z, z_refs):
            work.bind_own(ref, take(2))
            work.bind_z(take(2))
        dp, ex = lax.axis_index("dp"), lax.axis_index("expert")
        greet([(lax.rem(dp + d, ndp), ex) for d in range(1, ndp)])
        for work in works_y:
            work.start_y()
        for work in works_z:
            work.start_z()

        grad_out = go_ref[...].astype(F32)
        probs = probs_ref[...]
        shared_gate = probs[:, EXPERTS : EXPERTS + 1]
        flipped[...] = jnp.zeros_like(flipped)
        for n in range(nex):
            flipped[n * local : (n + 1) * local] = ggate_ref[n]
        grad_probs = flipped[...].T
        lane = lax.broadcasted_iota(jnp.int32, probs.shape, 1)
        inner = jnp.sum(
            jnp.where(lane < EXPERTS, probs * grad_probs, 0.0), axis=1, keepdims=True
        )
        svec = shared_gate * (1.0 - shared_gate)
        svec = svec * jnp.sum(grad_out * lin_ref[...], axis=1, keepdims=True)
        grad_misc = jnp.where(
            lane < EXPERTS,
            probs * (grad_probs - inner),
            jnp.where(lane == EXPERTS, svec, 0.0),
        ).astype(BF16)
        grad_act = gact_ref[...] + dot(grad_misc, small_ref[:, :MISC], 1, 1)
        for n in range(nex):
            grad_act += gin_ref[n].astype(F32)
        mixed = mixed_ref[...]
        scale = lax.rsqrt(jnp.mean(mixed * mixed, axis=-1, keepdims=True) + eps_norm)
        normed = mixed * scale
        gain_grad = jnp.sum(grad_act * normed, axis=0, keepdims=True)
        weighted = grad_act * gain_ref[2:3]
        grad_mixed = grad_out + scale * (
            weighted - normed * jnp.mean(weighted * normed, axis=-1, keepdims=True)
        )
        grad_mixed_ref[...] = grad_mixed
        grad_low = grad_mixed.astype(BF16)
        for s in range(SERIES_DEV):
            rows = slice(s * SEG, (s + 1) * SEG)
            grad = dot(small_ref[:, MISC:], grad_low[rows], 1, 1).astype(BF16)
            buf[s * HEADS : (s + 1) * HEADS] = grad.reshape(HEADS, HEAD_DIM, SEG)
        if units * ndp > UNITS_ALL:
            buf[UNITS_ALL:] = jnp.zeros((units * ndp - UNITS_ALL, HEAD_DIM, SEG), BF16)
        lanes = pl.ds(pl.multiple_of(dp * SEG, SEG), SEG)
        copies = []
        for d in far_first(ndp):
            target = lax.rem(dp + d, ndp)
            copy = remote(
                buf.at[pl.ds(target * units, units)], dst.at[:, :, lanes],
                send.at[d - 1], recv.at[d - 1], (target, ex),
            )
            copy.start()
            copies.append(copy)
        copy = pltpu.make_async_copy(
            buf.at[pl.ds(dp * units, units)], dst.at[:, :, lanes], loc
        )
        copy.start()
        copies.append(copy)
        group = group_matrix(grid)
        total = jnp.zeros((D, D), F32)
        for s in range(SERIES_DEV):
            attn = heads_ref[s * HEADS : (s + 1) * HEADS].reshape(D, SEG)
            attn = dot(group, attn).astype(BF16)
            total += dot(attn, grad_low[s * SEG : (s + 1) * SEG])
        middle_ref[:, :D] = total.astype(BF16)
        gain_rows = jnp.broadcast_to(gain_grad, (MISC, D)).astype(BF16)
        gain_column = dot(group, gain_rows, 1, 1)
        misc_grad = dot(across_ref[...], grad_misc)
        lane = lax.broadcasted_iota(jnp.int32, misc_grad.shape, 1)
        misc_grad = jnp.where(lane == EXPERTS + 2, gain_column, misc_grad)
        middle_ref[:, D:] = misc_grad.astype(BF16)
        for work, out in zip(works_y, y_outs):
            work.store_y(out)
        for copy in copies:
            copy.wait()
        for work, out in zip(works_z, z_outs):
            work.finish_z(out)

    dma = pltpu.SemaphoreType.DMA
    vmem = pl.BlockSpec(memory_space=pltpu.VMEM)
    hbm = pl.BlockSpec(memory_space=pltpu.HBM)
    inputs = [gin, ggate, mixed, probs, lin, gact, act_across, heads, grad_out, small, gain]
    in_specs = [vmem] * len(inputs) + [any_spec()] * (len(ys) + len(zs))
    out_shape = [
        jax.ShapeDtypeStruct((units, HEAD_DIM, SEG * ndp), BF16),
        jax.ShapeDtypeStruct((TOK_DEV, D), F32),
        jax.ShapeDtypeStruct((D, D + MISC), BF16),
    ]
    out_specs = [any_spec(), vmem, vmem]
    scratch = [
        pltpu.VMEM((MISC, TOK_DEV), F32),
        pltpu.VMEM((units * ndp, HEAD_DIM, SEG), BF16),
        dma((ndp - 1,)),
        dma((ndp - 1,)),
        dma,
    ]
    inputs += list(ys) + list(zs)
    for work in works_y:
        out_shape.append(jax.ShapeDtypeStruct((grid.nz, work.rows, work.width), BF16))
        out_specs.append(hbm)
        scratch += work.scratch_y()
    for work in works_z:
        out_shape.append(jax.ShapeDtypeStruct((work.rows, work.width), BF16))
        out_specs.append(vmem)
        scratch += work.scratch_own() + work.scratch_z()
    return pl.pallas_call(
        kernel,
        out_shape=tuple(out_shape),
        in_specs=in_specs,
        out_specs=tuple(out_specs),
        scratch_shapes=scratch,
        compiler_params=pltpu.CompilerParams(
            collective_id=2, has_side_effects=True, vmem_limit_bytes=60 * MIB
        ),
        name="middle_step",
    )(*inputs)


def local(
    tokens,
    cotangent,
    lengths,
    routes,
    dense_weights,
    dense_first,
    dense_second,
    dense_average,
    expert_weights,
    expert_first,
    expert_second,
    expert_average,
):
    ndp, nex = lax.axis_size("dp"), lax.axis_size("expert")
    dp, ex = lax.axis_index("dp"), lax.axis_index("expert")
    grid = Grid(ndp, nex)
    local_experts = EXPERTS // nex
    length = SEG * ndp
    rows_dev = D // grid.ndev
    shard_rows = 3 * D // ndp

    spot = jnp.arange(FF, dtype=jnp.int32)
    order = (FF // D) * (spot % D) + spot // D
    mix = (spot[:, None] == order[None, :]).astype(BF16)
    shard_row = dp * shard_rows + jnp.arange(shard_rows, dtype=jnp.int32)
    is_down = (shard_row >= 2 * D)[None, :, None]
    expert_low = expert_weights.astype(BF16).reshape(local_experts, shard_rows, FF)
    mixed_low = jnp.einsum(
        "erf,fg->erg", expert_low, mix, preferred_element_type=F32
    ).astype(BF16)
    expert_send = jnp.where(is_down, expert_low, mixed_low)
    table = dense_weights.astype(BF16).reshape(rows_dev, -1)
    after = 4 * D + EXPERTS

    def padded(*columns):
        return jnp.pad(jnp.concatenate(columns, axis=1), ((0, ROW_PAD - rows_dev), (0, 0)))

    shard_first = padded(
        table[:, : 3 * D],
        table[:, 4 * D : after],
        table[:, after + 3 * FF :],
        jnp.zeros((rows_dev, MISC - EXPERTS - 3), BF16),
        table[:, 3 * D : 4 * D],
    )
    shard_rest = padded(table[:, after : after + 3 * FF])

    names = jnp.arange(EXPERTS, dtype=jnp.int32)
    routes_rows = routes.reshape(TOK_DEV, TOP)
    member = (routes_rows[:, :, None] == names[None, None, :]).any(axis=1)
    before = jnp.arange(TOK_DEV)
    earlier = (before[None, :] < before[:, None]).astype(BF16)
    count = jnp.dot(earlier, member.astype(BF16), preferred_element_type=F32)
    ranks = jnp.where(member, count, -1.0).T.reshape(nex, local_experts, TOK_DEV)

    local_pos = dp * SEG + jnp.arange(SEG, dtype=jnp.int32)
    live = (local_pos[None, :] < lengths[:, None]).astype(F32)
    grad_out_low = (cotangent.astype(F32) * live[..., None]).astype(BF16).reshape(TOK_DEV, D)

    tok_all, dense_all, cot_all, rank_all = first_exchange(
        grid, tokens, shard_first, grad_out_low, ranks
    )
    expert_all = [
        lax.all_gather(expert_send[e], "dp", axis=0, tiled=True) for e in range(local_experts)
    ]
    tok_all = tok_all.reshape(grid.slots, length, D)

    dense_all = dense_all.reshape(grid.ndev * ROW_PAD, -1)

    half = HEAD_DIM // 2
    inverse = rope_base ** (-jnp.arange(half, dtype=F32) * 2.0 / HEAD_DIM)
    angles = inverse[:, None] * jnp.arange(length, dtype=jnp.int32).astype(F32)[None, :]
    cosine, sine = jnp.cos(angles), jnp.sin(angles)
    heads_here, rest, act_one, query, key, value, lse, qkv_rows = attend(
        grid, lengths, tok_all, dense_all, cosine, sine, shard_rest
    )
    heads_here = heads_here.reshape(-1, HEAD_DIM, SEG)[:UNITS_ALL]

    (act_all, gates_all, mixed_rows, probs, shared_lin, grad_act_shared, early, act_across, small,
     gains) = route_rows(
        grid, heads_here, tokens, dense_all, grad_out_low, rest.reshape(grid.ndev * ROW_PAD, -1)
    )
    before, ys, zs, halves = None, [], [], []
    for e in range(local_experts):
        before, early, own, sums = experts_step(
            grid, e, expert_all[e], act_all, cot_all, rank_all, gates_all, before, early, ys, zs
        )
        halves += sums[::-1] if zs else sums
        ys = [v.reshape(ndp, shard_rows, FF // 2) for v in own if v.ndim == 2]
        zs = [v for v in own if v.ndim == 3]
    gin_back, ggate_back, routed_parts = before

    grad_heads, grad_mixed, middle, *more = middle_step(
        grid, gin_back, ggate_back, mixed_rows, probs, shared_lin, grad_act_shared, act_across,
        heads_here, grad_out_low, small, gains, ys, zs,
    )
    halves += more[len(ys) :]

    output, grad_tokens, dense_table, *sums = attend_back(
        grid, lengths, tok_all, act_one, qkv_rows, query, key, value, lse, grad_heads, cosine, sine,
        middle, routed_parts, more[: len(ys)], tokens, mixed_rows, grad_mixed, probs, shared_lin, gains, early,
    )
    dense_grad = dense_table[:rows_dev, : dense_weights.shape[0] // rows_dev].reshape(-1)
    halves += sums
    expert_sums = jnp.stack(
        [jnp.concatenate(halves[e : e + 2], axis=1) for e in range(0, 2 * local_experts, 2)]
    )
    unmixed = jnp.einsum("erg,fg->erf", expert_sums, mix, preferred_element_type=F32)
    expert_grad = jnp.where(is_down, expert_sums.astype(F32), unmixed)
    expert_grad = expert_grad.reshape(expert_weights.shape)

    dense_first_new, dense_second_new, dense_new, dense_average_new = adamw_update(
        dense_weights, dense_grad, dense_first, dense_second, dense_average
    )
    expert_first_new, expert_second_new, expert_new, expert_average_new = adamw_update(
        expert_weights, expert_grad, expert_first, expert_second, expert_average
    )
    return (
        output.reshape(tokens.shape),
        grad_tokens.reshape(tokens.shape),
        dense_grad,
        dense_first_new,
        dense_second_new,
        dense_new,
        dense_average_new,
        expert_grad,
        expert_first_new,
        expert_second_new,
        expert_new,
        expert_average_new,
    )


def solution(mesh):
    rows = P("expert", "dp", None)
    dense = P(("dp", "expert"))
    experts = P("expert", "dp")
    return jax.shard_map(
        local,
        mesh=mesh,
        in_specs=(
            (rows, rows, P("expert"), P("dp", "expert", None, None)) + (dense,) * 4 + (experts,) * 4
        ),
        out_specs=(rows, rows) + (dense,) * 5 + (experts,) * 5,
        check_vma=False,
    )
```

```python
import functools
import math

import jax
import jax.numpy as jnp
from jax import lax
from jax.experimental import pallas as pl
from jax.experimental.pallas import tpu as pltpu
from jax.sharding import PartitionSpec as P

D = 384
HEADS = 12
HEAD_DIM = 32
FF = 1536
EXPERTS = 8
TOP = 2
SEG = 128
SERIES_DEV = 6
STEP = 8
TOK_DEV = 768
CAP = 384
ROW_PAD = 16
MISC = 128
UNITS_ALL = SERIES_DEV * HEADS
QBLOCK = 256
MIB = 1 << 20

eps_norm = 1e-06
beta_one = 0.5
beta_two = 0.5
learn_rate = 0.02
weight_decay = 0.1
eps_adam = 1e-08
average_keep = 0.9
rope_base = 10000.0
neg_fill = -1e30

MESH = pl.DeviceIdType.MESH
F32 = jnp.float32
BF16 = jnp.bfloat16


def adamw_update(weights, grads, first, second, average):
    first_new = beta_one * first + (1.0 - beta_one) * grads
    second_new = beta_two * second + (1.0 - beta_two) * grads * grads
    first_hat = first_new / (1.0 - beta_one**STEP)
    second_hat = second_new / (1.0 - beta_two**STEP)
    weights_new = weights - learn_rate * (
        first_hat / (jnp.sqrt(second_hat) + eps_adam) + weight_decay * weights
    )
    average_new = average_keep * average + (1.0 - average_keep) * weights_new
    return (first_new, second_new, weights_new, average_new)


def dot(left, right, left_dim=1, right_dim=0):
    return lax.dot_general(
        left, right, (((left_dim,), (right_dim,)), ((), ())), preferred_element_type=F32
    )


class Grid:
    def __init__(self, ndp, nex):
        self.ndp, self.nex = ndp, nex
        self.nz = math.gcd(ndp, 4)
        self.ny = ndp // self.nz
        self.nc = math.gcd(nex, 2)
        self.nx = nex // self.nc
        self.ndev = ndp * nex
        self.units = -(-UNITS_ALL // ndp)
        spans = [
            [u // HEADS for u in range(self.units * o, min(self.units * (o + 1), UNITS_ALL))]
            for o in range(ndp)
        ]
        self.owned = [sorted(set(s)) for s in spans]
        self.slots = max(len(s) for s in self.owned)

    def first_series(self, owner):
        return (owner * self.units) // HEADS

    def holds(self, owner, slot):
        begin = owner * self.units
        end = jnp.minimum(begin + self.units, UNITS_ALL)
        return (begin // HEADS + slot) * HEADS < end


def remote(src, dst, send, recv, target):
    return pltpu.make_async_remote_copy(
        src_ref=src,
        dst_ref=dst,
        send_sem=send,
        recv_sem=recv,
        device_id=target,
        device_id_type=MESH,
    )


def greet(peers):
    barrier = pltpu.get_barrier_semaphore()
    for peer in peers:
        pl.semaphore_signal(barrier, inc=1, device_id=peer, device_id_type=MESH)
    pl.semaphore_wait(barrier, len(peers))


def any_spec():
    return pl.BlockSpec(memory_space=pl.ANY)


def far_first(n):
    return sorted(range(1, n), key=lambda d: -min(d, n - d))


def comm_params(number):
    return pltpu.CompilerParams(collective_id=number, has_side_effects=True)


def unpad_matrix(grid):
    shape = (D, grid.ndev * ROW_PAD)
    rows_dev = D // grid.ndev
    row = lax.broadcasted_iota(jnp.int32, shape, 0)
    at = (row // rows_dev) * ROW_PAD + lax.rem(row, rows_dev)
    return (lax.broadcasted_iota(jnp.int32, shape, 1) == at).astype(F32).astype(BF16)


def group_matrix(grid):
    rows_dev = D // grid.ndev
    row = lax.broadcasted_iota(jnp.int32, (D, D), 1)
    owner = row // rows_dev
    at = (lax.rem(owner, grid.nex) * grid.ndp + owner // grid.nex) * rows_dev
    at = at + lax.rem(row, rows_dev)
    return (lax.broadcasted_iota(jnp.int32, (D, D), 0) == at).astype(F32).astype(BF16)


class DenseGather:
    def __init__(self, grid):
        self.grid = grid

    def scratch(self):
        dma = pltpu.SemaphoreType.DMA
        return [dma((self.grid.ndev,)), dma((self.grid.ndev,)), dma]

    def bind(self, shard, out, refs):
        g = self.grid
        self.shard, self.out = shard, out
        self.send, self.recv, self.loc = refs
        dp, ex = lax.axis_index("dp"), lax.axis_index("expert")
        self.z, self.y = dp // g.ny, lax.rem(dp, g.ny)
        self.x, self.c = ex // g.nc, lax.rem(ex, g.nc)
        self.zs = [0] + far_first(g.nz)[::-1]
        self.count = 0
        self.ends = []

    def place(self, dz, dy, dx, dc):
        g = self.grid
        return (
            lax.rem(self.z + dz, g.nz) * g.ny + lax.rem(self.y + dy, g.ny),
            lax.rem(self.x + dx, g.nx) * g.nc + lax.rem(self.c + dc, g.nc),
        )

    def slot(self, dz, dy, dx, dc):
        g = self.grid
        dp, ex = self.place(g.nz - dz, g.ny - dy, g.nx - dx, g.nc - dc)
        return dp * g.nex + ex

    def copy(self, ref, slot, number, target):
        return remote(ref, self.out.at[slot], self.send.at[number], self.recv.at[slot], target)

    def go(self, slot, target):
        ref = self.out.at[slot]
        if self.count < self.own_sends():
            ref = self.shard
        self.copy(ref, slot, self.count, target).start()
        self.count += 1

    def own_sends(self):
        g = self.grid
        return g.nz + g.ny + g.nx + g.nc - 4

    def wait(self, slot):
        self.copy(self.shard, slot, 0, self.place(0, 0, 0, 0)).wait_recv()

    def onward(self, slot, axes):
        g = self.grid
        if "y" in axes:
            for dy in range(1, g.ny):
                self.go(slot, self.place(0, dy, 0, 0))
        if "x" in axes:
            for dx in range(1, g.nx):
                self.go(slot, self.place(0, 0, dx, 0))
        for dc in range(1, g.nc):
            self.go(slot, self.place(0, 0, 0, dc))

    def own(self):
        return pltpu.make_async_copy(self.shard, self.out.at[self.slot(0, 0, 0, 0)], self.loc)

    def start(self):
        own = self.slot(0, 0, 0, 0)
        for dz in far_first(self.grid.nz):
            self.go(own, self.place(dz, 0, 0, 0))
        self.onward(own, "yx")
        self.own().start()

    def pass_z(self):
        for dz in self.zs[1:]:
            slot = self.slot(dz, 0, 0, 0)
            self.wait(slot)
            self.onward(slot, "yx")

    def pass_y(self):
        for dy in range(1, self.grid.ny):
            for dz in self.zs:
                slot = self.slot(dz, dy, 0, 0)
                self.wait(slot)
                self.onward(slot, "x")

    def pass_x(self):
        g = self.grid
        for dx in range(1, g.nx):
            for dy in range(g.ny):
                for dz in self.zs:
                    slot = self.slot(dz, dy, dx, 0)
                    self.wait(slot)
                    self.onward(slot, "")

    def finish(self):
        g = self.grid
        for dc in range(1, g.nc):
            for dx in range(g.nx):
                for dy in range(g.ny):
                    for dz in self.zs:
                        self.wait(self.slot(dz, dy, dx, dc))
        for number in range(g.ndev - 1):
            self.copy(self.shard, 0, number, self.place(0, 0, 0, 0)).wait_send()
        self.own().wait()


class RowGather:
    parts = 3

    def __init__(self, grid):
        self.grid = grid

    def scratch(self):
        g, n = self.grid, self.parts
        dma = pltpu.SemaphoreType.DMA
        return [dma((g.nx + g.nc, n)), dma((g.nex, n)), dma((g.nx, n)), dma]

    def bind(self, src, dst, refs):
        g = self.grid
        self.src, self.dst = src, dst
        self.send, self.recv, self.fsend, self.loc = refs
        self.dp, self.ex = lax.axis_index("dp"), lax.axis_index("expert")
        self.x, self.c = self.ex // g.nc, lax.rem(self.ex, g.nc)
        self.sends = []

    def rows(self, part):
        extent = TOK_DEV // self.parts
        return pl.ds(part * extent, extent)

    def slot_at(self, owner, target):
        return lax.rem(owner - target - 1 + 2 * self.grid.nex, self.grid.nex)

    def go(self, ref, owner, part, sem, target):
        slot = self.slot_at(owner, target)
        copy = remote(
            ref, self.dst.at[slot, self.rows(part)], sem, self.recv.at[slot, part],
            (self.dp, target),
        )
        copy.start()
        self.sends.append(copy)

    def arrived(self, owner, part):
        slot = self.slot_at(owner, self.ex)
        remote(
            self.src.at[self.rows(part)], self.dst.at[slot, self.rows(part)], self.send.at[0, 0],
            self.recv.at[slot, part], (self.dp, self.ex),
        ).wait_recv()

    def beside(self, dc):
        g = self.grid
        return self.x * g.nc + lax.rem(self.c + dc, g.nc)

    def start(self):
        g = self.grid
        for part in range(self.parts):
            for dx in range(1, g.nx):
                target = lax.rem(self.x + dx, g.nx) * g.nc + self.c
                ref = self.src.at[self.rows(part)]
                self.go(ref, self.ex, part, self.send.at[dx - 1, part], target)
        for part in range(self.parts):
            for dc in range(1, g.nc):
                ref = self.src.at[self.rows(part)]
                self.go(ref, self.ex, part, self.send.at[g.nx + dc - 2, part], self.beside(dc))
        self.own = pltpu.make_async_copy(self.src, self.dst.at[g.nex - 1], self.loc)
        self.own.start()

    def pass_on(self, part):
        g = self.grid
        for dx in range(1, g.nx):
            owner = lax.rem(self.x + g.nx - dx, g.nx) * g.nc + self.c
            self.arrived(owner, part)
            for dc in range(1, g.nc):
                ref = self.dst.at[self.slot_at(owner, self.ex), self.rows(part)]
                self.go(ref, owner, part, self.fsend.at[dx - 1, part], self.beside(dc))

    def finish(self):
        g = self.grid
        for part in range(self.parts):
            for dc in range(1, g.nc):
                for dx in range(g.nx):
                    owner = lax.rem(self.x + g.nx - dx, g.nx) * g.nc
                    self.arrived(owner + lax.rem(self.c + g.nc - dc, g.nc), part)
        for copy in self.sends:
            copy.wait_send()
        self.own.wait()


def first_exchange(grid, tokens, shard, cot, ranks):
    ndp, nex = grid.ndp, grid.nex

    def kernel(tok, shd, cot_in, rank_in, tok_out, dense_out, cot_out, rank_out,
               t_send, t_recv, e_send, e_recv, loc, *more_refs):
        dp, ex = lax.axis_index("dp"), lax.axis_index("expert")

        def off(value, by, n):
            return lax.rem(value + by, n)

        peers = [(off(dp, d, ndp), ex) for d in range(1, ndp)]
        peers += [(dp, off(ex, d, nex)) for d in range(1, nex)]
        greet(peers)
        dense = DenseGather(grid)
        dense.bind(shd, dense_out, more_refs[4:])
        dense.start()

        def token_copy(d, slot, src_series, sender, target):
            return remote(
                tok.at[src_series],
                tok_out.at[slot, sender],
                t_send.at[d - 1, slot],
                t_recv.at[d - 1, slot],
                (target, ex),
            )

        for d in far_first(ndp):
            target = off(dp, d, ndp)
            for slot in range(grid.slots):

                @pl.when(grid.holds(target, slot))
                def _():
                    token_copy(d, slot, grid.first_series(target) + slot, dp, target).start()

        rows = RowGather(grid)
        rows.bind(cot_in, cot_out, more_refs[:4])
        rows.start()
        e_sends = []
        for d in range(1, nex):
            target = off(ex, d, nex)
            copy = remote(
                rank_in.at[target], rank_out.at[nex - 1 - d], e_send.at[d - 1], e_recv.at[d - 1],
                (dp, target),
            )
            copy.start()
            e_sends.append(copy)
        copy = pltpu.make_async_copy(rank_in.at[ex], rank_out.at[nex - 1], loc.at[0])
        copy.start()
        e_sends.append(copy)

        for slot in range(grid.slots):

            @pl.when(grid.holds(dp, slot))
            def _():
                copy = pltpu.make_async_copy(
                    tok.at[grid.first_series(dp) + slot], tok_out.at[slot, dp], loc.at[1 + slot]
                )
                copy.start()
                copy.wait()

        dense.pass_z()
        rows.pass_on(0)
        dense.pass_y()
        for part in range(1, rows.parts):
            rows.pass_on(part)
        dense.pass_x()
        dense.finish()
        rows.finish()
        for d in range(1, ndp):
            for slot in range(grid.slots):

                @pl.when(grid.holds(dp, slot))
                def _():
                    token_copy(d, slot, 0, dp, off(dp, d, ndp)).wait_recv()

                @pl.when(grid.holds(off(dp, d, ndp), slot))
                def _():
                    token_copy(d, slot, 0, dp, off(dp, d, ndp)).wait_send()

        for copy in e_sends:
            copy.wait()

    seg, width = tokens.shape[1:]
    dma = pltpu.SemaphoreType.DMA
    return pl.pallas_call(
        kernel,
        out_shape=(
            jax.ShapeDtypeStruct((grid.slots, ndp, seg, width), tokens.dtype),
            jax.ShapeDtypeStruct((grid.ndev,) + shard.shape, shard.dtype),
            jax.ShapeDtypeStruct((nex,) + cot.shape, cot.dtype),
            jax.ShapeDtypeStruct(ranks.shape, ranks.dtype),
        ),
        in_specs=[any_spec()] * 4,
        out_specs=(any_spec(),) * 4,
        scratch_shapes=[
            dma((ndp - 1, grid.slots)),
            dma((ndp - 1, grid.slots)),
            dma((nex - 1,)),
            dma((nex - 1,)),
            dma((1 + grid.slots,)),
        ]
        + RowGather(grid).scratch()
        + DenseGather(grid).scratch(),
        compiler_params=comm_params(0),
        name="first_exchange",
    )(tokens, shard, cot, ranks)


class RowScatter:
    def __init__(self, grid, width):
        self.grid, self.width = grid, width
        self.rows = D // grid.nex
        self.rows_dev = D // grid.ndev

    def scratch_x(self):
        g = self.grid
        dma = pltpu.SemaphoreType.DMA
        blocks = pltpu.VMEM((g.nx, self.rows, self.width), BF16)
        return [blocks, blocks, blocks, dma((2, 2)), dma((g.nx, 2))]

    def scratch_dp(self):
        g = self.grid
        return [
            pltpu.VMEM((g.ndp, ROW_PAD, self.width), BF16),
            pltpu.SemaphoreType.DMA((g.ndp, 2)),
        ]

    def spread_shape(self):
        return (self.grid.ndp * ROW_PAD, self.width)

    def bind(self, spread):
        g = self.grid
        self.spread = spread
        self.dp, self.ex = lax.axis_index("dp"), lax.axis_index("expert")
        self.x, self.c = self.ex // g.nc, lax.rem(self.ex, g.nc)

    def bind_x(self, source, refs):
        self.source = source
        self.got_core, self.by_x, self.got_x, self.sem_core, self.sem_x = refs

    def bind_dp(self, refs):
        self.got_dp, self.sem_dp = refs

    def core_copy(self):
        other = 1 - self.c
        return remote(
            self.source.at[:, other], self.got_core, self.sem_core.at[0, 0],
            self.sem_core.at[0, 1], (self.dp, self.x * 2 + other),
        )

    def x_copy(self, d):
        target = lax.rem(self.x + d, self.grid.nx)
        return remote(
            self.by_x.at[target], self.got_x.at[d], self.sem_x.at[d, 0], self.sem_x.at[d, 1],
            (self.dp, target * self.grid.nc + self.c),
        )

    def dp_copy(self, d):
        target = lax.rem(self.dp + d, self.grid.ndp)
        rows = pl.ds(pl.multiple_of(target * ROW_PAD, ROW_PAD), ROW_PAD)
        return remote(
            self.spread.at[rows], self.got_dp.at[d], self.sem_dp.at[d, 0], self.sem_dp.at[d, 1],
            (target, self.ex),
        )

    def start(self):
        self.core_copy().start()

    def along_x(self):
        g = self.grid
        self.core_copy().wait()
        for n in range(g.nx):
            mine = self.source[n, pl.ds(self.c, 1)][0]
            self.by_x[n] = (mine.astype(F32) + self.got_core[n].astype(F32)).astype(BF16)
        for d in range(1, g.nx):
            self.x_copy(d).start()

    def after_x(self):
        g = self.grid
        for d in range(1, g.nx):
            self.x_copy(d).wait()
        total = self.by_x[pl.ds(self.x, 1)][0].astype(F32)
        for d in range(1, g.nx):
            total += self.got_x[d].astype(F32)
        to = lax.broadcasted_iota(jnp.int32, (g.ndp * ROW_PAD, self.rows), 0)
        of = lax.broadcasted_iota(jnp.int32, (g.ndp * ROW_PAD, self.rows), 1)
        place = (of // self.rows_dev) * ROW_PAD + lax.rem(of, self.rows_dev)
        move = (to == place).astype(F32).astype(BF16)
        self.spread[...] = dot(move, total.astype(BF16)).astype(BF16)

    def along_dp(self):
        for d in far_first(self.grid.ndp):
            self.dp_copy(d).start()

    def finish(self, out):
        g = self.grid
        rows = pl.ds(pl.multiple_of(self.dp * ROW_PAD, ROW_PAD), ROW_PAD)
        total = self.spread[rows].astype(F32)
        for d in range(1, g.ndp):
            self.dp_copy(d).wait()
            total += self.got_dp[d].astype(F32)
        out[...] = total


class ShardScatter:
    def __init__(self, grid, rows, width):
        self.grid, self.rows, self.width = grid, rows, width

    def scratch_y(self):
        g = self.grid
        block = (self.rows, self.width)
        dma = pltpu.SemaphoreType.DMA
        return [
            pltpu.VMEM((g.nz,) + block, BF16),
            pltpu.VMEM((max(g.ny - 1, 1), g.nz) + block, BF16),
            dma((g.ny, g.nz, 2)),
            dma((g.nz,)),
        ]

    def scratch_z(self):
        g = self.grid
        dma = pltpu.SemaphoreType.DMA
        return [pltpu.VMEM((g.nz, self.rows, self.width), BF16), dma((g.nz, 2))]

    def scratch_own(self):
        return [pltpu.VMEM((self.rows, self.width), BF16), pltpu.SemaphoreType.DMA]

    def where(self):
        g = self.grid
        self.dp, self.ex = lax.axis_index("dp"), lax.axis_index("expert")
        self.z, self.y = self.dp // g.ny, lax.rem(self.dp, g.ny)
        self.order = far_first(g.nz) + [0]

    def bind_y(self, source, refs):
        self.where()
        self.source = source
        self.mine, self.got_y, self.sem_y, self.loc = refs
        self.sums = self.mine

    def bind_z(self, refs):
        self.got_z, self.sem_z = refs

    def bind_own(self, sums, refs):
        self.where()
        self.sums = sums
        self.own, self.own_sem = refs

    def place(self, dz, dy):
        g = self.grid
        return lax.rem(self.z + dz, g.nz) * g.ny + lax.rem(self.y + dy, g.ny)

    def block(self, number):
        if len(self.source.shape) == 3:
            return self.source.at[number]
        return self.source.at[pl.ds(pl.multiple_of(number * self.rows, ROW_PAD), self.rows)]

    def y_copy(self, dy, dz):
        return remote(
            self.block(self.place(dz, dy)), self.got_y.at[dy - 1, dz],
            self.sem_y.at[dy, dz, 0], self.sem_y.at[dy, dz, 1], (self.place(0, dy), self.ex),
        )

    def load(self, dz):
        return pltpu.make_async_copy(
            self.block(self.place(dz, 0)), self.mine.at[dz], self.loc.at[dz]
        )

    def start_y(self):
        for dz in self.order:
            for dy in range(1, self.grid.ny):
                self.y_copy(dy, dz).start()
            self.load(dz).start()

    def sum_y(self, then=None):
        g = self.grid
        for dz in self.order:
            self.load(dz).wait()
            for dy in range(1, g.ny):
                self.y_copy(dy, dz).wait()
            if g.ny > 1:
                total = self.mine[dz].astype(F32)
                for dy in range(1, g.ny):
                    total += self.got_y[dy - 1, dz].astype(F32)
                self.mine[dz] = total.astype(BF16)
            if then is not None:
                then(dz)

    def store_y(self, out):
        def store(dz):
            return pltpu.make_async_copy(self.mine.at[dz], out.at[dz], self.loc.at[dz])

        self.sum_y(lambda dz: store(dz).start())
        for dz in self.order:
            store(dz).wait()

    def z_copy(self, dz):
        return remote(
            self.sums.at[dz], self.got_z.at[dz], self.sem_z.at[dz, 0], self.sem_z.at[dz, 1],
            (self.place(dz, 0), self.ex),
        )

    def own_copy(self):
        return pltpu.make_async_copy(self.sums.at[0], self.own, self.own_sem)

    def start_z(self):
        for dz in far_first(self.grid.nz):
            self.z_copy(dz).start()
        if self.sums is not getattr(self, "mine", None):
            self.own_copy().start()

    def finish_z(self, out):
        if self.sums is getattr(self, "mine", None):
            total = self.mine[0].astype(F32)
        else:
            self.own_copy().wait()
            total = self.own[...].astype(F32)
        for dz in range(1, self.grid.nz):
            self.z_copy(dz).wait()
            total += self.got_z[dz].astype(F32)
        out[...] = total.astype(out.dtype)


def route_rows(grid, heads, tokens, table, grad_out, weights):
    nex = grid.nex
    local = EXPERTS // nex
    count = len(OUTS_ROUTE)

    def kernel(heads_ref, tok_ref, table_ref, go_ref, w_ref, dst, gate_dst, *refs):
        outs, bufs = refs[:count], refs[count : 2 * count]
        mixed_buf, probs_buf, lin_ref, gact_ref, early_ref, across_ref, small_ref, gain_ref = bufs
        act_buf, gate_buf, g_send, g_recv, loc, out_sem = refs[2 * count : 2 * count + 6]
        row_refs = refs[2 * count + 6 :]
        dp, ex = lax.axis_index("dp"), lax.axis_index("expert")
        greet([(dp, lax.rem(ex + d, nex)) for d in range(1, nex)])

        def keep(n):
            return pltpu.make_async_copy(bufs[n], outs[n], out_sem.at[n])

        unpad, group = unpad_matrix(grid), group_matrix(grid)
        small_ref[...] = dot(unpad, table_ref[:, 3 * D :]).astype(BF16)
        gain_ref[...] = dot(table_ref[:, 3 * D : 3 * D + MISC], unpad, 0, 1)[
            EXPERTS : EXPERTS + 8
        ]
        for s in range(SERIES_DEV):
            attn = heads_ref[s * HEADS : (s + 1) * HEADS].reshape(D, SEG)
            rows = slice(s * SEG, (s + 1) * SEG)
            mixed_buf[rows] = tok_ref[s].astype(F32) + dot(attn, small_ref[:, MISC:], 0, 0)
        mixed = mixed_buf[...]
        scale = lax.rsqrt(jnp.mean(mixed * mixed, axis=-1, keepdims=True) + eps_norm)
        act = (mixed * scale * gain_ref[2:3]).astype(BF16)
        act_buf[...] = act
        gather = RowGather(grid)
        gather.bind(act_buf, dst, row_refs)
        gather.start()
        misc = dot(act, small_ref[:, :MISC])
        lane = lax.broadcasted_iota(jnp.int32, misc.shape, 1)
        logits = jnp.where(lane < EXPERTS, misc, neg_fill)
        powers = jnp.exp(logits - jnp.max(logits, axis=1, keepdims=True))
        probs = powers / jnp.sum(powers, axis=1, keepdims=True)
        shared_gate = 0.5 * jnp.tanh(0.5 * misc[:, EXPERTS : EXPERTS + 1]) + 0.5
        probs_buf[...] = jnp.where(lane == EXPERTS, shared_gate, probs)
        flipped = probs.T
        for n in range(nex):
            gate_buf[n] = flipped[n * local : (n + 1) * local]
        gate_copies = []
        for d in range(1, nex):
            target = lax.rem(ex + d, nex)
            copy = remote(
                gate_buf.at[target], gate_dst.at[nex - 1 - d], g_send.at[d - 1], g_recv.at[d - 1],
                (dp, target),
            )
            copy.start()
            gate_copies.append(copy)
        copy = pltpu.make_async_copy(gate_buf.at[ex], gate_dst.at[nex - 1], loc)
        copy.start()
        gate_copies.append(copy)
        for n in (0, 1, 6, 7):
            keep(n).start()

        grad_lin = (go_ref[...].astype(F32) * shared_gate).astype(BF16)
        across_ref[...] = dot(group, act, 1, 1).astype(BF16)
        keep(5).start()
        grad_across = dot(group, grad_lin, 1, 1).astype(BF16)
        wide = 2 * D
        for n in range(FF // wide):
            gate_w, up_w, down_w = (
                dot(unpad, w_ref[:, m * FF + n * wide : m * FF + (n + 1) * wide]).astype(BF16)
                for m in range(3)
            )
            gate_lin, up_lin = dot(act, gate_w), dot(act, up_w)
            sig = 0.5 * jnp.tanh(0.5 * gate_lin) + 0.5
            silu = gate_lin * sig
            hidden = (silu * up_lin).astype(BF16)
            grad_hidden = dot(grad_lin, down_w)
            grad_gate = (grad_hidden * up_lin * (sig + silu * (1.0 - sig))).astype(BF16)
            grad_up = (grad_hidden * silu).astype(BF16)
            lin = dot(hidden, down_w, 1, 1)
            gact = dot(grad_gate, gate_w, 1, 1) + dot(grad_up, up_w, 1, 1)
            if n:
                lin_ref[...] += lin
                gact_ref[...] += gact
            else:
                lin_ref[...] = lin
                gact_ref[...] = gact
            if n == 0:
                gather.pass_on(0)
            else:
                keep(2).start()
                keep(3).start()
            for m, (left, right) in enumerate(
                ((across_ref[...], grad_gate), (across_ref[...], grad_up), (grad_across, hidden))
            ):
                lanes = slice(m * FF + n * wide, m * FF + (n + 1) * wide)
                early_ref[:, lanes] = dot(left, right).astype(BF16)
            if n == 0:
                gather.pass_on(1)
        keep(4).start()
        for part in range(2, gather.parts):
            gather.pass_on(part)
        gather.finish()
        for copy in gate_copies:
            copy.wait()
        for n in range(count):
            keep(n).wait()

    dma = pltpu.SemaphoreType.DMA
    vmem = pl.BlockSpec(memory_space=pltpu.VMEM)
    hbm = pl.BlockSpec(memory_space=pltpu.HBM)
    inputs = (heads, tokens, table, grad_out, weights)
    return pl.pallas_call(
        kernel,
        out_shape=(
            jax.ShapeDtypeStruct((nex, TOK_DEV, D), BF16),
            jax.ShapeDtypeStruct((nex, local, TOK_DEV), F32),
        )
        + tuple(jax.ShapeDtypeStruct(shape, kind) for shape, kind in OUTS_ROUTE),
        in_specs=[vmem] * len(inputs),
        out_specs=(hbm,) * (2 + count),
        scratch_shapes=[pltpu.VMEM(shape, kind) for shape, kind in OUTS_ROUTE]
        + [
            pltpu.VMEM((TOK_DEV, D), BF16),
            pltpu.VMEM((nex, local, TOK_DEV), F32),
            dma((nex - 1,)),
            dma((nex - 1,)),
            dma,
            dma((count,)),
        ]
        + RowGather(grid).scratch(),
        compiler_params=pltpu.CompilerParams(
            collective_id=4, has_side_effects=True, vmem_limit_bytes=60 * MIB
        ),
        name="route_rows",
    )(*inputs)


OUTS_ROUTE = (
    ((TOK_DEV, D), F32),
    ((TOK_DEV, MISC), F32),
    ((TOK_DEV, D), F32),
    ((TOK_DEV, D), F32),
    ((D, 3 * FF), BF16),
    ((D, TOK_DEV), BF16),
    ((D, MISC + D), BF16),
    ((8, D), F32),
)


def turn(values, cosine, sine):
    first, second = values[: HEAD_DIM // 2], values[HEAD_DIM // 2 :]
    return jnp.concatenate(
        [first * cosine - second * sine, second * cosine + first * sine], axis=0
    )


def allowed_mask(extent, block, length):
    keys = lax.broadcasted_iota(jnp.int32, (extent, QBLOCK), 0)
    queries = lax.broadcasted_iota(jnp.int32, (extent, QBLOCK), 1) + block * QBLOCK
    return (keys <= queries) & (keys < length)


def attend(grid, lengths, tok, table, cosine, sine, shard):
    units, length, ndp, nex = grid.units, tok.shape[1], grid.ndp, grid.nex
    blocks = length // QBLOCK
    chunk = 1
    ends = sorted(set(range(chunk - 1, units, chunk)) | {units - 1})

    def kernel(len_ref, tok_ref, table_ref, cos_ref, sin_ref, shard_ref,
               heads_ref, dense_ref, act_out, q_out, k_out, v_out, lse_out, w_out,
               act_ref, q_ref, k_ref, v_ref, lse_ref, w_ref, k_sem,
               buf, h_send, h_recv, h_loc, *dense_refs):
        i = pl.program_id(0)
        dp, ex = lax.axis_index("dp"), lax.axis_index("expert")
        unit = jnp.minimum(dp * units + i, UNITS_ALL - 1)
        head = lax.rem(unit, HEADS)
        slot = jnp.minimum(unit // HEADS - grid.first_series(dp), grid.slots - 1)
        slot = jnp.maximum(slot, 0)
        dense = DenseGather(grid)
        dense.bind(shard_ref, dense_ref, dense_refs)

        def keep():
            pairs = (
                (act_ref, act_out), (q_ref, q_out), (k_ref, k_out), (v_ref, v_out),
                (lse_ref, lse_out), (w_ref, w_out),
            )
            return [
                pltpu.make_async_copy(src, dst, k_sem.at[n]) for n, (src, dst) in enumerate(pairs)
            ]

        def heads_copy(d, n):
            begin = ends[n - 1] + 1 if n else 0
            count = ends[n] + 1 - begin
            target = lax.rem(dp + d, ndp)
            lanes = pl.ds(pl.multiple_of(target * SEG, SEG), SEG)
            return remote(
                buf.at[pl.ds(begin, count), :, lanes],
                heads_ref.at[dp, pl.ds(begin, count)],
                h_send.at[d - 1, n],
                h_recv.at[d - 1, n],
                (target, ex),
            )

        @pl.when(i == 0)
        def _():
            greet(
                [(lax.rem(dp + d, ndp), ex) for d in range(1, ndp)]
                + [(dp, lax.rem(ex + d, nex)) for d in range(1, nex)]
            )
            dense.start()
            w_ref[...] = dot(table_ref[:, : 3 * D + MISC], unpad_matrix(grid), 0, 1).astype(BF16)

        @pl.when((i == 0) | (head == 0))
        def _():
            residual = tok_ref[slot].astype(F32)
            scale = lax.rsqrt(jnp.mean(residual * residual, axis=-1, keepdims=True) + eps_norm)
            gain = w_ref[3 * D : 3 * D + ROW_PAD].astype(F32)[EXPERTS + 1 : EXPERTS + 2]
            act_ref[slot] = (residual * scale * gain).astype(BF16)

        cos, sin = cos_ref[...], sin_ref[...]
        w_rows = [
            w_ref[pl.ds(pl.multiple_of(n * D + head * HEAD_DIM, HEAD_DIM), HEAD_DIM)]
            for n in range(3)
        ]
        qkv = dot(jnp.concatenate(w_rows, axis=0), act_ref[slot], 1, 1)
        query = turn(qkv[:HEAD_DIM], cos, sin).astype(BF16)
        key_wide = turn(qkv[HEAD_DIM : 2 * HEAD_DIM], cos, sin)
        value = qkv[2 * HEAD_DIM :].astype(BF16)
        key_rows = key_wide.T.astype(BF16)
        q_ref[i], k_ref[i], v_ref[i] = query, key_wide.astype(BF16), value
        live = len_ref[unit // HEADS]
        for block in range(blocks):
            extent = QBLOCK * (block + 1)
            lanes = slice(QBLOCK * block, extent)
            scores = dot(key_rows[:extent], query[:, lanes]) * HEAD_DIM ** (-0.5)
            scores = jnp.where(allowed_mask(extent, block, live), scores, neg_fill)
            top = jnp.max(scores, axis=0, keepdims=True)
            probs = jnp.exp(scores - top)
            total = jnp.sum(probs, axis=0, keepdims=True)
            result = dot(value[:, :extent], probs.astype(BF16))
            buf[i, :, lanes] = (result * (1.0 / total)).astype(BF16)
            lse_ref[i, :, lanes] = top + jnp.log(total)

        for n, end in enumerate(ends):

            @pl.when(i == end)
            def _():
                for d in far_first(ndp):
                    heads_copy(d, n).start()

        pl.when(i == min(3, units - 1))(dense.pass_z)
        pl.when(i == min(5, units - 1))(dense.pass_y)

        @pl.when(i == units - 1)
        def _():
            mine = pltpu.make_async_copy(
                buf.at[:, :, pl.ds(pl.multiple_of(dp * SEG, SEG), SEG)], heads_ref.at[dp], h_loc
            )
            mine.start()
            for copy in keep():
                copy.start()
            dense.pass_x()
            dense.finish()
            for n in range(len(ends)):
                for d in range(1, ndp):
                    heads_copy(d, n).wait()
            mine.wait()
            for copy in keep():
                copy.wait()

    def whole(array):
        return pl.BlockSpec(
            array.shape, lambda i: (0,) * array.ndim, pipeline_mode=pl.Buffered(1)
        )

    feature = jax.ShapeDtypeStruct((units, HEAD_DIM, length), BF16)
    inputs = (tok, table, cosine, sine)
    dma = pltpu.SemaphoreType.DMA
    return pl.pallas_call(
        kernel,
        grid=(units,),
        out_shape=(
            jax.ShapeDtypeStruct((ndp, units, HEAD_DIM, SEG), BF16),
            jax.ShapeDtypeStruct((grid.ndev,) + shard.shape, BF16),
            jax.ShapeDtypeStruct((grid.slots, length, D), BF16),
            feature,
            feature,
            feature,
            jax.ShapeDtypeStruct((units, 1, length), F32),
            jax.ShapeDtypeStruct((3 * D + MISC, D), BF16),
        ),
        in_specs=[pl.BlockSpec(memory_space=pltpu.SMEM)]
        + [whole(v) for v in inputs]
        + [any_spec()],
        out_specs=(
            any_spec(),
            any_spec(),
        )
        + (pl.BlockSpec(memory_space=pltpu.HBM),) * 6,
        scratch_shapes=[
            pltpu.VMEM((grid.slots, length, D), BF16),
            pltpu.VMEM(feature.shape, BF16),
            pltpu.VMEM(feature.shape, BF16),
            pltpu.VMEM(feature.shape, BF16),
            pltpu.VMEM((units, 1, length), F32),
            pltpu.VMEM((3 * D + MISC, D), BF16),
            dma((6,)),
            pltpu.VMEM((units, HEAD_DIM, length), BF16),
            dma((ndp - 1, len(ends))),
            dma((ndp - 1, len(ends))),
            dma,
        ]
        + DenseGather(grid).scratch(),
        compiler_params=pltpu.CompilerParams(
            collective_id=1, has_side_effects=True, vmem_limit_bytes=60 * MIB
        ),
        cost_estimate=pl.CostEstimate(
            flops=units * length * length * HEAD_DIM * 2 * 8,
            bytes_accessed=8 * MIB,
            transcendentals=units * length * length,
        ),
        name="attend",
    )(lengths, *inputs, shard)


def attend_back(grid, lengths, tok, act, weights, query, key, value, lse, grad_heads, cosine, sine,
                early, routed, zs, tokens, mixed, grad_mixed, probs, lin, gains, shared):
    units, length, ndp, nex = grid.units, act.shape[1], grid.ndp, grid.nex
    blocks = length // QBLOCK
    scale = HEAD_DIM ** (-0.5)
    early_width, late_width = early.shape[1], 3 * D + MISC
    early_sum, late_sum = RowScatter(grid, early_width), RowScatter(grid, late_width)
    early = early.reshape(grid.nx, grid.nc, early_sum.rows, early_width)
    steps = [min(n, units - 1) for n in (0, 3)]
    works_z = [ShardScatter(grid, *v.shape[1:]) for v in zs]
    many = len(zs)

    def kernel(*refs):
        refs = list(refs)
        z_refs, z_outs = refs[20 : 20 + many], refs[23 + many : 23 + 2 * many]
        del refs[23 + many : 23 + 2 * many], refs[20 : 20 + many]
        (len_ref, tok_ref, act_ref, w_ref, q_ref, k_ref, v_ref, lse_ref, do_ref, cos_ref, sin_ref,
         early_ref, tokens_ref, mixed_ref, grad_mixed_ref, probs_ref, lin_ref, gains_ref, shared_ref,
         routed_ref,
         output_ref, grad_tokens_ref, table_ref,
         rows_out, early_out, late_out, routed_out,
         acc, back, dq, dk, dv, grads, gain, late_ref, b_send, b_recv, b_loc,
         early_spread, late_spread, r_send, r_recv) = refs[:42]
        at = 42
        for work, source, spread in (
            (early_sum, early_ref, early_spread),
            (late_sum, late_ref, late_spread),
        ):
            work.bind(spread)
            work.bind_x(source, refs[at : at + 5])
            work.bind_dp(refs[at + 5 : at + 7])
            at += 7
        for work, ref in zip(works_z, z_refs):
            work.bind_own(ref, refs[at : at + 2])
            work.bind_z(refs[at + 2 : at + 4])
            at += 4

        def routed_copy(step):
            return remote(
                routed_ref.at[step], routed_out.at[step], r_send.at[step], r_recv.at[step],
                (dp, lax.rem(ex + 1 + step, nex)),
            )

        i = pl.program_id(0)
        dp, ex = lax.axis_index("dp"), lax.axis_index("expert")
        unit = dp * units + i
        working = unit < UNITS_ALL
        series, head = unit // HEADS, lax.rem(unit, HEADS)
        slot = jnp.minimum(series - grid.first_series(dp), grid.slots - 1)

        def back_copy(d, which):
            target = lax.rem(dp + d, ndp)
            return remote(
                back.at[which, pl.ds(pl.multiple_of(target * SEG, SEG), SEG)],
                rows_out.at[dp, which],
                b_send.at[d - 1, which],
                b_recv.at[d - 1, which],
                (target, ex),
            )

        def back_local(which):
            return pltpu.make_async_copy(
                back.at[which, pl.ds(pl.multiple_of(dp * SEG, SEG), SEG)],
                rows_out.at[dp, which],
                b_loc.at[which],
            )

        @pl.when(i == 0)
        def _():
            greet(
                [(lax.rem(dp + d, ndp), ex) for d in range(1, ndp)]
                + [(dp, lax.rem(ex + d, nex)) for d in range(1, nex)]
            )
            for work in works_z:
                work.start_z()
            early_sum.start()
            grads[...] = jnp.zeros_like(grads)
            gain[...] = jnp.zeros_like(gain)

        @pl.when((i == 0) | (head == 0))
        def _():
            acc[...] = jnp.zeros_like(acc)

        @pl.when(working)
        def _():
            live = len_ref[series]
            query, key, value, grad = q_ref[i], k_ref[i], v_ref[i], do_ref[i]
            key_rows = key.astype(F32).T.astype(BF16)
            value_rows = value.astype(F32).T.astype(BF16)
            dk[...] = jnp.zeros_like(dk)
            dv[...] = jnp.zeros_like(dv)
            for block in range(blocks):
                extent = QBLOCK * (block + 1)
                lanes = slice(QBLOCK * block, extent)
                scores = dot(key_rows[:extent], query[:, lanes]) * scale
                scores = jnp.where(allowed_mask(extent, block, live), scores, neg_fill)
                probs = jnp.exp(scores - lse_ref[i, :, lanes])
                grad_probs = dot(value_rows[:extent], grad[:, lanes])
                delta = jnp.sum(probs * grad_probs, axis=0, keepdims=True)
                grad_scores = (probs * (grad_probs - delta)).astype(BF16)
                probs_low = probs.astype(BF16)
                dq[:, lanes] = dot(key[:, :extent], grad_scores)
                dk[:, :extent] += dot(query[:, lanes], grad_scores, 1, 1)
                dv[:, :extent] += dot(grad[:, lanes], probs_low, 1, 1)
            cos, sin = cos_ref[...], -sin_ref[...]
            stacked = jnp.concatenate(
                [
                    turn(dq[...] * scale, cos, sin),
                    turn(dk[...] * scale, cos, sin),
                    dv[...],
                ],
                axis=0,
            ).astype(BF16)
            weight_grads = dot(stacked, act_ref[slot]).astype(BF16)
            w_rows = []
            for n in range(3):
                at = pl.multiple_of(n * D + head * HEAD_DIM, HEAD_DIM)
                part = slice(n * HEAD_DIM, (n + 1) * HEAD_DIM)
                grads[pl.ds(at, HEAD_DIM)] = weight_grads[part]
                w_rows.append(w_ref[pl.ds(at, HEAD_DIM)])
            acc[...] += dot(stacked, jnp.concatenate(w_rows, axis=0), 0, 0)

        @pl.when(working & ((head == HEADS - 1) | (i == units - 1)))
        def _():
            share = acc[...]
            residual = tok_ref[slot].astype(F32)
            normed = residual * lax.rsqrt(
                jnp.mean(residual * residual, axis=-1, keepdims=True) + eps_norm
            )
            gain[...] += jnp.sum(share * normed, axis=0, keepdims=True)
            back[slot] = share.astype(BF16)
            for d in far_first(ndp):
                back_copy(d, slot).start()
            back_local(slot).start()

        @pl.when(i == steps[0])
        def _():
            early_sum.along_x()
            for step in range(nex - 1):
                routed_copy(step).start()

        @pl.when(i == steps[1])
        def _():
            early_sum.after_x()
            early_sum.along_dp()

        @pl.when(i == units - 1)
        def _():
            grads[3 * D :] = jnp.broadcast_to(gain[...], (ROW_PAD, D)).astype(BF16)
            late = dot(group_matrix(grid), grads[...], 1, 1).astype(BF16)
            late = late.reshape(late_ref.shape[:3] + (late.shape[1],))
            late_ref[:, :, :, : late.shape[3]] = late
            late_ref[:, :, :, late.shape[3] :] = jnp.zeros(
                late_ref.shape[:3] + (late_width - late.shape[3],), BF16
            )
            late_sum.start()
            early_sum.finish(early_out)
            late_sum.along_x()
            for step in range(nex - 1):
                routed_copy(step).wait()
            total = routed_ref[nex - 1].astype(F32)
            for step in range(nex - 1):
                total += routed_out[step].astype(F32)
            shared_gate = probs_ref[:, EXPERTS : EXPERTS + 1]
            output_ref[...] = (mixed_ref[...] + total + shared_gate * lin_ref[...]).astype(BF16)
            late_sum.after_x()
            late_sum.along_dp()
            for which in range(grid.slots):
                for d in range(1, ndp):

                    @pl.when(grid.holds(lax.rem(dp + ndp - d, ndp), which))
                    def _():
                        back_copy(d, which).wait_recv()

                @pl.when(grid.holds(dp, which))
                def _():
                    for d in range(1, ndp):
                        back_copy(d, which).wait_send()
                    back_local(which).wait()

            for n in range(SERIES_DEV):
                rows = slice(n * SEG, (n + 1) * SEG)
                grad_act = sum(
                    rows_out[owner, owned.index(n)].astype(F32)
                    for owner, owned in enumerate(grid.owned)
                    if n in owned
                )
                residual = tokens_ref[n].astype(F32)
                scale_one = lax.rsqrt(
                    jnp.mean(residual * residual, axis=-1, keepdims=True) + eps_norm
                )
                normed = residual * scale_one
                weighted = grad_act * gains_ref[1:2]
                inner = jnp.mean(weighted * normed, axis=-1, keepdims=True)
                grad_tokens_ref[rows] = grad_mixed_ref[rows] + scale_one * (
                    weighted - normed * inner
                )
            late_sum.finish(late_out)
            late, mid = late_out[...], early_out[...]
            misc = mid[:, D:]
            lane = lax.broadcasted_iota(jnp.int32, misc.shape, 1)
            wide = jnp.concatenate([shared_ref[...], jnp.zeros_like(misc)], axis=1)
            wide = pltpu.roll(wide, EXPERTS, 1)
            table_ref[:, : 3 * D] = late[:, : 3 * D]
            table_ref[:, 3 * D : 4 * D] = mid[:, :D]
            table_ref[:, 4 * D : 4 * D + MISC] = wide[:, :MISC] + jnp.where(
                lane < EXPERTS, misc, 0.0
            )
            table_ref[:, 4 * D + MISC : 4 * D + 3 * FF] = wide[:, MISC : 3 * FF]
            ends = jnp.where(lane == EXPERTS + 1, late[:, 3 * D :], misc)
            ends = jnp.where((lane >= EXPERTS) & (lane < EXPERTS + 3), ends, 0.0)
            table_ref[:, 4 * D + 3 * FF :] = wide[:, 3 * FF :] + ends
            for work, out in zip(works_z, z_outs):
                work.finish_z(out)

    def whole(array):
        return pl.BlockSpec(
            array.shape, lambda i: (0,) * array.ndim, pipeline_mode=pl.Buffered(1)
        )

    def whole_out(shape):
        return pl.BlockSpec(shape, lambda i: (0,) * len(shape))

    dma = pltpu.SemaphoreType.DMA
    inputs = (tok, act, weights, query, key, value, lse, grad_heads, cosine, sine, early, tokens, mixed,
              grad_mixed, probs, lin, gains, shared, routed)
    table_shape = (ROW_PAD, 4 * D + 3 * FF + MISC)
    return pl.pallas_call(
        kernel,
        grid=(units,),
        out_shape=(
            jax.ShapeDtypeStruct((TOK_DEV, D), BF16),
            jax.ShapeDtypeStruct((TOK_DEV, D), F32),
            jax.ShapeDtypeStruct(table_shape, F32),
        )
        + tuple(jax.ShapeDtypeStruct((work.rows, work.width), BF16) for work in works_z),
        in_specs=[pl.BlockSpec(memory_space=pltpu.SMEM)]
        + [whole(v) for v in inputs]
        + [any_spec()] * many,
        out_specs=(
            whole_out((TOK_DEV, D)),
            whole_out((TOK_DEV, D)),
            whole_out(table_shape),
        )
        + tuple(whole_out((work.rows, work.width)) for work in works_z),
        scratch_shapes=[
            pltpu.VMEM((ndp, grid.slots, SEG, D), BF16),
            pltpu.VMEM((ROW_PAD, early_width), F32),
            pltpu.VMEM((ROW_PAD, late_width), F32),
            pltpu.VMEM((nex - 1,) + routed.shape[1:], BF16),
            pltpu.VMEM((length, D), F32),
            pltpu.VMEM((grid.slots, length, D), BF16),
            pltpu.VMEM((HEAD_DIM, length), F32),
            pltpu.VMEM((HEAD_DIM, length), F32),
            pltpu.VMEM((HEAD_DIM, length), F32),
            pltpu.VMEM((3 * D + ROW_PAD, D), BF16),
            pltpu.VMEM((1, D), F32),
            pltpu.VMEM((grid.nx, grid.nc, late_sum.rows, late_width), BF16),
            dma((ndp - 1, grid.slots)),
            dma((ndp - 1, grid.slots)),
            dma((grid.slots,)),
            pltpu.VMEM(early_sum.spread_shape(), BF16),
            pltpu.VMEM(late_sum.spread_shape(), BF16),
            dma((nex - 1,)),
            dma((nex - 1,)),
        ]
        + early_sum.scratch_x()
        + early_sum.scratch_dp()
        + late_sum.scratch_x()
        + late_sum.scratch_dp()
        + sum((work.scratch_own() + work.scratch_z() for work in works_z), []),
        compiler_params=pltpu.CompilerParams(
            collective_id=3, has_side_effects=True, vmem_limit_bytes=60 * MIB
        ),
        cost_estimate=pl.CostEstimate(
            flops=units * length * length * HEAD_DIM * 2 * 20,
            bytes_accessed=12 * MIB,
            transcendentals=units * length * length,
        ),
        name="attend_back",
    )(lengths, *inputs, *zs)


def experts_step(grid, number, weights, act_all, cot_all, ranks, gates, before, early, ys, zs):
    nex, nc, ndp = grid.nex, grid.nc, grid.ndp
    rows = act_all.shape[1]
    local = EXPERTS // nex
    parts, wide = FF // D, FF // 2
    first, last = number == 0, number == local - 1
    batch = math.gcd(nex, 4)
    flushes = nex // batch
    steps = 2 * nex
    shard_rows = 3 * D // ndp
    inline = shard_rows % ROW_PAD == 0
    scatter = RowScatter(grid, 3 * FF) if first or last else None
    early_work = ShardScatter(grid, ROW_PAD, 3 * FF) if last else None
    works_y = [ShardScatter(grid, *v.shape[1:]) for v in ys]
    works_z = [ShardScatter(grid, *v.shape[1:]) for v in zs]
    work_own = ShardScatter(grid, shard_rows, wide) if inline else None
    if first:
        early = early.reshape(grid.nx, nc, scatter.rows, 3 * FF)

    def kernel(*refs):
        refs = list(refs)

        def take(count):
            taken = refs[:count]
            del refs[:count]
            return taken

        w_ref, act_ref, cot_ref, rank_ref, gate_ref = take(5)
        prev = take(3) if before is not None else None
        early_ref = take(1)[0] if scatter is not None else None
        y_refs, z_refs = take(len(ys)), take(len(zs))
        gin_ref, ggate_ref, routed_ref = take(3)
        early_out = take(1)[0] if scatter is not None else None
        own_outs = take(2)
        sum_outs = take(len(ys) + len(zs))
        xt_ref, dyt_ref, dg_ref, du_ref, hid_ref, down_ref = take(6)
        taken_ref, rows_ref, result_ref, back_ref, grad_ref, own_sem = take(6)
        acc_ref = take(1)[0] if flushes > 1 else None
        if last:
            gin_buf, ggate_buf, send, recv, loc = take(5)
        if first:
            scatter.bind_x(early_ref, take(len(scatter.scratch_x())))
        if scatter is not None:
            spread_ref = early_out if not last else take(1)[0] if first else early_ref
            scatter.bind(spread_ref)
        if last:
            early_work.bind_y(spread_ref, take(4))
            early_work.bind_z(take(2))
        for work, ref in zip(works_y, y_refs):
            work.bind_y(ref, take(4))
            work.bind_z(take(2))
        for work, ref in zip(works_z, z_refs):
            work.bind_own(ref, take(2))
            work.bind_z(take(2))
        if inline:
            work_own.bind_y(grad_ref.at[0], take(4))
        t = pl.program_id(0)
        half, part = lax.rem(t // batch, 2), lax.rem(t, batch)
        s = (t // (2 * batch)) * batch + part
        dp, ex = lax.axis_index("dp"), lax.axis_index("expert")

        def copies(step):
            target = lax.rem(ex + 1 + step, nex)
            pairs = (
                (gin_buf.at[step], gin_ref.at[step]),
                (ggate_buf.at[step], ggate_ref.at[ex]),
            )
            return [
                remote(src, dst, send.at[step, n], recv.at[step, n], (dp, target))
                for n, (src, dst) in enumerate(pairs)
            ]

        @pl.when(t == 0)
        def _():
            greet(
                [(dp, lax.rem(ex + d, nex)) for d in range(1, nex)]
                + [(lax.rem(dp + d, ndp), ex) for d in range(1, ndp)]
            )
            for work in works_y:
                work.start_y()
            for work in works_z:
                work.start_z()
            if first:
                scatter.start()
            elif last:
                early_work.start_y()
            for n in range(parts):
                lanes = slice(n * D, (n + 1) * D)
                down_ref[lanes] = w_ref[2 * D : 3 * D, lanes]

        rank = rank_ref[0, number : number + 1, :]
        slot_down = lax.broadcasted_iota(jnp.int32, (CAP, rows), 0).astype(F32)
        pick = slot_down == rank
        gate_row = gate_ref[0, number : number + 1, :]
        gate = jnp.sum(jnp.where(pick, gate_row, 0.0), axis=1, keepdims=True)
        block = pl.ds(pl.multiple_of(part * CAP, CAP), CAP)

        @pl.when(half == 0)
        def _():
            pick_low = pick.astype(F32).astype(BF16)
            picked = dot(pick_low, jnp.concatenate([act_ref[0], cot_ref[0]], axis=1))
            taken_ref[part] = picked[:, :D].astype(BF16)
            rows_ref[part] = picked[:, D:].astype(BF16)
            xt_ref[:, block] = picked[:, :D].T.astype(BF16)
            dyt_ref[:, block] = (gate * picked[:, D:]).T.astype(BF16)

        taken, grad_rows = taken_ref[part], rows_ref[part].astype(F32)
        grad_result = (gate * grad_rows).astype(BF16)
        lanes = pl.ds(pl.multiple_of(half * wide, wide), wide)
        w_gate, w_up, w_down = w_ref[0:D, lanes], w_ref[D : 2 * D, lanes], down_ref[lanes]
        gate_lin = dot(taken, w_gate)
        up_lin = dot(taken, w_up)
        sig = 0.5 * jnp.tanh(0.5 * gate_lin) + 0.5
        silu = gate_lin * sig
        hidden = (silu * up_lin).astype(BF16)
        result = dot(hidden, w_down)
        grad_hidden = dot(grad_result, w_down, 1, 1)
        grad_gate = (grad_hidden * up_lin * (sig + silu * (1.0 - sig))).astype(BF16)
        grad_up = (grad_hidden * silu).astype(BF16)
        hid_ref[block], dg_ref[block], du_ref[block] = hidden, grad_gate, grad_up
        grad_taken = dot(grad_gate, w_gate, 1, 1) + dot(grad_up, w_up, 1, 1)

        @pl.when(half == 0)
        def _():
            result_ref[part], back_ref[part] = result, grad_taken

        @pl.when(half == 1)
        def _():
            out = (result_ref[part] + result).astype(BF16).astype(F32)
            grad_gate_slot = jnp.sum(grad_rows * out, axis=1, keepdims=True)
            grad_gate_row = jnp.sum(jnp.where(pick, grad_gate_slot, 0.0), axis=0, keepdims=True)
            rank_column = jnp.broadcast_to(rank, (8, rows)).T[:, :1]
            slot_across = lax.broadcasted_iota(jnp.int32, (rows, CAP), 1).astype(F32)
            spread = (slot_across == rank_column).astype(F32).astype(BF16)
            both = jnp.concatenate([gate * out, back_ref[part] + grad_taken], axis=1)
            both = dot(spread, both.astype(BF16))
            routed, grad_in = both[:, :D], both[:, D:]
            if prev is not None:
                grad_in += prev[0][0]
                routed += prev[2][0]
            if last:
                routed_ref[0] = routed.astype(BF16)
                gin_buf[s] = grad_in.astype(BF16)
                if prev is not None:
                    ggate_buf[s, 0:number] = prev[1][0]
                ggate_buf[s, number : number + 1] = grad_gate_row
            else:
                routed_ref[0] = routed
                gin_ref[0] = grad_in
                if prev is not None:
                    ggate_ref[0, 0:number] = prev[1][0]
                ggate_ref[0, number : number + 1] = grad_gate_row

        if last:

            @pl.when((half == 1) & (s < nex - 1))
            def _():
                for copy in copies(s):
                    copy.start()

        if first:

            @pl.when(t == 1)
            def _():
                scatter.along_x()

            @pl.when(t == nex + 2)
            def _():
                scatter.after_x()
                if last:
                    early_work.start_y()

        if last:

            @pl.when(t == (steps - 1 if first else nex + 1))
            def _():
                early_work.sum_y()
                early_work.start_z()

        @pl.when(t == nex)
        def _():
            for work in works_y:
                work.sum_y()
                work.start_z()

        def weight_grads(flush, which):
            def put(at, lanes, value):
                if flush:
                    value += acc_ref[which, at : at + D, lanes]
                if flush < flushes - 1:
                    acc_ref[which, at : at + D, lanes] = value
                else:
                    grad_ref[which, at : at + D, lanes] = value.astype(BF16)

            every = slice(0, wide)
            put(0, every, dot(xt_ref[...], dg_ref[...]))
            put(D, every, dot(xt_ref[...], du_ref[...]))
            down = dot(dyt_ref[...], hid_ref[...])
            for n in range(0, wide, D):
                put(2 * D, slice(n, n + D), down[:, n : n + D].T)

        def keep(which):
            return pltpu.make_async_copy(grad_ref.at[which], own_outs[which], own_sem.at[which])

        for flush in range(flushes):
            for which in range(2):
                end = (2 * flush + which + 1) * batch - 1
                pl.when(t == end)(functools.partial(weight_grads, flush, which))

        @pl.when(t == steps - batch - 1)
        def _():
            if inline:
                work_own.start_y()
            else:
                keep(0).start()

        @pl.when(t == steps - 1)
        def _():
            keep(1).start()
            own = []
            if last:
                own = [
                    pltpu.make_async_copy(src, dst, loc.at[n])
                    for n, (src, dst) in enumerate(
                        (
                            (gin_buf.at[nex - 1], gin_ref.at[nex - 1]),
                            (ggate_buf.at[nex - 1], ggate_ref.at[ex]),
                        )
                    )
                ]
                for copy in own:
                    copy.start()
            if inline:
                work_own.store_y(own_outs[0])
            else:
                keep(0).wait()
            for work, out in zip(works_y + works_z, sum_outs):
                work.finish_z(out)
            if last:
                early_work.finish_z(early_out)
                for step in range(nex - 1):
                    for copy in copies(step):
                        copy.wait()
                for copy in own:
                    copy.wait()
            keep(1).wait()

    def source(t):
        return (t // (2 * batch)) * batch + t % batch

    def early_source(t):
        half = (t // batch) % 2
        return (t // (2 * batch)) * batch + (1 - half) * (t % batch) + half * (batch - 1)

    def late_source(t):
        return (t // (2 * batch)) * batch + ((t // batch) % 2) * (t % batch)

    def per_source(which, *tail):
        return pl.BlockSpec((1,) + tail, lambda t: (which(t),) + (0,) * len(tail))

    def whole(shape):
        return pl.BlockSpec(shape, lambda t: (0,) * len(shape), pipeline_mode=pl.Buffered(1))

    def whole_out(shape):
        return pl.BlockSpec(shape, lambda t: (0,) * len(shape))

    dma = pltpu.SemaphoreType.DMA
    kind = BF16 if last else F32
    inputs = [weights, act_all, cot_all, ranks, gates]
    in_specs = [
        whole(weights.shape),
        per_source(early_source, rows, D),
        per_source(early_source, rows, D),
        per_source(source, local, rows),
        per_source(source, local, rows),
    ]
    out_shape = [
        jax.ShapeDtypeStruct((nex, rows, D), kind),
        jax.ShapeDtypeStruct((nex, number + 1, rows), F32),
        jax.ShapeDtypeStruct((nex, rows, D), kind),
    ]
    out_specs = [
        any_spec() if last else per_source(late_source, rows, D),
        any_spec() if last else per_source(late_source, number + 1, rows),
        per_source(late_source, rows, D),
    ]
    scratch = [
        pltpu.VMEM((D, batch * CAP), BF16),
        pltpu.VMEM((D, batch * CAP), BF16),
        pltpu.VMEM((batch * CAP, wide), BF16),
        pltpu.VMEM((batch * CAP, wide), BF16),
        pltpu.VMEM((batch * CAP, wide), BF16),
        pltpu.VMEM((FF, D), BF16),
        pltpu.VMEM((batch, CAP, D), BF16),
        pltpu.VMEM((batch, CAP, D), BF16),
        pltpu.VMEM((batch, CAP, D), F32),
        pltpu.VMEM((batch, CAP, D), F32),
        pltpu.VMEM((2, 3 * D, wide), BF16),
        dma((2,)),
    ]
    if before is not None:
        inputs += list(before)
        in_specs += [
            per_source(late_source, rows, D),
            per_source(late_source, number, rows),
            per_source(late_source, rows, D),
        ]
    if scatter is not None:
        inputs.append(early)
        in_specs.append(whole(early.shape))
        shape = (ROW_PAD, 3 * FF) if last else scatter.spread_shape()
        out_shape.append(jax.ShapeDtypeStruct(shape, F32 if last else BF16))
        out_specs.append(whole_out(shape))
    inputs += list(ys) + list(zs)
    in_specs += [any_spec()] * (len(ys) + len(zs))
    own_shape = (grid.nz, shard_rows, wide) if inline else (3 * D, wide)
    for shape in (own_shape, (3 * D, wide)):
        out_shape.append(jax.ShapeDtypeStruct(shape, BF16))
        out_specs.append(any_spec())
    for work in works_y + works_z:
        out_shape.append(jax.ShapeDtypeStruct((work.rows, work.width), BF16))
        out_specs.append(whole_out((work.rows, work.width)))
    if flushes > 1:
        scratch.append(pltpu.VMEM((2, 3 * D, wide), F32))
    if last:
        scratch += [
            pltpu.VMEM((nex, rows, D), BF16),
            pltpu.VMEM((nex, local, rows), F32),
            dma((nex - 1, 2)),
            dma((nex - 1, 2)),
            dma((2,)),
        ]
    if first:
        scratch += scatter.scratch_x()
    if first and last:
        scratch.append(pltpu.VMEM(scatter.spread_shape(), BF16))
    if last:
        scratch += early_work.scratch_y() + early_work.scratch_z()
    for work in works_y:
        scratch += work.scratch_y() + work.scratch_z()
    for work in works_z:
        scratch += work.scratch_own() + work.scratch_z()
    if inline:
        scratch += work_own.scratch_y()
    results = pl.pallas_call(
        kernel,
        grid=(steps,),
        out_shape=tuple(out_shape),
        in_specs=in_specs,
        out_specs=tuple(out_specs),
        scratch_shapes=scratch,
        compiler_params=pltpu.CompilerParams(
            vmem_limit_bytes=62 * MIB, collective_id=5 + number, has_side_effects=True
        ),
        cost_estimate=pl.CostEstimate(
            flops=nex * CAP * D * FF * 2 * 11,
            bytes_accessed=25 * MIB,
            transcendentals=nex * CAP * FF,
        ),
        name="experts_step",
    )(*inputs)
    results = list(results)
    sums = results[:3]
    del results[:3]
    if scatter is not None:
        early = results.pop(0)
    return sums, early, results[:2], results[2:]


def middle_step(grid, gin, ggate, mixed, probs, lin, gact, act_across, heads, grad_out, small, gain, ys,
                zs):
    ndp, nex, units = grid.ndp, grid.nex, grid.units
    local = EXPERTS // nex
    works_y = [ShardScatter(grid, *v.shape[1:]) for v in ys]
    works_z = [ShardScatter(grid, *v.shape[1:]) for v in zs]

    def kernel(gin_ref, ggate_ref, mixed_ref, probs_ref, lin_ref, gact_ref, across_ref, heads_ref,
               go_ref, small_ref, gain_ref, *refs):
        refs = list(refs)

        def take(count):
            taken = refs[:count]
            del refs[:count]
            return taken

        y_refs, z_refs = take(len(ys)), take(len(zs))
        dst, grad_mixed_ref, middle_ref = take(3)
        y_outs, z_outs = take(len(ys)), take(len(zs))
        flipped, buf, send, recv, loc = take(5)
        for work, ref in zip(works_y, y_refs):
            work.bind_y(ref, take(4))
        for work, ref in zip(works_z, z_refs):
            work.bind_own(ref, take(2))
            work.bind_z(take(2))
        dp, ex = lax.axis_index("dp"), lax.axis_index("expert")
        greet([(lax.rem(dp + d, ndp), ex) for d in range(1, ndp)])
        for work in works_y:
            work.start_y()
        for work in works_z:
            work.start_z()

        grad_out = go_ref[...].astype(F32)
        probs = probs_ref[...]
        shared_gate = probs[:, EXPERTS : EXPERTS + 1]
        flipped[...] = jnp.zeros_like(flipped)
        for n in range(nex):
            flipped[n * local : (n + 1) * local] = ggate_ref[n]
        grad_probs = flipped[...].T
        lane = lax.broadcasted_iota(jnp.int32, probs.shape, 1)
        inner = jnp.sum(
            jnp.where(lane < EXPERTS, probs * grad_probs, 0.0), axis=1, keepdims=True
        )
        svec = shared_gate * (1.0 - shared_gate)
        svec = svec * jnp.sum(grad_out * lin_ref[...], axis=1, keepdims=True)
        grad_misc = jnp.where(
            lane < EXPERTS,
            probs * (grad_probs - inner),
            jnp.where(lane == EXPERTS, svec, 0.0),
        ).astype(BF16)
        grad_act = gact_ref[...] + dot(grad_misc, small_ref[:, :MISC], 1, 1)
        for n in range(nex):
            grad_act += gin_ref[n].astype(F32)
        mixed = mixed_ref[...]
        scale = lax.rsqrt(jnp.mean(mixed * mixed, axis=-1, keepdims=True) + eps_norm)
        normed = mixed * scale
        gain_grad = jnp.sum(grad_act * normed, axis=0, keepdims=True)
        weighted = grad_act * gain_ref[2:3]
        grad_mixed = grad_out + scale * (
            weighted - normed * jnp.mean(weighted * normed, axis=-1, keepdims=True)
        )
        grad_mixed_ref[...] = grad_mixed
        grad_low = grad_mixed.astype(BF16)
        for s in range(SERIES_DEV):
            rows = slice(s * SEG, (s + 1) * SEG)
            grad = dot(small_ref[:, MISC:], grad_low[rows], 1, 1).astype(BF16)
            buf[s * HEADS : (s + 1) * HEADS] = grad.reshape(HEADS, HEAD_DIM, SEG)
        if units * ndp > UNITS_ALL:
            buf[UNITS_ALL:] = jnp.zeros((units * ndp - UNITS_ALL, HEAD_DIM, SEG), BF16)
        lanes = pl.ds(pl.multiple_of(dp * SEG, SEG), SEG)
        copies = []
        for d in far_first(ndp):
            target = lax.rem(dp + d, ndp)
            copy = remote(
                buf.at[pl.ds(target * units, units)], dst.at[:, :, lanes],
                send.at[d - 1], recv.at[d - 1], (target, ex),
            )
            copy.start()
            copies.append(copy)
        copy = pltpu.make_async_copy(
            buf.at[pl.ds(dp * units, units)], dst.at[:, :, lanes], loc
        )
        copy.start()
        copies.append(copy)
        group = group_matrix(grid)
        total = jnp.zeros((D, D), F32)
        for s in range(SERIES_DEV):
            attn = heads_ref[s * HEADS : (s + 1) * HEADS].reshape(D, SEG)
            attn = dot(group, attn).astype(BF16)
            total += dot(attn, grad_low[s * SEG : (s + 1) * SEG])
        middle_ref[:, :D] = total.astype(BF16)
        gain_rows = jnp.broadcast_to(gain_grad, (MISC, D)).astype(BF16)
        gain_column = dot(group, gain_rows, 1, 1)
        misc_grad = dot(across_ref[...], grad_misc)
        lane = lax.broadcasted_iota(jnp.int32, misc_grad.shape, 1)
        misc_grad = jnp.where(lane == EXPERTS + 2, gain_column, misc_grad)
        middle_ref[:, D:] = misc_grad.astype(BF16)
        for work, out in zip(works_y, y_outs):
            work.store_y(out)
        for copy in copies:
            copy.wait()
        for work, out in zip(works_z, z_outs):
            work.finish_z(out)

    dma = pltpu.SemaphoreType.DMA
    vmem = pl.BlockSpec(memory_space=pltpu.VMEM)
    hbm = pl.BlockSpec(memory_space=pltpu.HBM)
    inputs = [gin, ggate, mixed, probs, lin, gact, act_across, heads, grad_out, small, gain]
    in_specs = [vmem] * len(inputs) + [any_spec()] * (len(ys) + len(zs))
    out_shape = [
        jax.ShapeDtypeStruct((units, HEAD_DIM, SEG * ndp), BF16),
        jax.ShapeDtypeStruct((TOK_DEV, D), F32),
        jax.ShapeDtypeStruct((D, D + MISC), BF16),
    ]
    out_specs = [any_spec(), vmem, vmem]
    scratch = [
        pltpu.VMEM((MISC, TOK_DEV), F32),
        pltpu.VMEM((units * ndp, HEAD_DIM, SEG), BF16),
        dma((ndp - 1,)),
        dma((ndp - 1,)),
        dma,
    ]
    inputs += list(ys) + list(zs)
    for work in works_y:
        out_shape.append(jax.ShapeDtypeStruct((grid.nz, work.rows, work.width), BF16))
        out_specs.append(hbm)
        scratch += work.scratch_y()
    for work in works_z:
        out_shape.append(jax.ShapeDtypeStruct((work.rows, work.width), BF16))
        out_specs.append(vmem)
        scratch += work.scratch_own() + work.scratch_z()
    return pl.pallas_call(
        kernel,
        out_shape=tuple(out_shape),
        in_specs=in_specs,
        out_specs=tuple(out_specs),
        scratch_shapes=scratch,
        compiler_params=pltpu.CompilerParams(
            collective_id=2, has_side_effects=True, vmem_limit_bytes=60 * MIB
        ),
        name="middle_step",
    )(*inputs)


def local(
    tokens,
    cotangent,
    lengths,
    routes,
    dense_weights,
    dense_first,
    dense_second,
    dense_average,
    expert_weights,
    expert_first,
    expert_second,
    expert_average,
):
    ndp, nex = lax.axis_size("dp"), lax.axis_size("expert")
    dp, ex = lax.axis_index("dp"), lax.axis_index("expert")
    grid = Grid(ndp, nex)
    local_experts = EXPERTS // nex
    length = SEG * ndp
    rows_dev = D // grid.ndev
    shard_rows = 3 * D // ndp

    spot = jnp.arange(FF, dtype=jnp.int32)
    order = (FF // D) * (spot % D) + spot // D
    mix = (spot[:, None] == order[None, :]).astype(BF16)
    shard_row = dp * shard_rows + jnp.arange(shard_rows, dtype=jnp.int32)
    is_down = (shard_row >= 2 * D)[None, :, None]
    expert_low = expert_weights.astype(BF16).reshape(local_experts, shard_rows, FF)
    mixed_low = jnp.einsum(
        "erf,fg->erg", expert_low, mix, preferred_element_type=F32
    ).astype(BF16)
    expert_send = jnp.where(is_down, expert_low, mixed_low)
    table = dense_weights.astype(BF16).reshape(rows_dev, -1)
    after = 4 * D + EXPERTS

    def padded(*columns):
        return jnp.pad(jnp.concatenate(columns, axis=1), ((0, ROW_PAD - rows_dev), (0, 0)))

    shard_first = padded(
        table[:, : 3 * D],
        table[:, 4 * D : after],
        table[:, after + 3 * FF :],
        jnp.zeros((rows_dev, MISC - EXPERTS - 3), BF16),
        table[:, 3 * D : 4 * D],
    )
    shard_rest = padded(table[:, after : after + 3 * FF])

    names = jnp.arange(EXPERTS, dtype=jnp.int32)
    routes_rows = routes.reshape(TOK_DEV, TOP)
    member = (routes_rows[:, :, None] == names[None, None, :]).any(axis=1)
    before = jnp.arange(TOK_DEV)
    earlier = (before[None, :] < before[:, None]).astype(BF16)
    count = jnp.dot(earlier, member.astype(BF16), preferred_element_type=F32)
    ranks = jnp.where(member, count, -1.0).T.reshape(nex, local_experts, TOK_DEV)

    local_pos = dp * SEG + jnp.arange(SEG, dtype=jnp.int32)
    live = (local_pos[None, :] < lengths[:, None]).astype(F32)
    grad_out_low = (cotangent.astype(F32) * live[..., None]).astype(BF16).reshape(TOK_DEV, D)

    tok_all, dense_all, cot_all, rank_all = first_exchange(
        grid, tokens, shard_first, grad_out_low, ranks
    )
    expert_all = [
        lax.all_gather(expert_send[e], "dp", axis=0, tiled=True) for e in range(local_experts)
    ]
    tok_all = tok_all.reshape(grid.slots, length, D)

    dense_all = dense_all.reshape(grid.ndev * ROW_PAD, -1)

    half = HEAD_DIM // 2
    inverse = rope_base ** (-jnp.arange(half, dtype=F32) * 2.0 / HEAD_DIM)
    angles = inverse[:, None] * jnp.arange(length, dtype=jnp.int32).astype(F32)[None, :]
    cosine, sine = jnp.cos(angles), jnp.sin(angles)
    heads_here, rest, act_one, query, key, value, lse, qkv_rows = attend(
        grid, lengths, tok_all, dense_all, cosine, sine, shard_rest
    )
    heads_here = heads_here.reshape(-1, HEAD_DIM, SEG)[:UNITS_ALL]

    (act_all, gates_all, mixed_rows, probs, shared_lin, grad_act_shared, early, act_across, small,
     gains) = route_rows(
        grid, heads_here, tokens, dense_all, grad_out_low, rest.reshape(grid.ndev * ROW_PAD, -1)
    )
    before, ys, zs, halves = None, [], [], []
    for e in range(local_experts):
        before, early, own, sums = experts_step(
            grid, e, expert_all[e], act_all, cot_all, rank_all, gates_all, before, early, ys, zs
        )
        halves += sums[::-1] if zs else sums
        ys = [v.reshape(ndp, shard_rows, FF // 2) for v in own if v.ndim == 2]
        zs = [v for v in own if v.ndim == 3]
    gin_back, ggate_back, routed_parts = before

    grad_heads, grad_mixed, middle, *more = middle_step(
        grid, gin_back, ggate_back, mixed_rows, probs, shared_lin, grad_act_shared, act_across,
        heads_here, grad_out_low, small, gains, ys, zs,
    )
    halves += more[len(ys) :]

    output, grad_tokens, dense_table, *sums = attend_back(
        grid, lengths, tok_all, act_one, qkv_rows, query, key, value, lse, grad_heads, cosine, sine,
        middle, routed_parts, more[: len(ys)], tokens, mixed_rows, grad_mixed, probs, shared_lin, gains, early,
    )
    dense_grad = dense_table[:rows_dev, : dense_weights.shape[0] // rows_dev].reshape(-1)
    halves += sums
    expert_sums = jnp.stack(
        [jnp.concatenate(halves[e : e + 2], axis=1) for e in range(0, 2 * local_experts, 2)]
    )
    unmixed = jnp.einsum("erg,fg->erf", expert_sums, mix, preferred_element_type=F32)
    expert_grad = jnp.where(is_down, expert_sums.astype(F32), unmixed)
    expert_grad = expert_grad.reshape(expert_weights.shape)

    dense_first_new, dense_second_new, dense_new, dense_average_new = adamw_update(
        dense_weights, dense_grad, dense_first, dense_second, dense_average
    )
    expert_first_new, expert_second_new, expert_new, expert_average_new = adamw_update(
        expert_weights, expert_grad, expert_first, expert_second, expert_average
    )
    return (
        output.reshape(tokens.shape),
        grad_tokens.reshape(tokens.shape),
        dense_grad,
        dense_first_new,
        dense_second_new,
        dense_new,
        dense_average_new,
        expert_grad,
        expert_first_new,
        expert_second_new,
        expert_new,
        expert_average_new,
    )


def solution(mesh):
    rows = P("expert", "dp", None)
    dense = P(("dp", "expert"))
    experts = P("expert", "dp")
    return jax.shard_map(
        local,
        mesh=mesh,
        in_specs=(
            (rows, rows, P("expert"), P("dp", "expert", None, None)) + (dense,) * 4 + (experts,) * 4
        ),
        out_specs=(rows, rows) + (dense,) * 5 + (experts,) * 5,
        check_vma=False,
    )
```

```python
import functools
import math

import jax
import jax.numpy as jnp
from jax import lax
from jax.experimental import pallas as pl
from jax.experimental.pallas import tpu as pltpu
from jax.sharding import PartitionSpec as P

D = 384
HEADS = 12
HEAD_DIM = 32
FF = 1536
EXPERTS = 8
TOP = 2
SEG = 128
SERIES_DEV = 6
STEP = 8
TOK_DEV = 768
CAP = 384
ROW_PAD = 16
MISC = 128
UNITS_ALL = SERIES_DEV * HEADS
QBLOCK = 256
MIB = 1 << 20

eps_norm = 1e-06
beta_one = 0.5
beta_two = 0.5
learn_rate = 0.02
weight_decay = 0.1
eps_adam = 1e-08
average_keep = 0.9
rope_base = 10000.0
neg_fill = -1e30

MESH = pl.DeviceIdType.MESH
F32 = jnp.float32
BF16 = jnp.bfloat16


def adamw_update(weights, grads, first, second, average):
    first_new = beta_one * first + (1.0 - beta_one) * grads
    second_new = beta_two * second + (1.0 - beta_two) * grads * grads
    first_hat = first_new / (1.0 - beta_one**STEP)
    second_hat = second_new / (1.0 - beta_two**STEP)
    weights_new = weights - learn_rate * (
        first_hat / (jnp.sqrt(second_hat) + eps_adam) + weight_decay * weights
    )
    average_new = average_keep * average + (1.0 - average_keep) * weights_new
    return (first_new, second_new, weights_new, average_new)


def dot(left, right, left_dim=1, right_dim=0):
    return lax.dot_general(
        left, right, (((left_dim,), (right_dim,)), ((), ())), preferred_element_type=F32
    )


class Grid:
    def __init__(self, ndp, nex):
        self.ndp, self.nex = ndp, nex
        self.nz = math.gcd(ndp, 4)
        self.ny = ndp // self.nz
        self.nc = math.gcd(nex, 2)
        self.nx = nex // self.nc
        self.ndev = ndp * nex
        self.units = -(-UNITS_ALL // ndp)
        spans = [
            [u // HEADS for u in range(self.units * o, min(self.units * (o + 1), UNITS_ALL))]
            for o in range(ndp)
        ]
        self.owned = [sorted(set(s)) for s in spans]
        self.slots = max(len(s) for s in self.owned)

    def first_series(self, owner):
        return (owner * self.units) // HEADS

    def holds(self, owner, slot):
        begin = owner * self.units
        end = jnp.minimum(begin + self.units, UNITS_ALL)
        return (begin // HEADS + slot) * HEADS < end


def remote(src, dst, send, recv, target):
    return pltpu.make_async_remote_copy(
        src_ref=src,
        dst_ref=dst,
        send_sem=send,
        recv_sem=recv,
        device_id=target,
        device_id_type=MESH,
    )


def greet(peers):
    barrier = pltpu.get_barrier_semaphore()
    for peer in peers:
        pl.semaphore_signal(barrier, inc=1, device_id=peer, device_id_type=MESH)
    pl.semaphore_wait(barrier, len(peers))


def any_spec():
    return pl.BlockSpec(memory_space=pl.ANY)


def far_first(n):
    return sorted(range(1, n), key=lambda d: -min(d, n - d))


def comm_params(number):
    return pltpu.CompilerParams(collective_id=number, has_side_effects=True)


def unpad_matrix(grid):
    shape = (D, grid.ndev * ROW_PAD)
    rows_dev = D // grid.ndev
    row = lax.broadcasted_iota(jnp.int32, shape, 0)
    at = (row // rows_dev) * ROW_PAD + lax.rem(row, rows_dev)
    return (lax.broadcasted_iota(jnp.int32, shape, 1) == at).astype(F32).astype(BF16)


def group_matrix(grid):
    rows_dev = D // grid.ndev
    row = lax.broadcasted_iota(jnp.int32, (D, D), 1)
    owner = row // rows_dev
    at = (lax.rem(owner, grid.nex) * grid.ndp + owner // grid.nex) * rows_dev
    at = at + lax.rem(row, rows_dev)
    return (lax.broadcasted_iota(jnp.int32, (D, D), 0) == at).astype(F32).astype(BF16)


class DenseGather:
    def __init__(self, grid):
        self.grid = grid

    def scratch(self):
        dma = pltpu.SemaphoreType.DMA
        return [dma((self.grid.ndev,)), dma((self.grid.ndev,)), dma]

    def bind(self, shard, out, refs):
        g = self.grid
        self.shard, self.out = shard, out
        self.send, self.recv, self.loc = refs
        dp, ex = lax.axis_index("dp"), lax.axis_index("expert")
        self.z, self.y = dp // g.ny, lax.rem(dp, g.ny)
        self.x, self.c = ex // g.nc, lax.rem(ex, g.nc)
        self.zs = [0] + far_first(g.nz)[::-1]
        self.count = 0
        self.ends = []

    def place(self, dz, dy, dx, dc):
        g = self.grid
        return (
            lax.rem(self.z + dz, g.nz) * g.ny + lax.rem(self.y + dy, g.ny),
            lax.rem(self.x + dx, g.nx) * g.nc + lax.rem(self.c + dc, g.nc),
        )

    def slot(self, dz, dy, dx, dc):
        g = self.grid
        dp, ex = self.place(g.nz - dz, g.ny - dy, g.nx - dx, g.nc - dc)
        return dp * g.nex + ex

    def copy(self, ref, slot, number, target):
        return remote(ref, self.out.at[slot], self.send.at[number], self.recv.at[slot], target)

    def go(self, slot, target):
        ref = self.out.at[slot]
        if self.count < self.own_sends():
            ref = self.shard
        self.copy(ref, slot, self.count, target).start()
        self.count += 1

    def own_sends(self):
        g = self.grid
        return g.nz + g.ny + g.nx + g.nc - 4

    def wait(self, slot):
        self.copy(self.shard, slot, 0, self.place(0, 0, 0, 0)).wait_recv()

    def onward(self, slot, axes):
        g = self.grid
        if "y" in axes:
            for dy in range(1, g.ny):
                self.go(slot, self.place(0, dy, 0, 0))
        if "x" in axes:
            for dx in range(1, g.nx):
                self.go(slot, self.place(0, 0, dx, 0))
        for dc in range(1, g.nc):
            self.go(slot, self.place(0, 0, 0, dc))

    def own(self):
        return pltpu.make_async_copy(self.shard, self.out.at[self.slot(0, 0, 0, 0)], self.loc)

    def start(self):
        own = self.slot(0, 0, 0, 0)
        for dz in far_first(self.grid.nz):
            self.go(own, self.place(dz, 0, 0, 0))
        self.onward(own, "yx")
        self.own().start()

    def pass_z(self):
        for dz in self.zs[1:]:
            slot = self.slot(dz, 0, 0, 0)
            self.wait(slot)
            self.onward(slot, "yx")

    def pass_y(self):
        for dy in range(1, self.grid.ny):
            for dz in self.zs:
                slot = self.slot(dz, dy, 0, 0)
                self.wait(slot)
                self.onward(slot, "x")

    def pass_x(self):
        g = self.grid
        for dx in range(1, g.nx):
            for dy in range(g.ny):
                for dz in self.zs:
                    slot = self.slot(dz, dy, dx, 0)
                    self.wait(slot)
                    self.onward(slot, "")

    def finish(self):
        g = self.grid
        for dc in range(1, g.nc):
            for dx in range(g.nx):
                for dy in range(g.ny):
                    for dz in self.zs:
                        self.wait(self.slot(dz, dy, dx, dc))
        for number in range(g.ndev - 1):
            self.copy(self.shard, 0, number, self.place(0, 0, 0, 0)).wait_send()
        self.own().wait()


class RowGather:
    parts = 3

    def __init__(self, grid):
        self.grid = grid

    def scratch(self):
        g, n = self.grid, self.parts
        dma = pltpu.SemaphoreType.DMA
        return [dma((g.nx + g.nc, n)), dma((g.nex, n)), dma((g.nx, n)), dma]

    def bind(self, src, dst, refs):
        g = self.grid
        self.src, self.dst = src, dst
        self.send, self.recv, self.fsend, self.loc = refs
        self.dp, self.ex = lax.axis_index("dp"), lax.axis_index("expert")
        self.x, self.c = self.ex // g.nc, lax.rem(self.ex, g.nc)
        self.sends = []

    def rows(self, part):
        extent = TOK_DEV // self.parts
        return pl.ds(part * extent, extent)

    def slot_at(self, owner, target):
        return lax.rem(owner - target - 1 + 2 * self.grid.nex, self.grid.nex)

    def go(self, ref, owner, part, sem, target):
        slot = self.slot_at(owner, target)
        copy = remote(
            ref, self.dst.at[slot, self.rows(part)], sem, self.recv.at[slot, part],
            (self.dp, target),
        )
        copy.start()
        self.sends.append(copy)

    def arrived(self, owner, part):
        slot = self.slot_at(owner, self.ex)
        remote(
            self.src.at[self.rows(part)], self.dst.at[slot, self.rows(part)], self.send.at[0, 0],
            self.recv.at[slot, part], (self.dp, self.ex),
        ).wait_recv()

    def beside(self, dc):
        g = self.grid
        return self.x * g.nc + lax.rem(self.c + dc, g.nc)

    def start(self):
        g = self.grid
        for part in range(self.parts):
            for dx in range(1, g.nx):
                target = lax.rem(self.x + dx, g.nx) * g.nc + self.c
                ref = self.src.at[self.rows(part)]
                self.go(ref, self.ex, part, self.send.at[dx - 1, part], target)
        for part in range(self.parts):
            for dc in range(1, g.nc):
                ref = self.src.at[self.rows(part)]
                self.go(ref, self.ex, part, self.send.at[g.nx + dc - 2, part], self.beside(dc))
        self.own = pltpu.make_async_copy(self.src, self.dst.at[g.nex - 1], self.loc)
        self.own.start()

    def pass_on(self, part):
        g = self.grid
        for dx in range(1, g.nx):
            owner = lax.rem(self.x + g.nx - dx, g.nx) * g.nc + self.c
            self.arrived(owner, part)
            for dc in range(1, g.nc):
                ref = self.dst.at[self.slot_at(owner, self.ex), self.rows(part)]
                self.go(ref, owner, part, self.fsend.at[dx - 1, part], self.beside(dc))

    def finish(self):
        g = self.grid
        for part in range(self.parts):
            for dc in range(1, g.nc):
                for dx in range(g.nx):
                    owner = lax.rem(self.x + g.nx - dx, g.nx) * g.nc
                    self.arrived(owner + lax.rem(self.c + g.nc - dc, g.nc), part)
        for copy in self.sends:
            copy.wait_send()
        self.own.wait()


def first_exchange(grid, tokens, shard, cot, ranks):
    ndp, nex = grid.ndp, grid.nex

    def kernel(tok, shd, cot_in, rank_in, tok_out, dense_out, cot_out, rank_out,
               t_send, t_recv, e_send, e_recv, loc, *more_refs):
        dp, ex = lax.axis_index("dp"), lax.axis_index("expert")

        def off(value, by, n):
            return lax.rem(value + by, n)

        peers = [(off(dp, d, ndp), ex) for d in range(1, ndp)]
        peers += [(dp, off(ex, d, nex)) for d in range(1, nex)]
        greet(peers)
        dense = DenseGather(grid)
        dense.bind(shd, dense_out, more_refs[4:])
        dense.start()

        def token_copy(d, slot, src_series, sender, target):
            return remote(
                tok.at[src_series],
                tok_out.at[slot, sender],
                t_send.at[d - 1, slot],
                t_recv.at[d - 1, slot],
                (target, ex),
            )

        for d in far_first(ndp):
            target = off(dp, d, ndp)
            for slot in range(grid.slots):

                @pl.when(grid.holds(target, slot))
                def _():
                    token_copy(d, slot, grid.first_series(target) + slot, dp, target).start()

        rows = RowGather(grid)
        rows.bind(cot_in, cot_out, more_refs[:4])
        rows.start()
        e_sends = []
        for d in range(1, nex):
            target = off(ex, d, nex)
            copy = remote(
                rank_in.at[target], rank_out.at[nex - 1 - d], e_send.at[d - 1], e_recv.at[d - 1],
                (dp, target),
            )
            copy.start()
            e_sends.append(copy)
        copy = pltpu.make_async_copy(rank_in.at[ex], rank_out.at[nex - 1], loc.at[0])
        copy.start()
        e_sends.append(copy)

        for slot in range(grid.slots):

            @pl.when(grid.holds(dp, slot))
            def _():
                copy = pltpu.make_async_copy(
                    tok.at[grid.first_series(dp) + slot], tok_out.at[slot, dp], loc.at[1 + slot]
                )
                copy.start()
                copy.wait()

        dense.pass_z()
        rows.pass_on(0)
        dense.pass_y()
        for part in range(1, rows.parts):
            rows.pass_on(part)
        dense.pass_x()
        dense.finish()
        rows.finish()
        for d in range(1, ndp):
            for slot in range(grid.slots):

                @pl.when(grid.holds(dp, slot))
                def _():
                    token_copy(d, slot, 0, dp, off(dp, d, ndp)).wait_recv()

                @pl.when(grid.holds(off(dp, d, ndp), slot))
                def _():
                    token_copy(d, slot, 0, dp, off(dp, d, ndp)).wait_send()

        for copy in e_sends:
            copy.wait()

    seg, width = tokens.shape[1:]
    dma = pltpu.SemaphoreType.DMA
    return pl.pallas_call(
        kernel,
        out_shape=(
            jax.ShapeDtypeStruct((grid.slots, ndp, seg, width), tokens.dtype),
            jax.ShapeDtypeStruct((grid.ndev,) + shard.shape, shard.dtype),
            jax.ShapeDtypeStruct((nex,) + cot.shape, cot.dtype),
            jax.ShapeDtypeStruct(ranks.shape, ranks.dtype),
        ),
        in_specs=[any_spec()] * 4,
        out_specs=(any_spec(),) * 4,
        scratch_shapes=[
            dma((ndp - 1, grid.slots)),
            dma((ndp - 1, grid.slots)),
            dma((nex - 1,)),
            dma((nex - 1,)),
            dma((1 + grid.slots,)),
        ]
        + RowGather(grid).scratch()
        + DenseGather(grid).scratch(),
        compiler_params=comm_params(0),
        name="first_exchange",
    )(tokens, shard, cot, ranks)


class RowScatter:
    def __init__(self, grid, width):
        self.grid, self.width = grid, width
        self.rows = D // grid.nex
        self.rows_dev = D // grid.ndev

    def scratch_x(self):
        g = self.grid
        dma = pltpu.SemaphoreType.DMA
        blocks = pltpu.VMEM((g.nx, self.rows, self.width), BF16)
        return [blocks, blocks, blocks, dma((2, 2)), dma((g.nx, 2))]

    def scratch_dp(self):
        g = self.grid
        return [
            pltpu.VMEM((g.ndp, ROW_PAD, self.width), BF16),
            pltpu.SemaphoreType.DMA((g.ndp, 2)),
        ]

    def spread_shape(self):
        return (self.grid.ndp * ROW_PAD, self.width)

    def bind(self, spread):
        g = self.grid
        self.spread = spread
        self.dp, self.ex = lax.axis_index("dp"), lax.axis_index("expert")
        self.x, self.c = self.ex // g.nc, lax.rem(self.ex, g.nc)

    def bind_x(self, source, refs):
        self.source = source
        self.got_core, self.by_x, self.got_x, self.sem_core, self.sem_x = refs

    def bind_dp(self, refs):
        self.got_dp, self.sem_dp = refs

    def core_copy(self):
        other = 1 - self.c
        return remote(
            self.source.at[:, other], self.got_core, self.sem_core.at[0, 0],
            self.sem_core.at[0, 1], (self.dp, self.x * 2 + other),
        )

    def x_copy(self, d):
        target = lax.rem(self.x + d, self.grid.nx)
        return remote(
            self.by_x.at[target], self.got_x.at[d], self.sem_x.at[d, 0], self.sem_x.at[d, 1],
            (self.dp, target * self.grid.nc + self.c),
        )

    def dp_copy(self, d):
        target = lax.rem(self.dp + d, self.grid.ndp)
        rows = pl.ds(pl.multiple_of(target * ROW_PAD, ROW_PAD), ROW_PAD)
        return remote(
            self.spread.at[rows], self.got_dp.at[d], self.sem_dp.at[d, 0], self.sem_dp.at[d, 1],
            (target, self.ex),
        )

    def start(self):
        self.core_copy().start()

    def along_x(self):
        g = self.grid
        self.core_copy().wait()
        for n in range(g.nx):
            mine = self.source[n, pl.ds(self.c, 1)][0]
            self.by_x[n] = (mine.astype(F32) + self.got_core[n].astype(F32)).astype(BF16)
        for d in range(1, g.nx):
            self.x_copy(d).start()

    def after_x(self):
        g = self.grid
        for d in range(1, g.nx):
            self.x_copy(d).wait()
        total = self.by_x[pl.ds(self.x, 1)][0].astype(F32)
        for d in range(1, g.nx):
            total += self.got_x[d].astype(F32)
        to = lax.broadcasted_iota(jnp.int32, (g.ndp * ROW_PAD, self.rows), 0)
        of = lax.broadcasted_iota(jnp.int32, (g.ndp * ROW_PAD, self.rows), 1)
        place = (of // self.rows_dev) * ROW_PAD + lax.rem(of, self.rows_dev)
        move = (to == place).astype(F32).astype(BF16)
        self.spread[...] = dot(move, total.astype(BF16)).astype(BF16)

    def along_dp(self):
        for d in far_first(self.grid.ndp):
            self.dp_copy(d).start()

    def finish(self, out):
        g = self.grid
        rows = pl.ds(pl.multiple_of(self.dp * ROW_PAD, ROW_PAD), ROW_PAD)
        total = self.spread[rows].astype(F32)
        for d in range(1, g.ndp):
            self.dp_copy(d).wait()
            total += self.got_dp[d].astype(F32)
        out[...] = total


class ShardScatter:
    def __init__(self, grid, rows, width):
        self.grid, self.rows, self.width = grid, rows, width

    def scratch_y(self):
        g = self.grid
        block = (self.rows, self.width)
        dma = pltpu.SemaphoreType.DMA
        return [
            pltpu.VMEM((g.nz,) + block, BF16),
            pltpu.VMEM((max(g.ny - 1, 1), g.nz) + block, BF16),
            dma((g.ny, g.nz, 2)),
            dma((g.nz,)),
        ]

    def scratch_z(self):
        g = self.grid
        dma = pltpu.SemaphoreType.DMA
        return [pltpu.VMEM((g.nz, self.rows, self.width), BF16), dma((g.nz, 2))]

    def scratch_own(self):
        return [pltpu.VMEM((self.rows, self.width), BF16), pltpu.SemaphoreType.DMA]

    def where(self):
        g = self.grid
        self.dp, self.ex = lax.axis_index("dp"), lax.axis_index("expert")
        self.z, self.y = self.dp // g.ny, lax.rem(self.dp, g.ny)
        self.order = far_first(g.nz) + [0]

    def bind_y(self, source, refs):
        self.where()
        self.source = source
        self.mine, self.got_y, self.sem_y, self.loc = refs
        self.sums = self.mine

    def bind_z(self, refs):
        self.got_z, self.sem_z = refs

    def bind_own(self, sums, refs):
        self.where()
        self.sums = sums
        self.own, self.own_sem = refs

    def place(self, dz, dy):
        g = self.grid
        return lax.rem(self.z + dz, g.nz) * g.ny + lax.rem(self.y + dy, g.ny)

    def block(self, number):
        if len(self.source.shape) == 3:
            return self.source.at[number]
        return self.source.at[pl.ds(pl.multiple_of(number * self.rows, ROW_PAD), self.rows)]

    def y_copy(self, dy, dz):
        return remote(
            self.block(self.place(dz, dy)), self.got_y.at[dy - 1, dz],
            self.sem_y.at[dy, dz, 0], self.sem_y.at[dy, dz, 1], (self.place(0, dy), self.ex),
        )

    def load(self, dz):
        return pltpu.make_async_copy(
            self.block(self.place(dz, 0)), self.mine.at[dz], self.loc.at[dz]
        )

    def start_y(self):
        for dz in self.order:
            for dy in range(1, self.grid.ny):
                self.y_copy(dy, dz).start()
            self.load(dz).start()

    def sum_y(self, then=None):
        g = self.grid
        for dz in self.order:
            self.load(dz).wait()
            for dy in range(1, g.ny):
                self.y_copy(dy, dz).wait()
            if g.ny > 1:
                total = self.mine[dz].astype(F32)
                for dy in range(1, g.ny):
                    total += self.got_y[dy - 1, dz].astype(F32)
                self.mine[dz] = total.astype(BF16)
            if then is not None:
                then(dz)

    def store_y(self, out):
        def store(dz):
            return pltpu.make_async_copy(self.mine.at[dz], out.at[dz], self.loc.at[dz])

        self.sum_y(lambda dz: store(dz).start())
        for dz in self.order:
            store(dz).wait()

    def z_copy(self, dz):
        return remote(
            self.sums.at[dz], self.got_z.at[dz], self.sem_z.at[dz, 0], self.sem_z.at[dz, 1],
            (self.place(dz, 0), self.ex),
        )

    def own_copy(self):
        return pltpu.make_async_copy(self.sums.at[0], self.own, self.own_sem)

    def start_z(self):
        for dz in far_first(self.grid.nz):
            self.z_copy(dz).start()
        if self.sums is not getattr(self, "mine", None):
            self.own_copy().start()

    def finish_z(self, out):
        if self.sums is getattr(self, "mine", None):
            total = self.mine[0].astype(F32)
        else:
            self.own_copy().wait()
            total = self.own[...].astype(F32)
        for dz in range(1, self.grid.nz):
            self.z_copy(dz).wait()
            total += self.got_z[dz].astype(F32)
        out[...] = total.astype(out.dtype)


def route_rows(grid, heads, tokens, table, grad_out, weights):
    nex = grid.nex
    local = EXPERTS // nex
    count = len(OUTS_ROUTE)

    def kernel(heads_ref, tok_ref, table_ref, go_ref, w_ref, dst, gate_dst, *refs):
        outs, bufs = refs[:count], refs[count : 2 * count]
        mixed_buf, probs_buf, lin_ref, gact_ref, early_ref, across_ref, small_ref, gain_ref = bufs
        act_buf, gate_buf, g_send, g_recv, loc, out_sem = refs[2 * count : 2 * count + 6]
        row_refs = refs[2 * count + 6 :]
        dp, ex = lax.axis_index("dp"), lax.axis_index("expert")
        greet([(dp, lax.rem(ex + d, nex)) for d in range(1, nex)])

        def keep(n):
            return pltpu.make_async_copy(bufs[n], outs[n], out_sem.at[n])

        unpad, group = unpad_matrix(grid), group_matrix(grid)
        small_ref[...] = dot(unpad, table_ref[:, 3 * D :]).astype(BF16)
        gain_ref[...] = dot(table_ref[:, 3 * D : 3 * D + MISC], unpad, 0, 1)[
            EXPERTS : EXPERTS + 8
        ]
        for s in range(SERIES_DEV):
            attn = heads_ref[s * HEADS : (s + 1) * HEADS].reshape(D, SEG)
            rows = slice(s * SEG, (s + 1) * SEG)
            mixed_buf[rows] = tok_ref[s].astype(F32) + dot(attn, small_ref[:, MISC:], 0, 0)
        mixed = mixed_buf[...]
        scale = lax.rsqrt(jnp.mean(mixed * mixed, axis=-1, keepdims=True) + eps_norm)
        act = (mixed * scale * gain_ref[2:3]).astype(BF16)
        act_buf[...] = act
        gather = RowGather(grid)
        gather.bind(act_buf, dst, row_refs)
        gather.start()
        misc = dot(act, small_ref[:, :MISC])
        lane = lax.broadcasted_iota(jnp.int32, misc.shape, 1)
        logits = jnp.where(lane < EXPERTS, misc, neg_fill)
        powers = jnp.exp(logits - jnp.max(logits, axis=1, keepdims=True))
        probs = powers / jnp.sum(powers, axis=1, keepdims=True)
        shared_gate = 0.5 * jnp.tanh(0.5 * misc[:, EXPERTS : EXPERTS + 1]) + 0.5
        probs_buf[...] = jnp.where(lane == EXPERTS, shared_gate, probs)
        flipped = probs.T
        for n in range(nex):
            gate_buf[n] = flipped[n * local : (n + 1) * local]
        gate_copies = []
        for d in range(1, nex):
            target = lax.rem(ex + d, nex)
            copy = remote(
                gate_buf.at[target], gate_dst.at[nex - 1 - d], g_send.at[d - 1], g_recv.at[d - 1],
                (dp, target),
            )
            copy.start()
            gate_copies.append(copy)
        copy = pltpu.make_async_copy(gate_buf.at[ex], gate_dst.at[nex - 1], loc)
        copy.start()
        gate_copies.append(copy)
        for n in (0, 1, 6, 7):
            keep(n).start()

        grad_lin = (go_ref[...].astype(F32) * shared_gate).astype(BF16)
        across_ref[...] = dot(group, act, 1, 1).astype(BF16)
        keep(5).start()
        grad_across = dot(group, grad_lin, 1, 1).astype(BF16)
        wide = 2 * D
        for n in range(FF // wide):
            gate_w, up_w, down_w = (
                dot(unpad, w_ref[:, m * FF + n * wide : m * FF + (n + 1) * wide]).astype(BF16)
                for m in range(3)
            )
            gate_lin, up_lin = dot(act, gate_w), dot(act, up_w)
            sig = 0.5 * jnp.tanh(0.5 * gate_lin) + 0.5
            silu = gate_lin * sig
            hidden = (silu * up_lin).astype(BF16)
            grad_hidden = dot(grad_lin, down_w)
            grad_gate = (grad_hidden * up_lin * (sig + silu * (1.0 - sig))).astype(BF16)
            grad_up = (grad_hidden * silu).astype(BF16)
            lin = dot(hidden, down_w, 1, 1)
            gact = dot(grad_gate, gate_w, 1, 1) + dot(grad_up, up_w, 1, 1)
            if n:
                lin_ref[...] += lin
                gact_ref[...] += gact
            else:
                lin_ref[...] = lin
                gact_ref[...] = gact
            if n == 0:
                gather.pass_on(0)
            else:
                keep(2).start()
                keep(3).start()
            for m, (left, right) in enumerate(
                ((across_ref[...], grad_gate), (across_ref[...], grad_up), (grad_across, hidden))
            ):
                lanes = slice(m * FF + n * wide, m * FF + (n + 1) * wide)
                early_ref[:, lanes] = dot(left, right).astype(BF16)
            if n == 0:
                gather.pass_on(1)
        keep(4).start()
        for part in range(2, gather.parts):
            gather.pass_on(part)
        gather.finish()
        for copy in gate_copies:
            copy.wait()
        for n in range(count):
            keep(n).wait()

    dma = pltpu.SemaphoreType.DMA
    vmem = pl.BlockSpec(memory_space=pltpu.VMEM)
    hbm = pl.BlockSpec(memory_space=pltpu.HBM)
    inputs = (heads, tokens, table, grad_out, weights)
    return pl.pallas_call(
        kernel,
        out_shape=(
            jax.ShapeDtypeStruct((nex, TOK_DEV, D), BF16),
            jax.ShapeDtypeStruct((nex, local, TOK_DEV), F32),
        )
        + tuple(jax.ShapeDtypeStruct(shape, kind) for shape, kind in OUTS_ROUTE),
        in_specs=[vmem] * len(inputs),
        out_specs=(hbm,) * (2 + count),
        scratch_shapes=[pltpu.VMEM(shape, kind) for shape, kind in OUTS_ROUTE]
        + [
            pltpu.VMEM((TOK_DEV, D), BF16),
            pltpu.VMEM((nex, local, TOK_DEV), F32),
            dma((nex - 1,)),
            dma((nex - 1,)),
            dma,
            dma((count,)),
        ]
        + RowGather(grid).scratch(),
        compiler_params=pltpu.CompilerParams(
            collective_id=4, has_side_effects=True, vmem_limit_bytes=60 * MIB
        ),
        name="route_rows",
    )(*inputs)


OUTS_ROUTE = (
    ((TOK_DEV, D), F32),
    ((TOK_DEV, MISC), F32),
    ((TOK_DEV, D), F32),
    ((TOK_DEV, D), F32),
    ((D, 3 * FF), BF16),
    ((D, TOK_DEV), BF16),
    ((D, MISC + D), BF16),
    ((8, D), F32),
)


def turn(values, cosine, sine):
    first, second = values[: HEAD_DIM // 2], values[HEAD_DIM // 2 :]
    return jnp.concatenate(
        [first * cosine - second * sine, second * cosine + first * sine], axis=0
    )


def allowed_mask(extent, block, length):
    keys = lax.broadcasted_iota(jnp.int32, (extent, QBLOCK), 0)
    queries = lax.broadcasted_iota(jnp.int32, (1, QBLOCK), 1) + block * QBLOCK
    return keys <= jnp.minimum(queries, length - 1)


def attend(grid, lengths, tok, table, cosine, sine, shard):
    units, length, ndp, nex = grid.units, tok.shape[1], grid.ndp, grid.nex
    blocks = length // QBLOCK
    chunk = 1
    ends = sorted(set(range(chunk - 1, units, chunk)) | {units - 1})

    def kernel(len_ref, tok_ref, table_ref, cos_ref, sin_ref, shard_ref,
               heads_ref, dense_ref, act_out, q_out, k_out, v_out, lse_out, w_out,
               act_ref, q_ref, k_ref, v_ref, lse_ref, w_ref, k_sem,
               buf, h_send, h_recv, h_loc, *dense_refs):
        i = pl.program_id(0)
        dp, ex = lax.axis_index("dp"), lax.axis_index("expert")
        unit = jnp.minimum(dp * units + i, UNITS_ALL - 1)
        head = lax.rem(unit, HEADS)
        slot = jnp.minimum(unit // HEADS - grid.first_series(dp), grid.slots - 1)
        slot = jnp.maximum(slot, 0)
        dense = DenseGather(grid)
        dense.bind(shard_ref, dense_ref, dense_refs)

        def keep():
            pairs = (
                (act_ref, act_out), (q_ref, q_out), (k_ref, k_out), (v_ref, v_out),
                (lse_ref, lse_out), (w_ref, w_out),
            )
            return [
                pltpu.make_async_copy(src, dst, k_sem.at[n]) for n, (src, dst) in enumerate(pairs)
            ]

        def heads_copy(d, n):
            begin = ends[n - 1] + 1 if n else 0
            count = ends[n] + 1 - begin
            target = lax.rem(dp + d, ndp)
            lanes = pl.ds(pl.multiple_of(target * SEG, SEG), SEG)
            return remote(
                buf.at[pl.ds(begin, count), :, lanes],
                heads_ref.at[dp, pl.ds(begin, count)],
                h_send.at[d - 1, n],
                h_recv.at[d - 1, n],
                (target, ex),
            )

        @pl.when(i == 0)
        def _():
            greet(
                [(lax.rem(dp + d, ndp), ex) for d in range(1, ndp)]
                + [(dp, lax.rem(ex + d, nex)) for d in range(1, nex)]
            )
            dense.start()
            w_ref[...] = dot(table_ref[:, : 3 * D + MISC], unpad_matrix(grid), 0, 1).astype(BF16)

        @pl.when((i == 0) | (head == 0))
        def _():
            residual = tok_ref[slot].astype(F32)
            scale = lax.rsqrt(jnp.mean(residual * residual, axis=-1, keepdims=True) + eps_norm)
            gain = w_ref[3 * D : 3 * D + ROW_PAD].astype(F32)[EXPERTS + 1 : EXPERTS + 2]
            act_ref[slot] = (residual * scale * gain).astype(BF16)

        cos, sin = cos_ref[...], sin_ref[...]
        w_rows = [
            w_ref[pl.ds(pl.multiple_of(n * D + head * HEAD_DIM, HEAD_DIM), HEAD_DIM)]
            for n in range(3)
        ]
        qkv = dot(jnp.concatenate(w_rows, axis=0), act_ref[slot], 1, 1)
        query = turn(qkv[:HEAD_DIM], cos, sin).astype(BF16)
        key_wide = turn(qkv[HEAD_DIM : 2 * HEAD_DIM], cos, sin)
        value = qkv[2 * HEAD_DIM :].astype(BF16)
        key_rows = key_wide.T.astype(BF16)
        q_ref[i], k_ref[i], v_ref[i] = query, key_wide.astype(BF16), value
        live = len_ref[unit // HEADS]
        for block in range(blocks):
            extent = QBLOCK * (block + 1)
            lanes = slice(QBLOCK * block, extent)
            scores = dot(key_rows[:extent], query[:, lanes]) * HEAD_DIM ** (-0.5)
            scores = jnp.where(allowed_mask(extent, block, live), scores, neg_fill)
            top = jnp.max(scores, axis=0, keepdims=True)
            probs = jnp.exp(scores - top)
            total = jnp.sum(probs, axis=0, keepdims=True)
            result = dot(value[:, :extent], probs.astype(BF16))
            buf[i, :, lanes] = (result * (1.0 / total)).astype(BF16)
            lse_ref[i, :, lanes] = top + jnp.log(total)

        for n, end in enumerate(ends):

            @pl.when(i == end)
            def _():
                for d in far_first(ndp):
                    heads_copy(d, n).start()

        pl.when(i == min(3, units - 1))(dense.pass_z)
        pl.when(i == min(5, units - 1))(dense.pass_y)

        @pl.when(i == units - 1)
        def _():
            mine = pltpu.make_async_copy(
                buf.at[:, :, pl.ds(pl.multiple_of(dp * SEG, SEG), SEG)], heads_ref.at[dp], h_loc
            )
            mine.start()
            for copy in keep():
                copy.start()
            dense.pass_x()
            dense.finish()
            for n in range(len(ends)):
                for d in range(1, ndp):
                    heads_copy(d, n).wait()
            mine.wait()
            for copy in keep():
                copy.wait()

    def whole(array):
        return pl.BlockSpec(
            array.shape, lambda i: (0,) * array.ndim, pipeline_mode=pl.Buffered(1)
        )

    feature = jax.ShapeDtypeStruct((units, HEAD_DIM, length), BF16)
    inputs = (tok, table, cosine, sine)
    dma = pltpu.SemaphoreType.DMA
    return pl.pallas_call(
        kernel,
        grid=(units,),
        out_shape=(
            jax.ShapeDtypeStruct((ndp, units, HEAD_DIM, SEG), BF16),
            jax.ShapeDtypeStruct((grid.ndev,) + shard.shape, BF16),
            jax.ShapeDtypeStruct((grid.slots, length, D), BF16),
            feature,
            feature,
            feature,
            jax.ShapeDtypeStruct((units, 1, length), F32),
            jax.ShapeDtypeStruct((3 * D + MISC, D), BF16),
        ),
        in_specs=[pl.BlockSpec(memory_space=pltpu.SMEM)]
        + [whole(v) for v in inputs]
        + [any_spec()],
        out_specs=(
            any_spec(),
            any_spec(),
        )
        + (pl.BlockSpec(memory_space=pltpu.HBM),) * 6,
        scratch_shapes=[
            pltpu.VMEM((grid.slots, length, D), BF16),
            pltpu.VMEM(feature.shape, BF16),
            pltpu.VMEM(feature.shape, BF16),
            pltpu.VMEM(feature.shape, BF16),
            pltpu.VMEM((units, 1, length), F32),
            pltpu.VMEM((3 * D + MISC, D), BF16),
            dma((6,)),
            pltpu.VMEM((units, HEAD_DIM, length), BF16),
            dma((ndp - 1, len(ends))),
            dma((ndp - 1, len(ends))),
            dma,
        ]
        + DenseGather(grid).scratch(),
        compiler_params=pltpu.CompilerParams(
            collective_id=1, has_side_effects=True, vmem_limit_bytes=60 * MIB
        ),
        cost_estimate=pl.CostEstimate(
            flops=units * length * length * HEAD_DIM * 2 * 8,
            bytes_accessed=8 * MIB,
            transcendentals=units * length * length,
        ),
        name="attend",
    )(lengths, *inputs, shard)


def attend_back(grid, lengths, tok, act, weights, query, key, value, lse, grad_heads, cosine, sine,
                early, routed, zs, tokens, mixed, grad_mixed, probs, lin, gains, shared):
    units, length, ndp, nex = grid.units, act.shape[1], grid.ndp, grid.nex
    blocks = length // QBLOCK
    scale = HEAD_DIM ** (-0.5)
    early_width, late_width = early.shape[1], 3 * D + MISC
    early_sum, late_sum = RowScatter(grid, early_width), RowScatter(grid, late_width)
    early = early.reshape(grid.nx, grid.nc, early_sum.rows, early_width)
    steps = [min(n, units - 1) for n in (0, 3)]
    works_z = [ShardScatter(grid, *v.shape[1:]) for v in zs]
    many = len(zs)

    def kernel(*refs):
        refs = list(refs)
        z_refs, z_outs = refs[20 : 20 + many], refs[23 + many : 23 + 2 * many]
        del refs[23 + many : 23 + 2 * many], refs[20 : 20 + many]
        (len_ref, tok_ref, act_ref, w_ref, q_ref, k_ref, v_ref, lse_ref, do_ref, cos_ref, sin_ref,
         early_ref, tokens_ref, mixed_ref, grad_mixed_ref, probs_ref, lin_ref, gains_ref, shared_ref,
         routed_ref,
         output_ref, grad_tokens_ref, table_ref,
         rows_out, early_out, late_out, routed_out,
         acc, back, dq, dk, dv, grads, gain, late_ref, b_send, b_recv, b_loc,
         early_spread, late_spread, r_send, r_recv) = refs[:42]
        at = 42
        for work, source, spread in (
            (early_sum, early_ref, early_spread),
            (late_sum, late_ref, late_spread),
        ):
            work.bind(spread)
            work.bind_x(source, refs[at : at + 5])
            work.bind_dp(refs[at + 5 : at + 7])
            at += 7
        for work, ref in zip(works_z, z_refs):
            work.bind_own(ref, refs[at : at + 2])
            work.bind_z(refs[at + 2 : at + 4])
            at += 4

        def routed_copy(step):
            return remote(
                routed_ref.at[step], routed_out.at[step], r_send.at[step], r_recv.at[step],
                (dp, lax.rem(ex + 1 + step, nex)),
            )

        i = pl.program_id(0)
        dp, ex = lax.axis_index("dp"), lax.axis_index("expert")
        unit = dp * units + i
        working = unit < UNITS_ALL
        series, head = unit // HEADS, lax.rem(unit, HEADS)
        slot = jnp.minimum(series - grid.first_series(dp), grid.slots - 1)

        def back_copy(d, which):
            target = lax.rem(dp + d, ndp)
            return remote(
                back.at[which, pl.ds(pl.multiple_of(target * SEG, SEG), SEG)],
                rows_out.at[dp, which],
                b_send.at[d - 1, which],
                b_recv.at[d - 1, which],
                (target, ex),
            )

        def back_local(which):
            return pltpu.make_async_copy(
                back.at[which, pl.ds(pl.multiple_of(dp * SEG, SEG), SEG)],
                rows_out.at[dp, which],
                b_loc.at[which],
            )

        @pl.when(i == 0)
        def _():
            greet(
                [(lax.rem(dp + d, ndp), ex) for d in range(1, ndp)]
                + [(dp, lax.rem(ex + d, nex)) for d in range(1, nex)]
            )
            for work in works_z:
                work.start_z()
            early_sum.start()
            grads[...] = jnp.zeros_like(grads)
            gain[...] = jnp.zeros_like(gain)

        @pl.when((i == 0) | (head == 0))
        def _():
            acc[...] = jnp.zeros_like(acc)

        @pl.when(working)
        def _():
            live = len_ref[series]
            query, key, value, grad = q_ref[i], k_ref[i], v_ref[i], do_ref[i]
            key_rows = key.astype(F32).T.astype(BF16)
            value_rows = value.astype(F32).T.astype(BF16)
            dk[...] = jnp.zeros_like(dk)
            dv[...] = jnp.zeros_like(dv)
            for block in range(blocks):
                extent = QBLOCK * (block + 1)
                lanes = slice(QBLOCK * block, extent)
                scores = dot(key_rows[:extent], query[:, lanes]) * scale
                scores = jnp.where(allowed_mask(extent, block, live), scores, neg_fill)
                probs = jnp.exp(scores - lse_ref[i, :, lanes])
                grad_probs = dot(value_rows[:extent], grad[:, lanes])
                delta = jnp.sum(probs * grad_probs, axis=0, keepdims=True)
                grad_scores = (probs * (grad_probs - delta)).astype(BF16)
                probs_low = probs.astype(BF16)
                dq[:, lanes] = dot(key[:, :extent], grad_scores)
                dk[:, :extent] += dot(query[:, lanes], grad_scores, 1, 1)
                dv[:, :extent] += dot(grad[:, lanes], probs_low, 1, 1)
            cos, sin = cos_ref[...], -sin_ref[...]
            stacked = jnp.concatenate(
                [
                    turn(dq[...] * scale, cos, sin),
                    turn(dk[...] * scale, cos, sin),
                    dv[...],
                ],
                axis=0,
            ).astype(BF16)
            weight_grads = dot(stacked, act_ref[slot]).astype(BF16)
            w_rows = []
            for n in range(3):
                at = pl.multiple_of(n * D + head * HEAD_DIM, HEAD_DIM)
                part = slice(n * HEAD_DIM, (n + 1) * HEAD_DIM)
                grads[pl.ds(at, HEAD_DIM)] = weight_grads[part]
                w_rows.append(w_ref[pl.ds(at, HEAD_DIM)])
            acc[...] += dot(stacked, jnp.concatenate(w_rows, axis=0), 0, 0)

        @pl.when(working & ((head == HEADS - 1) | (i == units - 1)))
        def _():
            share = acc[...]
            residual = tok_ref[slot].astype(F32)
            normed = residual * lax.rsqrt(
                jnp.mean(residual * residual, axis=-1, keepdims=True) + eps_norm
            )
            gain[...] += jnp.sum(share * normed, axis=0, keepdims=True)
            back[slot] = share.astype(BF16)
            for d in far_first(ndp):
                back_copy(d, slot).start()
            back_local(slot).start()

        @pl.when(i == steps[0])
        def _():
            early_sum.along_x()
            for step in range(nex - 1):
                routed_copy(step).start()

        @pl.when(i == steps[1])
        def _():
            early_sum.after_x()
            early_sum.along_dp()

        @pl.when(i == units - 1)
        def _():
            grads[3 * D :] = jnp.broadcast_to(gain[...], (ROW_PAD, D)).astype(BF16)
            late = dot(group_matrix(grid), grads[...], 1, 1).astype(BF16)
            late = late.reshape(late_ref.shape[:3] + (late.shape[1],))
            late_ref[:, :, :, : late.shape[3]] = late
            late_ref[:, :, :, late.shape[3] :] = jnp.zeros(
                late_ref.shape[:3] + (late_width - late.shape[3],), BF16
            )
            late_sum.start()
            early_sum.finish(early_out)
            late_sum.along_x()
            for step in range(nex - 1):
                routed_copy(step).wait()
            total = routed_ref[nex - 1].astype(F32)
            for step in range(nex - 1):
                total += routed_out[step].astype(F32)
            shared_gate = probs_ref[:, EXPERTS : EXPERTS + 1]
            output_ref[...] = (mixed_ref[...] + total + shared_gate * lin_ref[...]).astype(BF16)
            late_sum.after_x()
            late_sum.along_dp()
            for which in range(grid.slots):
                for d in range(1, ndp):

                    @pl.when(grid.holds(lax.rem(dp + ndp - d, ndp), which))
                    def _():
                        back_copy(d, which).wait_recv()

                @pl.when(grid.holds(dp, which))
                def _():
                    for d in range(1, ndp):
                        back_copy(d, which).wait_send()
                    back_local(which).wait()

            for n in range(SERIES_DEV):
                rows = slice(n * SEG, (n + 1) * SEG)
                grad_act = sum(
                    rows_out[owner, owned.index(n)].astype(F32)
                    for owner, owned in enumerate(grid.owned)
                    if n in owned
                )
                residual = tokens_ref[n].astype(F32)
                scale_one = lax.rsqrt(
                    jnp.mean(residual * residual, axis=-1, keepdims=True) + eps_norm
                )
                normed = residual * scale_one
                weighted = grad_act * gains_ref[1:2]
                inner = jnp.mean(weighted * normed, axis=-1, keepdims=True)
                grad_tokens_ref[rows] = grad_mixed_ref[rows] + scale_one * (
                    weighted - normed * inner
                )
            late_sum.finish(late_out)
            late, mid = late_out[...], early_out[...]
            misc = mid[:, D:]
            lane = lax.broadcasted_iota(jnp.int32, misc.shape, 1)
            wide = jnp.concatenate([shared_ref[...], jnp.zeros_like(misc)], axis=1)
            wide = pltpu.roll(wide, EXPERTS, 1)
            table_ref[:, : 3 * D] = late[:, : 3 * D]
            table_ref[:, 3 * D : 4 * D] = mid[:, :D]
            table_ref[:, 4 * D : 4 * D + MISC] = wide[:, :MISC] + jnp.where(
                lane < EXPERTS, misc, 0.0
            )
            table_ref[:, 4 * D + MISC : 4 * D + 3 * FF] = wide[:, MISC : 3 * FF]
            ends = jnp.where(lane == EXPERTS + 1, late[:, 3 * D :], misc)
            ends = jnp.where((lane >= EXPERTS) & (lane < EXPERTS + 3), ends, 0.0)
            table_ref[:, 4 * D + 3 * FF :] = wide[:, 3 * FF :] + ends
            for work, out in zip(works_z, z_outs):
                work.finish_z(out)

    def whole(array):
        return pl.BlockSpec(
            array.shape, lambda i: (0,) * array.ndim, pipeline_mode=pl.Buffered(1)
        )

    def whole_out(shape):
        return pl.BlockSpec(shape, lambda i: (0,) * len(shape))

    dma = pltpu.SemaphoreType.DMA
    inputs = (tok, act, weights, query, key, value, lse, grad_heads, cosine, sine, early, tokens, mixed,
              grad_mixed, probs, lin, gains, shared, routed)
    table_shape = (ROW_PAD, 4 * D + 3 * FF + MISC)
    return pl.pallas_call(
        kernel,
        grid=(units,),
        out_shape=(
            jax.ShapeDtypeStruct((TOK_DEV, D), BF16),
            jax.ShapeDtypeStruct((TOK_DEV, D), F32),
            jax.ShapeDtypeStruct(table_shape, F32),
        )
        + tuple(jax.ShapeDtypeStruct((work.rows, work.width), BF16) for work in works_z),
        in_specs=[pl.BlockSpec(memory_space=pltpu.SMEM)]
        + [whole(v) for v in inputs]
        + [any_spec()] * many,
        out_specs=(
            whole_out((TOK_DEV, D)),
            whole_out((TOK_DEV, D)),
            whole_out(table_shape),
        )
        + tuple(whole_out((work.rows, work.width)) for work in works_z),
        scratch_shapes=[
            pltpu.VMEM((ndp, grid.slots, SEG, D), BF16),
            pltpu.VMEM((ROW_PAD, early_width), F32),
            pltpu.VMEM((ROW_PAD, late_width), F32),
            pltpu.VMEM((nex - 1,) + routed.shape[1:], BF16),
            pltpu.VMEM((length, D), F32),
            pltpu.VMEM((grid.slots, length, D), BF16),
            pltpu.VMEM((HEAD_DIM, length), F32),
            pltpu.VMEM((HEAD_DIM, length), F32),
            pltpu.VMEM((HEAD_DIM, length), F32),
            pltpu.VMEM((3 * D + ROW_PAD, D), BF16),
            pltpu.VMEM((1, D), F32),
            pltpu.VMEM((grid.nx, grid.nc, late_sum.rows, late_width), BF16),
            dma((ndp - 1, grid.slots)),
            dma((ndp - 1, grid.slots)),
            dma((grid.slots,)),
            pltpu.VMEM(early_sum.spread_shape(), BF16),
            pltpu.VMEM(late_sum.spread_shape(), BF16),
            dma((nex - 1,)),
            dma((nex - 1,)),
        ]
        + early_sum.scratch_x()
        + early_sum.scratch_dp()
        + late_sum.scratch_x()
        + late_sum.scratch_dp()
        + sum((work.scratch_own() + work.scratch_z() for work in works_z), []),
        compiler_params=pltpu.CompilerParams(
            collective_id=3, has_side_effects=True, vmem_limit_bytes=60 * MIB
        ),
        cost_estimate=pl.CostEstimate(
            flops=units * length * length * HEAD_DIM * 2 * 20,
            bytes_accessed=12 * MIB,
            transcendentals=units * length * length,
        ),
        name="attend_back",
    )(lengths, *inputs, *zs)


def experts_step(grid, number, weights, act_all, cot_all, ranks, gates, before, early, ys, zs):
    nex, nc, ndp = grid.nex, grid.nc, grid.ndp
    rows = act_all.shape[1]
    local = EXPERTS // nex
    parts, wide = FF // D, FF // 2
    first, last = number == 0, number == local - 1
    batch = math.gcd(nex, 4)
    flushes = nex // batch
    steps = 2 * nex
    shard_rows = 3 * D // ndp
    inline = shard_rows % ROW_PAD == 0
    scatter = RowScatter(grid, 3 * FF) if first or last else None
    early_work = ShardScatter(grid, ROW_PAD, 3 * FF) if last else None
    works_y = [ShardScatter(grid, *v.shape[1:]) for v in ys]
    works_z = [ShardScatter(grid, *v.shape[1:]) for v in zs]
    work_own = ShardScatter(grid, shard_rows, wide) if inline else None
    if first:
        early = early.reshape(grid.nx, nc, scatter.rows, 3 * FF)

    def kernel(*refs):
        refs = list(refs)

        def take(count):
            taken = refs[:count]
            del refs[:count]
            return taken

        w_ref, act_ref, cot_ref, rank_ref, gate_ref = take(5)
        prev = take(3) if before is not None else None
        early_ref = take(1)[0] if scatter is not None else None
        y_refs, z_refs = take(len(ys)), take(len(zs))
        gin_ref, ggate_ref, routed_ref = take(3)
        early_out = take(1)[0] if scatter is not None else None
        own_outs = take(2)
        sum_outs = take(len(ys) + len(zs))
        xt_ref, dyt_ref, dg_ref, du_ref, hid_ref, down_ref = take(6)
        taken_ref, rows_ref, result_ref, back_ref, grad_ref, own_sem = take(6)
        acc_ref = take(1)[0] if flushes > 1 else None
        if last:
            gin_buf, ggate_buf, send, recv, loc = take(5)
        if first:
            scatter.bind_x(early_ref, take(len(scatter.scratch_x())))
        if scatter is not None:
            spread_ref = early_out if not last else take(1)[0] if first else early_ref
            scatter.bind(spread_ref)
        if last:
            early_work.bind_y(spread_ref, take(4))
            early_work.bind_z(take(2))
        for work, ref in zip(works_y, y_refs):
            work.bind_y(ref, take(4))
            work.bind_z(take(2))
        for work, ref in zip(works_z, z_refs):
            work.bind_own(ref, take(2))
            work.bind_z(take(2))
        if inline:
            work_own.bind_y(grad_ref.at[0], take(4))
        t = pl.program_id(0)
        half, part = lax.rem(t // batch, 2), lax.rem(t, batch)
        s = (t // (2 * batch)) * batch + part
        dp, ex = lax.axis_index("dp"), lax.axis_index("expert")

        def copies(step):
            target = lax.rem(ex + 1 + step, nex)
            pairs = (
                (gin_buf.at[step], gin_ref.at[step]),
                (ggate_buf.at[step], ggate_ref.at[ex]),
            )
            return [
                remote(src, dst, send.at[step, n], recv.at[step, n], (dp, target))
                for n, (src, dst) in enumerate(pairs)
            ]

        @pl.when(t == 0)
        def _():
            greet(
                [(dp, lax.rem(ex + d, nex)) for d in range(1, nex)]
                + [(lax.rem(dp + d, ndp), ex) for d in range(1, ndp)]
            )
            for work in works_y:
                work.start_y()
            for work in works_z:
                work.start_z()
            if first:
                scatter.start()
            elif last:
                early_work.start_y()
            for n in range(parts):
                lanes = slice(n * D, (n + 1) * D)
                down_ref[lanes] = w_ref[2 * D : 3 * D, lanes]

        rank = rank_ref[0, number : number + 1, :]
        slot_down = lax.broadcasted_iota(jnp.int32, (CAP, rows), 0).astype(F32)
        pick = slot_down == rank
        gate_row = gate_ref[0, number : number + 1, :]
        gate = jnp.sum(jnp.where(pick, gate_row, 0.0), axis=1, keepdims=True)
        block = pl.ds(pl.multiple_of(part * CAP, CAP), CAP)

        @pl.when(half == 0)
        def _():
            pick_low = pick.astype(F32).astype(BF16)
            picked = dot(pick_low, jnp.concatenate([act_ref[0], cot_ref[0]], axis=1))
            taken_ref[part] = picked[:, :D].astype(BF16)
            rows_ref[part] = picked[:, D:].astype(BF16)
            xt_ref[:, block] = picked[:, :D].T.astype(BF16)
            dyt_ref[:, block] = (gate * picked[:, D:]).T.astype(BF16)

        taken, grad_rows = taken_ref[part], rows_ref[part].astype(F32)
        grad_result = (gate * grad_rows).astype(BF16)
        lanes = pl.ds(pl.multiple_of(half * wide, wide), wide)
        w_gate, w_up, w_down = w_ref[0:D, lanes], w_ref[D : 2 * D, lanes], down_ref[lanes]
        gate_lin = dot(taken, w_gate)
        up_lin = dot(taken, w_up)
        sig = 0.5 * jnp.tanh(0.5 * gate_lin) + 0.5
        silu = gate_lin * sig
        hidden = (silu * up_lin).astype(BF16)
        result = dot(hidden, w_down)
        grad_hidden = dot(grad_result, w_down, 1, 1)
        grad_gate = (grad_hidden * up_lin * (sig + silu * (1.0 - sig))).astype(BF16)
        grad_up = (grad_hidden * silu).astype(BF16)
        hid_ref[block], dg_ref[block], du_ref[block] = hidden, grad_gate, grad_up
        grad_taken = dot(grad_gate, w_gate, 1, 1) + dot(grad_up, w_up, 1, 1)

        @pl.when(half == 0)
        def _():
            result_ref[part], back_ref[part] = result, grad_taken

        @pl.when(half == 1)
        def _():
            out = (result_ref[part] + result).astype(BF16).astype(F32)
            grad_gate_slot = jnp.sum(grad_rows * out, axis=1, keepdims=True)
            grad_gate_row = jnp.sum(jnp.where(pick, grad_gate_slot, 0.0), axis=0, keepdims=True)
            rank_column = jnp.broadcast_to(rank, (8, rows)).T[:, :1]
            slot_across = lax.broadcasted_iota(jnp.int32, (rows, CAP), 1).astype(F32)
            spread = (slot_across == rank_column).astype(F32).astype(BF16)
            both = jnp.concatenate([gate * out, back_ref[part] + grad_taken], axis=1)
            both = dot(spread, both.astype(BF16))
            routed, grad_in = both[:, :D], both[:, D:]
            if prev is not None:
                grad_in += prev[0][0]
                routed += prev[2][0]
            if last:
                routed_ref[0] = routed.astype(BF16)
                gin_buf[s] = grad_in.astype(BF16)
                if prev is not None:
                    ggate_buf[s, 0:number] = prev[1][0]
                ggate_buf[s, number : number + 1] = grad_gate_row
            else:
                routed_ref[0] = routed
                gin_ref[0] = grad_in
                if prev is not None:
                    ggate_ref[0, 0:number] = prev[1][0]
                ggate_ref[0, number : number + 1] = grad_gate_row

        if last:

            @pl.when((half == 1) & (s < nex - 1))
            def _():
                for copy in copies(s):
                    copy.start()

        if first:

            @pl.when(t == 1)
            def _():
                scatter.along_x()

            @pl.when(t == nex + 2)
            def _():
                scatter.after_x()
                if last:
                    early_work.start_y()

        if last:

            @pl.when(t == (steps - 1 if first else nex + 1))
            def _():
                early_work.sum_y()
                early_work.start_z()

        @pl.when(t == nex)
        def _():
            for work in works_y:
                work.sum_y()
                work.start_z()

        def weight_grads(flush, which):
            def put(at, lanes, value):
                if flush:
                    value += acc_ref[which, at : at + D, lanes]
                if flush < flushes - 1:
                    acc_ref[which, at : at + D, lanes] = value
                else:
                    grad_ref[which, at : at + D, lanes] = value.astype(BF16)

            every = slice(0, wide)
            put(0, every, dot(xt_ref[...], dg_ref[...]))
            put(D, every, dot(xt_ref[...], du_ref[...]))
            down = dot(dyt_ref[...], hid_ref[...])
            for n in range(0, wide, D):
                put(2 * D, slice(n, n + D), down[:, n : n + D].T)

        def keep(which):
            return pltpu.make_async_copy(grad_ref.at[which], own_outs[which], own_sem.at[which])

        for flush in range(flushes):
            for which in range(2):
                end = (2 * flush + which + 1) * batch - 1
                pl.when(t == end)(functools.partial(weight_grads, flush, which))

        @pl.when(t == steps - batch - 1)
        def _():
            if inline:
                work_own.start_y()
            else:
                keep(0).start()

        @pl.when(t == steps - 1)
        def _():
            keep(1).start()
            own = []
            if last:
                own = [
                    pltpu.make_async_copy(src, dst, loc.at[n])
                    for n, (src, dst) in enumerate(
                        (
                            (gin_buf.at[nex - 1], gin_ref.at[nex - 1]),
                            (ggate_buf.at[nex - 1], ggate_ref.at[ex]),
                        )
                    )
                ]
                for copy in own:
                    copy.start()
            if inline:
                work_own.store_y(own_outs[0])
            else:
                keep(0).wait()
            for work, out in zip(works_y + works_z, sum_outs):
                work.finish_z(out)
            if last:
                early_work.finish_z(early_out)
                for step in range(nex - 1):
                    for copy in copies(step):
                        copy.wait()
                for copy in own:
                    copy.wait()
            keep(1).wait()

    def source(t):
        return (t // (2 * batch)) * batch + t % batch

    def early_source(t):
        half = (t // batch) % 2
        return (t // (2 * batch)) * batch + (1 - half) * (t % batch) + half * (batch - 1)

    def late_source(t):
        return (t // (2 * batch)) * batch + ((t // batch) % 2) * (t % batch)

    def per_source(which, *tail):
        return pl.BlockSpec((1,) + tail, lambda t: (which(t),) + (0,) * len(tail))

    def whole(shape):
        return pl.BlockSpec(shape, lambda t: (0,) * len(shape), pipeline_mode=pl.Buffered(1))

    def whole_out(shape):
        return pl.BlockSpec(shape, lambda t: (0,) * len(shape))

    dma = pltpu.SemaphoreType.DMA
    kind = BF16 if last else F32
    inputs = [weights, act_all, cot_all, ranks, gates]
    in_specs = [
        whole(weights.shape),
        per_source(early_source, rows, D),
        per_source(early_source, rows, D),
        per_source(source, local, rows),
        per_source(source, local, rows),
    ]
    out_shape = [
        jax.ShapeDtypeStruct((nex, rows, D), kind),
        jax.ShapeDtypeStruct((nex, number + 1, rows), F32),
        jax.ShapeDtypeStruct((nex, rows, D), kind),
    ]
    out_specs = [
        any_spec() if last else per_source(late_source, rows, D),
        any_spec() if last else per_source(late_source, number + 1, rows),
        per_source(late_source, rows, D),
    ]
    scratch = [
        pltpu.VMEM((D, batch * CAP), BF16),
        pltpu.VMEM((D, batch * CAP), BF16),
        pltpu.VMEM((batch * CAP, wide), BF16),
        pltpu.VMEM((batch * CAP, wide), BF16),
        pltpu.VMEM((batch * CAP, wide), BF16),
        pltpu.VMEM((FF, D), BF16),
        pltpu.VMEM((batch, CAP, D), BF16),
        pltpu.VMEM((batch, CAP, D), BF16),
        pltpu.VMEM((batch, CAP, D), F32),
        pltpu.VMEM((batch, CAP, D), F32),
        pltpu.VMEM((2, 3 * D, wide), BF16),
        dma((2,)),
    ]
    if before is not None:
        inputs += list(before)
        in_specs += [
            per_source(late_source, rows, D),
            per_source(late_source, number, rows),
            per_source(late_source, rows, D),
        ]
    if scatter is not None:
        inputs.append(early)
        in_specs.append(whole(early.shape))
        shape = (ROW_PAD, 3 * FF) if last else scatter.spread_shape()
        out_shape.append(jax.ShapeDtypeStruct(shape, F32 if last else BF16))
        out_specs.append(whole_out(shape))
    inputs += list(ys) + list(zs)
    in_specs += [any_spec()] * (len(ys) + len(zs))
    own_shape = (grid.nz, shard_rows, wide) if inline else (3 * D, wide)
    for shape in (own_shape, (3 * D, wide)):
        out_shape.append(jax.ShapeDtypeStruct(shape, BF16))
        out_specs.append(any_spec())
    for work in works_y + works_z:
        out_shape.append(jax.ShapeDtypeStruct((work.rows, work.width), BF16))
        out_specs.append(whole_out((work.rows, work.width)))
    if flushes > 1:
        scratch.append(pltpu.VMEM((2, 3 * D, wide), F32))
    if last:
        scratch += [
            pltpu.VMEM((nex, rows, D), BF16),
            pltpu.VMEM((nex, local, rows), F32),
            dma((nex - 1, 2)),
            dma((nex - 1, 2)),
            dma((2,)),
        ]
    if first:
        scratch += scatter.scratch_x()
    if first and last:
        scratch.append(pltpu.VMEM(scatter.spread_shape(), BF16))
    if last:
        scratch += early_work.scratch_y() + early_work.scratch_z()
    for work in works_y:
        scratch += work.scratch_y() + work.scratch_z()
    for work in works_z:
        scratch += work.scratch_own() + work.scratch_z()
    if inline:
        scratch += work_own.scratch_y()
    results = pl.pallas_call(
        kernel,
        grid=(steps,),
        out_shape=tuple(out_shape),
        in_specs=in_specs,
        out_specs=tuple(out_specs),
        scratch_shapes=scratch,
        compiler_params=pltpu.CompilerParams(
            vmem_limit_bytes=62 * MIB, collective_id=5 + number, has_side_effects=True
        ),
        cost_estimate=pl.CostEstimate(
            flops=nex * CAP * D * FF * 2 * 11,
            bytes_accessed=25 * MIB,
            transcendentals=nex * CAP * FF,
        ),
        name="experts_step",
    )(*inputs)
    results = list(results)
    sums = results[:3]
    del results[:3]
    if scatter is not None:
        early = results.pop(0)
    return sums, early, results[:2], results[2:]


def middle_step(grid, gin, ggate, mixed, probs, lin, gact, act_across, heads, grad_out, small, gain, ys,
                zs):
    ndp, nex, units = grid.ndp, grid.nex, grid.units
    local = EXPERTS // nex
    works_y = [ShardScatter(grid, *v.shape[1:]) for v in ys]
    works_z = [ShardScatter(grid, *v.shape[1:]) for v in zs]

    def kernel(gin_ref, ggate_ref, mixed_ref, probs_ref, lin_ref, gact_ref, across_ref, heads_ref,
               go_ref, small_ref, gain_ref, *refs):
        refs = list(refs)

        def take(count):
            taken = refs[:count]
            del refs[:count]
            return taken

        y_refs, z_refs = take(len(ys)), take(len(zs))
        dst, grad_mixed_ref, middle_ref = take(3)
        y_outs, z_outs = take(len(ys)), take(len(zs))
        flipped, buf, send, recv, loc = take(5)
        for work, ref in zip(works_y, y_refs):
            work.bind_y(ref, take(4))
        for work, ref in zip(works_z, z_refs):
            work.bind_own(ref, take(2))
            work.bind_z(take(2))
        dp, ex = lax.axis_index("dp"), lax.axis_index("expert")
        greet([(lax.rem(dp + d, ndp), ex) for d in range(1, ndp)])
        for work in works_y:
            work.start_y()
        for work in works_z:
            work.start_z()

        grad_out = go_ref[...].astype(F32)
        probs = probs_ref[...]
        shared_gate = probs[:, EXPERTS : EXPERTS + 1]
        flipped[...] = jnp.zeros_like(flipped)
        for n in range(nex):
            flipped[n * local : (n + 1) * local] = ggate_ref[n]
        grad_probs = flipped[...].T
        lane = lax.broadcasted_iota(jnp.int32, probs.shape, 1)
        inner = jnp.sum(
            jnp.where(lane < EXPERTS, probs * grad_probs, 0.0), axis=1, keepdims=True
        )
        svec = shared_gate * (1.0 - shared_gate)
        svec = svec * jnp.sum(grad_out * lin_ref[...], axis=1, keepdims=True)
        grad_misc = jnp.where(
            lane < EXPERTS,
            probs * (grad_probs - inner),
            jnp.where(lane == EXPERTS, svec, 0.0),
        ).astype(BF16)
        grad_act = gact_ref[...] + dot(grad_misc, small_ref[:, :MISC], 1, 1)
        for n in range(nex):
            grad_act += gin_ref[n].astype(F32)
        mixed = mixed_ref[...]
        scale = lax.rsqrt(jnp.mean(mixed * mixed, axis=-1, keepdims=True) + eps_norm)
        normed = mixed * scale
        gain_grad = jnp.sum(grad_act * normed, axis=0, keepdims=True)
        weighted = grad_act * gain_ref[2:3]
        grad_mixed = grad_out + scale * (
            weighted - normed * jnp.mean(weighted * normed, axis=-1, keepdims=True)
        )
        grad_mixed_ref[...] = grad_mixed
        grad_low = grad_mixed.astype(BF16)
        for s in range(SERIES_DEV):
            rows = slice(s * SEG, (s + 1) * SEG)
            grad = dot(small_ref[:, MISC:], grad_low[rows], 1, 1).astype(BF16)
            buf[s * HEADS : (s + 1) * HEADS] = grad.reshape(HEADS, HEAD_DIM, SEG)
        if units * ndp > UNITS_ALL:
            buf[UNITS_ALL:] = jnp.zeros((units * ndp - UNITS_ALL, HEAD_DIM, SEG), BF16)
        lanes = pl.ds(pl.multiple_of(dp * SEG, SEG), SEG)
        copies = []
        for d in far_first(ndp):
            target = lax.rem(dp + d, ndp)
            copy = remote(
                buf.at[pl.ds(target * units, units)], dst.at[:, :, lanes],
                send.at[d - 1], recv.at[d - 1], (target, ex),
            )
            copy.start()
            copies.append(copy)
        copy = pltpu.make_async_copy(
            buf.at[pl.ds(dp * units, units)], dst.at[:, :, lanes], loc
        )
        copy.start()
        copies.append(copy)
        group = group_matrix(grid)
        total = jnp.zeros((D, D), F32)
        for s in range(SERIES_DEV):
            attn = heads_ref[s * HEADS : (s + 1) * HEADS].reshape(D, SEG)
            attn = dot(group, attn).astype(BF16)
            total += dot(attn, grad_low[s * SEG : (s + 1) * SEG])
        middle_ref[:, :D] = total.astype(BF16)
        gain_rows = jnp.broadcast_to(gain_grad, (MISC, D)).astype(BF16)
        gain_column = dot(group, gain_rows, 1, 1)
        misc_grad = dot(across_ref[...], grad_misc)
        lane = lax.broadcasted_iota(jnp.int32, misc_grad.shape, 1)
        misc_grad = jnp.where(lane == EXPERTS + 2, gain_column, misc_grad)
        middle_ref[:, D:] = misc_grad.astype(BF16)
        for work, out in zip(works_y, y_outs):
            work.store_y(out)
        for copy in copies:
            copy.wait()
        for work, out in zip(works_z, z_outs):
            work.finish_z(out)

    dma = pltpu.SemaphoreType.DMA
    vmem = pl.BlockSpec(memory_space=pltpu.VMEM)
    hbm = pl.BlockSpec(memory_space=pltpu.HBM)
    inputs = [gin, ggate, mixed, probs, lin, gact, act_across, heads, grad_out, small, gain]
    in_specs = [vmem] * len(inputs) + [any_spec()] * (len(ys) + len(zs))
    out_shape = [
        jax.ShapeDtypeStruct((units, HEAD_DIM, SEG * ndp), BF16),
        jax.ShapeDtypeStruct((TOK_DEV, D), F32),
        jax.ShapeDtypeStruct((D, D + MISC), BF16),
    ]
    out_specs = [any_spec(), vmem, vmem]
    scratch = [
        pltpu.VMEM((MISC, TOK_DEV), F32),
        pltpu.VMEM((units * ndp, HEAD_DIM, SEG), BF16),
        dma((ndp - 1,)),
        dma((ndp - 1,)),
        dma,
    ]
    inputs += list(ys) + list(zs)
    for work in works_y:
        out_shape.append(jax.ShapeDtypeStruct((grid.nz, work.rows, work.width), BF16))
        out_specs.append(hbm)
        scratch += work.scratch_y()
    for work in works_z:
        out_shape.append(jax.ShapeDtypeStruct((work.rows, work.width), BF16))
        out_specs.append(vmem)
        scratch += work.scratch_own() + work.scratch_z()
    return pl.pallas_call(
        kernel,
        out_shape=tuple(out_shape),
        in_specs=in_specs,
        out_specs=tuple(out_specs),
        scratch_shapes=scratch,
        compiler_params=pltpu.CompilerParams(
            collective_id=2, has_side_effects=True, vmem_limit_bytes=60 * MIB
        ),
        name="middle_step",
    )(*inputs)


def local(
    tokens,
    cotangent,
    lengths,
    routes,
    dense_weights,
    dense_first,
    dense_second,
    dense_average,
    expert_weights,
    expert_first,
    expert_second,
    expert_average,
):
    ndp, nex = lax.axis_size("dp"), lax.axis_size("expert")
    dp, ex = lax.axis_index("dp"), lax.axis_index("expert")
    grid = Grid(ndp, nex)
    local_experts = EXPERTS // nex
    length = SEG * ndp
    rows_dev = D // grid.ndev
    shard_rows = 3 * D // ndp

    spot = jnp.arange(FF, dtype=jnp.int32)
    order = (FF // D) * (spot % D) + spot // D
    mix = (spot[:, None] == order[None, :]).astype(BF16)
    shard_row = dp * shard_rows + jnp.arange(shard_rows, dtype=jnp.int32)
    is_down = (shard_row >= 2 * D)[None, :, None]
    expert_low = expert_weights.astype(BF16).reshape(local_experts, shard_rows, FF)
    mixed_low = jnp.einsum(
        "erf,fg->erg", expert_low, mix, preferred_element_type=F32
    ).astype(BF16)
    expert_send = jnp.where(is_down, expert_low, mixed_low)
    table = dense_weights.astype(BF16).reshape(rows_dev, -1)
    after = 4 * D + EXPERTS

    def padded(*columns):
        return jnp.pad(jnp.concatenate(columns, axis=1), ((0, ROW_PAD - rows_dev), (0, 0)))

    shard_first = padded(
        table[:, : 3 * D],
        table[:, 4 * D : after],
        table[:, after + 3 * FF :],
        jnp.zeros((rows_dev, MISC - EXPERTS - 3), BF16),
        table[:, 3 * D : 4 * D],
    )
    shard_rest = padded(table[:, after : after + 3 * FF])

    names = jnp.arange(EXPERTS, dtype=jnp.int32)
    routes_rows = routes.reshape(TOK_DEV, TOP)
    member = (routes_rows[:, :, None] == names[None, None, :]).any(axis=1)
    before = jnp.arange(TOK_DEV)
    earlier = (before[None, :] < before[:, None]).astype(BF16)
    count = jnp.dot(earlier, member.astype(BF16), preferred_element_type=F32)
    ranks = jnp.where(member, count, -1.0).T.reshape(nex, local_experts, TOK_DEV)

    local_pos = dp * SEG + jnp.arange(SEG, dtype=jnp.int32)
    live = (local_pos[None, :] < lengths[:, None]).astype(F32)
    grad_out_low = (cotangent.astype(F32) * live[..., None]).astype(BF16).reshape(TOK_DEV, D)

    tok_all, dense_all, cot_all, rank_all = first_exchange(
        grid, tokens, shard_first, grad_out_low, ranks
    )
    expert_all = [
        lax.all_gather(expert_send[e], "dp", axis=0, tiled=True) for e in range(local_experts)
    ]
    tok_all = tok_all.reshape(grid.slots, length, D)

    dense_all = dense_all.reshape(grid.ndev * ROW_PAD, -1)

    half = HEAD_DIM // 2
    inverse = rope_base ** (-jnp.arange(half, dtype=F32) * 2.0 / HEAD_DIM)
    angles = inverse[:, None] * jnp.arange(length, dtype=jnp.int32).astype(F32)[None, :]
    cosine, sine = jnp.cos(angles), jnp.sin(angles)
    heads_here, rest, act_one, query, key, value, lse, qkv_rows = attend(
        grid, lengths, tok_all, dense_all, cosine, sine, shard_rest
    )
    heads_here = heads_here.reshape(-1, HEAD_DIM, SEG)[:UNITS_ALL]

    (act_all, gates_all, mixed_rows, probs, shared_lin, grad_act_shared, early, act_across, small,
     gains) = route_rows(
        grid, heads_here, tokens, dense_all, grad_out_low, rest.reshape(grid.ndev * ROW_PAD, -1)
    )
    before, ys, zs, halves = None, [], [], []
    for e in range(local_experts):
        before, early, own, sums = experts_step(
            grid, e, expert_all[e], act_all, cot_all, rank_all, gates_all, before, early, ys, zs
        )
        halves += sums[::-1] if zs else sums
        ys = [v.reshape(ndp, shard_rows, FF // 2) for v in own if v.ndim == 2]
        zs = [v for v in own if v.ndim == 3]
    gin_back, ggate_back, routed_parts = before

    grad_heads, grad_mixed, middle, *more = middle_step(
        grid, gin_back, ggate_back, mixed_rows, probs, shared_lin, grad_act_shared, act_across,
        heads_here, grad_out_low, small, gains, ys, zs,
    )
    halves += more[len(ys) :]

    output, grad_tokens, dense_table, *sums = attend_back(
        grid, lengths, tok_all, act_one, qkv_rows, query, key, value, lse, grad_heads, cosine, sine,
        middle, routed_parts, more[: len(ys)], tokens, mixed_rows, grad_mixed, probs, shared_lin, gains, early,
    )
    dense_grad = dense_table[:rows_dev, : dense_weights.shape[0] // rows_dev].reshape(-1)
    halves += sums
    expert_sums = jnp.stack(
        [jnp.concatenate(halves[e : e + 2], axis=1) for e in range(0, 2 * local_experts, 2)]
    )
    unmixed = jnp.einsum("erg,fg->erf", expert_sums, mix, preferred_element_type=F32)
    expert_grad = jnp.where(is_down, expert_sums.astype(F32), unmixed)
    expert_grad = expert_grad.reshape(expert_weights.shape)

    dense_first_new, dense_second_new, dense_new, dense_average_new = adamw_update(
        dense_weights, dense_grad, dense_first, dense_second, dense_average
    )
    expert_first_new, expert_second_new, expert_new, expert_average_new = adamw_update(
        expert_weights, expert_grad, expert_first, expert_second, expert_average
    )
    return (
        output.reshape(tokens.shape),
        grad_tokens.reshape(tokens.shape),
        dense_grad,
        dense_first_new,
        dense_second_new,
        dense_new,
        dense_average_new,
        expert_grad,
        expert_first_new,
        expert_second_new,
        expert_new,
        expert_average_new,
    )


def solution(mesh):
    rows = P("expert", "dp", None)
    dense = P(("dp", "expert"))
    experts = P("expert", "dp")
    return jax.shard_map(
        local,
        mesh=mesh,
        in_specs=(
            (rows, rows, P("expert"), P("dp", "expert", None, None)) + (dense,) * 4 + (experts,) * 4
        ),
        out_specs=(rows, rows) + (dense,) * 5 + (experts,) * 5,
        check_vma=False,
    )
```
